32 devices in a mesh: gx: 4 (over y, core), gy: 2 (over x), gz: 4 (over z).
Axes of the slice: x: 2, y: 2, z: 4, core: 2. Of those that a mesh axis runs over, the one named last changes fastest.
Arguments:
- rhs: float32 [4, 2, 4, 2, 64, 256], P('gx', 'gy', 'gz'), may hold values from -6 to 6
- viscosity: float32 [4, 2, 4, 64], P('gx', 'gy', 'gz'), may hold values from 0.3 to 3
- counts: int32 [4, 2, 4], P('gx', 'gy', 'gz'), may hold values from 8 to 64, as said below
- neighbours: int32 [4, 2, 4, 16], P('gx', 'gy', 'gz'), may hold values from -1 to 3, as said below
- face_index: int32 [4, 2, 4, 16, 512], P('gx', 'gy', 'gz'), may hold values from 0 to 16383, as said below
- k_matrix: float32 [256, 256], replicated, may hold values from -0.04 to 1.04, as said below
- p_matrix: float32 [256, 256], replicated, may hold values from -0.04 to 1.04, as said below
Outputs:
- solution: float32 [4, 2, 4, 2, 64, 256], P('gx', 'gy', 'gz')
The draws below stay inside these ranges and needn't reach their ends.
Inputs may be any that keep to these rules, and one draw needn't show every extreme that they name: `counts`: in every gz group some partition has exactly 64 live elements. `neighbours`: each list names distinct partitions of the same gz group in increasing order, followed by -1 entries; the relation is symmetric and no partition names itself. `face_index`: every index lies within the live elements of its partition, that is below 256 times counts. `k_matrix`: the identity plus independent entries. `p_matrix`: the identity plus independent entries.
All inputs are finite; a program needn't handle non-finite values.
Results may differ from the reference program's by a relative error of at most 0.0003.
Values sent between devices are 32-bit elements; how exact they have to be, the bound alone decides.
No kernel may reach another device: no remote copies, remote signals or barrier semaphores. Data moves between devices by JAX's collectives and lax.ppermute only.
A program may use at most 64 MiB of HBM per device.

```python
import math
import jax
import jax.numpy as jnp
from jax import lax

E_DEV = 64
EDOF = 256
PROBES = 2
NBR = 16
FACE = 512
N_GX = 4
N_GY = 2
N_GZ = 4


def draw_block(key, salt):
    noise = jax.random.uniform(jax.random.fold_in(key, salt), (EDOF, EDOF), jnp.float32, -0.0325, 0.0325)
    return jnp.eye(EDOF, dtype=jnp.float32) + noise


def draw_k_matrix(key, part):
    return draw_block(key, 101)


def draw_p_matrix(key, part):
    return draw_block(key, 202)


def live_counts(key):
    inner_key = jax.random.fold_in(key, 303)
    shifts = jax.random.randint(jax.random.fold_in(inner_key, 1), (N_GX, N_GY, N_GZ), 0, 4)
    chosen = jax.random.randint(jax.random.fold_in(inner_key, 2), (N_GX, N_GY, 1), 0, N_GZ)
    places = jnp.arange(N_GZ, dtype=jnp.int32)[None, None, :]
    shifts = jnp.where(places == chosen, 0, shifts)
    return (E_DEV // jnp.left_shift(jnp.ones_like(shifts), shifts)).astype(jnp.int32)


def draw_counts(key, part):
    return live_counts(key)


def draw_face_index(key, part):
    bounds = (live_counts(key) * EDOF)[:, :, :, None, None]
    return jax.random.randint(jax.random.fold_in(key, 404), (N_GX, N_GY, N_GZ, NBR, FACE), 0, bounds).astype(jnp.int32)


def group_links(key):
    members = N_GZ
    adjacency = jnp.zeros((members, members), jnp.int32)
    cycles = max(1, min(NBR // 2, members // 4))
    for turn in range(cycles):
        order = jax.random.permutation(jax.random.fold_in(key, turn), members)
        after = jnp.roll(order, -1)
        adjacency = adjacency.at[order, after].set(1)
        adjacency = adjacency.at[after, order].set(1)
    columns = jnp.arange(members, dtype=jnp.int32)
    scores = (1 - adjacency) * members + columns[None, :]
    ranked = jnp.argsort(scores, axis=1, stable=True).astype(jnp.int32)
    keep = min(members, NBR)
    ranked = jnp.pad(ranked[:, :keep], ((0, 0), (0, NBR - keep)), constant_values=-1)
    degree = jnp.sum(adjacency, axis=1)
    slots = jnp.arange(NBR, dtype=jnp.int32)
    return jnp.where(slots[None, :] < degree[:, None], ranked, -1).astype(jnp.int32)


def draw_neighbours(key, part):
    keys = jax.random.split(jax.random.fold_in(key, 505), N_GX * N_GY)
    return jax.vmap(group_links)(keys).reshape(N_GX, N_GY, N_GZ, NBR)


def shard_levels(own_key, extent, cuts, least, top_value):
    def one(position, shards_of):
        heights = jax.random.uniform(jax.random.fold_in(jax.random.fold_in(own_key, 6), position), (shards_of,), jnp.float32, least / len(cuts), top_value / len(cuts))
        return jnp.repeat(jnp.exp(heights), extent[position] // shards_of).reshape((-1,) + (1,) * (len(extent) - position - 1))

    gain = one(*cuts[0])
    for cut in cuts[1:]:
        gain = gain * one(*cut)
    return gain


def bell_draw(rng, extent, spread, limit, pieces=(), kind=jnp.bfloat16):
    entries = spread * jax.random.normal(rng, extent, jnp.float32)
    if pieces:
        entries = entries * shard_levels(rng, extent, pieces, -0.22, 0.18)
    return jnp.clip(entries, -limit, limit).astype(kind)


def setup_inputs(seed: int = 0) -> dict:
    arg_keys = jax.random.split(jax.random.key(seed), 8)
    return {
        "rhs": bell_draw(arg_keys[0], (N_GX, N_GY, N_GZ, PROBES, E_DEV, EDOF), 1.0, 6.0, ((0, 4), (1, 2), (2, 4)), jnp.float32),
        "viscosity": jnp.clip(jnp.exp(math.log(3.0) - 2.3025851 * jax.random.uniform(arg_keys[1], (N_GX, N_GY, N_GZ, E_DEV), jnp.float32) ** shard_levels(arg_keys[1], (N_GX, N_GY, N_GZ, E_DEV), ((0, 4), (1, 2), (2, 4)), -0.2, 0.2)), 0.3, 3.0),
        "counts": draw_counts(jax.random.fold_in(arg_keys[7], 71), 0),
        "neighbours": draw_neighbours(jax.random.fold_in(arg_keys[7], 71), 0),
        "face_index": draw_face_index(jax.random.fold_in(arg_keys[7], 71), 0),
        "k_matrix": draw_k_matrix(jax.random.fold_in(arg_keys[7], 71), 0),
        "p_matrix": draw_p_matrix(jax.random.fold_in(arg_keys[7], 71), 0),
    }


coupling = 0.5
largest_rank = lax.Precision.HIGHEST


def per_element(vector, matrix):
    shaped = vector.shape
    product = jnp.dot(vector.reshape(-1, shaped[-1]), matrix, precision=largest_rank, preferred_element_type=jnp.float32)
    return product.reshape(shaped)


def face_term(vector, links, blocks):
    members, probes, elements, dofs = vector.shape
    flat_vec = vector.reshape(members, probes, elements * dofs)

    def take_faces(row_vals, index):
        return row_vals[:, index.reshape(-1)].reshape(probes, index.shape[0], index.shape[1])

    departing_rows = jax.vmap(take_faces)(flat_vec, blocks)
    sources = jnp.arange(members, dtype=jnp.int32)
    connected_parts = (links[:, :, None] == sources[None, None, :]).astype(jnp.float32)
    received_rows = jnp.einsum("bon,nlb,nzla->bzoa", connected_parts, connected_parts, departing_rows, precision=largest_rank)

    def place(value_list, index):
        empty = jnp.zeros((probes, elements * dofs), jnp.float32)
        return empty.at[:, index.reshape(-1)].add(value_list.reshape(probes, -1))

    placed = jax.vmap(place)(received_rows, blocks)
    return placed.reshape(vector.shape)


def group_pass(group, k_matrix, p_matrix):
    vector, visc, live_count, links, blocks = group
    elements = vector.shape[2]
    live_mask = (jnp.arange(elements, dtype=jnp.int32)[None, :] < live_count[:, None]).astype(jnp.float32)[:, None, :, None]
    visc_col = visc[:, None, :, None]
    source = vector * live_mask

    def smooth(field_in):
        return per_element(field_in, p_matrix) / visc_col * live_mask

    def apply_op(field_in):
        return (per_element(field_in, k_matrix) * visc_col - coupling * face_term(field_in, links, blocks)) * live_mask

    def inner_prod(left_vec, right_vec):
        return jnp.sum(left_vec * right_vec, axis=(0, 2, 3))

    first_pre = smooth(source)
    first_img = apply_op(first_pre)
    second_pre = smooth(first_img)
    second_img = apply_op(second_pre)
    matrix_entries = jnp.stack([inner_prod(first_img, first_img), inner_prod(first_img, second_img), inner_prod(second_img, second_img), inner_prod(first_img, source), inner_prod(second_img, source)])
    return first_pre, second_pre, matrix_entries


def reference(rhs, viscosity, counts, neighbours, face_index, k_matrix, p_matrix):
    groups = N_GX * N_GY
    stacked = (rhs.reshape(groups, N_GZ, PROBES, E_DEV, EDOF), viscosity.reshape(groups, N_GZ, E_DEV), counts.reshape(groups, N_GZ), neighbours.reshape(groups, N_GZ, NBR), face_index.reshape(groups, N_GZ, NBR, FACE))
    first_pre, second_pre, matrix_entries = lax.map(lambda group: group_pass(group, k_matrix, p_matrix), stacked)
    totals = jnp.sum(matrix_entries, axis=0)
    self_one, cross_mid, self_two, load_one, load_two = totals[0], totals[1], totals[2], totals[3], totals[4]
    determinant = self_one * self_two - cross_mid * cross_mid
    weight_one = (self_two * load_one - cross_mid * load_two) / determinant
    weight_two = (self_one * load_two - cross_mid * load_one) / determinant
    solution = weight_one[:, None, None] * first_pre + weight_two[:, None, None] * second_pre
    return solution.reshape(N_GX, N_GY, N_GZ, PROBES, E_DEV, EDOF)
```

```python
import functools

import jax
import jax.numpy as jnp
from jax import lax
from jax.experimental import pallas as pl
from jax.experimental.pallas import tpu as pltpu
from jax.sharding import PartitionSpec as P

coupling = 0.5
vmem_grant = 48 * 1024 * 1024
f32 = jnp.float32
bf16 = jnp.bfloat16
vmem_spec = pl.BlockSpec(memory_space=pltpu.VMEM)
smem_spec = pl.BlockSpec(memory_space=pltpu.SMEM)


def two_parts(value):
    high = value.astype(bf16)
    return high, (value - high.astype(f32)).astype(bf16)


def dot(left, right):
    return jnp.dot(left, right, preferred_element_type=f32)


def dot_transposed(left, right):
    return lax.dot_general(left, right, (((1,), (1,)), ((), ())), preferred_element_type=f32)


def times_matrix(rows, matrix):
    count = rows.shape[0]
    row_high, row_low = two_parts(rows)
    mat_high, mat_low = two_parts(matrix)
    both = dot(jnp.concatenate([row_high, row_low], axis=0), mat_high)
    return both[:count] + (both[count:] + dot(row_high, mat_low))


def split_index(index, dofs):
    if dofs & (dofs - 1) == 0:
        return lax.shift_right_arithmetic(index, dofs.bit_length() - 1), index & (dofs - 1)
    element = jnp.floor_divide(index, dofs)
    return element, index - element * dofs


def shift_slot(links_ref, index_ref, shift, members):
    target = lax.rem(lax.axis_index("gz") + shift, members)
    slot = jnp.int32(-1)
    for position in range(links_ref.shape[0]):
        slot = jnp.where(links_ref[position] == target, jnp.int32(position), slot)
    row = index_ref[pl.ds(jnp.maximum(slot, 0), 1), :]
    return jnp.where(slot >= 0, row, -1)


def hot_columns(flat_row, elements, dofs):
    element, dof = split_index(flat_row, dofs)
    width = flat_row.shape[1]
    over_elements = lax.broadcasted_iota(jnp.int32, (elements, width), 0) == element
    over_dofs = (lax.broadcasted_iota(jnp.int32, (dofs, width), 0) == dof).astype(f32).astype(bf16)
    return over_elements, over_dofs


def viscosity_rows(visc_ref, probes):
    elements = visc_ref.shape[1]
    line = lax.broadcasted_iota(jnp.int32, (elements, elements), 0)
    column = lax.broadcasted_iota(jnp.int32, (elements, elements), 1)
    diagonal = jnp.where(line == column, jnp.broadcast_to(visc_ref[...], (elements, elements)), 0.0)
    visc_col = jnp.sum(diagonal, axis=1, keepdims=True)
    return jnp.concatenate([visc_col] * probes, axis=0)


def live_rows(count_ref, elements, probes):
    slot = lax.broadcasted_iota(jnp.int32, (elements, 1), 0)
    live = (slot < count_ref[0]).astype(f32)
    return jnp.concatenate([live] * probes, axis=0)


def send_faces(field, probes, links_ref, index_ref, face_refs):
    rows, dofs = field.shape
    elements = rows // probes
    high, low = two_parts(field)
    parts = jnp.concatenate([high, low], axis=0)
    members = len(face_refs) + 1
    for shift in range(1, members):
        flat_row = shift_slot(links_ref, index_ref, shift, members)
        over_elements, over_dofs = hot_columns(flat_row, elements, dofs)
        picked = dot(parts, over_dofs)
        picked = picked[:rows] + picked[rows:]
        for probe in range(probes):
            block = picked[probe * elements : (probe + 1) * elements]
            face_refs[shift - 1][pl.ds(probe, 1), :] = jnp.sum(
                jnp.where(over_elements, block, 0.0), axis=0, keepdims=True
            )


def placed_faces(shape, probes, links_ref, index_ref, face_refs):
    rows, dofs = shape
    elements = rows // probes
    members = len(face_refs) + 1
    total = jnp.zeros((2 * rows, dofs), f32)
    for shift in range(1, members):
        flat_row = shift_slot(links_ref, index_ref, shift, members)
        over_elements, over_dofs = hot_columns(flat_row, elements, dofs)
        came = face_refs[members - shift - 1]
        spread = jnp.concatenate(
            [
                jnp.where(over_elements, came[pl.ds(probe, 1), :], 0.0)
                for probe in range(probes)
            ],
            axis=0,
        )
        high, low = two_parts(spread)
        total += dot_transposed(jnp.concatenate([high, low], axis=0), over_dofs)
    return total[:rows] + total[rows:]


def first_kernel(probes, count_ref, links_ref, index_ref, visc_ref, rhs_ref, p_ref, first_ref, *face_refs):
    rows, _ = rhs_ref.shape
    live = live_rows(count_ref, rows // probes, probes)
    visc = viscosity_rows(visc_ref, probes)
    first_pre = times_matrix(rhs_ref[...] * live, p_ref[...]) / visc * live
    first_ref[...] = first_pre
    send_faces(first_pre, probes, links_ref, index_ref, face_refs)


def second_kernel(
    probes, members, count_ref, links_ref, index_ref, visc_ref, first_ref, k_ref, p_ref, *refs
):
    came_refs = refs[: members - 1]
    image_ref, second_ref = refs[members - 1 : members + 1]
    face_refs = refs[members + 1 :]
    rows, _ = first_ref.shape
    live = live_rows(count_ref, rows // probes, probes)
    visc = viscosity_rows(visc_ref, probes)
    placed = placed_faces(first_ref.shape, probes, links_ref, index_ref, came_refs)
    image = (times_matrix(first_ref[...], k_ref[...]) * visc - coupling * placed) * live
    image_ref[...] = image
    second_pre = times_matrix(image, p_ref[...]) / visc * live
    second_ref[...] = second_pre
    send_faces(second_pre, probes, links_ref, index_ref, face_refs)


def third_kernel(
    probes, count_ref, links_ref, index_ref, visc_ref, rhs_ref, image_ref, second_ref, k_ref, *refs
):
    came_refs, products_ref = refs[:-1], refs[-1]
    rows, dofs = rhs_ref.shape
    elements = rows // probes
    live = live_rows(count_ref, elements, probes)
    visc = viscosity_rows(visc_ref, probes)
    placed = placed_faces(rhs_ref.shape, probes, links_ref, index_ref, came_refs)
    second_img = (times_matrix(second_ref[...], k_ref[...]) * visc - coupling * placed) * live
    first_img = image_ref[...]
    source = rhs_ref[...] * live
    pairs = (
        (first_img, first_img),
        (first_img, second_img),
        (second_img, second_img),
        (first_img, source),
        (second_img, source),
    )
    products_ref[...] = jnp.zeros(products_ref.shape, f32)
    for place, (left, right) in enumerate(pairs):
        product = left * right
        for probe in range(probes):
            products_ref[pl.ds(place * probes + probe, 1), :] = jnp.sum(
                product[probe * elements : (probe + 1) * elements], axis=0, keepdims=True
            )


def last_kernel(probes, first_ref, second_ref, *refs):
    part_refs, out_ref = refs[:-1], refs[-1]
    rows, _ = first_ref.shape
    elements = rows // probes
    total = part_refs[0][...]
    for part in part_refs[1:]:
        total = total + part[...]
    sums = jnp.sum(total, axis=1, keepdims=True)
    for probe in range(probes):
        self_one, cross_mid, self_two, load_one, load_two = (
            sums[place * probes + probe : place * probes + probe + 1, :] for place in range(5)
        )
        determinant = self_one * self_two - cross_mid * cross_mid
        weight_one = (self_two * load_one - cross_mid * load_two) / determinant
        weight_two = (self_one * load_two - cross_mid * load_one) / determinant
        block = pl.ds(probe * elements, elements)
        out_ref[block, :] = weight_one * first_ref[block, :] + weight_two * second_ref[block, :]


def shifted(array, axis, size, shift):
    return lax.ppermute(array, axis, [(source, (source + shift) % size) for source in range(size)])


def call(kernel, in_specs, out_shapes, flops, *args):
    return pl.pallas_call(
        kernel,
        out_shape=out_shapes,
        in_specs=in_specs,
        out_specs=jax.tree.map(lambda _: vmem_spec, out_shapes),
        compiler_params=pltpu.CompilerParams(vmem_limit_bytes=vmem_grant),
        cost_estimate=pl.CostEstimate(flops=flops, bytes_accessed=1 << 20, transcendentals=0),
    )(*args)


def per_device(mesh, rhs, viscosity, counts, neighbours, face_index, k_matrix, p_matrix):
    probes, elements, dofs = rhs.shape[3:]
    slots, width = face_index.shape[3:]
    members = mesh.shape["gz"]
    rows = probes * elements
    flat_rhs = rhs.reshape(rows, dofs)
    shared = (
        counts.reshape(1),
        neighbours.reshape(slots),
        face_index.reshape(slots, width),
        viscosity.reshape(1, elements),
    )
    shared_specs = [smem_spec, smem_spec, vmem_spec, vmem_spec]
    field = jax.ShapeDtypeStruct((rows, dofs), f32)
    faces = [jax.ShapeDtypeStruct((probes, width), f32)] * (members - 1)
    flops = 8 * rows * dofs * (members - 1) * width

    def exchange(values):
        return [shifted(value, "gz", members, shift + 1) for shift, value in enumerate(values)]

    first_pre, *leaving = call(
        functools.partial(first_kernel, probes),
        shared_specs + [vmem_spec] * 2,
        [field] + faces,
        flops,
        *shared,
        flat_rhs,
        p_matrix,
    )
    came = exchange(leaving)
    first_img, second_pre, *leaving = call(
        functools.partial(second_kernel, probes, members),
        shared_specs + [vmem_spec] * (2 + members),
        [field, field] + faces,
        2 * flops,
        *shared,
        first_pre,
        k_matrix,
        p_matrix,
        *came,
    )
    came = exchange(leaving)
    products = call(
        functools.partial(third_kernel, probes),
        shared_specs + [vmem_spec] * (3 + members),
        jax.ShapeDtypeStruct((-(-5 * probes // 8) * 8, dofs), f32),
        flops,
        *shared,
        flat_rhs,
        first_img,
        second_pre,
        k_matrix,
        *came,
    )
    parts = [products]
    for axis in ("gz", "gx", "gy"):
        total = functools.reduce(jnp.add, parts)
        size = mesh.shape[axis]
        parts = [total] + [shifted(total, axis, size, shift) for shift in range(1, size)]
    result = call(
        functools.partial(last_kernel, probes),
        [vmem_spec] * (2 + len(parts)),
        field,
        rows * dofs,
        first_pre,
        second_pre,
        *parts,
    )
    return result.reshape(rhs.shape)


def solution(mesh):
    return jax.shard_map(
        functools.partial(per_device, mesh),
        mesh=mesh,
        in_specs=(
            P("gx", "gy", "gz", None, None, None),
            P("gx", "gy", "gz", None),
            P("gx", "gy", "gz"),
            P("gx", "gy", "gz", None),
            P("gx", "gy", "gz", None, None),
            P(),
            P(),
        ),
        out_specs=P("gx", "gy", "gz", None, None, None),
        check_vma=False,
    )
```

```python
import functools

import jax
import jax.numpy as jnp
from jax import lax
from jax.experimental import pallas as pl
from jax.experimental.pallas import tpu as pltpu
from jax.sharding import PartitionSpec as P

coupling = 0.5
vmem_grant = 48 * 1024 * 1024
f32 = jnp.float32
bf16 = jnp.bfloat16
vmem_spec = pl.BlockSpec(memory_space=pltpu.VMEM)
smem_spec = pl.BlockSpec(memory_space=pltpu.SMEM)
hbm_spec = pl.BlockSpec(memory_space=pltpu.HBM)


def two_parts(value):
    high = value.astype(bf16)
    return high, (value - high.astype(f32)).astype(bf16)


def dot(left, right):
    return jnp.dot(left, right, preferred_element_type=f32)


def dot_transposed(left, right):
    return lax.dot_general(left, right, (((1,), (1,)), ((), ())), preferred_element_type=f32)


def times_matrix(rows, matrix):
    count = rows.shape[0]
    row_high, row_low = two_parts(rows)
    mat_high, mat_low = two_parts(matrix)
    both = dot(jnp.concatenate([row_high, row_low], axis=0), mat_high)
    return both[:count] + (both[count:] + dot(row_high, mat_low))


def split_index(index, dofs):
    if dofs & (dofs - 1) == 0:
        return lax.shift_right_arithmetic(index, dofs.bit_length() - 1), index & (dofs - 1)
    element = jnp.floor_divide(index, dofs)
    return element, index - element * dofs


def shift_slot(links_ref, index_ref, shift, members):
    target = lax.rem(lax.axis_index("gz") + shift, members)
    slot = jnp.int32(-1)
    for position in range(links_ref.shape[-1]):
        slot = jnp.where(links_ref[0, 0, 0, position] == target, jnp.int32(position), slot)
    row = index_ref[0, 0, 0, pl.ds(jnp.maximum(slot, 0), 1), :]
    return jnp.where(slot >= 0, row, -1)


def hot_columns(flat_row, elements, dofs):
    element, dof = split_index(flat_row, dofs)
    width = flat_row.shape[1]
    over_elements = lax.broadcasted_iota(jnp.int32, (elements, width), 0) == element
    over_dofs = (lax.broadcasted_iota(jnp.int32, (dofs, width), 0) == dof).astype(f32).astype(bf16)
    return over_elements, over_dofs


def viscosity_column(visc_row):
    elements = visc_row.shape[1]
    line = lax.broadcasted_iota(jnp.int32, (elements, elements), 0)
    column = lax.broadcasted_iota(jnp.int32, (elements, elements), 1)
    spread = jnp.where(line == column, jnp.broadcast_to(visc_row, (elements, elements)), 0.0)
    return jnp.sum(spread, axis=1, keepdims=True)


def wide(column, dofs):
    return jnp.broadcast_to(column, (column.shape[0], dofs))


def send_faces(field, probes, slots_ref, leave_ref):
    rows, dofs = field.shape
    elements = rows // probes
    members = slots_ref.shape[0] + 1
    high, low = two_parts(field)
    parts = jnp.concatenate([high, low], axis=0)
    me = lax.axis_index("gz")
    for shift in range(1, members):
        over_elements, over_dofs = hot_columns(slots_ref[pl.ds(shift - 1, 1), :], elements, dofs)
        picked = dot(parts, over_dofs)
        picked = picked[:rows] + picked[rows:]
        target = lax.rem(me + shift, members)
        for probe in range(probes):
            block = picked[probe * elements : (probe + 1) * elements]
            leave_ref[target, pl.ds(probe, 1), :] = jnp.sum(
                jnp.where(over_elements, block, 0.0), axis=0, keepdims=True
            )
    leave_ref[me] = jnp.zeros(leave_ref.shape[1:], f32)


def placed_faces(shape, probes, slots_ref, came_ref):
    rows, dofs = shape
    elements = rows // probes
    members = slots_ref.shape[0] + 1
    me = lax.axis_index("gz")
    total = jnp.zeros((2 * rows, dofs), f32)
    for shift in range(1, members):
        over_elements, over_dofs = hot_columns(slots_ref[pl.ds(shift - 1, 1), :], elements, dofs)
        came = came_ref[lax.rem(me + shift, members)]
        spread = jnp.concatenate(
            [
                jnp.where(over_elements, came[probe : probe + 1, :], 0.0)
                for probe in range(probes)
            ],
            axis=0,
        )
        high, low = two_parts(spread)
        total += dot_transposed(jnp.concatenate([high, low], axis=0), over_dofs)
    return total[:rows] + total[rows:]


def first_kernel(
    count_ref, links_hbm, index_hbm, visc_hbm, rhs_hbm, p_hbm,
    first_ref, source_ref, up_ref, down_ref, slots_ref, leave_ref,
    links_ref, index_ref, visc_ref, rhs_ref, p_ref, arrived,
):
    pairs = (
        (links_hbm, links_ref),
        (index_hbm, index_ref),
        (visc_hbm, visc_ref),
        (rhs_hbm, rhs_ref),
        (p_hbm, p_ref),
    )
    copies = [
        pltpu.make_async_copy(held, here, arrived.at[place])
        for place, (held, here) in enumerate(pairs)
    ]
    for copy in copies:
        copy.start()
    copies[0].wait()
    copies[1].wait()
    members = slots_ref.shape[0] + 1
    for shift in range(1, members):
        slots_ref[pl.ds(shift - 1, 1), :] = shift_slot(links_ref, index_ref, shift, members)
    copies[2].wait()
    probes, elements, dofs = rhs_ref.shape[3:]
    slot = lax.broadcasted_iota(jnp.int32, (elements, 1), 0)
    live = (slot < count_ref[0, 0, 0]).astype(f32)
    visc = viscosity_column(visc_ref[0, 0])
    up = wide(jnp.concatenate([live * visc] * probes, axis=0), dofs)
    down = wide(jnp.concatenate([live / visc] * probes, axis=0), dofs)
    up_ref[...] = up
    down_ref[...] = down
    copies[3].wait()
    source = rhs_ref[...].reshape(probes * elements, dofs)
    source = source * wide(jnp.concatenate([live] * probes, axis=0), dofs)
    source_ref[...] = source
    copies[4].wait()
    first_pre = times_matrix(source, p_ref[...]) * down
    first_ref[...] = first_pre
    send_faces(first_pre, probes, slots_ref, leave_ref)


def masked(placed, up):
    return jnp.where(up > 0.0, placed, 0.0)


def second_kernel(
    probes, slots_ref, up_ref, down_ref, first_ref, k_ref, p_ref, came_ref,
    image_ref, second_ref, leave_ref,
):
    up = up_ref[...]
    placed = placed_faces(first_ref.shape, probes, slots_ref, came_ref)
    image = times_matrix(first_ref[...], k_ref[...]) * up - masked(coupling * placed, up)
    image_ref[...] = image
    second_pre = times_matrix(image, p_ref[...]) * down_ref[...]
    second_ref[...] = second_pre
    send_faces(second_pre, probes, slots_ref, leave_ref)


def as_row(lines, lanes):
    count = -(-len(lines) // 8) * 8
    spare = jnp.zeros((count - len(lines), lines[0].shape[1]), f32)
    sums = jnp.sum(jnp.concatenate(lines + [spare], axis=0), axis=1, keepdims=True)
    line = lax.broadcasted_iota(jnp.int32, (count, lanes), 0)
    lane = lax.broadcasted_iota(jnp.int32, (count, lanes), 1)
    return jnp.sum(jnp.where(line == lane, sums, 0.0), axis=0, keepdims=True)


def third_kernel(
    probes, slots_ref, up_ref, source_ref, image_ref, second_ref, k_ref, came_ref, products_ref
):
    rows, dofs = source_ref.shape
    elements = rows // probes
    up = up_ref[...]
    placed = placed_faces(source_ref.shape, probes, slots_ref, came_ref)
    second_img = times_matrix(second_ref[...], k_ref[...]) * up - masked(coupling * placed, up)
    first_img = image_ref[...]
    source = source_ref[...]
    pairs = (
        (first_img, first_img),
        (first_img, second_img),
        (second_img, second_img),
        (first_img, source),
        (second_img, source),
    )
    lines = []
    for left, right in pairs:
        product = left * right
        for probe in range(probes):
            lines.append(
                jnp.sum(product[probe * elements : (probe + 1) * elements], axis=0, keepdims=True)
            )
    products_ref[...] = jnp.broadcast_to(as_row(lines, products_ref.shape[-1]), products_ref.shape)


def last_kernel(probes, first_ref, second_ref, parts_ref, out_ref):
    rows, _ = first_ref.shape
    elements = rows // probes
    total = jnp.sum(parts_ref[...], axis=0)
    for probe in range(probes):
        self_one, cross_mid, self_two, load_one, load_two = (
            total[:, place * probes + probe : place * probes + probe + 1] for place in range(5)
        )
        determinant = self_one * self_two - cross_mid * cross_mid
        weight_one = (self_two * load_one - cross_mid * load_two) / determinant
        weight_two = (self_one * load_two - cross_mid * load_one) / determinant
        block = pl.ds(probe * elements, elements)
        out_ref[block, :] = weight_one * first_ref[block, :] + weight_two * second_ref[block, :]


def call(kernel, in_specs, out_shapes, flops, *args, scratch=()):
    return pl.pallas_call(
        kernel,
        out_shape=out_shapes,
        in_specs=in_specs,
        out_specs=jax.tree.map(lambda _: vmem_spec, out_shapes),
        scratch_shapes=scratch,
        compiler_params=pltpu.CompilerParams(vmem_limit_bytes=vmem_grant),
        cost_estimate=pl.CostEstimate(flops=flops, bytes_accessed=1 << 20, transcendentals=0),
    )(*args)


def per_device(mesh, rhs, viscosity, counts, neighbours, face_index, k_matrix, p_matrix):
    probes, elements, dofs = rhs.shape[3:]
    width = face_index.shape[-1]
    members = mesh.shape["gz"]
    rows = probes * elements
    field = jax.ShapeDtypeStruct((rows, dofs), f32)
    slots_shape = jax.ShapeDtypeStruct((members - 1, width), jnp.int32)
    faces = jax.ShapeDtypeStruct((members, probes, width), f32)
    flops = 8 * rows * dofs * (members - 1) * width

    def exchange(value):
        return lax.all_to_all(value, "gz", split_axis=0, concat_axis=0)

    first_pre, source, up, down, slots, leaving = call(
        first_kernel,
        [smem_spec] + [hbm_spec] * 5,
        [field] * 4 + [slots_shape, faces],
        flops,
        counts,
        *(
            pltpu.with_memory_space_constraint(value, pltpu.HBM)
            for value in (neighbours, face_index, viscosity, rhs, p_matrix)
        ),
        scratch=[
            pltpu.SMEM(neighbours.shape, jnp.int32),
            pltpu.VMEM(face_index.shape, jnp.int32),
            pltpu.VMEM(viscosity.shape, f32),
            pltpu.VMEM(rhs.shape, f32),
            pltpu.VMEM(p_matrix.shape, f32),
            pltpu.SemaphoreType.DMA((5,)),
        ],
    )
    came = exchange(leaving)
    first_img, second_pre, leaving = call(
        functools.partial(second_kernel, probes),
        [vmem_spec] * 7,
        [field, field, faces],
        2 * flops,
        slots,
        up,
        down,
        first_pre,
        k_matrix,
        p_matrix,
        came,
    )
    came = exchange(leaving)
    devices = mesh.size
    lanes = -(-5 * probes // 128) * 128
    products = call(
        functools.partial(third_kernel, probes),
        [vmem_spec] * 7,
        jax.ShapeDtypeStruct((devices, 1, lanes), f32),
        flops,
        slots,
        up,
        source,
        first_img,
        second_pre,
        k_matrix,
        came,
    )
    parts = lax.all_to_all(products, ("gx", "gy", "gz"), split_axis=0, concat_axis=0)
    result = call(
        functools.partial(last_kernel, probes),
        [vmem_spec] * 3,
        field,
        rows * dofs,
        first_pre,
        second_pre,
        parts,
    )
    return result.reshape(rhs.shape)


def solution(mesh):
    return jax.shard_map(
        functools.partial(per_device, mesh),
        mesh=mesh,
        in_specs=(
            P("gx", "gy", "gz", None, None, None),
            P("gx", "gy", "gz", None),
            P("gx", "gy", "gz"),
            P("gx", "gy", "gz", None),
            P("gx", "gy", "gz", None, None),
            P(),
            P(),
        ),
        out_specs=P("gx", "gy", "gz", None, None, None),
        check_vma=False,
    )
```

```python
import functools

import jax
import jax.numpy as jnp
from jax import lax
from jax.experimental import pallas as pl
from jax.experimental.pallas import tpu as pltpu
from jax.sharding import PartitionSpec as P

coupling = 0.5
vmem_grant = 48 * 1024 * 1024
short_group = 4
f32 = jnp.float32
bf16 = jnp.bfloat16
vmem_spec = pl.BlockSpec(memory_space=pltpu.VMEM)
smem_spec = pl.BlockSpec(memory_space=pltpu.SMEM)
hbm_spec = pl.BlockSpec(memory_space=pltpu.HBM)


def two_parts(value):
    high = value.astype(bf16)
    return high, (value - high.astype(f32)).astype(bf16)


def dot(left, right):
    return jnp.dot(left, right, preferred_element_type=f32)


def dot_transposed(left, right):
    return lax.dot_general(left, right, (((1,), (1,)), ((), ())), preferred_element_type=f32)


def times_matrix(rows, matrix):
    count = rows.shape[0]
    row_high, row_low = two_parts(rows)
    mat_high, mat_low = two_parts(matrix)
    both = dot(jnp.concatenate([row_high, row_low], axis=0), mat_high)
    return both[:count] + (both[count:] + dot(row_high, mat_low))


def split_index(index, dofs):
    if dofs & (dofs - 1) == 0:
        return lax.shift_right_arithmetic(index, dofs.bit_length() - 1), index & (dofs - 1)
    element = jnp.floor_divide(index, dofs)
    return element, index - element * dofs


def shift_slot(links_ref, index_ref, shift, members):
    target = lax.rem(lax.axis_index("gz") + shift, members)
    slot = jnp.int32(-1)
    for position in range(links_ref.shape[-1]):
        slot = jnp.where(links_ref[0, 0, 0, position] == target, jnp.int32(position), slot)
    row = index_ref[0, 0, 0, pl.ds(jnp.maximum(slot, 0), 1), :]
    return jnp.where(slot >= 0, row, -1)


def hot_elements(flat_row, elements, dofs):
    element, _ = split_index(flat_row, dofs)
    return lax.broadcasted_iota(jnp.int32, (elements, flat_row.shape[1]), 0) == element


def hot_dofs(flat_row, dofs):
    _, dof = split_index(flat_row, dofs)
    line = lax.broadcasted_iota(jnp.int32, (dofs, flat_row.shape[1]), 0)
    return (line == dof).astype(f32).astype(bf16)


def as_column(row):
    elements = row.shape[1]
    line = lax.broadcasted_iota(jnp.int32, (elements, elements), 0)
    column = lax.broadcasted_iota(jnp.int32, (elements, elements), 1)
    spread = jnp.where(line == column, jnp.broadcast_to(row, (elements, elements)), 0.0)
    return jnp.sum(spread, axis=1, keepdims=True)


def wide(column, probes, dofs):
    return jnp.broadcast_to(jnp.concatenate([column] * probes, axis=0), (probes * column.shape[0], dofs))


def stacked(value):
    return jnp.concatenate(two_parts(value), axis=0)


def take_faces(parts, over_elements, over_dofs):
    elements = over_elements.shape[0]
    rows = parts.shape[0] // 2
    picked = dot(parts, over_dofs)
    picked = picked[:rows] + picked[rows:]
    return [
        jnp.sum(jnp.where(over_elements, picked[low : low + elements], 0.0), axis=0, keepdims=True)
        for low in range(0, rows, elements)
    ]


def add_faces(values, over_elements, over_dofs):
    highs = [value.astype(bf16).astype(f32) for value in values]
    lows = [value - high for value, high in zip(values, highs)]
    spread = jnp.concatenate(
        [jnp.where(over_elements, part, 0.0).astype(bf16) for part in highs + lows], axis=0
    )
    return dot_transposed(spread, over_dofs)


def folded(parts):
    rows = parts.shape[0] // 2
    return parts[:rows] + parts[rows:]


def as_row(lines, lanes):
    count = -(-len(lines) // 8) * 8
    spare = jnp.zeros((count - len(lines), lines[0].shape[1]), f32)
    sums = jnp.sum(jnp.concatenate(lines + [spare], axis=0), axis=1, keepdims=True)
    line = lax.broadcasted_iota(jnp.int32, (count, lanes), 0)
    lane = lax.broadcasted_iota(jnp.int32, (count, lanes), 1)
    return jnp.sum(jnp.where(line == lane, sums, 0.0), axis=0, keepdims=True)


def inner_products(first_img, second_img, source, probes, products_ref):
    elements = source.shape[0] // probes
    pairs = (
        (first_img, first_img),
        (first_img, second_img),
        (second_img, second_img),
        (first_img, source),
        (second_img, source),
    )
    lines = []
    for left, right in pairs:
        product = left * right
        for probe in range(probes):
            lines.append(
                jnp.sum(product[probe * elements : (probe + 1) * elements], axis=0, keepdims=True)
            )
    products_ref[...] = jnp.broadcast_to(as_row(lines, products_ref.shape[-1]), products_ref.shape)


def begin(refs):
    count_ref, links_hbm, index_hbm, visc_hbm, rhs_hbm, *matrices_hbm = refs["operands"]
    links_ref, index_ref, visc_ref, rhs_ref, *matrix_refs, arrived = refs["scratch"]
    pairs = (
        (links_hbm, links_ref),
        (index_hbm, index_ref),
        (visc_hbm, visc_ref),
        (rhs_hbm, rhs_ref),
        *zip(matrices_hbm, matrix_refs),
    )
    copies = [
        pltpu.make_async_copy(held, here, arrived.at[place])
        for place, (held, here) in enumerate(pairs)
    ]
    for copy in copies:
        copy.start()
    copies[0].wait()
    copies[1].wait()
    slots_ref = refs["slots"]
    members = slots_ref.shape[0] + 1
    for shift in range(1, members):
        slots_ref[shift - 1] = shift_slot(links_ref, index_ref, shift, members)
    copies[2].wait()
    probes, elements, dofs = rhs_ref.shape[3:]
    slot = lax.broadcasted_iota(jnp.int32, (elements, 1), 0)
    live = (slot < count_ref[0, 0, 0]).astype(f32)
    visc = as_column(visc_ref[0, 0])
    up = wide(live * visc, probes, dofs)
    down = wide(live / visc, probes, dofs)
    refs["up"][...] = up
    refs["down"][...] = down
    copies[3].wait()
    source = rhs_ref[...].reshape(probes * elements, dofs) * wide(live, probes, dofs)
    refs["source"][...] = source
    for copy in copies[4:]:
        copy.wait()
    first_pre = times_matrix(source, matrix_refs[0][...]) * down
    refs["first"][...] = first_pre
    return first_pre, up, down


def message_places(shifts, probes):
    values = shifts * probes
    return values, values + probes, values + probes + shifts


def near_first_kernel(*refs):
    operands, refs = refs[:7], refs[7:]
    first_ref, source_ref, up_ref, down_ref, base_ref, slots_ref, hot_ref = refs[:7]
    shifts, _, width = slots_ref.shape
    leave_refs, scratch = refs[7 : 7 + shifts], refs[7 + shifts :]
    visc_ref, rhs_ref, p_ref, k_ref = scratch[2:6]
    probes, elements, dofs = rhs_ref.shape[3:]
    first_pre, up, down = begin(
        {
            "operands": operands,
            "scratch": scratch,
            "slots": slots_ref,
            "up": up_ref,
            "down": down_ref,
            "source": source_ref,
            "first": first_ref,
        }
    )
    base = times_matrix(first_pre, k_ref[...]) * up
    base_ref[...] = base
    first_parts = stacked(first_pre)
    second_parts = stacked(times_matrix(base, p_ref[...]) * down)
    second_at, index_at, visc_at = message_places(shifts, probes)
    slot = lax.broadcasted_iota(jnp.int32, (1, elements), 1)
    live_visc = jnp.where(slot < operands[0][0, 0, 0], visc_ref[0, 0], 0.0)
    for shift in range(1, shifts + 1):
        flat_row = slots_ref[shift - 1]
        over_elements = hot_elements(flat_row, elements, dofs)
        over_dofs = hot_dofs(flat_row, dofs)
        hot_ref[:, (shift - 1) * width : shift * width] = over_dofs
        first_rows = take_faces(first_parts, over_elements, over_dofs)
        second_rows = take_faces(second_parts, over_elements, over_dofs)
        for probe in range(probes):
            leave_refs[shift - 1][second_at + probe] = second_rows[probe]
            for leave_ref in leave_refs:
                leave_ref[(shift - 1) * probes + probe] = first_rows[probe]
        for leave_ref in leave_refs:
            leave_ref[index_at + shift - 1] = flat_row.astype(f32)
    for leave_ref in leave_refs:
        leave_ref[visc_at, :, :elements] = live_visc


def near_second_kernel(
    source_ref, up_ref, down_ref, base_ref, slots_ref, hot_ref, k_ref, p_ref, mine_ref, *refs
):
    came_refs = refs[:-3]
    image_ref, second_ref, products_ref = refs[-3:]
    shifts, _, width = slots_ref.shape
    members = shifts + 1
    rows, dofs = source_ref.shape
    second_at, index_at, visc_at = message_places(shifts, 0)
    probes = (mine_ref.shape[0] - visc_at - 1) // members
    elements = rows // probes
    second_at, index_at, visc_at = message_places(shifts, probes)

    def message(ahead):
        ahead = ahead % members
        return mine_ref if ahead == 0 else came_refs[members - ahead - 1]

    def inbound_first(ahead, shift):
        row = (members - shift - 1) * probes
        sent = message(ahead + shift)
        return [sent[row + probe] for probe in range(probes)]

    own_elements = [hot_elements(slots_ref[shift], elements, dofs) for shift in range(shifts)]
    own_dofs = [hot_ref[:, shift * width : (shift + 1) * width] for shift in range(shifts)]

    def placed_here(values):
        return folded(
            sum(add_faces(values[i], own_elements[i], own_dofs[i]) for i in range(shifts))
        )

    up, down = up_ref[...], down_ref[...]
    live = up > 0.0
    placed = placed_here([inbound_first(0, shift) for shift in range(1, members)])
    image = base_ref[...] - jnp.where(live, coupling * placed, 0.0)
    image_ref[...] = image
    images, back = [image], []
    for ahead in range(1, members):
        total = 0.0
        for shift in range(1, members):
            flat_row = message(ahead)[index_at + shift - 1].astype(jnp.int32)
            over_elements = hot_elements(flat_row, elements, dofs)
            over_dofs = hot_dofs(flat_row, dofs)
            total = total + add_faces(inbound_first(ahead, shift), over_elements, over_dofs)
            if shift + ahead == members:
                back.append((over_elements, over_dofs))
        images.append(-coupling * folded(total))
    smooth = times_matrix(jnp.concatenate(images, axis=0), p_ref[...])
    second_pre = smooth[:rows] * down
    second_ref[...] = second_pre
    values = []
    for ahead in range(1, members):
        sent = message(ahead)
        visc = as_column(sent[visc_at, :, :elements])
        scale = wide(jnp.where(visc > 0.0, 1.0 / visc, 0.0), probes, dofs)
        change = smooth[ahead * rows : (ahead + 1) * rows] * scale
        taken = take_faces(stacked(change), *back[ahead - 1])
        values.append([taken[probe] + sent[second_at + probe] for probe in range(probes)])
    placed = placed_here(values)
    second_img = times_matrix(second_pre, k_ref[...]) * up - jnp.where(live, coupling * placed, 0.0)
    inner_products(image, second_img, source_ref[...], probes, products_ref)


def leave_faces(field, probes, slots_ref, leave_ref):
    elements, dofs = field.shape[0] // probes, field.shape[1]
    members = slots_ref.shape[0] + 1
    parts = stacked(field)
    me = lax.axis_index("gz")
    for shift in range(1, members):
        flat_row = slots_ref[shift - 1]
        taken = take_faces(parts, hot_elements(flat_row, elements, dofs), hot_dofs(flat_row, dofs))
        target = lax.rem(me + shift, members)
        for probe in range(probes):
            leave_ref[target, pl.ds(probe, 1), :] = taken[probe]
    leave_ref[me] = jnp.zeros(leave_ref.shape[1:], f32)


def placed_faces(shape, probes, slots_ref, came_ref):
    rows, dofs = shape
    elements = rows // probes
    members = slots_ref.shape[0] + 1
    me = lax.axis_index("gz")
    total = jnp.zeros((2 * rows, dofs), f32)
    for shift in range(1, members):
        flat_row = slots_ref[shift - 1]
        came = came_ref[lax.rem(me + shift, members)]
        total += add_faces(
            [came[probe : probe + 1, :] for probe in range(probes)],
            hot_elements(flat_row, elements, dofs),
            hot_dofs(flat_row, dofs),
        )
    return folded(total)


def far_first_kernel(*refs):
    operands, refs = refs[:6], refs[6:]
    first_ref, source_ref, up_ref, down_ref, slots_ref, leave_ref = refs[:6]
    first_pre, _, _ = begin(
        {
            "operands": operands,
            "scratch": refs[6:],
            "slots": slots_ref,
            "up": up_ref,
            "down": down_ref,
            "source": source_ref,
            "first": first_ref,
        }
    )
    leave_faces(first_pre, leave_ref.shape[1], slots_ref, leave_ref)


def far_second_kernel(
    slots_ref, up_ref, down_ref, first_ref, k_ref, p_ref, came_ref,
    image_ref, second_ref, leave_ref,
):
    probes = came_ref.shape[1]
    up = up_ref[...]
    placed = placed_faces(first_ref.shape, probes, slots_ref, came_ref)
    image = times_matrix(first_ref[...], k_ref[...]) * up - jnp.where(up > 0.0, coupling * placed, 0.0)
    image_ref[...] = image
    second_pre = times_matrix(image, p_ref[...]) * down_ref[...]
    second_ref[...] = second_pre
    leave_faces(second_pre, probes, slots_ref, leave_ref)


def far_third_kernel(
    slots_ref, up_ref, source_ref, image_ref, second_ref, k_ref, came_ref, products_ref
):
    probes = came_ref.shape[1]
    up = up_ref[...]
    placed = placed_faces(source_ref.shape, probes, slots_ref, came_ref)
    second_img = times_matrix(second_ref[...], k_ref[...]) * up - jnp.where(up > 0.0, coupling * placed, 0.0)
    inner_products(image_ref[...], second_img, source_ref[...], probes, products_ref)


def last_kernel(probes, first_ref, second_ref, parts_ref, out_ref):
    rows, _ = first_ref.shape
    elements = rows // probes
    total = jnp.sum(parts_ref[...], axis=0)
    for probe in range(probes):
        self_one, cross_mid, self_two, load_one, load_two = (
            total[:, place * probes + probe : place * probes + probe + 1] for place in range(5)
        )
        determinant = self_one * self_two - cross_mid * cross_mid
        weight_one = (self_two * load_one - cross_mid * load_two) / determinant
        weight_two = (self_one * load_two - cross_mid * load_one) / determinant
        block = pl.ds(probe * elements, elements)
        out_ref[block, :] = weight_one * first_ref[block, :] + weight_two * second_ref[block, :]


def call(kernel, in_specs, out_shapes, flops, *args, scratch=()):
    return pl.pallas_call(
        kernel,
        out_shape=out_shapes,
        in_specs=in_specs,
        out_specs=jax.tree.map(lambda _: vmem_spec, out_shapes),
        scratch_shapes=scratch,
        compiler_params=pltpu.CompilerParams(vmem_limit_bytes=vmem_grant),
        cost_estimate=pl.CostEstimate(flops=flops, bytes_accessed=1 << 20, transcendentals=0),
    )(*args)


def begin_call(kernel, out_shapes, flops, counts, *fetched):
    links, *others = fetched
    scratch = [pltpu.SMEM(links.shape, links.dtype)]
    scratch += [pltpu.VMEM(value.shape, value.dtype) for value in others]
    return call(
        kernel,
        [smem_spec] + [hbm_spec] * len(fetched),
        out_shapes,
        flops,
        counts,
        *(pltpu.with_memory_space_constraint(value, pltpu.HBM) for value in fetched),
        scratch=scratch + [pltpu.SemaphoreType.DMA((len(fetched),))],
    )


def near_steps(members, shapes, arguments):
    rhs, viscosity, counts, neighbours, face_index, k_matrix, p_matrix = arguments
    field, slots_shape, products_shape = shapes
    rows, dofs = field.shape
    shifts, _, width = slots_shape.shape
    probes = rhs.shape[3]
    flops = 8 * rows * dofs * shifts * width
    hot = jax.ShapeDtypeStruct((dofs, shifts * width), bf16)
    length = message_places(shifts, probes)[2] + 1
    messages = [jax.ShapeDtypeStruct((length, 1, width), f32)] * shifts
    first_pre, source, up, down, base, slots, hot_own, *leaving = begin_call(
        near_first_kernel,
        [field] * 5 + [slots_shape, hot] + messages,
        2 * flops,
        counts,
        neighbours,
        face_index,
        viscosity,
        rhs,
        p_matrix,
        k_matrix,
    )
    came = [
        lax.ppermute(
            value, "gz", [(source, (source + shift) % members) for source in range(members)]
        )
        for shift, value in enumerate(leaving, 1)
    ]
    _, second_pre, products = call(
        near_second_kernel,
        [vmem_spec] * (9 + shifts),
        [field, field, products_shape],
        6 * flops,
        source,
        up,
        down,
        base,
        slots,
        hot_own,
        k_matrix,
        p_matrix,
        leaving[0],
        *came,
    )
    return first_pre, second_pre, products


def far_steps(members, shapes, arguments):
    rhs, viscosity, counts, neighbours, face_index, k_matrix, p_matrix = arguments
    field, slots_shape, products_shape = shapes
    rows, dofs = field.shape
    shifts, _, width = slots_shape.shape
    flops = 8 * rows * dofs * shifts * width
    faces = jax.ShapeDtypeStruct((members, rhs.shape[3], width), f32)

    def exchange(value):
        return lax.all_to_all(value, "gz", split_axis=0, concat_axis=0)

    first_pre, source, up, down, slots, leaving = begin_call(
        far_first_kernel,
        [field] * 4 + [slots_shape, faces],
        flops,
        counts,
        neighbours,
        face_index,
        viscosity,
        rhs,
        p_matrix,
    )
    first_img, second_pre, leaving = call(
        far_second_kernel,
        [vmem_spec] * 7,
        [field, field, faces],
        2 * flops,
        slots,
        up,
        down,
        first_pre,
        k_matrix,
        p_matrix,
        exchange(leaving),
    )
    products = call(
        far_third_kernel,
        [vmem_spec] * 7,
        products_shape,
        flops,
        slots,
        up,
        source,
        first_img,
        second_pre,
        k_matrix,
        exchange(leaving),
    )
    return first_pre, second_pre, products


def per_device(mesh, *arguments):
    rhs, face_index = arguments[0], arguments[4]
    probes, elements, dofs = rhs.shape[3:]
    members = mesh.shape["gz"]
    lanes = -(-5 * probes // 128) * 128
    shapes = (
        jax.ShapeDtypeStruct((probes * elements, dofs), f32),
        jax.ShapeDtypeStruct((members - 1, 1, face_index.shape[-1]), jnp.int32),
        jax.ShapeDtypeStruct((mesh.size, 1, lanes), f32),
    )
    near = 1 < members <= short_group and elements <= face_index.shape[-1]
    near = near and elements * dofs < 1 << 24
    steps = near_steps if near else far_steps
    first_pre, second_pre, products = steps(members, shapes, arguments)
    result = call(
        functools.partial(last_kernel, probes),
        [vmem_spec] * 3,
        shapes[0],
        probes * elements * dofs,
        first_pre,
        second_pre,
        lax.all_to_all(products, ("gx", "gy", "gz"), split_axis=0, concat_axis=0),
    )
    return result.reshape(rhs.shape)


def solution(mesh):
    return jax.shard_map(
        functools.partial(per_device, mesh),
        mesh=mesh,
        in_specs=(
            P("gx", "gy", "gz", None, None, None),
            P("gx", "gy", "gz", None),
            P("gx", "gy", "gz"),
            P("gx", "gy", "gz", None),
            P("gx", "gy", "gz", None, None),
            P(),
            P(),
        ),
        out_specs=P("gx", "gy", "gz", None, None, None),
        check_vma=False,
    )
```

```python
import functools

import jax
import jax.numpy as jnp
from jax import lax
from jax.experimental import pallas as pl
from jax.experimental.pallas import tpu as pltpu
from jax.sharding import PartitionSpec as P

coupling = 0.5
vmem_grant = 48 * 1024 * 1024
short_group = 4
f32 = jnp.float32
bf16 = jnp.bfloat16
vmem_spec = pl.BlockSpec(memory_space=pltpu.VMEM)
smem_spec = pl.BlockSpec(memory_space=pltpu.SMEM)
hbm_spec = pl.BlockSpec(memory_space=pltpu.HBM)


def two_parts(value):
    high = value.astype(bf16)
    return high, (value - high.astype(f32)).astype(bf16)


def dot(left, right):
    return jnp.dot(left, right, preferred_element_type=f32)


def dot_transposed(left, right):
    return lax.dot_general(left, right, (((1,), (1,)), ((), ())), preferred_element_type=f32)


def times_matrix(rows, matrix):
    count = rows.shape[0]
    row_high, row_low = two_parts(rows)
    mat_high, mat_low = two_parts(matrix)
    both = dot(jnp.concatenate([row_high, row_low], axis=0), mat_high)
    return both[:count] + (both[count:] + dot(row_high, mat_low))


def split_index(index, dofs):
    if dofs & (dofs - 1) == 0:
        return lax.shift_right_arithmetic(index, dofs.bit_length() - 1), index & (dofs - 1)
    element = jnp.floor_divide(index, dofs)
    return element, index - element * dofs


def slot_of(target, links_ref, index_ref):
    slot = jnp.int32(-1)
    for position in range(links_ref.shape[-1]):
        slot = jnp.where(links_ref[0, 0, 0, position] == target, jnp.int32(position), slot)
    row = index_ref[0, 0, 0, pl.ds(jnp.maximum(slot, 0), 1), :]
    return jnp.where(slot >= 0, row, -1)


def hot_elements(flat_row, elements, dofs):
    element, _ = split_index(flat_row, dofs)
    return lax.broadcasted_iota(jnp.int32, (elements, flat_row.shape[1]), 0) == element


def hot_dofs(flat_row, dofs):
    _, dof = split_index(flat_row, dofs)
    line = lax.broadcasted_iota(jnp.int32, (dofs, flat_row.shape[1]), 0)
    return (line == dof).astype(f32).astype(bf16)


def as_column(row):
    elements = row.shape[1]
    line = lax.broadcasted_iota(jnp.int32, (elements, elements), 0)
    column = lax.broadcasted_iota(jnp.int32, (elements, elements), 1)
    spread = jnp.where(line == column, jnp.broadcast_to(row, (elements, elements)), 0.0)
    return jnp.sum(spread, axis=1, keepdims=True)


def wide(column, probes, dofs):
    return jnp.broadcast_to(jnp.concatenate([column] * probes, axis=0), (probes * column.shape[0], dofs))


def stacked(value):
    return jnp.concatenate(two_parts(value), axis=0)


def take_faces(parts, over_elements, over_dofs):
    elements = over_elements.shape[0]
    rows = parts.shape[0] // 2
    picked = dot(parts, over_dofs)
    picked = picked[:rows] + picked[rows:]
    return [
        jnp.sum(jnp.where(over_elements, picked[low : low + elements], 0.0), axis=0, keepdims=True)
        for low in range(0, rows, elements)
    ]


def add_faces(values, over_elements, over_dofs):
    highs = [value.astype(bf16).astype(f32) for value in values]
    lows = [value - high for value, high in zip(values, highs)]
    spread = jnp.concatenate(
        [jnp.where(over_elements, part, 0.0).astype(bf16) for part in highs + lows], axis=0
    )
    return dot_transposed(spread, over_dofs)


def folded(parts):
    rows = parts.shape[0] // 2
    return parts[:rows] + parts[rows:]


def as_row(lines, lanes):
    count = -(-len(lines) // 8) * 8
    spare = jnp.zeros((count - len(lines), lines[0].shape[1]), f32)
    sums = jnp.sum(jnp.concatenate(lines + [spare], axis=0), axis=1, keepdims=True)
    line = lax.broadcasted_iota(jnp.int32, (count, lanes), 0)
    lane = lax.broadcasted_iota(jnp.int32, (count, lanes), 1)
    return jnp.sum(jnp.where(line == lane, sums, 0.0), axis=0, keepdims=True)


def inner_products(first_img, second_img, source, probes, products_ref):
    elements = source.shape[0] // probes
    pairs = (
        (first_img, first_img),
        (first_img, second_img),
        (second_img, second_img),
        (first_img, source),
        (second_img, source),
    )
    lines = []
    for left, right in pairs:
        product = left * right
        for probe in range(probes):
            lines.append(
                jnp.sum(product[probe * elements : (probe + 1) * elements], axis=0, keepdims=True)
            )
    products_ref[...] = jnp.broadcast_to(as_row(lines, products_ref.shape[-1]), products_ref.shape)


def begin(refs, partner):
    count_ref, links_hbm, index_hbm, visc_hbm, rhs_hbm, *matrices_hbm = refs["operands"]
    links_ref, index_ref, visc_ref, rhs_ref, *matrix_refs, arrived = refs["scratch"]
    pairs = (
        (links_hbm, links_ref),
        (index_hbm, index_ref),
        (visc_hbm, visc_ref),
        (rhs_hbm, rhs_ref),
        *zip(matrices_hbm, matrix_refs),
    )
    copies = [
        pltpu.make_async_copy(held, here, arrived.at[place])
        for place, (held, here) in enumerate(pairs)
    ]
    for copy in copies:
        copy.start()
    copies[0].wait()
    copies[1].wait()
    slots_ref = refs["slots"]
    me = lax.axis_index("gz")
    for step in range(1, slots_ref.shape[0] + 1):
        slots_ref[step - 1] = slot_of(partner(me, step), links_ref, index_ref)
    copies[2].wait()
    probes, elements, dofs = rhs_ref.shape[3:]
    slot = lax.broadcasted_iota(jnp.int32, (elements, 1), 0)
    live = (slot < count_ref[0, 0, 0]).astype(f32)
    visc = as_column(visc_ref[0, 0])
    up = wide(live * visc, probes, dofs)
    down = wide(live / visc, probes, dofs)
    refs["up"][...] = up
    refs["down"][...] = down
    copies[3].wait()
    source = rhs_ref[...].reshape(probes * elements, dofs) * wide(live, probes, dofs)
    refs["source"][...] = source
    for copy in copies[4:]:
        copy.wait()
    first_pre = times_matrix(source, matrix_refs[0][...]) * down
    refs["first"][...] = first_pre
    return first_pre, up, down


def message_places(steps, probes):
    values = steps * probes
    return values, values + probes, values + probes + steps


def near_first_kernel(*refs):
    operands, refs = refs[:7], refs[7:]
    first_ref, source_ref, up_ref, down_ref, base_ref, slots_ref, hot_ref = refs[:7]
    steps, _, width = slots_ref.shape
    leave_refs, scratch = refs[7 : 7 + steps], refs[7 + steps :]
    visc_ref, rhs_ref, p_ref, k_ref = scratch[2:6]
    probes, elements, dofs = rhs_ref.shape[3:]
    first_pre, up, down = begin(
        {
            "operands": operands,
            "scratch": scratch,
            "slots": slots_ref,
            "up": up_ref,
            "down": down_ref,
            "source": source_ref,
            "first": first_ref,
        },
        lambda me, step: me ^ step,
    )
    base = times_matrix(first_pre, k_ref[...]) * up
    base_ref[...] = base
    first_parts = stacked(first_pre)
    second_parts = stacked(times_matrix(base, p_ref[...]) * down)
    second_at, index_at, visc_at = message_places(steps, probes)
    slot = lax.broadcasted_iota(jnp.int32, (1, elements), 1)
    live_visc = jnp.where(slot < operands[0][0, 0, 0], visc_ref[0, 0], 0.0)
    for step in range(1, steps + 1):
        flat_row = slots_ref[step - 1]
        over_elements = hot_elements(flat_row, elements, dofs)
        over_dofs = hot_dofs(flat_row, dofs)
        hot_ref[:, (step - 1) * width : step * width] = over_dofs
        first_rows = take_faces(first_parts, over_elements, over_dofs)
        second_rows = take_faces(second_parts, over_elements, over_dofs)
        for probe in range(probes):
            leave_refs[step - 1][second_at + probe] = second_rows[probe]
            for leave_ref in leave_refs:
                leave_ref[(step - 1) * probes + probe] = first_rows[probe]
        for leave_ref in leave_refs:
            leave_ref[index_at + step - 1] = flat_row.astype(f32)
    for leave_ref in leave_refs:
        leave_ref[visc_at, :, :elements] = live_visc


def near_second_kernel(
    source_ref, up_ref, down_ref, base_ref, slots_ref, hot_ref, k_ref, p_ref, mine_ref, *refs
):
    came_refs = refs[:-2]
    second_ref, products_ref = refs[-2:]
    steps, _, width = slots_ref.shape
    members = steps + 1
    rows, dofs = source_ref.shape
    second_at, index_at, visc_at = message_places(steps, 0)
    probes = (mine_ref.shape[0] - visc_at - 1) // members
    elements = rows // probes
    second_at, index_at, visc_at = message_places(steps, probes)

    def message(step):
        return mine_ref if step == 0 else came_refs[steps - step]

    def inbound_first(member, step):
        sent = message(member ^ step)
        return [sent[(step - 1) * probes + probe] for probe in range(probes)]

    own_elements = [hot_elements(slots_ref[step], elements, dofs) for step in range(steps)]
    own_dofs = [hot_ref[:, step * width : (step + 1) * width] for step in range(steps)]

    def placed_here(values):
        return folded(
            sum(add_faces(values[i], own_elements[i], own_dofs[i]) for i in range(steps))
        )

    up, down = up_ref[...], down_ref[...]
    live = up > 0.0
    placed = placed_here([inbound_first(0, step) for step in range(1, members)])
    image = base_ref[...] - jnp.where(live, coupling * placed, 0.0)
    images, back = [image], []
    for member in range(1, members):
        total = 0.0
        for step in range(1, members):
            flat_row = message(member)[index_at + step - 1].astype(jnp.int32)
            over_elements = hot_elements(flat_row, elements, dofs)
            over_dofs = hot_dofs(flat_row, dofs)
            total = total + add_faces(inbound_first(member, step), over_elements, over_dofs)
            if step == member:
                back.append((over_elements, over_dofs))
        images.append(-coupling * folded(total))
    smooth = times_matrix(jnp.concatenate(images, axis=0), p_ref[...])
    second_pre = smooth[:rows] * down
    second_ref[...] = second_pre
    values = []
    for member in range(1, members):
        sent = message(member)
        visc = as_column(sent[visc_at, :, :elements])
        scale = wide(jnp.where(visc > 0.0, 1.0 / visc, 0.0), probes, dofs)
        change = smooth[member * rows : (member + 1) * rows] * scale
        taken = take_faces(stacked(change), *back[member - 1])
        values.append([taken[probe] + sent[second_at + probe] for probe in range(probes)])
    placed = placed_here(values)
    second_img = times_matrix(second_pre, k_ref[...]) * up - jnp.where(live, coupling * placed, 0.0)
    inner_products(image, second_img, source_ref[...], probes, products_ref)


def leave_faces(field, probes, slots_ref, leave_ref):
    elements, dofs = field.shape[0] // probes, field.shape[1]
    members = slots_ref.shape[0] + 1
    parts = stacked(field)
    me = lax.axis_index("gz")
    for shift in range(1, members):
        flat_row = slots_ref[shift - 1]
        taken = take_faces(parts, hot_elements(flat_row, elements, dofs), hot_dofs(flat_row, dofs))
        target = lax.rem(me + shift, members)
        for probe in range(probes):
            leave_ref[target, pl.ds(probe, 1), :] = taken[probe]
    leave_ref[me] = jnp.zeros(leave_ref.shape[1:], f32)


def placed_faces(shape, probes, slots_ref, came_ref):
    rows, dofs = shape
    elements = rows // probes
    members = slots_ref.shape[0] + 1
    me = lax.axis_index("gz")
    total = jnp.zeros((2 * rows, dofs), f32)
    for shift in range(1, members):
        flat_row = slots_ref[shift - 1]
        came = came_ref[lax.rem(me + shift, members)]
        total += add_faces(
            [came[probe : probe + 1, :] for probe in range(probes)],
            hot_elements(flat_row, elements, dofs),
            hot_dofs(flat_row, dofs),
        )
    return folded(total)


def far_first_kernel(*refs):
    operands, refs = refs[:6], refs[6:]
    first_ref, source_ref, up_ref, down_ref, slots_ref, leave_ref = refs[:6]
    members = slots_ref.shape[0] + 1
    first_pre, _, _ = begin(
        {
            "operands": operands,
            "scratch": refs[6:],
            "slots": slots_ref,
            "up": up_ref,
            "down": down_ref,
            "source": source_ref,
            "first": first_ref,
        },
        lambda me, step: lax.rem(me + step, members),
    )
    leave_faces(first_pre, leave_ref.shape[1], slots_ref, leave_ref)


def far_second_kernel(
    slots_ref, up_ref, down_ref, first_ref, k_ref, p_ref, came_ref,
    image_ref, second_ref, leave_ref,
):
    probes = came_ref.shape[1]
    up = up_ref[...]
    placed = placed_faces(first_ref.shape, probes, slots_ref, came_ref)
    image = times_matrix(first_ref[...], k_ref[...]) * up - jnp.where(up > 0.0, coupling * placed, 0.0)
    image_ref[...] = image
    second_pre = times_matrix(image, p_ref[...]) * down_ref[...]
    second_ref[...] = second_pre
    leave_faces(second_pre, probes, slots_ref, leave_ref)


def far_third_kernel(
    slots_ref, up_ref, source_ref, image_ref, second_ref, k_ref, came_ref, products_ref
):
    probes = came_ref.shape[1]
    up = up_ref[...]
    placed = placed_faces(source_ref.shape, probes, slots_ref, came_ref)
    second_img = times_matrix(second_ref[...], k_ref[...]) * up - jnp.where(up > 0.0, coupling * placed, 0.0)
    inner_products(image_ref[...], second_img, source_ref[...], probes, products_ref)


def last_kernel(probes, first_ref, second_ref, parts_ref, out_ref):
    rows, _ = first_ref.shape
    elements = rows // probes
    total = jnp.sum(parts_ref[...], axis=0)
    for probe in range(probes):
        self_one, cross_mid, self_two, load_one, load_two = (
            total[:, place * probes + probe : place * probes + probe + 1] for place in range(5)
        )
        determinant = self_one * self_two - cross_mid * cross_mid
        weight_one = (self_two * load_one - cross_mid * load_two) / determinant
        weight_two = (self_one * load_two - cross_mid * load_one) / determinant
        block = pl.ds(probe * elements, elements)
        out_ref[block, :] = weight_one * first_ref[block, :] + weight_two * second_ref[block, :]


def call(kernel, in_specs, out_shapes, flops, *args, scratch=()):
    return pl.pallas_call(
        kernel,
        out_shape=out_shapes,
        in_specs=in_specs,
        out_specs=jax.tree.map(lambda _: vmem_spec, out_shapes),
        scratch_shapes=scratch,
        compiler_params=pltpu.CompilerParams(vmem_limit_bytes=vmem_grant),
        cost_estimate=pl.CostEstimate(flops=flops, bytes_accessed=1 << 20, transcendentals=0),
    )(*args)


def begin_call(kernel, out_shapes, flops, counts, *fetched):
    links, *others = fetched
    scratch = [pltpu.SMEM(links.shape, links.dtype)]
    scratch += [pltpu.VMEM(value.shape, value.dtype) for value in others]
    return call(
        kernel,
        [smem_spec] + [hbm_spec] * len(fetched),
        out_shapes,
        flops,
        counts,
        *(pltpu.with_memory_space_constraint(value, pltpu.HBM) for value in fetched),
        scratch=scratch + [pltpu.SemaphoreType.DMA((len(fetched),))],
    )


def near_steps(members, shapes, arguments):
    rhs, viscosity, counts, neighbours, face_index, k_matrix, p_matrix = arguments
    field, slots_shape, products_shape = shapes
    rows, dofs = field.shape
    steps, _, width = slots_shape.shape
    probes = rhs.shape[3]
    flops = 8 * rows * dofs * steps * width
    hot = jax.ShapeDtypeStruct((dofs, steps * width), bf16)
    length = message_places(steps, probes)[2] + 1
    messages = [jax.ShapeDtypeStruct((length, 1, width), f32)] * steps
    first_pre, source, up, down, base, slots, hot_own, *leaving = begin_call(
        near_first_kernel,
        [field] * 5 + [slots_shape, hot] + messages,
        2 * flops,
        counts,
        neighbours,
        face_index,
        viscosity,
        rhs,
        p_matrix,
        k_matrix,
    )
    came = [
        lax.ppermute(
            leaving[step - 1], "gz", [(source, source ^ step) for source in range(members)]
        )
        for step in range(steps, 0, -1)
    ]
    second_pre, products = call(
        near_second_kernel,
        [vmem_spec] * (9 + steps),
        [field, products_shape],
        6 * flops,
        source,
        up,
        down,
        base,
        slots,
        hot_own,
        k_matrix,
        p_matrix,
        leaving[0],
        *came,
    )
    return first_pre, second_pre, products


def far_steps(members, shapes, arguments):
    rhs, viscosity, counts, neighbours, face_index, k_matrix, p_matrix = arguments
    field, slots_shape, products_shape = shapes
    rows, dofs = field.shape
    shifts, _, width = slots_shape.shape
    flops = 8 * rows * dofs * shifts * width
    faces = jax.ShapeDtypeStruct((members, rhs.shape[3], width), f32)

    def exchange(value):
        return lax.all_to_all(value, "gz", split_axis=0, concat_axis=0)

    first_pre, source, up, down, slots, leaving = begin_call(
        far_first_kernel,
        [field] * 4 + [slots_shape, faces],
        flops,
        counts,
        neighbours,
        face_index,
        viscosity,
        rhs,
        p_matrix,
    )
    first_img, second_pre, leaving = call(
        far_second_kernel,
        [vmem_spec] * 7,
        [field, field, faces],
        2 * flops,
        slots,
        up,
        down,
        first_pre,
        k_matrix,
        p_matrix,
        exchange(leaving),
    )
    products = call(
        far_third_kernel,
        [vmem_spec] * 7,
        products_shape,
        flops,
        slots,
        up,
        source,
        first_img,
        second_pre,
        k_matrix,
        exchange(leaving),
    )
    return first_pre, second_pre, products


def per_device(mesh, *arguments):
    rhs, face_index = arguments[0], arguments[4]
    probes, elements, dofs = rhs.shape[3:]
    members = mesh.shape["gz"]
    lanes = -(-5 * probes // 128) * 128
    shapes = (
        jax.ShapeDtypeStruct((probes * elements, dofs), f32),
        jax.ShapeDtypeStruct((members - 1, 1, face_index.shape[-1]), jnp.int32),
        jax.ShapeDtypeStruct((mesh.size, 1, lanes), f32),
    )
    near = 1 < members <= short_group and elements <= face_index.shape[-1]
    near = near and elements * dofs < 1 << 24
    steps = near_steps if near else far_steps
    first_pre, second_pre, products = steps(members, shapes, arguments)
    result = call(
        functools.partial(last_kernel, probes),
        [vmem_spec] * 3,
        shapes[0],
        probes * elements * dofs,
        first_pre,
        second_pre,
        lax.all_to_all(products, ("gx", "gy", "gz"), split_axis=0, concat_axis=0),
    )
    return result.reshape(rhs.shape)


def solution(mesh):
    return jax.shard_map(
        functools.partial(per_device, mesh),
        mesh=mesh,
        in_specs=(
            P("gx", "gy", "gz", None, None, None),
            P("gx", "gy", "gz", None),
            P("gx", "gy", "gz"),
            P("gx", "gy", "gz", None),
            P("gx", "gy", "gz", None, None),
            P(),
            P(),
        ),
        out_specs=P("gx", "gy", "gz", None, None, None),
        check_vma=False,
    )
```

```python
import functools

import jax
import jax.numpy as jnp
from jax import lax
from jax.experimental import pallas as pl
from jax.experimental.pallas import tpu as pltpu
from jax.sharding import PartitionSpec as P

coupling = 0.5
vmem_grant = 48 * 1024 * 1024
short_group = 4
lane_count = 128
f32 = jnp.float32
bf16 = jnp.bfloat16
vmem_spec = pl.BlockSpec(memory_space=pltpu.VMEM)
smem_spec = pl.BlockSpec(memory_space=pltpu.SMEM)
hbm_spec = pl.BlockSpec(memory_space=pltpu.HBM)


def two_parts(value):
    high = value.astype(bf16)
    return high, (value - high.astype(f32)).astype(bf16)


def dot(left, right):
    return jnp.dot(left, right, preferred_element_type=f32)


def dot_transposed(left, right):
    return lax.dot_general(left, right, (((1,), (1,)), ((), ())), preferred_element_type=f32)


def times_matrix(rows, matrix):
    count = rows.shape[0]
    row_high, row_low = two_parts(rows)
    mat_high, mat_low = two_parts(matrix)
    both = dot(jnp.concatenate([row_high, row_low], axis=0), mat_high)
    return both[:count] + (both[count:] + dot(row_high, mat_low))


def split_index(index, dofs):
    if dofs & (dofs - 1) == 0:
        return lax.shift_right_arithmetic(index, dofs.bit_length() - 1), index & (dofs - 1)
    element = jnp.floor_divide(index, dofs)
    return element, index - element * dofs


def slot_of(target, links_ref, index_ref):
    slot = jnp.int32(-1)
    for position in range(links_ref.shape[-1]):
        slot = jnp.where(links_ref[0, 0, 0, position] == target, jnp.int32(position), slot)
    row = index_ref[0, 0, 0, pl.ds(jnp.maximum(slot, 0), 1), :]
    return jnp.where(slot >= 0, row, -1)


def hot_elements(flat_row, elements, dofs):
    element, _ = split_index(flat_row, dofs)
    return lax.broadcasted_iota(jnp.int32, (elements, flat_row.shape[1]), 0) == element


def hot_dofs(flat_row, dofs):
    _, dof = split_index(flat_row, dofs)
    shape = (dofs, flat_row.shape[1])
    line = lax.broadcasted_iota(jnp.int32, shape, 0).astype(jnp.int16)
    hit = line == jnp.broadcast_to(dof.astype(jnp.int16), shape)
    return jnp.where(hit, jnp.ones(shape, bf16), jnp.zeros(shape, bf16))


def as_column(row):
    elements = row.shape[1]
    line = lax.broadcasted_iota(jnp.int32, (elements, elements), 0)
    column = lax.broadcasted_iota(jnp.int32, (elements, elements), 1)
    spread = jnp.where(line == column, jnp.broadcast_to(row, (elements, elements)), 0.0)
    return jnp.sum(spread, axis=1, keepdims=True)


def wide(column, probes, dofs):
    return jnp.broadcast_to(jnp.concatenate([column] * probes, axis=0), (probes * column.shape[0], dofs))


def stacked(value):
    return jnp.concatenate(two_parts(value), axis=0)


def take_faces(parts, over_elements, over_dofs):
    elements = over_elements.shape[0]
    rows = parts.shape[0] // 2
    picked = dot(parts, over_dofs)
    picked = picked[:rows] + picked[rows:]
    return [
        jnp.sum(jnp.where(over_elements, picked[low : low + elements], 0.0), axis=0, keepdims=True)
        for low in range(0, rows, elements)
    ]


def add_faces(values, over_elements, over_dofs):
    highs = [value.astype(bf16).astype(f32) for value in values]
    lows = [value - high for value, high in zip(values, highs)]
    spread = jnp.concatenate(
        [jnp.where(over_elements, part, 0.0).astype(bf16) for part in highs + lows], axis=0
    )
    return dot_transposed(spread, over_dofs)


def folded(parts):
    rows = parts.shape[0] // 2
    return parts[:rows] + parts[rows:]


def as_row(lines, lanes):
    count = -(-len(lines) // 8) * 8
    spare = jnp.zeros((count - len(lines), lines[0].shape[1]), f32)
    sums = jnp.sum(jnp.concatenate(lines + [spare], axis=0), axis=1, keepdims=True)
    line = lax.broadcasted_iota(jnp.int32, (count, lanes), 0)
    lane = lax.broadcasted_iota(jnp.int32, (count, lanes), 1)
    return jnp.sum(jnp.where(line == lane, sums, 0.0), axis=0, keepdims=True)


def inner_products(first_img, second_img, source, probes, products_ref):
    elements = source.shape[0] // probes
    pairs = (
        (first_img, first_img),
        (first_img, second_img),
        (second_img, second_img),
        (first_img, source),
        (second_img, source),
    )
    lines = []
    for left, right in pairs:
        product = left * right
        for probe in range(probes):
            lines.append(
                jnp.sum(product[probe * elements : (probe + 1) * elements], axis=0, keepdims=True)
            )
    products_ref[...] = jnp.broadcast_to(as_row(lines, products_ref.shape[-1]), products_ref.shape)


def begin(refs, partner):
    count_ref, links_hbm, index_hbm, visc_hbm, rhs_hbm, *matrices_hbm = refs["operands"]
    links_ref, index_ref, visc_ref, rhs_ref, *matrix_refs, arrived = refs["scratch"]
    pairs = (
        (links_hbm, links_ref),
        (index_hbm, index_ref),
        (visc_hbm, visc_ref),
        (rhs_hbm, rhs_ref),
        *zip(matrices_hbm, matrix_refs),
    )
    copies = [
        pltpu.make_async_copy(held, here, arrived.at[place])
        for place, (held, here) in enumerate(pairs)
    ]
    for copy in copies:
        copy.start()
    copies[0].wait()
    copies[1].wait()
    slots_ref = refs["slots"]
    me = lax.axis_index("gz")
    for step in range(1, slots_ref.shape[0] + 1):
        slots_ref[step - 1] = slot_of(partner(me, step), links_ref, index_ref)
    copies[2].wait()
    probes, elements, dofs = rhs_ref.shape[3:]
    slot = lax.broadcasted_iota(jnp.int32, (elements, 1), 0)
    live = (slot < count_ref[0, 0, 0]).astype(f32)
    visc = as_column(visc_ref[0, 0])
    up = wide(live * visc, probes, dofs)
    down = wide(live / visc, probes, dofs)
    refs["up"][...] = up
    refs["down"][...] = down
    copies[3].wait()
    source = rhs_ref[...].reshape(probes * elements, dofs) * wide(live, probes, dofs)
    refs["source"][...] = source
    for copy in copies[4:]:
        copy.wait()
    first_pre = times_matrix(source, matrix_refs[0][...]) * down
    refs["first"][...] = first_pre
    return first_pre, up, down


def message_places(steps, probes):
    values = steps * probes
    return values, values + probes, values + probes + steps


def message_length(steps, probes, width):
    return -(-(message_places(steps, probes)[2] * (width // lane_count) + 1) // 8) * 8


def write_row(message_ref, place, row):
    pieces = row.shape[1] // lane_count
    for piece in range(pieces):
        line = place * pieces + piece
        message_ref[line : line + 1, :] = row[:, piece * lane_count : (piece + 1) * lane_count]


def read_row(message_ref, place, width):
    pieces = width // lane_count
    lines = range(place * pieces, (place + 1) * pieces)
    return jnp.concatenate([message_ref[line : line + 1, :] for line in lines], axis=1)


def near_first_kernel(*refs):
    operands, refs = refs[:7], refs[7:]
    first_ref, source_ref, up_ref, down_ref, base_ref, slots_ref, hot_ref = refs[:7]
    steps, _, width = slots_ref.shape
    leave_refs, scratch = refs[7 : 7 + steps], refs[7 + steps :]
    visc_ref, rhs_ref, p_ref, k_ref = scratch[2:6]
    probes, elements, dofs = rhs_ref.shape[3:]
    first_pre, up, down = begin(
        {
            "operands": operands,
            "scratch": scratch,
            "slots": slots_ref,
            "up": up_ref,
            "down": down_ref,
            "source": source_ref,
            "first": first_ref,
        },
        lambda me, step: me ^ step,
    )
    base = times_matrix(first_pre, k_ref[...]) * up
    base_ref[...] = base
    first_parts = stacked(first_pre)
    second_parts = stacked(times_matrix(base, p_ref[...]) * down)
    second_at, index_at, visc_at = message_places(steps, probes)
    slot = lax.broadcasted_iota(jnp.int32, (1, elements), 1)
    live_visc = jnp.where(slot < operands[0][0, 0, 0], visc_ref[0, 0], 0.0)
    for step in range(1, steps + 1):
        flat_row = slots_ref[step - 1]
        over_elements = hot_elements(flat_row, elements, dofs)
        over_dofs = hot_dofs(flat_row, dofs)
        hot_ref[:, (step - 1) * width : step * width] = over_dofs
        first_rows = take_faces(first_parts, over_elements, over_dofs)
        second_rows = take_faces(second_parts, over_elements, over_dofs)
        for probe in range(probes):
            write_row(leave_refs[step - 1], second_at + probe, second_rows[probe])
            for leave_ref in leave_refs:
                write_row(leave_ref, (step - 1) * probes + probe, first_rows[probe])
        for leave_ref in leave_refs:
            write_row(leave_ref, index_at + step - 1, flat_row.astype(f32))
    visc_line = visc_at * (width // lane_count)
    for leave_ref in leave_refs:
        leave_ref[visc_line : visc_line + 1, :elements] = live_visc


def near_second_kernel(
    probes, source_ref, up_ref, down_ref, base_ref, slots_ref, hot_ref, k_ref, p_ref, mine_ref, *refs
):
    came_refs = refs[:-2]
    second_ref, products_ref = refs[-2:]
    steps, _, width = slots_ref.shape
    members = steps + 1
    rows, dofs = source_ref.shape
    elements = rows // probes
    second_at, index_at, visc_at = message_places(steps, probes)

    def message(step):
        return mine_ref if step == 0 else came_refs[step - 1]

    def inbound_first(member, step):
        sent = message(member ^ step)
        return [
            read_row(sent, (step - 1) * probes + probe, width) for probe in range(probes)
        ]

    own_elements = [hot_elements(slots_ref[step], elements, dofs) for step in range(steps)]
    own_dofs = [hot_ref[:, step * width : (step + 1) * width] for step in range(steps)]

    def placed_here(values):
        return folded(
            sum(add_faces(values[i], own_elements[i], own_dofs[i]) for i in range(steps))
        )

    up, down = up_ref[...], down_ref[...]
    live = up > 0.0
    placed = placed_here([inbound_first(0, step) for step in range(1, members)])
    image = base_ref[...] - jnp.where(live, coupling * placed, 0.0)
    images, back = [image], []
    for member in range(1, members):
        total = 0.0
        for step in range(1, members):
            flat_row = read_row(message(member), index_at + step - 1, width).astype(jnp.int32)
            over_elements = hot_elements(flat_row, elements, dofs)
            over_dofs = hot_dofs(flat_row, dofs)
            total = total + add_faces(inbound_first(member, step), over_elements, over_dofs)
            if step == member:
                back.append((over_elements, over_dofs))
        images.append(-coupling * folded(total))
    smooth = times_matrix(jnp.concatenate(images, axis=0), p_ref[...])
    second_pre = smooth[:rows] * down
    second_ref[...] = second_pre
    values = []
    visc_line = visc_at * (width // lane_count)
    for member in range(1, members):
        sent = message(member)
        visc = as_column(sent[visc_line : visc_line + 1, :elements])
        scale = wide(jnp.where(visc > 0.0, 1.0 / visc, 0.0), probes, dofs)
        change = smooth[member * rows : (member + 1) * rows] * scale
        taken = take_faces(stacked(change), *back[member - 1])
        values.append(
            [taken[probe] + read_row(sent, second_at + probe, width) for probe in range(probes)]
        )
    placed = placed_here(values)
    second_img = times_matrix(second_pre, k_ref[...]) * up - jnp.where(live, coupling * placed, 0.0)
    inner_products(image, second_img, source_ref[...], probes, products_ref)


def leave_faces(field, probes, slots_ref, leave_ref):
    elements, dofs = field.shape[0] // probes, field.shape[1]
    members = slots_ref.shape[0] + 1
    parts = stacked(field)
    me = lax.axis_index("gz")
    for shift in range(1, members):
        flat_row = slots_ref[shift - 1]
        taken = take_faces(parts, hot_elements(flat_row, elements, dofs), hot_dofs(flat_row, dofs))
        target = lax.rem(me + shift, members)
        for probe in range(probes):
            leave_ref[target, pl.ds(probe, 1), :] = taken[probe]
    leave_ref[me] = jnp.zeros(leave_ref.shape[1:], f32)


def placed_faces(shape, probes, slots_ref, came_ref):
    rows, dofs = shape
    elements = rows // probes
    members = slots_ref.shape[0] + 1
    me = lax.axis_index("gz")
    total = jnp.zeros((2 * rows, dofs), f32)
    for shift in range(1, members):
        flat_row = slots_ref[shift - 1]
        came = came_ref[lax.rem(me + shift, members)]
        total += add_faces(
            [came[probe : probe + 1, :] for probe in range(probes)],
            hot_elements(flat_row, elements, dofs),
            hot_dofs(flat_row, dofs),
        )
    return folded(total)


def far_first_kernel(*refs):
    operands, refs = refs[:6], refs[6:]
    first_ref, source_ref, up_ref, down_ref, slots_ref, leave_ref = refs[:6]
    members = slots_ref.shape[0] + 1
    first_pre, _, _ = begin(
        {
            "operands": operands,
            "scratch": refs[6:],
            "slots": slots_ref,
            "up": up_ref,
            "down": down_ref,
            "source": source_ref,
            "first": first_ref,
        },
        lambda me, step: lax.rem(me + step, members),
    )
    leave_faces(first_pre, leave_ref.shape[1], slots_ref, leave_ref)


def far_second_kernel(
    slots_ref, up_ref, down_ref, first_ref, k_ref, p_ref, came_ref,
    image_ref, second_ref, leave_ref,
):
    probes = came_ref.shape[1]
    up = up_ref[...]
    placed = placed_faces(first_ref.shape, probes, slots_ref, came_ref)
    image = times_matrix(first_ref[...], k_ref[...]) * up - jnp.where(up > 0.0, coupling * placed, 0.0)
    image_ref[...] = image
    second_pre = times_matrix(image, p_ref[...]) * down_ref[...]
    second_ref[...] = second_pre
    leave_faces(second_pre, probes, slots_ref, leave_ref)


def far_third_kernel(
    slots_ref, up_ref, source_ref, image_ref, second_ref, k_ref, came_ref, products_ref
):
    probes = came_ref.shape[1]
    up = up_ref[...]
    placed = placed_faces(source_ref.shape, probes, slots_ref, came_ref)
    second_img = times_matrix(second_ref[...], k_ref[...]) * up - jnp.where(up > 0.0, coupling * placed, 0.0)
    inner_products(image_ref[...], second_img, source_ref[...], probes, products_ref)


def last_kernel(probes, first_ref, second_ref, parts_ref, out_ref):
    rows, _ = first_ref.shape
    elements = rows // probes
    total = jnp.sum(parts_ref[...], axis=0)
    for probe in range(probes):
        self_one, cross_mid, self_two, load_one, load_two = (
            total[:, place * probes + probe : place * probes + probe + 1] for place in range(5)
        )
        determinant = self_one * self_two - cross_mid * cross_mid
        weight_one = (self_two * load_one - cross_mid * load_two) / determinant
        weight_two = (self_one * load_two - cross_mid * load_one) / determinant
        block = pl.ds(probe * elements, elements)
        out_ref[block, :] = weight_one * first_ref[block, :] + weight_two * second_ref[block, :]


def call(kernel, in_specs, out_shapes, flops, *args, scratch=()):
    return pl.pallas_call(
        kernel,
        out_shape=out_shapes,
        in_specs=in_specs,
        out_specs=jax.tree.map(lambda _: vmem_spec, out_shapes),
        scratch_shapes=scratch,
        compiler_params=pltpu.CompilerParams(vmem_limit_bytes=vmem_grant),
        cost_estimate=pl.CostEstimate(flops=flops, bytes_accessed=1 << 20, transcendentals=0),
    )(*args)


def begin_call(kernel, out_shapes, flops, counts, *fetched):
    links, *others = fetched
    scratch = [pltpu.SMEM(links.shape, links.dtype)]
    scratch += [pltpu.VMEM(value.shape, value.dtype) for value in others]
    return call(
        kernel,
        [smem_spec] + [hbm_spec] * len(fetched),
        out_shapes,
        flops,
        counts,
        *(pltpu.with_memory_space_constraint(value, pltpu.HBM) for value in fetched),
        scratch=scratch + [pltpu.SemaphoreType.DMA((len(fetched),))],
    )


def near_steps(members, shapes, arguments):
    rhs, viscosity, counts, neighbours, face_index, k_matrix, p_matrix = arguments
    field, slots_shape, products_shape = shapes
    rows, dofs = field.shape
    steps, _, width = slots_shape.shape
    probes = rhs.shape[3]
    flops = 8 * rows * dofs * steps * width
    hot = jax.ShapeDtypeStruct((dofs, steps * width), bf16)
    message = jax.ShapeDtypeStruct((message_length(steps, probes, width), lane_count), f32)
    first_pre, source, up, down, base, slots, hot_own, *leaving = begin_call(
        near_first_kernel,
        [field] * 5 + [slots_shape, hot] + [message] * steps,
        2 * flops,
        counts,
        neighbours,
        face_index,
        viscosity,
        rhs,
        p_matrix,
        k_matrix,
    )
    came = [
        lax.ppermute(
            leaving[step - 1], "gz", [(source, source ^ step) for source in range(members)]
        )
        for step in range(1, members)
    ]
    second_pre, products = call(
        functools.partial(near_second_kernel, probes),
        [vmem_spec] * (9 + steps),
        [field, products_shape],
        6 * flops,
        source,
        up,
        down,
        base,
        slots,
        hot_own,
        k_matrix,
        p_matrix,
        leaving[0],
        *came,
    )
    return first_pre, second_pre, products


def far_steps(members, shapes, arguments):
    rhs, viscosity, counts, neighbours, face_index, k_matrix, p_matrix = arguments
    field, slots_shape, products_shape = shapes
    rows, dofs = field.shape
    shifts, _, width = slots_shape.shape
    flops = 8 * rows * dofs * shifts * width
    faces = jax.ShapeDtypeStruct((members, rhs.shape[3], width), f32)

    def exchange(value):
        return lax.all_to_all(value, "gz", split_axis=0, concat_axis=0)

    first_pre, source, up, down, slots, leaving = begin_call(
        far_first_kernel,
        [field] * 4 + [slots_shape, faces],
        flops,
        counts,
        neighbours,
        face_index,
        viscosity,
        rhs,
        p_matrix,
    )
    first_img, second_pre, leaving = call(
        far_second_kernel,
        [vmem_spec] * 7,
        [field, field, faces],
        2 * flops,
        slots,
        up,
        down,
        first_pre,
        k_matrix,
        p_matrix,
        exchange(leaving),
    )
    products = call(
        far_third_kernel,
        [vmem_spec] * 7,
        products_shape,
        flops,
        slots,
        up,
        source,
        first_img,
        second_pre,
        k_matrix,
        exchange(leaving),
    )
    return first_pre, second_pre, products


def per_device(mesh, *arguments):
    rhs, face_index = arguments[0], arguments[4]
    probes, elements, dofs = rhs.shape[3:]
    members = mesh.shape["gz"]
    lanes = -(-5 * probes // 128) * 128
    shapes = (
        jax.ShapeDtypeStruct((probes * elements, dofs), f32),
        jax.ShapeDtypeStruct((members - 1, 1, face_index.shape[-1]), jnp.int32),
        jax.ShapeDtypeStruct((mesh.size, 1, lanes), f32),
    )
    near = 1 < members <= short_group and elements <= face_index.shape[-1]
    near = near and elements * dofs < 1 << 24
    steps = near_steps if near else far_steps
    first_pre, second_pre, products = steps(members, shapes, arguments)
    result = call(
        functools.partial(last_kernel, probes),
        [vmem_spec] * 3,
        shapes[0],
        probes * elements * dofs,
        first_pre,
        second_pre,
        lax.all_to_all(products, ("gx", "gy", "gz"), split_axis=0, concat_axis=0),
    )
    return result.reshape(rhs.shape)


def solution(mesh):
    return jax.shard_map(
        functools.partial(per_device, mesh),
        mesh=mesh,
        in_specs=(
            P("gx", "gy", "gz", None, None, None),
            P("gx", "gy", "gz", None),
            P("gx", "gy", "gz"),
            P("gx", "gy", "gz", None),
            P("gx", "gy", "gz", None, None),
            P(),
            P(),
        ),
        out_specs=P("gx", "gy", "gz", None, None, None),
        check_vma=False,
    )
```

```python
import functools

import jax
import jax.numpy as jnp
from jax import lax
from jax.experimental import pallas as pl
from jax.experimental.pallas import tpu as pltpu
from jax.sharding import PartitionSpec as P

coupling = 0.5
vmem_grant = 48 * 1024 * 1024
short_group = 4
lane_count = 128
f32 = jnp.float32
bf16 = jnp.bfloat16
vmem_spec = pl.BlockSpec(memory_space=pltpu.VMEM)
smem_spec = pl.BlockSpec(memory_space=pltpu.SMEM)
hbm_spec = pl.BlockSpec(memory_space=pltpu.HBM)


def two_parts(value):
    high = value.astype(bf16)
    return high, (value - high.astype(f32)).astype(bf16)


def dot(left, right):
    return jnp.dot(left, right, preferred_element_type=f32)


def dot_transposed(left, right):
    return lax.dot_general(left, right, (((1,), (1,)), ((), ())), preferred_element_type=f32)


def times_matrix(rows, matrix):
    count = rows.shape[0]
    row_high, row_low = two_parts(rows)
    mat_high, mat_low = two_parts(matrix)
    both = dot(jnp.concatenate([row_high, row_low], axis=0), mat_high)
    return both[:count] + (both[count:] + dot(row_high, mat_low))


def split_index(index, dofs):
    if dofs & (dofs - 1) == 0:
        return lax.shift_right_arithmetic(index, dofs.bit_length() - 1), index & (dofs - 1)
    element = jnp.floor_divide(index, dofs)
    return element, index - element * dofs


def slot_of(target, links_ref, index_ref):
    slot = jnp.int32(-1)
    for position in range(links_ref.shape[-1]):
        slot = jnp.where(links_ref[0, 0, 0, position] == target, jnp.int32(position), slot)
    row = index_ref[0, 0, 0, pl.ds(jnp.maximum(slot, 0), 1), :]
    return jnp.where(slot >= 0, row, -1)


def hot_elements(flat_row, elements, dofs):
    element, _ = split_index(flat_row, dofs)
    return lax.broadcasted_iota(jnp.int32, (elements, flat_row.shape[1]), 0) == element


def hot_dofs(flat_row, dofs):
    _, dof = split_index(flat_row, dofs)
    shape = (dofs, flat_row.shape[1])
    line = lax.broadcasted_iota(jnp.int32, shape, 0).astype(jnp.int16)
    hit = line == jnp.broadcast_to(dof.astype(jnp.int16), shape)
    return jnp.where(hit, jnp.ones(shape, bf16), jnp.zeros(shape, bf16))


def as_column(row):
    elements = row.shape[1]
    line = lax.broadcasted_iota(jnp.int32, (elements, elements), 0)
    column = lax.broadcasted_iota(jnp.int32, (elements, elements), 1)
    spread = jnp.where(line == column, jnp.broadcast_to(row, (elements, elements)), 0.0)
    return jnp.sum(spread, axis=1, keepdims=True)


def wide(column, probes, dofs):
    return jnp.broadcast_to(jnp.concatenate([column] * probes, axis=0), (probes * column.shape[0], dofs))


def stacked(value):
    return jnp.concatenate(two_parts(value), axis=0)


def take_faces(parts, over_elements, over_dofs):
    elements = over_elements.shape[0]
    rows = parts.shape[0] // 2
    picked = dot(parts, over_dofs)
    picked = picked[:rows] + picked[rows:]
    return [
        jnp.sum(jnp.where(over_elements, picked[low : low + elements], 0.0), axis=0, keepdims=True)
        for low in range(0, rows, elements)
    ]


def add_faces(values, over_elements, over_dofs):
    highs = [value.astype(bf16).astype(f32) for value in values]
    lows = [value - high for value, high in zip(values, highs)]
    spread = jnp.concatenate(
        [jnp.where(over_elements, part, 0.0).astype(bf16) for part in highs + lows], axis=0
    )
    return dot_transposed(spread, over_dofs)


def folded(parts):
    rows = parts.shape[0] // 2
    return parts[:rows] + parts[rows:]


def as_row(lines, lanes):
    count = -(-len(lines) // 8) * 8
    spare = jnp.zeros((count - len(lines), lines[0].shape[1]), f32)
    sums = jnp.sum(jnp.concatenate(lines + [spare], axis=0), axis=1, keepdims=True)
    line = lax.broadcasted_iota(jnp.int32, (count, lanes), 0)
    lane = lax.broadcasted_iota(jnp.int32, (count, lanes), 1)
    return jnp.sum(jnp.where(line == lane, sums, 0.0), axis=0, keepdims=True)


def inner_products(first_img, second_img, source, probes, products_ref):
    elements = source.shape[0] // probes
    pairs = (
        (first_img, first_img),
        (first_img, second_img),
        (second_img, second_img),
        (first_img, source),
        (second_img, source),
    )
    lines = []
    for left, right in pairs:
        product = left * right
        for probe in range(probes):
            lines.append(
                jnp.sum(product[probe * elements : (probe + 1) * elements], axis=0, keepdims=True)
            )
    products_ref[...] = as_row(lines, products_ref.shape[-1])


def begin(refs, partner):
    count_ref, links_hbm, index_hbm, visc_hbm, rhs_hbm, *matrices_hbm = refs["operands"]
    links_ref, index_ref, visc_ref, rhs_ref, *matrix_refs, arrived = refs["scratch"]
    pairs = (
        (links_hbm, links_ref),
        (index_hbm, index_ref),
        (visc_hbm, visc_ref),
        (rhs_hbm, rhs_ref),
        *zip(matrices_hbm, matrix_refs),
    )
    copies = [
        pltpu.make_async_copy(held, here, arrived.at[place])
        for place, (held, here) in enumerate(pairs)
    ]
    for copy in copies:
        copy.start()
    copies[0].wait()
    copies[1].wait()
    slots_ref = refs["slots"]
    me = lax.axis_index("gz")
    for step in range(1, slots_ref.shape[0] + 1):
        slots_ref[step - 1] = slot_of(partner(me, step), links_ref, index_ref)
    copies[2].wait()
    probes, elements, dofs = rhs_ref.shape[3:]
    slot = lax.broadcasted_iota(jnp.int32, (elements, 1), 0)
    live = (slot < count_ref[0, 0, 0]).astype(f32)
    visc = as_column(visc_ref[0, 0])
    up = wide(live * visc, probes, dofs)
    down = wide(live / visc, probes, dofs)
    refs["up"][...] = up
    refs["down"][...] = down
    copies[3].wait()
    source = rhs_ref[...].reshape(probes * elements, dofs) * wide(live, probes, dofs)
    refs["source"][...] = source
    for copy in copies[4:]:
        copy.wait()
    first_pre = times_matrix(source, matrix_refs[0][...]) * down
    refs["first"][...] = first_pre
    return first_pre, up, down


def message_places(steps, probes):
    values = steps * probes
    return values, values + probes, values + probes + steps


def message_length(steps, probes, width):
    return -(-(message_places(steps, probes)[2] * (width // lane_count) + 1) // 8) * 8


def write_row(message_ref, place, row):
    pieces = row.shape[1] // lane_count
    for piece in range(pieces):
        line = place * pieces + piece
        message_ref[line : line + 1, :] = row[:, piece * lane_count : (piece + 1) * lane_count]


def read_row(message_ref, place, width):
    pieces = width // lane_count
    lines = range(place * pieces, (place + 1) * pieces)
    return jnp.concatenate([message_ref[line : line + 1, :] for line in lines], axis=1)


def near_first_kernel(*refs):
    operands, refs = refs[:7], refs[7:]
    first_ref, source_ref, up_ref, down_ref, base_ref, slots_ref, hot_ref = refs[:7]
    steps, _, width = slots_ref.shape
    leave_refs, scratch = refs[7 : 7 + steps], refs[7 + steps :]
    visc_ref, rhs_ref, p_ref, k_ref = scratch[2:6]
    probes, elements, dofs = rhs_ref.shape[3:]
    first_pre, up, down = begin(
        {
            "operands": operands,
            "scratch": scratch,
            "slots": slots_ref,
            "up": up_ref,
            "down": down_ref,
            "source": source_ref,
            "first": first_ref,
        },
        lambda me, step: me ^ step,
    )
    base = times_matrix(first_pre, k_ref[...]) * up
    base_ref[...] = base
    first_parts = stacked(first_pre)
    second_parts = stacked(times_matrix(base, p_ref[...]) * down)
    second_at, index_at, visc_at = message_places(steps, probes)
    slot = lax.broadcasted_iota(jnp.int32, (1, elements), 1)
    live_visc = jnp.where(slot < operands[0][0, 0, 0], visc_ref[0, 0], 0.0)
    for step in range(1, steps + 1):
        flat_row = slots_ref[step - 1]
        over_elements = hot_elements(flat_row, elements, dofs)
        over_dofs = hot_dofs(flat_row, dofs)
        hot_ref[:, (step - 1) * width : step * width] = over_dofs
        first_rows = take_faces(first_parts, over_elements, over_dofs)
        second_rows = take_faces(second_parts, over_elements, over_dofs)
        for probe in range(probes):
            write_row(leave_refs[step - 1], second_at + probe, second_rows[probe])
            for leave_ref in leave_refs:
                write_row(leave_ref, (step - 1) * probes + probe, first_rows[probe])
        for leave_ref in leave_refs:
            write_row(leave_ref, index_at + step - 1, flat_row.astype(f32))
    visc_line = visc_at * (width // lane_count)
    for leave_ref in leave_refs:
        leave_ref[visc_line : visc_line + 1, :elements] = live_visc


def near_second_kernel(
    probes, source_ref, up_ref, down_ref, base_ref, slots_ref, hot_ref, k_ref, p_ref, mine_ref, *refs
):
    came_refs = refs[:-2]
    second_ref, products_ref = refs[-2:]
    steps, _, width = slots_ref.shape
    members = steps + 1
    rows, dofs = source_ref.shape
    elements = rows // probes
    second_at, index_at, visc_at = message_places(steps, probes)

    def message(step):
        return mine_ref if step == 0 else came_refs[step - 1]

    def inbound_first(member, step):
        sent = message(member ^ step)
        return [
            read_row(sent, (step - 1) * probes + probe, width) for probe in range(probes)
        ]

    own_elements = [hot_elements(slots_ref[step], elements, dofs) for step in range(steps)]
    own_dofs = [hot_ref[:, step * width : (step + 1) * width] for step in range(steps)]

    def placed_here(values):
        return folded(
            sum(add_faces(values[i], own_elements[i], own_dofs[i]) for i in range(steps))
        )

    up, down = up_ref[...], down_ref[...]
    live = up > 0.0
    placed = placed_here([inbound_first(0, step) for step in range(1, members)])
    image = base_ref[...] - jnp.where(live, coupling * placed, 0.0)
    images, back = [image], []
    for member in range(1, members):
        total = 0.0
        for step in range(1, members):
            flat_row = read_row(message(member), index_at + step - 1, width).astype(jnp.int32)
            over_elements = hot_elements(flat_row, elements, dofs)
            over_dofs = hot_dofs(flat_row, dofs)
            total = total + add_faces(inbound_first(member, step), over_elements, over_dofs)
            if step == member:
                back.append((over_elements, over_dofs))
        images.append(-coupling * folded(total))
    smooth = times_matrix(jnp.concatenate(images, axis=0), p_ref[...])
    second_pre = smooth[:rows] * down
    second_ref[...] = second_pre
    values = []
    visc_line = visc_at * (width // lane_count)
    for member in range(1, members):
        sent = message(member)
        visc = as_column(sent[visc_line : visc_line + 1, :elements])
        scale = wide(jnp.where(visc > 0.0, 1.0 / visc, 0.0), probes, dofs)
        change = smooth[member * rows : (member + 1) * rows] * scale
        taken = take_faces(stacked(change), *back[member - 1])
        values.append(
            [taken[probe] + read_row(sent, second_at + probe, width) for probe in range(probes)]
        )
    placed = placed_here(values)
    second_img = times_matrix(second_pre, k_ref[...]) * up - jnp.where(live, coupling * placed, 0.0)
    inner_products(image, second_img, source_ref[...], probes, products_ref)


def leave_faces(field, probes, slots_ref, leave_ref):
    elements, dofs = field.shape[0] // probes, field.shape[1]
    members = slots_ref.shape[0] + 1
    parts = stacked(field)
    me = lax.axis_index("gz")
    for shift in range(1, members):
        flat_row = slots_ref[shift - 1]
        taken = take_faces(parts, hot_elements(flat_row, elements, dofs), hot_dofs(flat_row, dofs))
        target = lax.rem(me + shift, members)
        for probe in range(probes):
            leave_ref[target, pl.ds(probe, 1), :] = taken[probe]
    leave_ref[me] = jnp.zeros(leave_ref.shape[1:], f32)


def placed_faces(shape, probes, slots_ref, came_ref):
    rows, dofs = shape
    elements = rows // probes
    members = slots_ref.shape[0] + 1
    me = lax.axis_index("gz")
    total = jnp.zeros((2 * rows, dofs), f32)
    for shift in range(1, members):
        flat_row = slots_ref[shift - 1]
        came = came_ref[lax.rem(me + shift, members)]
        total += add_faces(
            [came[probe : probe + 1, :] for probe in range(probes)],
            hot_elements(flat_row, elements, dofs),
            hot_dofs(flat_row, dofs),
        )
    return folded(total)


def far_first_kernel(*refs):
    operands, refs = refs[:6], refs[6:]
    first_ref, source_ref, up_ref, down_ref, slots_ref, leave_ref = refs[:6]
    members = slots_ref.shape[0] + 1
    first_pre, _, _ = begin(
        {
            "operands": operands,
            "scratch": refs[6:],
            "slots": slots_ref,
            "up": up_ref,
            "down": down_ref,
            "source": source_ref,
            "first": first_ref,
        },
        lambda me, step: lax.rem(me + step, members),
    )
    leave_faces(first_pre, leave_ref.shape[1], slots_ref, leave_ref)


def far_second_kernel(
    slots_ref, up_ref, down_ref, first_ref, k_ref, p_ref, came_ref,
    image_ref, second_ref, leave_ref,
):
    probes = came_ref.shape[1]
    up = up_ref[...]
    placed = placed_faces(first_ref.shape, probes, slots_ref, came_ref)
    image = times_matrix(first_ref[...], k_ref[...]) * up - jnp.where(up > 0.0, coupling * placed, 0.0)
    image_ref[...] = image
    second_pre = times_matrix(image, p_ref[...]) * down_ref[...]
    second_ref[...] = second_pre
    leave_faces(second_pre, probes, slots_ref, leave_ref)


def far_third_kernel(
    slots_ref, up_ref, source_ref, image_ref, second_ref, k_ref, came_ref, products_ref
):
    probes = came_ref.shape[1]
    up = up_ref[...]
    placed = placed_faces(source_ref.shape, probes, slots_ref, came_ref)
    second_img = times_matrix(second_ref[...], k_ref[...]) * up - jnp.where(up > 0.0, coupling * placed, 0.0)
    inner_products(image_ref[...], second_img, source_ref[...], probes, products_ref)


def last_kernel(probes, first_ref, second_ref, total_ref, out_ref):
    rows, _ = first_ref.shape
    elements = rows // probes
    total = total_ref[...]
    for probe in range(probes):
        self_one, cross_mid, self_two, load_one, load_two = (
            total[:, place * probes + probe : place * probes + probe + 1] for place in range(5)
        )
        determinant = self_one * self_two - cross_mid * cross_mid
        weight_one = (self_two * load_one - cross_mid * load_two) / determinant
        weight_two = (self_one * load_two - cross_mid * load_one) / determinant
        block = pl.ds(probe * elements, elements)
        out_ref[block, :] = weight_one * first_ref[block, :] + weight_two * second_ref[block, :]


def call(kernel, in_specs, out_shapes, flops, *args, scratch=()):
    return pl.pallas_call(
        kernel,
        out_shape=out_shapes,
        in_specs=in_specs,
        out_specs=jax.tree.map(lambda _: vmem_spec, out_shapes),
        scratch_shapes=scratch,
        compiler_params=pltpu.CompilerParams(vmem_limit_bytes=vmem_grant),
        cost_estimate=pl.CostEstimate(flops=flops, bytes_accessed=1 << 20, transcendentals=0),
    )(*args)


def begin_call(kernel, out_shapes, flops, counts, *fetched):
    links, *others = fetched
    scratch = [pltpu.SMEM(links.shape, links.dtype)]
    scratch += [pltpu.VMEM(value.shape, value.dtype) for value in others]
    return call(
        kernel,
        [smem_spec] + [hbm_spec] * len(fetched),
        out_shapes,
        flops,
        counts,
        *(pltpu.with_memory_space_constraint(value, pltpu.HBM) for value in fetched),
        scratch=scratch + [pltpu.SemaphoreType.DMA((len(fetched),))],
    )


def near_steps(members, shapes, arguments):
    rhs, viscosity, counts, neighbours, face_index, k_matrix, p_matrix = arguments
    field, slots_shape, products_shape = shapes
    rows, dofs = field.shape
    steps, _, width = slots_shape.shape
    probes = rhs.shape[3]
    flops = 8 * rows * dofs * steps * width
    hot = jax.ShapeDtypeStruct((dofs, steps * width), bf16)
    message = jax.ShapeDtypeStruct((message_length(steps, probes, width), lane_count), f32)
    first_pre, source, up, down, base, slots, hot_own, *leaving = begin_call(
        near_first_kernel,
        [field] * 5 + [slots_shape, hot] + [message] * steps,
        2 * flops,
        counts,
        neighbours,
        face_index,
        viscosity,
        rhs,
        p_matrix,
        k_matrix,
    )
    came = [
        lax.ppermute(
            leaving[step - 1], "gz", [(source, source ^ step) for source in range(members)]
        )
        for step in range(1, members)
    ]
    second_pre, products = call(
        functools.partial(near_second_kernel, probes),
        [vmem_spec] * (9 + steps),
        [field, products_shape],
        6 * flops,
        source,
        up,
        down,
        base,
        slots,
        hot_own,
        k_matrix,
        p_matrix,
        leaving[0],
        *came,
    )
    return first_pre, second_pre, products


def far_steps(members, shapes, arguments):
    rhs, viscosity, counts, neighbours, face_index, k_matrix, p_matrix = arguments
    field, slots_shape, products_shape = shapes
    rows, dofs = field.shape
    shifts, _, width = slots_shape.shape
    flops = 8 * rows * dofs * shifts * width
    faces = jax.ShapeDtypeStruct((members, rhs.shape[3], width), f32)

    def exchange(value):
        return lax.all_to_all(value, "gz", split_axis=0, concat_axis=0)

    first_pre, source, up, down, slots, leaving = begin_call(
        far_first_kernel,
        [field] * 4 + [slots_shape, faces],
        flops,
        counts,
        neighbours,
        face_index,
        viscosity,
        rhs,
        p_matrix,
    )
    first_img, second_pre, leaving = call(
        far_second_kernel,
        [vmem_spec] * 7,
        [field, field, faces],
        2 * flops,
        slots,
        up,
        down,
        first_pre,
        k_matrix,
        p_matrix,
        exchange(leaving),
    )
    products = call(
        far_third_kernel,
        [vmem_spec] * 7,
        products_shape,
        flops,
        slots,
        up,
        source,
        first_img,
        second_pre,
        k_matrix,
        exchange(leaving),
    )
    return first_pre, second_pre, products


def per_device(mesh, *arguments):
    rhs, face_index = arguments[0], arguments[4]
    probes, elements, dofs = rhs.shape[3:]
    members = mesh.shape["gz"]
    lanes = -(-5 * probes // 128) * 128
    shapes = (
        jax.ShapeDtypeStruct((probes * elements, dofs), f32),
        jax.ShapeDtypeStruct((members - 1, 1, face_index.shape[-1]), jnp.int32),
        jax.ShapeDtypeStruct((1, lanes), f32),
    )
    near = 1 < members <= short_group and elements <= face_index.shape[-1]
    near = near and elements * dofs < 1 << 24
    steps = near_steps if near else far_steps
    first_pre, second_pre, products = steps(members, shapes, arguments)
    result = call(
        functools.partial(last_kernel, probes),
        [vmem_spec] * 3,
        shapes[0],
        probes * elements * dofs,
        first_pre,
        second_pre,
        lax.psum(products, ("gx", "gy", "gz")),
    )
    return result.reshape(rhs.shape)


def solution(mesh):
    return jax.shard_map(
        functools.partial(per_device, mesh),
        mesh=mesh,
        in_specs=(
            P("gx", "gy", "gz", None, None, None),
            P("gx", "gy", "gz", None),
            P("gx", "gy", "gz"),
            P("gx", "gy", "gz", None),
            P("gx", "gy", "gz", None, None),
            P(),
            P(),
        ),
        out_specs=P("gx", "gy", "gz", None, None, None),
        check_vma=False,
    )
```

```python
import functools

import jax
import jax.numpy as jnp
from jax import lax
from jax.experimental import pallas as pl
from jax.experimental.pallas import tpu as pltpu
from jax.sharding import PartitionSpec as P

coupling = 0.5
vmem_grant = 48 * 1024 * 1024
short_group = 4
lane_count = 128
f32 = jnp.float32
bf16 = jnp.bfloat16
vmem_spec = pl.BlockSpec(memory_space=pltpu.VMEM)
smem_spec = pl.BlockSpec(memory_space=pltpu.SMEM)
hbm_spec = pl.BlockSpec(memory_space=pltpu.HBM)


def two_parts(value):
    high = value.astype(bf16)
    return high, (value - high.astype(f32)).astype(bf16)


def dot(left, right):
    return jnp.dot(left, right, preferred_element_type=f32)


def dot_transposed(left, right):
    return lax.dot_general(left, right, (((1,), (1,)), ((), ())), preferred_element_type=f32)


def times_matrix(rows, matrix):
    count = rows.shape[0]
    row_high, row_low = two_parts(rows)
    mat_high, mat_low = two_parts(matrix)
    both = dot(jnp.concatenate([row_high, row_low], axis=0), mat_high)
    return both[:count] + (both[count:] + dot(row_high, mat_low))


def split_index(index, dofs):
    if dofs & (dofs - 1) == 0:
        return lax.shift_right_arithmetic(index, dofs.bit_length() - 1), index & (dofs - 1)
    element = jnp.floor_divide(index, dofs)
    return element, index - element * dofs


def slot_of(target, links_ref, index_ref):
    slot = jnp.int32(-1)
    for position in range(links_ref.shape[-1]):
        slot = jnp.where(links_ref[0, 0, 0, position] == target, jnp.int32(position), slot)
    row = index_ref[0, 0, 0, pl.ds(jnp.maximum(slot, 0), 1), :]
    return jnp.where(slot >= 0, row, -1)


def hot_elements(flat_row, elements, dofs):
    element, _ = split_index(flat_row, dofs)
    return lax.broadcasted_iota(jnp.int32, (elements, flat_row.shape[1]), 0) == element


def hot_dofs(flat_row, dofs):
    _, dof = split_index(flat_row, dofs)
    shape = (dofs, flat_row.shape[1])
    line = lax.broadcasted_iota(jnp.int32, shape, 0).astype(jnp.int16)
    hit = line == jnp.broadcast_to(dof.astype(jnp.int16), shape)
    return jnp.where(hit, jnp.ones(shape, bf16), jnp.zeros(shape, bf16))


def as_column(row):
    elements = row.shape[1]
    line = lax.broadcasted_iota(jnp.int32, (elements, elements), 0)
    column = lax.broadcasted_iota(jnp.int32, (elements, elements), 1)
    spread = jnp.where(line == column, jnp.broadcast_to(row, (elements, elements)), 0.0)
    return jnp.sum(spread, axis=1, keepdims=True)


def wide(column, probes, dofs):
    return jnp.broadcast_to(jnp.concatenate([column] * probes, axis=0), (probes * column.shape[0], dofs))


def stacked(value):
    return jnp.concatenate(two_parts(value), axis=0)


def take_faces(parts, over_elements, over_dofs):
    elements = over_elements.shape[0]
    rows = parts.shape[0] // 2
    picked = dot(parts, over_dofs)
    picked = picked[:rows] + picked[rows:]
    return [
        jnp.sum(jnp.where(over_elements, picked[low : low + elements], 0.0), axis=0, keepdims=True)
        for low in range(0, rows, elements)
    ]


def add_faces(values, over_elements, over_dofs):
    highs = [value.astype(bf16).astype(f32) for value in values]
    lows = [value - high for value, high in zip(values, highs)]
    spread = jnp.concatenate(
        [jnp.where(over_elements, part, 0.0).astype(bf16) for part in highs + lows], axis=0
    )
    return dot_transposed(spread, over_dofs)


def folded(parts):
    rows = parts.shape[0] // 2
    return parts[:rows] + parts[rows:]


def as_row(lines, lanes):
    count = -(-len(lines) // 8) * 8
    spare = jnp.zeros((count - len(lines), lines[0].shape[1]), f32)
    sums = jnp.sum(jnp.concatenate(lines + [spare], axis=0), axis=1, keepdims=True)
    line = lax.broadcasted_iota(jnp.int32, (count, lanes), 0)
    lane = lax.broadcasted_iota(jnp.int32, (count, lanes), 1)
    return jnp.sum(jnp.where(line == lane, sums, 0.0), axis=0, keepdims=True)


def inner_products(first_img, second_img, source, probes, products_ref):
    elements = source.shape[0] // probes
    pairs = (
        (first_img, first_img),
        (first_img, second_img),
        (second_img, second_img),
        (first_img, source),
        (second_img, source),
    )
    lines = []
    for left, right in pairs:
        product = left * right
        for probe in range(probes):
            lines.append(
                jnp.sum(product[probe * elements : (probe + 1) * elements], axis=0, keepdims=True)
            )
    products_ref[...] = as_row(lines, products_ref.shape[-1])


def begin(refs, partner):
    count_ref, links_hbm, index_hbm, visc_hbm, rhs_hbm, *matrices_hbm = refs["operands"]
    links_ref, index_ref, visc_ref, rhs_ref, *matrix_refs, arrived = refs["scratch"]
    pairs = (
        (links_hbm, links_ref),
        (index_hbm, index_ref),
        (visc_hbm, visc_ref),
        (rhs_hbm, rhs_ref),
        *zip(matrices_hbm, matrix_refs),
    )
    copies = [
        pltpu.make_async_copy(held, here, arrived.at[place])
        for place, (held, here) in enumerate(pairs)
    ]
    for copy in copies:
        copy.start()
    copies[0].wait()
    copies[1].wait()
    slots_ref = refs["slots"]
    me = lax.axis_index("gz")
    for step in range(1, slots_ref.shape[0] + 1):
        slots_ref[step - 1] = slot_of(partner(me, step), links_ref, index_ref)
    copies[2].wait()
    probes, elements, dofs = rhs_ref.shape[3:]
    slot = lax.broadcasted_iota(jnp.int32, (elements, 1), 0)
    live = (slot < count_ref[0, 0, 0]).astype(f32)
    visc = as_column(visc_ref[0, 0])
    up = wide(live * visc, probes, dofs)
    down = wide(live / visc, probes, dofs)
    refs["up"][...] = up
    refs["down"][...] = down
    copies[3].wait()
    source = rhs_ref[...].reshape(probes * elements, dofs) * wide(live, probes, dofs)
    refs["source"][...] = source
    for copy in copies[4:]:
        copy.wait()
    first_pre = times_matrix(source, matrix_refs[0][...]) * down
    refs["first"][...] = first_pre
    return first_pre, up, down


def message_places(steps, probes):
    values = steps * probes
    return values, values + probes, values + probes + steps


def message_length(steps, probes, width):
    return -(-(message_places(steps, probes)[2] * (width // lane_count) + 1) // 8) * 8


def write_row(message_ref, place, row):
    pieces = row.shape[1] // lane_count
    for piece in range(pieces):
        line = place * pieces + piece
        message_ref[line : line + 1, :] = row[:, piece * lane_count : (piece + 1) * lane_count]


def read_row(message_ref, place, width):
    pieces = width // lane_count
    lines = range(place * pieces, (place + 1) * pieces)
    return jnp.concatenate([message_ref[line : line + 1, :] for line in lines], axis=1)


def near_first_kernel(*refs):
    operands, refs = refs[:7], refs[7:]
    first_ref, source_ref, up_ref, down_ref, base_ref, slots_ref, hot_ref = refs[:7]
    steps, _, width = slots_ref.shape
    leave_refs, scratch = refs[7 : 7 + steps], refs[7 + steps :]
    visc_ref, rhs_ref, p_ref, k_ref = scratch[2:6]
    probes, elements, dofs = rhs_ref.shape[3:]
    first_pre, up, down = begin(
        {
            "operands": operands,
            "scratch": scratch,
            "slots": slots_ref,
            "up": up_ref,
            "down": down_ref,
            "source": source_ref,
            "first": first_ref,
        },
        lambda me, step: me ^ step,
    )
    base = times_matrix(first_pre, k_ref[...]) * up
    base_ref[...] = base
    first_parts = stacked(first_pre)
    second_parts = stacked(times_matrix(base, p_ref[...]) * down)
    second_at, index_at, visc_at = message_places(steps, probes)
    slot = lax.broadcasted_iota(jnp.int32, (1, elements), 1)
    live_visc = jnp.where(slot < operands[0][0, 0, 0], visc_ref[0, 0], 0.0)
    for step in range(1, steps + 1):
        flat_row = slots_ref[step - 1]
        over_elements = hot_elements(flat_row, elements, dofs)
        over_dofs = hot_dofs(flat_row, dofs)
        hot_ref[:, (step - 1) * width : step * width] = over_dofs
        first_rows = take_faces(first_parts, over_elements, over_dofs)
        second_rows = take_faces(second_parts, over_elements, over_dofs)
        for probe in range(probes):
            write_row(leave_refs[step - 1], second_at + probe, second_rows[probe])
            for leave_ref in leave_refs:
                write_row(leave_ref, (step - 1) * probes + probe, first_rows[probe])
        for leave_ref in leave_refs:
            write_row(leave_ref, index_at + step - 1, flat_row.astype(f32))
    visc_line = visc_at * (width // lane_count)
    for leave_ref in leave_refs:
        leave_ref[visc_line : visc_line + 1, :elements] = live_visc


def near_second_kernel(
    probes, source_ref, up_ref, down_ref, base_ref, slots_ref, hot_ref, k_ref, p_ref, mine_ref, *refs
):
    came_refs = refs[:-2]
    second_ref, products_ref = refs[-2:]
    steps, _, width = slots_ref.shape
    members = steps + 1
    rows, dofs = source_ref.shape
    elements = rows // probes
    second_at, index_at, visc_at = message_places(steps, probes)

    def message(step):
        return mine_ref if step == 0 else came_refs[step - 1]

    def inbound_first(member, step):
        sent = message(member ^ step)
        return [
            read_row(sent, (step - 1) * probes + probe, width) for probe in range(probes)
        ]

    own_elements = [hot_elements(slots_ref[step], elements, dofs) for step in range(steps)]
    own_dofs = [hot_ref[:, step * width : (step + 1) * width] for step in range(steps)]

    def placed_here(values):
        return folded(
            sum(add_faces(values[i], own_elements[i], own_dofs[i]) for i in range(steps))
        )

    up, down = up_ref[...], down_ref[...]
    live = up > 0.0
    placed = placed_here([inbound_first(0, step) for step in range(1, members)])
    image = base_ref[...] - jnp.where(live, coupling * placed, 0.0)
    images, back = [image], []
    for member in range(1, members):
        total = 0.0
        for step in range(1, members):
            flat_row = read_row(message(member), index_at + step - 1, width).astype(jnp.int32)
            over_elements = hot_elements(flat_row, elements, dofs)
            over_dofs = hot_dofs(flat_row, dofs)
            total = total + add_faces(inbound_first(member, step), over_elements, over_dofs)
            if step == member:
                back.append((over_elements, over_dofs))
        images.append(-coupling * folded(total))
    smooth = times_matrix(jnp.concatenate(images, axis=0), p_ref[...])
    second_pre = smooth[:rows] * down
    second_ref[...] = second_pre
    values = []
    visc_line = visc_at * (width // lane_count)
    for member in range(1, members):
        sent = message(member)
        visc = as_column(sent[visc_line : visc_line + 1, :elements])
        scale = wide(jnp.where(visc > 0.0, 1.0 / visc, 0.0), probes, dofs)
        change = smooth[member * rows : (member + 1) * rows] * scale
        taken = take_faces(stacked(change), *back[member - 1])
        values.append(
            [taken[probe] + read_row(sent, second_at + probe, width) for probe in range(probes)]
        )
    placed = placed_here(values)
    second_img = times_matrix(second_pre, k_ref[...]) * up - jnp.where(live, coupling * placed, 0.0)
    inner_products(image, second_img, source_ref[...], probes, products_ref)


def leave_faces(field, probes, slots_ref, leave_ref):
    elements, dofs = field.shape[0] // probes, field.shape[1]
    members = slots_ref.shape[0] + 1
    parts = stacked(field)
    me = lax.axis_index("gz")
    for shift in range(1, members):
        flat_row = slots_ref[shift - 1]
        taken = take_faces(parts, hot_elements(flat_row, elements, dofs), hot_dofs(flat_row, dofs))
        target = lax.rem(me + shift, members)
        for probe in range(probes):
            leave_ref[target, pl.ds(probe, 1), :] = taken[probe]
    leave_ref[me] = jnp.zeros(leave_ref.shape[1:], f32)


def placed_faces(shape, probes, slots_ref, came_ref):
    rows, dofs = shape
    elements = rows // probes
    members = slots_ref.shape[0] + 1
    me = lax.axis_index("gz")
    total = jnp.zeros((2 * rows, dofs), f32)
    for shift in range(1, members):
        flat_row = slots_ref[shift - 1]
        came = came_ref[lax.rem(me + shift, members)]
        total += add_faces(
            [came[probe : probe + 1, :] for probe in range(probes)],
            hot_elements(flat_row, elements, dofs),
            hot_dofs(flat_row, dofs),
        )
    return folded(total)


def far_first_kernel(*refs):
    operands, refs = refs[:6], refs[6:]
    first_ref, source_ref, up_ref, down_ref, slots_ref, leave_ref = refs[:6]
    members = slots_ref.shape[0] + 1
    first_pre, _, _ = begin(
        {
            "operands": operands,
            "scratch": refs[6:],
            "slots": slots_ref,
            "up": up_ref,
            "down": down_ref,
            "source": source_ref,
            "first": first_ref,
        },
        lambda me, step: lax.rem(me + step, members),
    )
    leave_faces(first_pre, leave_ref.shape[1], slots_ref, leave_ref)


def far_second_kernel(
    slots_ref, up_ref, down_ref, first_ref, k_ref, p_ref, came_ref,
    image_ref, second_ref, leave_ref,
):
    probes = came_ref.shape[1]
    up = up_ref[...]
    placed = placed_faces(first_ref.shape, probes, slots_ref, came_ref)
    image = times_matrix(first_ref[...], k_ref[...]) * up - jnp.where(up > 0.0, coupling * placed, 0.0)
    image_ref[...] = image
    second_pre = times_matrix(image, p_ref[...]) * down_ref[...]
    second_ref[...] = second_pre
    leave_faces(second_pre, probes, slots_ref, leave_ref)


def far_third_kernel(
    slots_ref, up_ref, source_ref, image_ref, second_ref, k_ref, came_ref, products_ref
):
    probes = came_ref.shape[1]
    up = up_ref[...]
    placed = placed_faces(source_ref.shape, probes, slots_ref, came_ref)
    second_img = times_matrix(second_ref[...], k_ref[...]) * up - jnp.where(up > 0.0, coupling * placed, 0.0)
    inner_products(image_ref[...], second_img, source_ref[...], probes, products_ref)


def last_kernel(probes, first_ref, second_ref, parts_ref, out_ref):
    rows, _ = first_ref.shape
    elements = rows // probes
    total = jnp.sum(parts_ref[...], axis=0)
    for probe in range(probes):
        self_one, cross_mid, self_two, load_one, load_two = (
            total[:, place * probes + probe : place * probes + probe + 1] for place in range(5)
        )
        determinant = self_one * self_two - cross_mid * cross_mid
        weight_one = (self_two * load_one - cross_mid * load_two) / determinant
        weight_two = (self_one * load_two - cross_mid * load_one) / determinant
        block = pl.ds(probe * elements, elements)
        out_ref[block, :] = weight_one * first_ref[block, :] + weight_two * second_ref[block, :]


def call(kernel, in_specs, out_shapes, flops, *args, scratch=()):
    return pl.pallas_call(
        kernel,
        out_shape=out_shapes,
        in_specs=in_specs,
        out_specs=jax.tree.map(lambda _: vmem_spec, out_shapes),
        scratch_shapes=scratch,
        compiler_params=pltpu.CompilerParams(vmem_limit_bytes=vmem_grant),
        cost_estimate=pl.CostEstimate(flops=flops, bytes_accessed=1 << 20, transcendentals=0),
    )(*args)


def begin_call(kernel, out_shapes, flops, counts, *fetched):
    links, *others = fetched
    scratch = [pltpu.SMEM(links.shape, links.dtype)]
    scratch += [pltpu.VMEM(value.shape, value.dtype) for value in others]
    return call(
        kernel,
        [smem_spec] + [hbm_spec] * len(fetched),
        out_shapes,
        flops,
        counts,
        *(pltpu.with_memory_space_constraint(value, pltpu.HBM) for value in fetched),
        scratch=scratch + [pltpu.SemaphoreType.DMA((len(fetched),))],
    )


def near_steps(members, shapes, arguments):
    rhs, viscosity, counts, neighbours, face_index, k_matrix, p_matrix = arguments
    field, slots_shape, products_shape = shapes
    rows, dofs = field.shape
    steps, _, width = slots_shape.shape
    probes = rhs.shape[3]
    flops = 8 * rows * dofs * steps * width
    hot = jax.ShapeDtypeStruct((dofs, steps * width), bf16)
    message = jax.ShapeDtypeStruct((message_length(steps, probes, width), lane_count), f32)
    first_pre, source, up, down, base, slots, hot_own, *leaving = begin_call(
        near_first_kernel,
        [field] * 5 + [slots_shape, hot] + [message] * steps,
        2 * flops,
        counts,
        neighbours,
        face_index,
        viscosity,
        rhs,
        p_matrix,
        k_matrix,
    )
    came = [
        lax.ppermute(
            leaving[step - 1], "gz", [(source, source ^ step) for source in range(members)]
        )
        for step in range(1, members)
    ]
    second_pre, products = call(
        functools.partial(near_second_kernel, probes),
        [vmem_spec] * (9 + steps),
        [field, products_shape],
        6 * flops,
        source,
        up,
        down,
        base,
        slots,
        hot_own,
        k_matrix,
        p_matrix,
        leaving[0],
        *came,
    )
    return first_pre, second_pre, products


def far_steps(members, shapes, arguments):
    rhs, viscosity, counts, neighbours, face_index, k_matrix, p_matrix = arguments
    field, slots_shape, products_shape = shapes
    rows, dofs = field.shape
    shifts, _, width = slots_shape.shape
    flops = 8 * rows * dofs * shifts * width
    faces = jax.ShapeDtypeStruct((members, rhs.shape[3], width), f32)

    def exchange(value):
        return lax.all_to_all(value, "gz", split_axis=0, concat_axis=0)

    first_pre, source, up, down, slots, leaving = begin_call(
        far_first_kernel,
        [field] * 4 + [slots_shape, faces],
        flops,
        counts,
        neighbours,
        face_index,
        viscosity,
        rhs,
        p_matrix,
    )
    first_img, second_pre, leaving = call(
        far_second_kernel,
        [vmem_spec] * 7,
        [field, field, faces],
        2 * flops,
        slots,
        up,
        down,
        first_pre,
        k_matrix,
        p_matrix,
        exchange(leaving),
    )
    products = call(
        far_third_kernel,
        [vmem_spec] * 7,
        products_shape,
        flops,
        slots,
        up,
        source,
        first_img,
        second_pre,
        k_matrix,
        exchange(leaving),
    )
    return first_pre, second_pre, products


def all_rows(row, mesh):
    axes = ("gx", "gy", "gz")
    size = mesh.shape["gx"]
    groups = None
    rows = mesh.size
    if size % 2 == 0:
        row = row + lax.ppermute(row, "gx", [(place, place ^ 1) for place in range(size)])
        rest = mesh.size // size
        groups = [
            [place * rest + other for place in range(half, size, 2) for other in range(rest)]
            for half in range(2)
        ]
        rows //= 2
    copies = jnp.broadcast_to(row[None], (rows,) + row.shape)
    return lax.all_to_all(copies, axes, split_axis=0, concat_axis=0, axis_index_groups=groups)


def per_device(mesh, *arguments):
    rhs, face_index = arguments[0], arguments[4]
    probes, elements, dofs = rhs.shape[3:]
    members = mesh.shape["gz"]
    lanes = -(-5 * probes // 128) * 128
    shapes = (
        jax.ShapeDtypeStruct((probes * elements, dofs), f32),
        jax.ShapeDtypeStruct((members - 1, 1, face_index.shape[-1]), jnp.int32),
        jax.ShapeDtypeStruct((1, lanes), f32),
    )
    near = 1 < members <= short_group and elements <= face_index.shape[-1]
    near = near and elements * dofs < 1 << 24
    steps = near_steps if near else far_steps
    first_pre, second_pre, products = steps(members, shapes, arguments)
    result = call(
        functools.partial(last_kernel, probes),
        [vmem_spec] * 3,
        shapes[0],
        probes * elements * dofs,
        first_pre,
        second_pre,
        all_rows(products, mesh),
    )
    return result.reshape(rhs.shape)


def solution(mesh):
    return jax.shard_map(
        functools.partial(per_device, mesh),
        mesh=mesh,
        in_specs=(
            P("gx", "gy", "gz", None, None, None),
            P("gx", "gy", "gz", None),
            P("gx", "gy", "gz"),
            P("gx", "gy", "gz", None),
            P("gx", "gy", "gz", None, None),
            P(),
            P(),
        ),
        out_specs=P("gx", "gy", "gz", None, None, None),
        check_vma=False,
    )
```

```python
import functools

import jax
import jax.numpy as jnp
import numpy as np
from jax import lax
from jax.experimental import pallas as pl
from jax.experimental.pallas import tpu as pltpu
from jax.sharding import PartitionSpec as P

coupling = 0.5
vmem_grant = 48 * 1024 * 1024
short_group = 4
lane_count = 128
f32 = jnp.float32
bf16 = jnp.bfloat16
vmem_spec = pl.BlockSpec(memory_space=pltpu.VMEM)
smem_spec = pl.BlockSpec(memory_space=pltpu.SMEM)
hbm_spec = pl.BlockSpec(memory_space=pltpu.HBM)


def two_parts(value):
    high = value.astype(bf16)
    return high, (value - high.astype(f32)).astype(bf16)


def dot(left, right):
    return jnp.dot(left, right, preferred_element_type=f32)


def dot_transposed(left, right):
    return lax.dot_general(left, right, (((1,), (1,)), ((), ())), preferred_element_type=f32)


def times_matrix(rows, matrix):
    count = rows.shape[0]
    row_high, row_low = two_parts(rows)
    mat_high, mat_low = two_parts(matrix)
    both = dot(jnp.concatenate([row_high, row_low], axis=0), mat_high)
    return both[:count] + (both[count:] + dot(row_high, mat_low))


def split_index(index, dofs):
    if dofs & (dofs - 1) == 0:
        return lax.shift_right_arithmetic(index, dofs.bit_length() - 1), index & (dofs - 1)
    element = jnp.floor_divide(index, dofs)
    return element, index - element * dofs


def slot_of(target, links_ref, index_ref):
    slot = jnp.int32(-1)
    for position in range(links_ref.shape[-1]):
        slot = jnp.where(links_ref[0, 0, 0, position] == target, jnp.int32(position), slot)
    row = index_ref[0, 0, 0, pl.ds(jnp.maximum(slot, 0), 1), :]
    return jnp.where(slot >= 0, row, -1)


def hot_elements(flat_row, elements, dofs):
    element, _ = split_index(flat_row, dofs)
    return lax.broadcasted_iota(jnp.int32, (elements, flat_row.shape[1]), 0) == element


def hot_dofs(flat_row, dofs):
    _, dof = split_index(flat_row, dofs)
    shape = (dofs, flat_row.shape[1])
    line = lax.broadcasted_iota(jnp.int32, shape, 0).astype(jnp.int16)
    hit = line == jnp.broadcast_to(dof.astype(jnp.int16), shape)
    return jnp.where(hit, jnp.ones(shape, bf16), jnp.zeros(shape, bf16))


def as_column(row):
    elements = row.shape[1]
    line = lax.broadcasted_iota(jnp.int32, (elements, elements), 0)
    column = lax.broadcasted_iota(jnp.int32, (elements, elements), 1)
    spread = jnp.where(line == column, jnp.broadcast_to(row, (elements, elements)), 0.0)
    return jnp.sum(spread, axis=1, keepdims=True)


def wide(column, probes, dofs):
    return jnp.broadcast_to(jnp.concatenate([column] * probes, axis=0), (probes * column.shape[0], dofs))


def stacked(value):
    return jnp.concatenate(two_parts(value), axis=0)


def take_faces(parts, over_elements, over_dofs):
    elements = over_elements.shape[0]
    rows = parts.shape[0] // 2
    picked = dot(parts, over_dofs)
    picked = picked[:rows] + picked[rows:]
    return [
        jnp.sum(jnp.where(over_elements, picked[low : low + elements], 0.0), axis=0, keepdims=True)
        for low in range(0, rows, elements)
    ]


def add_faces(values, over_elements, over_dofs):
    highs = [value.astype(bf16).astype(f32) for value in values]
    lows = [value - high for value, high in zip(values, highs)]
    spread = jnp.concatenate(
        [jnp.where(over_elements, part, 0.0).astype(bf16) for part in highs + lows], axis=0
    )
    return dot_transposed(spread, over_dofs)


def folded(parts):
    rows = parts.shape[0] // 2
    return parts[:rows] + parts[rows:]


def as_row(lines, lanes):
    count = -(-len(lines) // 8) * 8
    spare = jnp.zeros((count - len(lines), lines[0].shape[1]), f32)
    sums = jnp.sum(jnp.concatenate(lines + [spare], axis=0), axis=1, keepdims=True)
    line = lax.broadcasted_iota(jnp.int32, (count, lanes), 0)
    lane = lax.broadcasted_iota(jnp.int32, (count, lanes), 1)
    return jnp.sum(jnp.where(line == lane, sums, 0.0), axis=0, keepdims=True)


def inner_products(first_img, second_img, source, probes, products_ref):
    elements = source.shape[0] // probes
    pairs = (
        (first_img, first_img),
        (first_img, second_img),
        (second_img, second_img),
        (first_img, source),
        (second_img, source),
    )
    lines = []
    for left, right in pairs:
        product = left * right
        for probe in range(probes):
            lines.append(
                jnp.sum(product[probe * elements : (probe + 1) * elements], axis=0, keepdims=True)
            )
    products_ref[...] = as_row(lines, products_ref.shape[-1])


def begin(refs, partner):
    count_ref, links_hbm, index_hbm, visc_hbm, rhs_hbm, *matrices_hbm = refs["operands"]
    links_ref, index_ref, visc_ref, rhs_ref, *matrix_refs, arrived = refs["scratch"]
    pairs = (
        (links_hbm, links_ref),
        (index_hbm, index_ref),
        (visc_hbm, visc_ref),
        (rhs_hbm, rhs_ref),
        *zip(matrices_hbm, matrix_refs),
    )
    copies = [
        pltpu.make_async_copy(held, here, arrived.at[place])
        for place, (held, here) in enumerate(pairs)
    ]
    for copy in copies:
        copy.start()
    copies[0].wait()
    copies[1].wait()
    slots_ref = refs["slots"]
    me = lax.axis_index("gz")
    for step in range(1, slots_ref.shape[0] + 1):
        slots_ref[step - 1] = slot_of(partner(me, step), links_ref, index_ref)
    copies[2].wait()
    probes, elements, dofs = rhs_ref.shape[3:]
    slot = lax.broadcasted_iota(jnp.int32, (elements, 1), 0)
    live = (slot < count_ref[0, 0, 0]).astype(f32)
    visc = as_column(visc_ref[0, 0])
    up = wide(live * visc, probes, dofs)
    down = wide(live / visc, probes, dofs)
    refs["up"][...] = up
    refs["down"][...] = down
    copies[3].wait()
    source = rhs_ref[...].reshape(probes * elements, dofs) * wide(live, probes, dofs)
    refs["source"][...] = source
    for copy in copies[4:]:
        copy.wait()
    first_pre = times_matrix(source, matrix_refs[0][...]) * down
    refs["first"][...] = first_pre
    return first_pre, up, down


def message_places(steps, probes):
    values = steps * probes
    return values, values + probes, values + probes + steps


def message_length(steps, probes, width):
    return -(-(message_places(steps, probes)[2] * (width // lane_count) + 1) // 8) * 8


def write_row(message_ref, place, row):
    pieces = row.shape[1] // lane_count
    for piece in range(pieces):
        line = place * pieces + piece
        message_ref[line : line + 1, :] = row[:, piece * lane_count : (piece + 1) * lane_count]


def read_row(message_ref, place, width):
    pieces = width // lane_count
    lines = range(place * pieces, (place + 1) * pieces)
    return jnp.concatenate([message_ref[line : line + 1, :] for line in lines], axis=1)


def near_first_kernel(*refs):
    operands, refs = refs[:7], refs[7:]
    first_ref, source_ref, up_ref, down_ref, base_ref, slots_ref, hot_ref = refs[:7]
    steps, _, width = slots_ref.shape
    leave_refs, scratch = refs[7 : 7 + steps], refs[7 + steps :]
    visc_ref, rhs_ref, p_ref, k_ref = scratch[2:6]
    probes, elements, dofs = rhs_ref.shape[3:]
    first_pre, up, down = begin(
        {
            "operands": operands,
            "scratch": scratch,
            "slots": slots_ref,
            "up": up_ref,
            "down": down_ref,
            "source": source_ref,
            "first": first_ref,
        },
        lambda me, step: me ^ step,
    )
    base = times_matrix(first_pre, k_ref[...]) * up
    base_ref[...] = base
    first_parts = stacked(first_pre)
    second_parts = stacked(times_matrix(base, p_ref[...]) * down)
    second_at, index_at, visc_at = message_places(steps, probes)
    slot = lax.broadcasted_iota(jnp.int32, (1, elements), 1)
    live_visc = jnp.where(slot < operands[0][0, 0, 0], visc_ref[0, 0], 0.0)
    for step in range(1, steps + 1):
        flat_row = slots_ref[step - 1]
        over_elements = hot_elements(flat_row, elements, dofs)
        over_dofs = hot_dofs(flat_row, dofs)
        hot_ref[:, (step - 1) * width : step * width] = over_dofs
        first_rows = take_faces(first_parts, over_elements, over_dofs)
        second_rows = take_faces(second_parts, over_elements, over_dofs)
        for probe in range(probes):
            write_row(leave_refs[step - 1], second_at + probe, second_rows[probe])
            for leave_ref in leave_refs:
                write_row(leave_ref, (step - 1) * probes + probe, first_rows[probe])
        for leave_ref in leave_refs:
            write_row(leave_ref, index_at + step - 1, flat_row.astype(f32))
    visc_line = visc_at * (width // lane_count)
    for leave_ref in leave_refs:
        leave_ref[visc_line : visc_line + 1, :elements] = live_visc


def near_second_kernel(
    probes, source_ref, up_ref, down_ref, base_ref, slots_ref, hot_ref, k_ref, p_ref, mine_ref, *refs
):
    came_refs = refs[:-2]
    second_ref, products_ref = refs[-2:]
    steps, _, width = slots_ref.shape
    members = steps + 1
    rows, dofs = source_ref.shape
    elements = rows // probes
    second_at, index_at, visc_at = message_places(steps, probes)

    def message(step):
        return mine_ref if step == 0 else came_refs[step - 1]

    def inbound_first(member, step):
        sent = message(member ^ step)
        return [
            read_row(sent, (step - 1) * probes + probe, width) for probe in range(probes)
        ]

    own_elements = [hot_elements(slots_ref[step], elements, dofs) for step in range(steps)]
    own_dofs = [hot_ref[:, step * width : (step + 1) * width] for step in range(steps)]

    def placed_here(values):
        return folded(
            sum(add_faces(values[i], own_elements[i], own_dofs[i]) for i in range(steps))
        )

    up, down = up_ref[...], down_ref[...]
    live = up > 0.0
    placed = placed_here([inbound_first(0, step) for step in range(1, members)])
    image = base_ref[...] - jnp.where(live, coupling * placed, 0.0)
    images, back = [image], []
    for member in range(1, members):
        total = 0.0
        for step in range(1, members):
            flat_row = read_row(message(member), index_at + step - 1, width).astype(jnp.int32)
            over_elements = hot_elements(flat_row, elements, dofs)
            over_dofs = hot_dofs(flat_row, dofs)
            total = total + add_faces(inbound_first(member, step), over_elements, over_dofs)
            if step == member:
                back.append((over_elements, over_dofs))
        images.append(-coupling * folded(total))
    smooth = times_matrix(jnp.concatenate(images, axis=0), p_ref[...])
    second_pre = smooth[:rows] * down
    second_ref[...] = second_pre
    values = []
    visc_line = visc_at * (width // lane_count)
    for member in range(1, members):
        sent = message(member)
        visc = as_column(sent[visc_line : visc_line + 1, :elements])
        scale = wide(jnp.where(visc > 0.0, 1.0 / visc, 0.0), probes, dofs)
        change = smooth[member * rows : (member + 1) * rows] * scale
        taken = take_faces(stacked(change), *back[member - 1])
        values.append(
            [taken[probe] + read_row(sent, second_at + probe, width) for probe in range(probes)]
        )
    placed = placed_here(values)
    second_img = times_matrix(second_pre, k_ref[...]) * up - jnp.where(live, coupling * placed, 0.0)
    inner_products(image, second_img, source_ref[...], probes, products_ref)


def leave_faces(field, probes, slots_ref, leave_ref):
    elements, dofs = field.shape[0] // probes, field.shape[1]
    members = slots_ref.shape[0] + 1
    parts = stacked(field)
    me = lax.axis_index("gz")
    for shift in range(1, members):
        flat_row = slots_ref[shift - 1]
        taken = take_faces(parts, hot_elements(flat_row, elements, dofs), hot_dofs(flat_row, dofs))
        target = lax.rem(me + shift, members)
        for probe in range(probes):
            leave_ref[target, pl.ds(probe, 1), :] = taken[probe]
    leave_ref[me] = jnp.zeros(leave_ref.shape[1:], f32)


def placed_faces(shape, probes, slots_ref, came_ref):
    rows, dofs = shape
    elements = rows // probes
    members = slots_ref.shape[0] + 1
    me = lax.axis_index("gz")
    total = jnp.zeros((2 * rows, dofs), f32)
    for shift in range(1, members):
        flat_row = slots_ref[shift - 1]
        came = came_ref[lax.rem(me + shift, members)]
        total += add_faces(
            [came[probe : probe + 1, :] for probe in range(probes)],
            hot_elements(flat_row, elements, dofs),
            hot_dofs(flat_row, dofs),
        )
    return folded(total)


def far_first_kernel(*refs):
    operands, refs = refs[:6], refs[6:]
    first_ref, source_ref, up_ref, down_ref, slots_ref, leave_ref = refs[:6]
    members = slots_ref.shape[0] + 1
    first_pre, _, _ = begin(
        {
            "operands": operands,
            "scratch": refs[6:],
            "slots": slots_ref,
            "up": up_ref,
            "down": down_ref,
            "source": source_ref,
            "first": first_ref,
        },
        lambda me, step: lax.rem(me + step, members),
    )
    leave_faces(first_pre, leave_ref.shape[1], slots_ref, leave_ref)


def far_second_kernel(
    slots_ref, up_ref, down_ref, first_ref, k_ref, p_ref, came_ref,
    image_ref, second_ref, leave_ref,
):
    probes = came_ref.shape[1]
    up = up_ref[...]
    placed = placed_faces(first_ref.shape, probes, slots_ref, came_ref)
    image = times_matrix(first_ref[...], k_ref[...]) * up - jnp.where(up > 0.0, coupling * placed, 0.0)
    image_ref[...] = image
    second_pre = times_matrix(image, p_ref[...]) * down_ref[...]
    second_ref[...] = second_pre
    leave_faces(second_pre, probes, slots_ref, leave_ref)


def far_third_kernel(
    slots_ref, up_ref, source_ref, image_ref, second_ref, k_ref, came_ref, products_ref
):
    probes = came_ref.shape[1]
    up = up_ref[...]
    placed = placed_faces(source_ref.shape, probes, slots_ref, came_ref)
    second_img = times_matrix(second_ref[...], k_ref[...]) * up - jnp.where(up > 0.0, coupling * placed, 0.0)
    inner_products(image_ref[...], second_img, source_ref[...], probes, products_ref)


def last_kernel(probes, first_ref, second_ref, total_ref, out_ref):
    rows, _ = first_ref.shape
    elements = rows // probes
    total = total_ref[...]
    for probe in range(probes):
        self_one, cross_mid, self_two, load_one, load_two = (
            total[:, place * probes + probe : place * probes + probe + 1] for place in range(5)
        )
        determinant = self_one * self_two - cross_mid * cross_mid
        weight_one = (self_two * load_one - cross_mid * load_two) / determinant
        weight_two = (self_one * load_two - cross_mid * load_one) / determinant
        block = pl.ds(probe * elements, elements)
        out_ref[block, :] = weight_one * first_ref[block, :] + weight_two * second_ref[block, :]


def call(kernel, in_specs, out_shapes, flops, *args, scratch=()):
    return pl.pallas_call(
        kernel,
        out_shape=out_shapes,
        in_specs=in_specs,
        out_specs=jax.tree.map(lambda _: vmem_spec, out_shapes),
        scratch_shapes=scratch,
        compiler_params=pltpu.CompilerParams(vmem_limit_bytes=vmem_grant),
        cost_estimate=pl.CostEstimate(flops=flops, bytes_accessed=1 << 20, transcendentals=0),
    )(*args)


def begin_call(kernel, out_shapes, flops, counts, *fetched):
    links, *others = fetched
    scratch = [pltpu.SMEM(links.shape, links.dtype)]
    scratch += [pltpu.VMEM(value.shape, value.dtype) for value in others]
    return call(
        kernel,
        [smem_spec] + [hbm_spec] * len(fetched),
        out_shapes,
        flops,
        counts,
        *(pltpu.with_memory_space_constraint(value, pltpu.HBM) for value in fetched),
        scratch=scratch + [pltpu.SemaphoreType.DMA((len(fetched),))],
    )


def near_steps(members, shapes, arguments):
    rhs, viscosity, counts, neighbours, face_index, k_matrix, p_matrix = arguments
    field, slots_shape, products_shape = shapes
    rows, dofs = field.shape
    steps, _, width = slots_shape.shape
    probes = rhs.shape[3]
    flops = 8 * rows * dofs * steps * width
    hot = jax.ShapeDtypeStruct((dofs, steps * width), bf16)
    message = jax.ShapeDtypeStruct((message_length(steps, probes, width), lane_count), f32)
    first_pre, source, up, down, base, slots, hot_own, *leaving = begin_call(
        near_first_kernel,
        [field] * 5 + [slots_shape, hot] + [message] * steps,
        2 * flops,
        counts,
        neighbours,
        face_index,
        viscosity,
        rhs,
        p_matrix,
        k_matrix,
    )
    came = [
        lax.ppermute(
            leaving[step - 1], "gz", [(source, source ^ step) for source in range(members)]
        )
        for step in range(1, members)
    ]
    second_pre, products = call(
        functools.partial(near_second_kernel, probes),
        [vmem_spec] * (9 + steps),
        [field, products_shape],
        6 * flops,
        source,
        up,
        down,
        base,
        slots,
        hot_own,
        k_matrix,
        p_matrix,
        leaving[0],
        *came,
    )
    return first_pre, second_pre, products


def far_steps(members, shapes, arguments):
    rhs, viscosity, counts, neighbours, face_index, k_matrix, p_matrix = arguments
    field, slots_shape, products_shape = shapes
    rows, dofs = field.shape
    shifts, _, width = slots_shape.shape
    flops = 8 * rows * dofs * shifts * width
    faces = jax.ShapeDtypeStruct((members, rhs.shape[3], width), f32)

    def exchange(value):
        return lax.all_to_all(value, "gz", split_axis=0, concat_axis=0)

    first_pre, source, up, down, slots, leaving = begin_call(
        far_first_kernel,
        [field] * 4 + [slots_shape, faces],
        flops,
        counts,
        neighbours,
        face_index,
        viscosity,
        rhs,
        p_matrix,
    )
    first_img, second_pre, leaving = call(
        far_second_kernel,
        [vmem_spec] * 7,
        [field, field, faces],
        2 * flops,
        slots,
        up,
        down,
        first_pre,
        k_matrix,
        p_matrix,
        exchange(leaving),
    )
    products = call(
        far_third_kernel,
        [vmem_spec] * 7,
        products_shape,
        flops,
        slots,
        up,
        source,
        first_img,
        second_pre,
        k_matrix,
        exchange(leaving),
    )
    return first_pre, second_pre, products


def tree_levels(line):
    levels = []
    while len(line) > 1:
        count = next((n for n in range(short_group, 1, -1) if len(line) % n == 0), len(line))
        groups = [line[low : low + count] for low in range(0, len(line), count)]
        middle = (count - 1) // 2
        line = [group[middle] for group in groups]
        levels.append([(group[middle], group[:middle] + group[middle + 1 :]) for group in groups])
    return levels, line[0]


def tree_sum(row, mesh):
    axes = ("gx", "gy", "gz")
    ids = np.arange(mesh.size).reshape([mesh.shape[axis] for axis in axes])
    levels = []
    if ids.shape[0] % 2 == 0:
        pairs = zip(ids[1::2].ravel().tolist(), ids[::2].ravel().tolist())
        levels.append([(root, [other]) for root, other in pairs])
        ids = ids[1::2]
    trees = [tree_levels(line) for line in ids.reshape(-1, ids.shape[2]).tolist()]
    levels += [sum(parts, []) for parts in zip(*(tree for tree, _ in trees))]
    upper, top = tree_levels([root for _, root in trees])
    levels += upper

    def one_way(value, level, down):
        came = []
        for place in range(len(level[0][1])):
            pairs = [(others[place], root) for root, others in level]
            pairs = [pair[::-1] for pair in pairs] if down else pairs
            came.append(lax.ppermute(value, axes, pairs))
        return functools.reduce(jnp.add, came, value)

    for level in levels:
        row = one_way(row, level, False)
    row = jnp.where(lax.axis_index(axes) == top, row, 0.0)
    for level in reversed(levels):
        row = one_way(row, level, True)
    return row


def per_device(mesh, *arguments):
    rhs, face_index = arguments[0], arguments[4]
    probes, elements, dofs = rhs.shape[3:]
    members = mesh.shape["gz"]
    lanes = -(-5 * probes // 128) * 128
    shapes = (
        jax.ShapeDtypeStruct((probes * elements, dofs), f32),
        jax.ShapeDtypeStruct((members - 1, 1, face_index.shape[-1]), jnp.int32),
        jax.ShapeDtypeStruct((1, lanes), f32),
    )
    near = 1 < members <= short_group and elements <= face_index.shape[-1]
    near = near and elements * dofs < 1 << 24
    steps = near_steps if near else far_steps
    first_pre, second_pre, products = steps(members, shapes, arguments)
    result = call(
        functools.partial(last_kernel, probes),
        [vmem_spec] * 3,
        shapes[0],
        probes * elements * dofs,
        first_pre,
        second_pre,
        tree_sum(products, mesh),
    )
    return result.reshape(rhs.shape)


def solution(mesh):
    return jax.shard_map(
        functools.partial(per_device, mesh),
        mesh=mesh,
        in_specs=(
            P("gx", "gy", "gz", None, None, None),
            P("gx", "gy", "gz", None),
            P("gx", "gy", "gz"),
            P("gx", "gy", "gz", None),
            P("gx", "gy", "gz", None, None),
            P(),
            P(),
        ),
        out_specs=P("gx", "gy", "gz", None, None, None),
        check_vma=False,
    )
```

```python
import functools

import jax
import jax.numpy as jnp
from jax import lax
from jax.experimental import pallas as pl
from jax.experimental.pallas import tpu as pltpu
from jax.sharding import PartitionSpec as P

coupling = 0.5
vmem_grant = 48 * 1024 * 1024
short_group = 4
lane_count = 128
f32 = jnp.float32
bf16 = jnp.bfloat16
vmem_spec = pl.BlockSpec(memory_space=pltpu.VMEM)
smem_spec = pl.BlockSpec(memory_space=pltpu.SMEM)
hbm_spec = pl.BlockSpec(memory_space=pltpu.HBM)


def two_parts(value):
    high = value.astype(bf16)
    return high, (value - high.astype(f32)).astype(bf16)


def dot(left, right):
    return jnp.dot(left, right, preferred_element_type=f32)


def dot_transposed(left, right):
    return lax.dot_general(left, right, (((1,), (1,)), ((), ())), preferred_element_type=f32)


def times_matrix(rows, matrix):
    count = rows.shape[0]
    row_high, row_low = two_parts(rows)
    mat_high, mat_low = two_parts(matrix)
    both = dot(jnp.concatenate([row_high, row_low], axis=0), mat_high)
    return both[:count] + (both[count:] + dot(row_high, mat_low))


def split_index(index, dofs):
    if dofs & (dofs - 1) == 0:
        return lax.shift_right_arithmetic(index, dofs.bit_length() - 1), index & (dofs - 1)
    element = jnp.floor_divide(index, dofs)
    return element, index - element * dofs


def slot_of(target, links_ref, index_ref):
    slot = jnp.int32(-1)
    for position in range(links_ref.shape[-1]):
        slot = jnp.where(links_ref[0, 0, 0, position] == target, jnp.int32(position), slot)
    row = index_ref[0, 0, 0, pl.ds(jnp.maximum(slot, 0), 1), :]
    return jnp.where(slot >= 0, row, -1)


def hot_elements(flat_row, elements, dofs):
    element, _ = split_index(flat_row, dofs)
    return lax.broadcasted_iota(jnp.int32, (elements, flat_row.shape[1]), 0) == element


def hot_dofs(flat_row, dofs):
    _, dof = split_index(flat_row, dofs)
    shape = (dofs, flat_row.shape[1])
    line = lax.broadcasted_iota(jnp.int32, shape, 0).astype(jnp.int16)
    hit = line == jnp.broadcast_to(dof.astype(jnp.int16), shape)
    return jnp.where(hit, jnp.ones(shape, bf16), jnp.zeros(shape, bf16))


def as_column(row):
    elements = row.shape[1]
    line = lax.broadcasted_iota(jnp.int32, (elements, elements), 0)
    column = lax.broadcasted_iota(jnp.int32, (elements, elements), 1)
    spread = jnp.where(line == column, jnp.broadcast_to(row, (elements, elements)), 0.0)
    return jnp.sum(spread, axis=1, keepdims=True)


def wide(column, probes, dofs):
    return jnp.broadcast_to(jnp.concatenate([column] * probes, axis=0), (probes * column.shape[0], dofs))


def stacked(value):
    return jnp.concatenate(two_parts(value), axis=0)


def take_faces(parts, over_elements, over_dofs):
    elements = over_elements.shape[0]
    rows = parts.shape[0] // 2
    picked = dot(parts, over_dofs)
    picked = picked[:rows] + picked[rows:]
    return [
        jnp.sum(jnp.where(over_elements, picked[low : low + elements], 0.0), axis=0, keepdims=True)
        for low in range(0, rows, elements)
    ]


def add_faces(values, over_elements, over_dofs):
    highs = [value.astype(bf16).astype(f32) for value in values]
    lows = [value - high for value, high in zip(values, highs)]
    spread = jnp.concatenate(
        [jnp.where(over_elements, part, 0.0).astype(bf16) for part in highs + lows], axis=0
    )
    return dot_transposed(spread, over_dofs)


def folded(parts):
    rows = parts.shape[0] // 2
    return parts[:rows] + parts[rows:]


def as_row(lines, lanes):
    count = -(-len(lines) // 8) * 8
    spare = jnp.zeros((count - len(lines), lines[0].shape[1]), f32)
    sums = jnp.sum(jnp.concatenate(lines + [spare], axis=0), axis=1, keepdims=True)
    line = lax.broadcasted_iota(jnp.int32, (count, lanes), 0)
    lane = lax.broadcasted_iota(jnp.int32, (count, lanes), 1)
    return jnp.sum(jnp.where(line == lane, sums, 0.0), axis=0, keepdims=True)


def inner_products(first_img, second_img, source, probes, products_ref):
    elements = source.shape[0] // probes
    pairs = (
        (first_img, first_img),
        (first_img, second_img),
        (second_img, second_img),
        (first_img, source),
        (second_img, source),
    )
    lines = []
    for left, right in pairs:
        product = left * right
        for probe in range(probes):
            lines.append(
                jnp.sum(product[probe * elements : (probe + 1) * elements], axis=0, keepdims=True)
            )
    products_ref[...] = jnp.broadcast_to(as_row(lines, products_ref.shape[-1]), products_ref.shape)


def live_column(count_ref, elements):
    return lax.broadcasted_iota(jnp.int32, (elements, 1), 0) < count_ref[0, 0, 0]


def begin(refs, partner, count_ref, prepare):
    links_hbm, index_hbm, visc_hbm, rhs_hbm, *matrices_hbm = refs["operands"]
    links_ref, index_ref, visc_ref, rhs_ref, *matrix_refs, arrived = refs["scratch"]
    pairs = (
        (links_hbm, links_ref),
        (index_hbm, index_ref),
        (visc_hbm, visc_ref),
        (rhs_hbm, rhs_ref),
        *zip(matrices_hbm, matrix_refs),
    )
    copies = [
        pltpu.make_async_copy(held, here, arrived.at[place])
        for place, (held, here) in enumerate(pairs)
    ]
    for copy in copies:
        copy.start()
    copies[0].wait()
    copies[1].wait()
    slots_ref = refs["slots"]
    me = lax.axis_index("gz")
    for step in range(1, slots_ref.shape[0] + 1):
        slots_ref[step - 1] = slot_of(partner(me, step), links_ref, index_ref)
    prepare()
    copies[2].wait()
    probes, elements, dofs = rhs_ref.shape[3:]
    live = jnp.ones((elements, 1), f32)
    if count_ref is not None:
        live = live_column(count_ref, elements).astype(f32)
    visc = as_column(visc_ref[0, 0])
    up = wide(live * visc, probes, dofs)
    down = wide(live / visc, probes, dofs)
    refs["up"][...] = up
    refs["down"][...] = down
    copies[3].wait()
    source = rhs_ref[...].reshape(probes * elements, dofs)
    if count_ref is not None:
        source = source * wide(live, probes, dofs)
    refs["source"][...] = source
    for copy in copies[4:]:
        copy.wait()
    first_pre = times_matrix(source, matrix_refs[0][...]) * down
    refs["first"][...] = first_pre
    return first_pre, up, down


def message_places(steps, probes):
    values = steps * probes
    return values, values + probes, values + probes + steps


def message_length(steps, probes, width):
    return -(-(message_places(steps, probes)[2] * (width // lane_count) + 1) // 8) * 8


def write_row(message_ref, place, row):
    pieces = row.shape[1] // lane_count
    for piece in range(pieces):
        line = place * pieces + piece
        message_ref[line : line + 1, :] = row[:, piece * lane_count : (piece + 1) * lane_count]


def read_row(message_ref, place, width):
    pieces = width // lane_count
    lines = range(place * pieces, (place + 1) * pieces)
    return jnp.concatenate([message_ref[line : line + 1, :] for line in lines], axis=1)


def near_first_kernel(*refs):
    operands, refs = refs[:6], refs[6:]
    first_ref, source_ref, up_ref, down_ref, base_ref, slots_ref, hot_ref = refs[:7]
    steps, _, width = slots_ref.shape
    leave_refs, scratch = refs[7 : 7 + steps], refs[7 + steps :]
    visc_ref, rhs_ref, p_ref, k_ref = scratch[2:6]
    probes, elements, dofs = rhs_ref.shape[3:]

    def prepare():
        for step in range(steps):
            hot_ref[:, step * width : (step + 1) * width] = hot_dofs(slots_ref[step], dofs)

    first_pre, up, down = begin(
        {
            "operands": operands,
            "scratch": scratch,
            "slots": slots_ref,
            "up": up_ref,
            "down": down_ref,
            "source": source_ref,
            "first": first_ref,
        },
        lambda me, step: me ^ step,
        None,
        prepare,
    )
    base = times_matrix(first_pre, k_ref[...]) * up
    base_ref[...] = base
    first_parts = stacked(first_pre)
    second_parts = stacked(times_matrix(base, p_ref[...]) * down)
    second_at, index_at, visc_at = message_places(steps, probes)
    for step in range(1, steps + 1):
        flat_row = slots_ref[step - 1]
        over_elements = hot_elements(flat_row, elements, dofs)
        over_dofs = hot_ref[:, (step - 1) * width : step * width]
        first_rows = take_faces(first_parts, over_elements, over_dofs)
        second_rows = take_faces(second_parts, over_elements, over_dofs)
        for probe in range(probes):
            write_row(leave_refs[step - 1], second_at + probe, second_rows[probe])
            for leave_ref in leave_refs:
                write_row(leave_ref, (step - 1) * probes + probe, first_rows[probe])
        for leave_ref in leave_refs:
            write_row(leave_ref, index_at + step - 1, flat_row.astype(f32))
    visc_line = visc_at * (width // lane_count)
    for leave_ref in leave_refs:
        leave_ref[visc_line : visc_line + 1, :elements] = visc_ref[0, 0]


def near_second_kernel(
    probes, count_ref, source_ref, up_ref, down_ref, base_ref, slots_ref, hot_ref, k_ref, p_ref, mine_ref, *refs
):
    came_refs = refs[:-2]
    second_ref, products_ref = refs[-2:]
    steps, _, width = slots_ref.shape
    members = steps + 1
    rows, dofs = source_ref.shape
    elements = rows // probes
    second_at, index_at, visc_at = message_places(steps, probes)

    def message(step):
        return mine_ref if step == 0 else came_refs[step - 1]

    def inbound_first(member, step):
        sent = message(member ^ step)
        return [
            read_row(sent, (step - 1) * probes + probe, width) for probe in range(probes)
        ]

    own_elements = [hot_elements(slots_ref[step], elements, dofs) for step in range(steps)]
    own_dofs = [hot_ref[:, step * width : (step + 1) * width] for step in range(steps)]

    def placed_here(values):
        return folded(
            sum(add_faces(values[i], own_elements[i], own_dofs[i]) for i in range(steps))
        )

    up, down = up_ref[...], down_ref[...]
    live = wide(live_column(count_ref, elements).astype(f32), probes, dofs) > 0.0
    placed = placed_here([inbound_first(0, step) for step in range(1, members)])
    image = jnp.where(live, base_ref[...] - coupling * placed, 0.0)
    images, back = [image], []
    for member in range(1, members):
        total = 0.0
        for step in range(1, members):
            flat_row = read_row(message(member), index_at + step - 1, width).astype(jnp.int32)
            over_elements = hot_elements(flat_row, elements, dofs)
            over_dofs = hot_dofs(flat_row, dofs)
            total = total + add_faces(inbound_first(member, step), over_elements, over_dofs)
            if step == member:
                back.append((over_elements, over_dofs))
        images.append(-coupling * folded(total))
    smooth = times_matrix(jnp.concatenate(images, axis=0), p_ref[...])
    second_pre = smooth[:rows] * down
    second_ref[...] = second_pre
    values = []
    visc_line = visc_at * (width // lane_count)
    for member in range(1, members):
        sent = message(member)
        visc = as_column(sent[visc_line : visc_line + 1, :elements])
        scale = wide(1.0 / visc, probes, dofs)
        change = smooth[member * rows : (member + 1) * rows] * scale
        taken = take_faces(stacked(change), *back[member - 1])
        values.append(
            [taken[probe] + read_row(sent, second_at + probe, width) for probe in range(probes)]
        )
    placed = placed_here(values)
    second_img = times_matrix(second_pre, k_ref[...]) * up - coupling * placed
    second_img = jnp.where(live, second_img, 0.0)
    source = jnp.where(live, source_ref[...], 0.0)
    inner_products(image, second_img, source, probes, products_ref)


def leave_faces(field, probes, slots_ref, leave_ref):
    elements, dofs = field.shape[0] // probes, field.shape[1]
    members = slots_ref.shape[0] + 1
    parts = stacked(field)
    me = lax.axis_index("gz")
    for shift in range(1, members):
        flat_row = slots_ref[shift - 1]
        taken = take_faces(parts, hot_elements(flat_row, elements, dofs), hot_dofs(flat_row, dofs))
        target = lax.rem(me + shift, members)
        for probe in range(probes):
            leave_ref[target, pl.ds(probe, 1), :] = taken[probe]
    leave_ref[me] = jnp.zeros(leave_ref.shape[1:], f32)


def placed_faces(shape, probes, slots_ref, came_ref):
    rows, dofs = shape
    elements = rows // probes
    members = slots_ref.shape[0] + 1
    me = lax.axis_index("gz")
    total = jnp.zeros((2 * rows, dofs), f32)
    for shift in range(1, members):
        flat_row = slots_ref[shift - 1]
        came = came_ref[lax.rem(me + shift, members)]
        total += add_faces(
            [came[probe : probe + 1, :] for probe in range(probes)],
            hot_elements(flat_row, elements, dofs),
            hot_dofs(flat_row, dofs),
        )
    return folded(total)


def far_first_kernel(*refs):
    count_ref, *operands = refs[:6]
    refs = refs[6:]
    first_ref, source_ref, up_ref, down_ref, slots_ref, leave_ref = refs[:6]
    members = slots_ref.shape[0] + 1
    first_pre, _, _ = begin(
        {
            "operands": operands,
            "scratch": refs[6:],
            "slots": slots_ref,
            "up": up_ref,
            "down": down_ref,
            "source": source_ref,
            "first": first_ref,
        },
        lambda me, step: lax.rem(me + step, members),
        count_ref,
        lambda: None,
    )
    leave_faces(first_pre, leave_ref.shape[1], slots_ref, leave_ref)


def far_second_kernel(
    slots_ref, up_ref, down_ref, first_ref, k_ref, p_ref, came_ref,
    image_ref, second_ref, leave_ref,
):
    probes = came_ref.shape[1]
    up = up_ref[...]
    placed = placed_faces(first_ref.shape, probes, slots_ref, came_ref)
    image = times_matrix(first_ref[...], k_ref[...]) * up - jnp.where(up > 0.0, coupling * placed, 0.0)
    image_ref[...] = image
    second_pre = times_matrix(image, p_ref[...]) * down_ref[...]
    second_ref[...] = second_pre
    leave_faces(second_pre, probes, slots_ref, leave_ref)


def far_third_kernel(
    slots_ref, up_ref, source_ref, image_ref, second_ref, k_ref, came_ref, products_ref
):
    probes = came_ref.shape[1]
    up = up_ref[...]
    placed = placed_faces(source_ref.shape, probes, slots_ref, came_ref)
    second_img = times_matrix(second_ref[...], k_ref[...]) * up - jnp.where(up > 0.0, coupling * placed, 0.0)
    inner_products(image_ref[...], second_img, source_ref[...], probes, products_ref)


def last_kernel(probes, count_ref, first_ref, second_ref, parts_ref, out_ref):
    rows, _ = first_ref.shape
    elements = rows // probes
    total = jnp.sum(parts_ref[...], axis=0)
    live = live_column(count_ref, elements)
    for probe in range(probes):
        self_one, cross_mid, self_two, load_one, load_two = (
            total[:, place * probes + probe : place * probes + probe + 1] for place in range(5)
        )
        determinant = self_one * self_two - cross_mid * cross_mid
        weight_one = (self_two * load_one - cross_mid * load_two) / determinant
        weight_two = (self_one * load_two - cross_mid * load_one) / determinant
        block = pl.ds(probe * elements, elements)
        value = weight_one * first_ref[block, :] + weight_two * second_ref[block, :]
        out_ref[block, :] = jnp.where(live, value, 0.0)


def call(kernel, in_specs, out_shapes, flops, *args, scratch=()):
    return pl.pallas_call(
        kernel,
        out_shape=out_shapes,
        in_specs=in_specs,
        out_specs=jax.tree.map(lambda _: vmem_spec, out_shapes),
        scratch_shapes=scratch,
        compiler_params=pltpu.CompilerParams(vmem_limit_bytes=vmem_grant),
        cost_estimate=pl.CostEstimate(flops=flops, bytes_accessed=1 << 20, transcendentals=0),
    )(*args)


def begin_call(kernel, out_shapes, flops, scalars, *fetched):
    links, *others = fetched
    scratch = [pltpu.SMEM(links.shape, links.dtype)]
    scratch += [pltpu.VMEM(value.shape, value.dtype) for value in others]
    return call(
        kernel,
        [smem_spec] * len(scalars) + [hbm_spec] * len(fetched),
        out_shapes,
        flops,
        *scalars,
        *(pltpu.with_memory_space_constraint(value, pltpu.HBM) for value in fetched),
        scratch=scratch + [pltpu.SemaphoreType.DMA((len(fetched),))],
    )


def near_steps(members, shapes, arguments):
    rhs, viscosity, counts, neighbours, face_index, k_matrix, p_matrix = arguments
    field, slots_shape, products_shape = shapes
    rows, dofs = field.shape
    steps, _, width = slots_shape.shape
    probes = rhs.shape[3]
    flops = 8 * rows * dofs * steps * width
    hot = jax.ShapeDtypeStruct((dofs, steps * width), bf16)
    message = jax.ShapeDtypeStruct((message_length(steps, probes, width), lane_count), f32)
    first_pre, source, up, down, base, slots, hot_own, *leaving = begin_call(
        near_first_kernel,
        [field] * 5 + [slots_shape, hot] + [message] * steps,
        2 * flops,
        (),
        neighbours,
        face_index,
        viscosity,
        rhs,
        p_matrix,
        k_matrix,
    )
    came = [
        lax.ppermute(
            leaving[step - 1], "gz", [(source, source ^ step) for source in range(members)]
        )
        for step in range(1, members)
    ]
    second_pre, products = call(
        functools.partial(near_second_kernel, probes),
        [smem_spec] + [vmem_spec] * (9 + steps),
        [field, products_shape],
        6 * flops,
        counts,
        source,
        up,
        down,
        base,
        slots,
        hot_own,
        k_matrix,
        p_matrix,
        leaving[0],
        *came,
    )
    return first_pre, second_pre, products


def far_steps(members, shapes, arguments):
    rhs, viscosity, counts, neighbours, face_index, k_matrix, p_matrix = arguments
    field, slots_shape, products_shape = shapes
    rows, dofs = field.shape
    shifts, _, width = slots_shape.shape
    flops = 8 * rows * dofs * shifts * width
    faces = jax.ShapeDtypeStruct((members, rhs.shape[3], width), f32)

    def exchange(value):
        return lax.all_to_all(value, "gz", split_axis=0, concat_axis=0)

    first_pre, source, up, down, slots, leaving = begin_call(
        far_first_kernel,
        [field] * 4 + [slots_shape, faces],
        flops,
        (counts,),
        neighbours,
        face_index,
        viscosity,
        rhs,
        p_matrix,
    )
    first_img, second_pre, leaving = call(
        far_second_kernel,
        [vmem_spec] * 7,
        [field, field, faces],
        2 * flops,
        slots,
        up,
        down,
        first_pre,
        k_matrix,
        p_matrix,
        exchange(leaving),
    )
    products = call(
        far_third_kernel,
        [vmem_spec] * 7,
        products_shape,
        flops,
        slots,
        up,
        source,
        first_img,
        second_pre,
        k_matrix,
        exchange(leaving),
    )
    return first_pre, second_pre, products


def per_device(mesh, *arguments):
    rhs, face_index = arguments[0], arguments[4]
    probes, elements, dofs = rhs.shape[3:]
    members = mesh.shape["gz"]
    lanes = -(-5 * probes // 128) * 128
    shapes = (
        jax.ShapeDtypeStruct((probes * elements, dofs), f32),
        jax.ShapeDtypeStruct((members - 1, 1, face_index.shape[-1]), jnp.int32),
        jax.ShapeDtypeStruct((mesh.size, 1, lanes), f32),
    )
    near = 1 < members <= short_group and elements <= face_index.shape[-1]
    near = near and elements * dofs < 1 << 24
    steps = near_steps if near else far_steps
    first_pre, second_pre, products = steps(members, shapes, arguments)
    result = call(
        functools.partial(last_kernel, probes),
        [smem_spec] + [vmem_spec] * 3,
        shapes[0],
        probes * elements * dofs,
        arguments[2],
        first_pre,
        second_pre,
        lax.all_to_all(products, ("gx", "gy", "gz"), split_axis=0, concat_axis=0),
    )
    return result.reshape(rhs.shape)


def solution(mesh):
    return jax.shard_map(
        functools.partial(per_device, mesh),
        mesh=mesh,
        in_specs=(
            P("gx", "gy", "gz", None, None, None),
            P("gx", "gy", "gz", None),
            P("gx", "gy", "gz"),
            P("gx", "gy", "gz", None),
            P("gx", "gy", "gz", None, None),
            P(),
            P(),
        ),
        out_specs=P("gx", "gy", "gz", None, None, None),
        check_vma=False,
    )
```

```python
import functools

import jax
import jax.numpy as jnp
from jax import lax
from jax.experimental import pallas as pl
from jax.experimental.pallas import tpu as pltpu
from jax.sharding import PartitionSpec as P

coupling = 0.5
vmem_grant = 48 * 1024 * 1024
short_group = 4
lane_count = 128
f32 = jnp.float32
bf16 = jnp.bfloat16
vmem_spec = pl.BlockSpec(memory_space=pltpu.VMEM)
smem_spec = pl.BlockSpec(memory_space=pltpu.SMEM)
hbm_spec = pl.BlockSpec(memory_space=pltpu.HBM)


def two_parts(value):
    high = value.astype(bf16)
    return high, (value - high.astype(f32)).astype(bf16)


def dot(left, right):
    return jnp.dot(left, right, preferred_element_type=f32)


def dot_transposed(left, right):
    return lax.dot_general(left, right, (((1,), (1,)), ((), ())), preferred_element_type=f32)


def times_matrix(rows, matrix):
    return times_parts(rows, *two_parts(matrix))


def times_parts(rows, mat_high, mat_low):
    count = rows.shape[0]
    row_high, row_low = two_parts(rows)
    both = dot(jnp.concatenate([row_high, row_low], axis=0), mat_high)
    return both[:count] + (both[count:] + dot(row_high, mat_low))


def split_index(index, dofs):
    if dofs & (dofs - 1) == 0:
        return lax.shift_right_arithmetic(index, dofs.bit_length() - 1), index & (dofs - 1)
    element = jnp.floor_divide(index, dofs)
    return element, index - element * dofs


def slot_of(target, links_ref, index_ref):
    slot = jnp.int32(-1)
    for position in range(links_ref.shape[-1]):
        slot = jnp.where(links_ref[0, 0, 0, position] == target, jnp.int32(position), slot)
    row = index_ref[0, 0, 0, pl.ds(jnp.maximum(slot, 0), 1), :]
    return jnp.where(slot >= 0, row, -1)


def hot_elements(flat_row, elements, dofs):
    element, _ = split_index(flat_row, dofs)
    return lax.broadcasted_iota(jnp.int32, (elements, flat_row.shape[1]), 0) == element


def hot_dofs(flat_row, dofs):
    _, dof = split_index(flat_row, dofs)
    shape = (dofs, flat_row.shape[1])
    line = lax.broadcasted_iota(jnp.int32, shape, 0).astype(jnp.int16)
    hit = line == jnp.broadcast_to(dof.astype(jnp.int16), shape)
    return jnp.where(hit, jnp.ones(shape, bf16), jnp.zeros(shape, bf16))


def as_column(row):
    elements = row.shape[1]
    line = lax.broadcasted_iota(jnp.int32, (elements, elements), 0)
    column = lax.broadcasted_iota(jnp.int32, (elements, elements), 1)
    spread = jnp.where(line == column, jnp.broadcast_to(row, (elements, elements)), 0.0)
    return jnp.sum(spread, axis=1, keepdims=True)


def wide(column, probes, dofs):
    return jnp.broadcast_to(jnp.concatenate([column] * probes, axis=0), (probes * column.shape[0], dofs))


def stacked(value):
    return jnp.concatenate(two_parts(value), axis=0)


def take_faces(parts, over_elements, over_dofs):
    elements = over_elements.shape[0]
    rows = parts.shape[0] // 2
    picked = dot(parts, over_dofs)
    picked = picked[:rows] + picked[rows:]
    return [
        jnp.sum(jnp.where(over_elements, picked[low : low + elements], 0.0), axis=0, keepdims=True)
        for low in range(0, rows, elements)
    ]


def add_faces(values, over_elements, over_dofs):
    highs = [value.astype(bf16).astype(f32) for value in values]
    lows = [value - high for value, high in zip(values, highs)]
    spread = jnp.concatenate(
        [jnp.where(over_elements, part, 0.0).astype(bf16) for part in highs + lows], axis=0
    )
    return dot_transposed(spread, over_dofs)


def folded(parts):
    rows = parts.shape[0] // 2
    return parts[:rows] + parts[rows:]


def as_row(lines, lanes):
    count = -(-len(lines) // 8) * 8
    spare = jnp.zeros((count - len(lines), lines[0].shape[1]), f32)
    sums = jnp.sum(jnp.concatenate(lines + [spare], axis=0), axis=1, keepdims=True)
    line = lax.broadcasted_iota(jnp.int32, (count, lanes), 0)
    lane = lax.broadcasted_iota(jnp.int32, (count, lanes), 1)
    return jnp.sum(jnp.where(line == lane, sums, 0.0), axis=0, keepdims=True)


def inner_products(first_img, second_img, source, probes, products_ref):
    elements = source.shape[0] // probes
    pairs = (
        (first_img, first_img),
        (first_img, second_img),
        (second_img, second_img),
        (first_img, source),
        (second_img, source),
    )
    lines = []
    for left, right in pairs:
        product = left * right
        for probe in range(probes):
            lines.append(
                jnp.sum(product[probe * elements : (probe + 1) * elements], axis=0, keepdims=True)
            )
    products_ref[...] = jnp.broadcast_to(as_row(lines, products_ref.shape[-1]), products_ref.shape)


def live_column(count_ref, elements):
    return lax.broadcasted_iota(jnp.int32, (elements, 1), 0) < count_ref[0, 0, 0]


def begin(refs, partner, count_ref, prepare):
    links_hbm, index_hbm, visc_hbm, rhs_hbm, *matrices_hbm = refs["operands"]
    links_ref, index_ref, visc_ref, rhs_ref, *matrix_refs, arrived = refs["scratch"]
    pairs = (
        (links_hbm, links_ref),
        (index_hbm, index_ref),
        (rhs_hbm, rhs_ref),
        (matrices_hbm[0], matrix_refs[0]),
        (visc_hbm, visc_ref),
        *zip(matrices_hbm[1:], matrix_refs[1:]),
    )
    copies = [
        pltpu.make_async_copy(held, here, arrived.at[place])
        for place, (held, here) in enumerate(pairs)
    ]
    for copy in copies:
        copy.start()
    copies[0].wait()
    copies[1].wait()
    slots_ref = refs["slots"]
    me = lax.axis_index("gz")
    for step in range(1, slots_ref.shape[0] + 1):
        slots_ref[step - 1] = slot_of(partner(me, step), links_ref, index_ref)
    prepare()
    copies[4].wait()
    probes, elements, dofs = rhs_ref.shape[3:]
    live = jnp.ones((elements, 1), f32)
    if count_ref is not None:
        live = live_column(count_ref, elements).astype(f32)
    visc = as_column(visc_ref[0, 0])
    up = wide(live * visc, probes, dofs)
    down = wide(live / visc, probes, dofs)
    refs["up"][...] = up
    refs["down"][...] = down
    copies[2].wait()
    source = rhs_ref[...].reshape(probes * elements, dofs)
    if count_ref is not None:
        source = source * wide(live, probes, dofs)
    refs["source"][...] = source
    copies[3].wait()
    smoother = two_parts(matrix_refs[0][...])
    first_pre = times_parts(source, *smoother) * down
    refs["first"][...] = first_pre
    for copy in copies[5:]:
        copy.wait()
    return first_pre, up, down, smoother


def message_places(steps, probes):
    values = steps * probes
    return values, values + probes, values + probes + steps


def message_length(steps, probes, width):
    return -(-(message_places(steps, probes)[2] * (width // lane_count) + 1) // 8) * 8


def write_row(message_ref, place, row):
    pieces = row.shape[1] // lane_count
    for piece in range(pieces):
        line = place * pieces + piece
        message_ref[line : line + 1, :] = row[:, piece * lane_count : (piece + 1) * lane_count]


def read_row(message_ref, place, width):
    pieces = width // lane_count
    lines = range(place * pieces, (place + 1) * pieces)
    return jnp.concatenate([message_ref[line : line + 1, :] for line in lines], axis=1)


def near_first_kernel(*refs):
    operands, refs = refs[:6], refs[6:]
    first_ref, source_ref, up_ref, down_ref, base_ref, slots_ref, hot_ref = refs[:7]
    part_refs, refs = refs[7:11], refs[11:]
    steps, _, width = slots_ref.shape
    leave_refs, scratch = refs[:steps], refs[steps:]
    visc_ref, rhs_ref, _, k_ref = scratch[2:6]
    probes, elements, dofs = rhs_ref.shape[3:]

    def prepare():
        for step in range(steps):
            hot_ref[:, step * width : (step + 1) * width] = hot_dofs(slots_ref[step], dofs)

    first_pre, up, down, smoother = begin(
        {
            "operands": operands,
            "scratch": scratch,
            "slots": slots_ref,
            "up": up_ref,
            "down": down_ref,
            "source": source_ref,
            "first": first_ref,
        },
        lambda me, step: me ^ step,
        None,
        prepare,
    )
    stiffness = two_parts(k_ref[...])
    base = times_parts(first_pre, *stiffness) * up
    base_ref[...] = base
    first_parts = stacked(first_pre)
    second_parts = stacked(times_parts(base, *smoother) * down)
    for part_ref, part in zip(part_refs, smoother + stiffness):
        part_ref[...] = part
    second_at, index_at, visc_at = message_places(steps, probes)
    for step in range(1, steps + 1):
        flat_row = slots_ref[step - 1]
        over_elements = hot_elements(flat_row, elements, dofs)
        over_dofs = hot_ref[:, (step - 1) * width : step * width]
        first_rows = take_faces(first_parts, over_elements, over_dofs)
        second_rows = take_faces(second_parts, over_elements, over_dofs)
        for probe in range(probes):
            write_row(leave_refs[step - 1], second_at + probe, second_rows[probe])
            for leave_ref in leave_refs:
                write_row(leave_ref, (step - 1) * probes + probe, first_rows[probe])
        for leave_ref in leave_refs:
            write_row(leave_ref, index_at + step - 1, flat_row.astype(f32))
    visc_line = visc_at * (width // lane_count)
    for leave_ref in leave_refs:
        leave_ref[visc_line : visc_line + 1, :elements] = visc_ref[0, 0]


def near_second_kernel(
    probes, count_ref, source_ref, up_ref, down_ref, base_ref, slots_ref, hot_ref,
    p_high_ref, p_low_ref, k_high_ref, k_low_ref, mine_ref, *refs
):
    came_refs = refs[:-2]
    second_ref, products_ref = refs[-2:]
    steps, _, width = slots_ref.shape
    members = steps + 1
    rows, dofs = source_ref.shape
    elements = rows // probes
    second_at, index_at, visc_at = message_places(steps, probes)

    def message(step):
        return mine_ref if step == 0 else came_refs[step - 1]

    def inbound_first(member, step):
        sent = message(member ^ step)
        return [
            read_row(sent, (step - 1) * probes + probe, width) for probe in range(probes)
        ]

    own_elements = [hot_elements(slots_ref[step], elements, dofs) for step in range(steps)]
    own_dofs = [hot_ref[:, step * width : (step + 1) * width] for step in range(steps)]

    def placed_here(values):
        return folded(
            sum(add_faces(values[i], own_elements[i], own_dofs[i]) for i in range(steps))
        )

    up, down = up_ref[...], down_ref[...]
    live = wide(live_column(count_ref, elements).astype(f32), probes, dofs) > 0.0
    placed = placed_here([inbound_first(0, step) for step in range(1, members)])
    image = jnp.where(live, base_ref[...] - coupling * placed, 0.0)
    images, back = [image], []
    for member in range(1, members):
        total = 0.0
        for step in range(1, members):
            flat_row = read_row(message(member), index_at + step - 1, width).astype(jnp.int32)
            over_elements = hot_elements(flat_row, elements, dofs)
            over_dofs = hot_dofs(flat_row, dofs)
            total = total + add_faces(inbound_first(member, step), over_elements, over_dofs)
            if step == member:
                back.append((over_elements, over_dofs))
        images.append(-coupling * folded(total))
    smooth = times_parts(jnp.concatenate(images, axis=0), p_high_ref[...], p_low_ref[...])
    second_pre = smooth[:rows] * down
    second_ref[...] = second_pre
    values = []
    visc_line = visc_at * (width // lane_count)
    for member in range(1, members):
        sent = message(member)
        visc = as_column(sent[visc_line : visc_line + 1, :elements])
        scale = wide(1.0 / visc, probes, dofs)
        change = smooth[member * rows : (member + 1) * rows] * scale
        taken = take_faces(stacked(change), *back[member - 1])
        values.append(
            [taken[probe] + read_row(sent, second_at + probe, width) for probe in range(probes)]
        )
    placed = placed_here(values)
    second_img = times_parts(second_pre, k_high_ref[...], k_low_ref[...]) * up - coupling * placed
    second_img = jnp.where(live, second_img, 0.0)
    source = jnp.where(live, source_ref[...], 0.0)
    inner_products(image, second_img, source, probes, products_ref)


def leave_faces(field, probes, slots_ref, leave_ref):
    elements, dofs = field.shape[0] // probes, field.shape[1]
    members = slots_ref.shape[0] + 1
    parts = stacked(field)
    me = lax.axis_index("gz")
    for shift in range(1, members):
        flat_row = slots_ref[shift - 1]
        taken = take_faces(parts, hot_elements(flat_row, elements, dofs), hot_dofs(flat_row, dofs))
        target = lax.rem(me + shift, members)
        for probe in range(probes):
            leave_ref[target, pl.ds(probe, 1), :] = taken[probe]
    leave_ref[me] = jnp.zeros(leave_ref.shape[1:], f32)


def placed_faces(shape, probes, slots_ref, came_ref):
    rows, dofs = shape
    elements = rows // probes
    members = slots_ref.shape[0] + 1
    me = lax.axis_index("gz")
    total = jnp.zeros((2 * rows, dofs), f32)
    for shift in range(1, members):
        flat_row = slots_ref[shift - 1]
        came = came_ref[lax.rem(me + shift, members)]
        total += add_faces(
            [came[probe : probe + 1, :] for probe in range(probes)],
            hot_elements(flat_row, elements, dofs),
            hot_dofs(flat_row, dofs),
        )
    return folded(total)


def far_first_kernel(*refs):
    count_ref, *operands = refs[:6]
    refs = refs[6:]
    first_ref, source_ref, up_ref, down_ref, slots_ref, leave_ref = refs[:6]
    members = slots_ref.shape[0] + 1
    first_pre, *_ = begin(
        {
            "operands": operands,
            "scratch": refs[6:],
            "slots": slots_ref,
            "up": up_ref,
            "down": down_ref,
            "source": source_ref,
            "first": first_ref,
        },
        lambda me, step: lax.rem(me + step, members),
        count_ref,
        lambda: None,
    )
    leave_faces(first_pre, leave_ref.shape[1], slots_ref, leave_ref)


def far_second_kernel(
    slots_ref, up_ref, down_ref, first_ref, k_ref, p_ref, came_ref,
    image_ref, second_ref, leave_ref,
):
    probes = came_ref.shape[1]
    up = up_ref[...]
    placed = placed_faces(first_ref.shape, probes, slots_ref, came_ref)
    image = times_matrix(first_ref[...], k_ref[...]) * up - jnp.where(up > 0.0, coupling * placed, 0.0)
    image_ref[...] = image
    second_pre = times_matrix(image, p_ref[...]) * down_ref[...]
    second_ref[...] = second_pre
    leave_faces(second_pre, probes, slots_ref, leave_ref)


def far_third_kernel(
    slots_ref, up_ref, source_ref, image_ref, second_ref, k_ref, came_ref, products_ref
):
    probes = came_ref.shape[1]
    up = up_ref[...]
    placed = placed_faces(source_ref.shape, probes, slots_ref, came_ref)
    second_img = times_matrix(second_ref[...], k_ref[...]) * up - jnp.where(up > 0.0, coupling * placed, 0.0)
    inner_products(image_ref[...], second_img, source_ref[...], probes, products_ref)


def last_kernel(probes, count_ref, first_ref, second_ref, parts_ref, out_ref):
    rows, _ = first_ref.shape
    elements = rows // probes
    total = jnp.sum(parts_ref[...], axis=0)
    live = live_column(count_ref, elements)
    for probe in range(probes):
        self_one, cross_mid, self_two, load_one, load_two = (
            total[:, place * probes + probe : place * probes + probe + 1] for place in range(5)
        )
        determinant = self_one * self_two - cross_mid * cross_mid
        weight_one = (self_two * load_one - cross_mid * load_two) / determinant
        weight_two = (self_one * load_two - cross_mid * load_one) / determinant
        block = pl.ds(probe * elements, elements)
        value = weight_one * first_ref[block, :] + weight_two * second_ref[block, :]
        out_ref[block, :] = jnp.where(live, value, 0.0)


def call(kernel, in_specs, out_shapes, flops, *args, scratch=()):
    return pl.pallas_call(
        kernel,
        out_shape=out_shapes,
        in_specs=in_specs,
        out_specs=jax.tree.map(lambda _: vmem_spec, out_shapes),
        scratch_shapes=scratch,
        compiler_params=pltpu.CompilerParams(vmem_limit_bytes=vmem_grant),
        cost_estimate=pl.CostEstimate(flops=flops, bytes_accessed=1 << 20, transcendentals=0),
    )(*args)


def begin_call(kernel, out_shapes, flops, scalars, *fetched):
    links, *others = fetched
    scratch = [pltpu.SMEM(links.shape, links.dtype)]
    scratch += [pltpu.VMEM(value.shape, value.dtype) for value in others]
    return call(
        kernel,
        [smem_spec] * len(scalars) + [hbm_spec] * len(fetched),
        out_shapes,
        flops,
        *scalars,
        *(pltpu.with_memory_space_constraint(value, pltpu.HBM) for value in fetched),
        scratch=scratch + [pltpu.SemaphoreType.DMA((len(fetched),))],
    )


def near_steps(members, shapes, arguments):
    rhs, viscosity, counts, neighbours, face_index, k_matrix, p_matrix = arguments
    field, slots_shape, products_shape = shapes
    rows, dofs = field.shape
    steps, _, width = slots_shape.shape
    probes = rhs.shape[3]
    flops = 8 * rows * dofs * steps * width
    hot = jax.ShapeDtypeStruct((dofs, steps * width), bf16)
    message = jax.ShapeDtypeStruct((message_length(steps, probes, width), lane_count), f32)
    part = jax.ShapeDtypeStruct(p_matrix.shape, bf16)
    first_pre, source, up, down, base, slots, hot_own, *rest = begin_call(
        near_first_kernel,
        [field] * 5 + [slots_shape, hot] + [part] * 4 + [message] * steps,
        2 * flops,
        (),
        neighbours,
        face_index,
        viscosity,
        rhs,
        p_matrix,
        k_matrix,
    )
    parts, leaving = rest[:4], rest[4:]
    came = [
        lax.ppermute(
            leaving[step - 1], "gz", [(source, source ^ step) for source in range(members)]
        )
        for step in range(1, members)
    ]
    second_pre, products = call(
        functools.partial(near_second_kernel, probes),
        [smem_spec] + [vmem_spec] * (11 + steps),
        [field, products_shape],
        6 * flops,
        counts,
        source,
        up,
        down,
        base,
        slots,
        hot_own,
        *parts,
        leaving[0],
        *came,
    )
    return first_pre, second_pre, products


def far_steps(members, shapes, arguments):
    rhs, viscosity, counts, neighbours, face_index, k_matrix, p_matrix = arguments
    field, slots_shape, products_shape = shapes
    rows, dofs = field.shape
    shifts, _, width = slots_shape.shape
    flops = 8 * rows * dofs * shifts * width
    faces = jax.ShapeDtypeStruct((members, rhs.shape[3], width), f32)

    def exchange(value):
        return lax.all_to_all(value, "gz", split_axis=0, concat_axis=0)

    first_pre, source, up, down, slots, leaving = begin_call(
        far_first_kernel,
        [field] * 4 + [slots_shape, faces],
        flops,
        (counts,),
        neighbours,
        face_index,
        viscosity,
        rhs,
        p_matrix,
    )
    first_img, second_pre, leaving = call(
        far_second_kernel,
        [vmem_spec] * 7,
        [field, field, faces],
        2 * flops,
        slots,
        up,
        down,
        first_pre,
        k_matrix,
        p_matrix,
        exchange(leaving),
    )
    products = call(
        far_third_kernel,
        [vmem_spec] * 7,
        products_shape,
        flops,
        slots,
        up,
        source,
        first_img,
        second_pre,
        k_matrix,
        exchange(leaving),
    )
    return first_pre, second_pre, products


def per_device(mesh, *arguments):
    rhs, face_index = arguments[0], arguments[4]
    probes, elements, dofs = rhs.shape[3:]
    members = mesh.shape["gz"]
    lanes = -(-5 * probes // 128) * 128
    shapes = (
        jax.ShapeDtypeStruct((probes * elements, dofs), f32),
        jax.ShapeDtypeStruct((members - 1, 1, face_index.shape[-1]), jnp.int32),
        jax.ShapeDtypeStruct((mesh.size, 1, lanes), f32),
    )
    near = 1 < members <= short_group and elements <= face_index.shape[-1]
    near = near and elements * dofs < 1 << 24
    steps = near_steps if near else far_steps
    first_pre, second_pre, products = steps(members, shapes, arguments)
    result = call(
        functools.partial(last_kernel, probes),
        [smem_spec] + [vmem_spec] * 3,
        shapes[0],
        probes * elements * dofs,
        arguments[2],
        first_pre,
        second_pre,
        lax.all_to_all(products, ("gx", "gy", "gz"), split_axis=0, concat_axis=0),
    )
    return result.reshape(rhs.shape)


def solution(mesh):
    return jax.shard_map(
        functools.partial(per_device, mesh),
        mesh=mesh,
        in_specs=(
            P("gx", "gy", "gz", None, None, None),
            P("gx", "gy", "gz", None),
            P("gx", "gy", "gz"),
            P("gx", "gy", "gz", None),
            P("gx", "gy", "gz", None, None),
            P(),
            P(),
        ),
        out_specs=P("gx", "gy", "gz", None, None, None),
        check_vma=False,
    )
```

```python
import functools

import jax
import jax.numpy as jnp
from jax import lax
from jax.experimental import pallas as pl
from jax.experimental.pallas import tpu as pltpu
from jax.sharding import PartitionSpec as P

coupling = 0.5
vmem_grant = 48 * 1024 * 1024
short_group = 4
lane_count = 128
f32 = jnp.float32
bf16 = jnp.bfloat16
vmem_spec = pl.BlockSpec(memory_space=pltpu.VMEM)
smem_spec = pl.BlockSpec(memory_space=pltpu.SMEM)
hbm_spec = pl.BlockSpec(memory_space=pltpu.HBM)


def two_parts(value):
    high = value.astype(bf16)
    return high, (value - high.astype(f32)).astype(bf16)


def dot(left, right):
    return jnp.dot(left, right, preferred_element_type=f32)


def dot_transposed(left, right):
    return lax.dot_general(left, right, (((1,), (1,)), ((), ())), preferred_element_type=f32)


def times_matrix(rows, matrix):
    return times_parts(rows, *two_parts(matrix))


def times_parts(rows, mat_high, mat_low):
    row_high, row_low = two_parts(rows)
    return dot(
        jnp.concatenate([row_high, row_low, row_high], axis=1),
        jnp.concatenate([mat_high, mat_high, mat_low], axis=0),
    )


def split_index(index, dofs):
    if dofs & (dofs - 1) == 0:
        return lax.shift_right_arithmetic(index, dofs.bit_length() - 1), index & (dofs - 1)
    element = jnp.floor_divide(index, dofs)
    return element, index - element * dofs


def slot_of(target, links_ref, index_ref):
    slot = jnp.int32(-1)
    for position in range(links_ref.shape[-1]):
        slot = jnp.where(links_ref[0, 0, 0, position] == target, jnp.int32(position), slot)
    row = index_ref[0, 0, 0, pl.ds(jnp.maximum(slot, 0), 1), :]
    return jnp.where(slot >= 0, row, -1)


def hot_elements(flat_row, elements, dofs):
    element, _ = split_index(flat_row, dofs)
    return lax.broadcasted_iota(jnp.int32, (elements, flat_row.shape[1]), 0) == element


def hot_dofs(flat_row, dofs):
    _, dof = split_index(flat_row, dofs)
    shape = (dofs, flat_row.shape[1])
    line = lax.broadcasted_iota(jnp.int32, shape, 0).astype(jnp.int16)
    hit = line == jnp.broadcast_to(dof.astype(jnp.int16), shape)
    return jnp.where(hit, jnp.ones(shape, bf16), jnp.zeros(shape, bf16))


def as_column(row):
    elements = row.shape[1]
    line = lax.broadcasted_iota(jnp.int32, (elements, elements), 0)
    column = lax.broadcasted_iota(jnp.int32, (elements, elements), 1)
    spread = jnp.where(line == column, jnp.broadcast_to(row, (elements, elements)), 0.0)
    return jnp.sum(spread, axis=1, keepdims=True)


def wide(column, probes, dofs):
    return jnp.broadcast_to(jnp.concatenate([column] * probes, axis=0), (probes * column.shape[0], dofs))


def take_faces(fields, over_elements, over_dofs):
    elements = over_elements.shape[0]
    picked = dot(
        jnp.concatenate(two_parts(fields), axis=1), jnp.concatenate([over_dofs, over_dofs], axis=0)
    )
    return [
        jnp.sum(jnp.where(over_elements, picked[low : low + elements], 0.0), axis=0, keepdims=True)
        for low in range(0, fields.shape[0], elements)
    ]


def spread_faces(values, over_elements):
    highs = [value.astype(bf16).astype(f32) for value in values]
    lows = [value - high for value, high in zip(values, highs)]
    return jnp.concatenate(
        [jnp.where(over_elements, part, 0.0).astype(bf16) for part in highs + lows], axis=0
    )


def add_faces(spreads, over_dofs):
    parts = dot_transposed(jnp.concatenate(spreads, axis=1), over_dofs)
    rows = parts.shape[0] // 2
    return parts[:rows] + parts[rows:]


def as_row(lines, lanes):
    count = -(-len(lines) // 8) * 8
    spare = jnp.zeros((count - len(lines), lines[0].shape[1]), f32)
    sums = jnp.sum(jnp.concatenate(lines + [spare], axis=0), axis=1, keepdims=True)
    line = lax.broadcasted_iota(jnp.int32, (count, lanes), 0)
    lane = lax.broadcasted_iota(jnp.int32, (count, lanes), 1)
    return jnp.sum(jnp.where(line == lane, sums, 0.0), axis=0, keepdims=True)


def inner_products(first_img, second_img, source, probes, products_ref):
    elements = source.shape[0] // probes
    pairs = (
        (first_img, first_img),
        (first_img, second_img),
        (second_img, second_img),
        (first_img, source),
        (second_img, source),
    )
    lines = []
    for left, right in pairs:
        product = left * right
        for probe in range(probes):
            lines.append(
                jnp.sum(product[probe * elements : (probe + 1) * elements], axis=0, keepdims=True)
            )
    products_ref[...] = jnp.broadcast_to(as_row(lines, products_ref.shape[-1]), products_ref.shape)


def live_column(count_ref, elements):
    return lax.broadcasted_iota(jnp.int32, (elements, 1), 0) < count_ref[0, 0, 0]


def begin(refs, partner, count_ref, prepare):
    links_hbm, index_hbm, visc_hbm, rhs_hbm, *matrices_hbm = refs["operands"]
    links_ref, index_ref, visc_ref, rhs_ref, *matrix_refs, arrived = refs["scratch"]
    pairs = (
        (links_hbm, links_ref),
        (index_hbm, index_ref),
        (rhs_hbm, rhs_ref),
        (matrices_hbm[0], matrix_refs[0]),
        (visc_hbm, visc_ref),
        *zip(matrices_hbm[1:], matrix_refs[1:]),
    )
    copies = [
        pltpu.make_async_copy(held, here, arrived.at[place])
        for place, (held, here) in enumerate(pairs)
    ]
    for copy in copies:
        copy.start()
    copies[0].wait()
    copies[1].wait()
    slots_ref = refs["slots"]
    me = lax.axis_index("gz")
    for step in range(1, slots_ref.shape[0] + 1):
        slots_ref[step - 1] = slot_of(partner(me, step), links_ref, index_ref)
    prepare()
    copies[4].wait()
    probes, elements, dofs = rhs_ref.shape[3:]
    live = jnp.ones((elements, 1), f32)
    if count_ref is not None:
        live = live_column(count_ref, elements).astype(f32)
    visc = as_column(visc_ref[0, 0])
    up = wide(live * visc, probes, dofs)
    down = wide(live / visc, probes, dofs)
    refs["up"][...] = up
    refs["down"][...] = down
    copies[2].wait()
    source = rhs_ref[...].reshape(probes * elements, dofs)
    if count_ref is not None:
        source = source * wide(live, probes, dofs)
    refs["source"][...] = source
    copies[3].wait()
    smoother = two_parts(matrix_refs[0][...])
    first_pre = times_parts(source, *smoother) * down
    refs["first"][...] = first_pre
    for copy in copies[5:]:
        copy.wait()
    return first_pre, up, down, smoother


def message_places(steps, probes):
    values = steps * probes
    return values, values + probes, values + probes + steps


def message_length(steps, probes, width):
    return -(-(message_places(steps, probes)[2] * (width // lane_count) + 1) // 8) * 8


def write_row(message_ref, place, row):
    pieces = row.shape[1] // lane_count
    for piece in range(pieces):
        line = place * pieces + piece
        message_ref[line : line + 1, :] = row[:, piece * lane_count : (piece + 1) * lane_count]


def read_row(message_ref, place, width):
    pieces = width // lane_count
    lines = range(place * pieces, (place + 1) * pieces)
    return jnp.concatenate([message_ref[line : line + 1, :] for line in lines], axis=1)


def near_first_kernel(*refs):
    operands, refs = refs[:6], refs[6:]
    first_ref, source_ref, up_ref, down_ref, base_ref, slots_ref, hot_ref = refs[:7]
    part_refs, refs = refs[7:11], refs[11:]
    steps, _, width = slots_ref.shape
    leave_refs, scratch = refs[:steps], refs[steps:]
    visc_ref, rhs_ref, _, k_ref = scratch[2:6]
    probes, elements, dofs = rhs_ref.shape[3:]

    def prepare():
        for step in range(steps):
            hot_ref[:, step * width : (step + 1) * width] = hot_dofs(slots_ref[step], dofs)

    first_pre, up, down, smoother = begin(
        {
            "operands": operands,
            "scratch": scratch,
            "slots": slots_ref,
            "up": up_ref,
            "down": down_ref,
            "source": source_ref,
            "first": first_ref,
        },
        lambda me, step: me ^ step,
        None,
        prepare,
    )
    stiffness = two_parts(k_ref[...])
    base = times_parts(first_pre, *stiffness) * up
    base_ref[...] = base
    fields = jnp.concatenate([first_pre, times_parts(base, *smoother) * down], axis=0)
    for part_ref, part in zip(part_refs, smoother + stiffness):
        part_ref[...] = part
    second_at, index_at, visc_at = message_places(steps, probes)
    for step in range(1, steps + 1):
        flat_row = slots_ref[step - 1]
        over_elements = hot_elements(flat_row, elements, dofs)
        over_dofs = hot_ref[:, (step - 1) * width : step * width]
        taken = take_faces(fields, over_elements, over_dofs)
        for probe in range(probes):
            write_row(leave_refs[step - 1], second_at + probe, taken[probes + probe])
            for leave_ref in leave_refs:
                write_row(leave_ref, (step - 1) * probes + probe, taken[probe])
        for leave_ref in leave_refs:
            write_row(leave_ref, index_at + step - 1, flat_row.astype(f32))
    visc_line = visc_at * (width // lane_count)
    for leave_ref in leave_refs:
        leave_ref[visc_line : visc_line + 1, :elements] = visc_ref[0, 0]


def near_second_kernel(
    probes, count_ref, source_ref, up_ref, down_ref, base_ref, slots_ref, hot_ref,
    p_high_ref, p_low_ref, k_high_ref, k_low_ref, mine_ref, *refs
):
    came_refs = refs[:-2]
    second_ref, products_ref = refs[-2:]
    steps, _, width = slots_ref.shape
    members = steps + 1
    rows, dofs = source_ref.shape
    elements = rows // probes
    second_at, index_at, visc_at = message_places(steps, probes)

    def message(step):
        return mine_ref if step == 0 else came_refs[step - 1]

    def inbound_first(member, step):
        sent = message(member ^ step)
        return [
            read_row(sent, (step - 1) * probes + probe, width) for probe in range(probes)
        ]

    own_elements = [hot_elements(slots_ref[step], elements, dofs) for step in range(steps)]

    def placed_here(values):
        return add_faces(
            [spread_faces(values[step], own_elements[step]) for step in range(steps)], hot_ref[...]
        )

    up, down = up_ref[...], down_ref[...]
    live = wide(live_column(count_ref, elements).astype(f32), probes, dofs) > 0.0
    placed = placed_here([inbound_first(0, step) for step in range(1, members)])
    image = jnp.where(live, base_ref[...] - coupling * placed, 0.0)
    images, back = [image], []
    for member in range(1, members):
        rows_of = [
            read_row(message(member), index_at + step, width).astype(jnp.int32)
            for step in range(steps)
        ]
        over_elements = [hot_elements(flat_row, elements, dofs) for flat_row in rows_of]
        over_dofs = [hot_dofs(flat_row, dofs) for flat_row in rows_of]
        spreads = [
            spread_faces(inbound_first(member, step + 1), over_elements[step])
            for step in range(steps)
        ]
        images.append(-coupling * add_faces(spreads, jnp.concatenate(over_dofs, axis=1)))
        back.append((over_elements[member - 1], over_dofs[member - 1]))
    smooth = times_parts(jnp.concatenate(images, axis=0), p_high_ref[...], p_low_ref[...])
    second_pre = smooth[:rows] * down
    second_ref[...] = second_pre
    values = []
    visc_line = visc_at * (width // lane_count)
    for member in range(1, members):
        sent = message(member)
        visc = as_column(sent[visc_line : visc_line + 1, :elements])
        scale = wide(1.0 / visc, probes, dofs)
        change = smooth[member * rows : (member + 1) * rows] * scale
        taken = take_faces(change, *back[member - 1])
        values.append(
            [taken[probe] + read_row(sent, second_at + probe, width) for probe in range(probes)]
        )
    placed = placed_here(values)
    second_img = times_parts(second_pre, k_high_ref[...], k_low_ref[...]) * up - coupling * placed
    second_img = jnp.where(live, second_img, 0.0)
    source = jnp.where(live, source_ref[...], 0.0)
    inner_products(image, second_img, source, probes, products_ref)


def leave_faces(field, probes, slots_ref, leave_ref):
    elements, dofs = field.shape[0] // probes, field.shape[1]
    members = slots_ref.shape[0] + 1
    me = lax.axis_index("gz")
    for shift in range(1, members):
        flat_row = slots_ref[shift - 1]
        taken = take_faces(field, hot_elements(flat_row, elements, dofs), hot_dofs(flat_row, dofs))
        target = lax.rem(me + shift, members)
        for probe in range(probes):
            leave_ref[target, pl.ds(probe, 1), :] = taken[probe]
    leave_ref[me] = jnp.zeros(leave_ref.shape[1:], f32)


def placed_faces(shape, probes, slots_ref, came_ref):
    rows, dofs = shape
    elements = rows // probes
    members = slots_ref.shape[0] + 1
    me = lax.axis_index("gz")
    total = jnp.zeros(shape, f32)
    for shift in range(1, members):
        flat_row = slots_ref[shift - 1]
        came = came_ref[lax.rem(me + shift, members)]
        values = [came[probe : probe + 1, :] for probe in range(probes)]
        spread = spread_faces(values, hot_elements(flat_row, elements, dofs))
        total += add_faces([spread], hot_dofs(flat_row, dofs))
    return total


def far_first_kernel(*refs):
    count_ref, *operands = refs[:6]
    refs = refs[6:]
    first_ref, source_ref, up_ref, down_ref, slots_ref, leave_ref = refs[:6]
    members = slots_ref.shape[0] + 1
    first_pre, *_ = begin(
        {
            "operands": operands,
            "scratch": refs[6:],
            "slots": slots_ref,
            "up": up_ref,
            "down": down_ref,
            "source": source_ref,
            "first": first_ref,
        },
        lambda me, step: lax.rem(me + step, members),
        count_ref,
        lambda: None,
    )
    leave_faces(first_pre, leave_ref.shape[1], slots_ref, leave_ref)


def far_second_kernel(
    slots_ref, up_ref, down_ref, first_ref, k_ref, p_ref, came_ref,
    image_ref, second_ref, leave_ref,
):
    probes = came_ref.shape[1]
    up = up_ref[...]
    placed = placed_faces(first_ref.shape, probes, slots_ref, came_ref)
    image = times_matrix(first_ref[...], k_ref[...]) * up - jnp.where(up > 0.0, coupling * placed, 0.0)
    image_ref[...] = image
    second_pre = times_matrix(image, p_ref[...]) * down_ref[...]
    second_ref[...] = second_pre
    leave_faces(second_pre, probes, slots_ref, leave_ref)


def far_third_kernel(
    slots_ref, up_ref, source_ref, image_ref, second_ref, k_ref, came_ref, products_ref
):
    probes = came_ref.shape[1]
    up = up_ref[...]
    placed = placed_faces(source_ref.shape, probes, slots_ref, came_ref)
    second_img = times_matrix(second_ref[...], k_ref[...]) * up - jnp.where(up > 0.0, coupling * placed, 0.0)
    inner_products(image_ref[...], second_img, source_ref[...], probes, products_ref)


def last_kernel(probes, count_ref, first_ref, second_ref, parts_ref, out_ref):
    rows, _ = first_ref.shape
    elements = rows // probes
    total = jnp.sum(parts_ref[...], axis=0)
    live = live_column(count_ref, elements)
    for probe in range(probes):
        self_one, cross_mid, self_two, load_one, load_two = (
            total[:, place * probes + probe : place * probes + probe + 1] for place in range(5)
        )
        determinant = self_one * self_two - cross_mid * cross_mid
        weight_one = (self_two * load_one - cross_mid * load_two) / determinant
        weight_two = (self_one * load_two - cross_mid * load_one) / determinant
        block = pl.ds(probe * elements, elements)
        value = weight_one * first_ref[block, :] + weight_two * second_ref[block, :]
        out_ref[block, :] = jnp.where(live, value, 0.0)


def call(kernel, in_specs, out_shapes, flops, *args, scratch=()):
    return pl.pallas_call(
        kernel,
        out_shape=out_shapes,
        in_specs=in_specs,
        out_specs=jax.tree.map(lambda _: vmem_spec, out_shapes),
        scratch_shapes=scratch,
        compiler_params=pltpu.CompilerParams(vmem_limit_bytes=vmem_grant),
        cost_estimate=pl.CostEstimate(flops=flops, bytes_accessed=1 << 20, transcendentals=0),
    )(*args)


def begin_call(kernel, out_shapes, flops, scalars, *fetched):
    links, *others = fetched
    scratch = [pltpu.SMEM(links.shape, links.dtype)]
    scratch += [pltpu.VMEM(value.shape, value.dtype) for value in others]
    return call(
        kernel,
        [smem_spec] * len(scalars) + [hbm_spec] * len(fetched),
        out_shapes,
        flops,
        *scalars,
        *(pltpu.with_memory_space_constraint(value, pltpu.HBM) for value in fetched),
        scratch=scratch + [pltpu.SemaphoreType.DMA((len(fetched),))],
    )


def near_steps(members, shapes, arguments):
    rhs, viscosity, counts, neighbours, face_index, k_matrix, p_matrix = arguments
    field, slots_shape, products_shape = shapes
    rows, dofs = field.shape
    steps, _, width = slots_shape.shape
    probes = rhs.shape[3]
    flops = 8 * rows * dofs * steps * width
    hot = jax.ShapeDtypeStruct((dofs, steps * width), bf16)
    message = jax.ShapeDtypeStruct((message_length(steps, probes, width), lane_count), f32)
    part = jax.ShapeDtypeStruct(p_matrix.shape, bf16)
    first_pre, source, up, down, base, slots, hot_own, *rest = begin_call(
        near_first_kernel,
        [field] * 5 + [slots_shape, hot] + [part] * 4 + [message] * steps,
        2 * flops,
        (),
        neighbours,
        face_index,
        viscosity,
        rhs,
        p_matrix,
        k_matrix,
    )
    parts, leaving = rest[:4], rest[4:]
    came = [
        lax.ppermute(
            leaving[step - 1], "gz", [(source, source ^ step) for source in range(members)]
        )
        for step in range(1, members)
    ]
    second_pre, products = call(
        functools.partial(near_second_kernel, probes),
        [smem_spec] + [vmem_spec] * (11 + steps),
        [field, products_shape],
        6 * flops,
        counts,
        source,
        up,
        down,
        base,
        slots,
        hot_own,
        *parts,
        leaving[0],
        *came,
    )
    return first_pre, second_pre, products


def far_steps(members, shapes, arguments):
    rhs, viscosity, counts, neighbours, face_index, k_matrix, p_matrix = arguments
    field, slots_shape, products_shape = shapes
    rows, dofs = field.shape
    shifts, _, width = slots_shape.shape
    flops = 8 * rows * dofs * shifts * width
    faces = jax.ShapeDtypeStruct((members, rhs.shape[3], width), f32)

    def exchange(value):
        return lax.all_to_all(value, "gz", split_axis=0, concat_axis=0)

    first_pre, source, up, down, slots, leaving = begin_call(
        far_first_kernel,
        [field] * 4 + [slots_shape, faces],
        flops,
        (counts,),
        neighbours,
        face_index,
        viscosity,
        rhs,
        p_matrix,
    )
    first_img, second_pre, leaving = call(
        far_second_kernel,
        [vmem_spec] * 7,
        [field, field, faces],
        2 * flops,
        slots,
        up,
        down,
        first_pre,
        k_matrix,
        p_matrix,
        exchange(leaving),
    )
    products = call(
        far_third_kernel,
        [vmem_spec] * 7,
        products_shape,
        flops,
        slots,
        up,
        source,
        first_img,
        second_pre,
        k_matrix,
        exchange(leaving),
    )
    return first_pre, second_pre, products


def per_device(mesh, *arguments):
    rhs, face_index = arguments[0], arguments[4]
    probes, elements, dofs = rhs.shape[3:]
    members = mesh.shape["gz"]
    lanes = -(-5 * probes // 128) * 128
    shapes = (
        jax.ShapeDtypeStruct((probes * elements, dofs), f32),
        jax.ShapeDtypeStruct((members - 1, 1, face_index.shape[-1]), jnp.int32),
        jax.ShapeDtypeStruct((mesh.size, 1, lanes), f32),
    )
    near = 1 < members <= short_group and elements <= face_index.shape[-1]
    near = near and elements * dofs < 1 << 24
    steps = near_steps if near else far_steps
    first_pre, second_pre, products = steps(members, shapes, arguments)
    result = call(
        functools.partial(last_kernel, probes),
        [smem_spec] + [vmem_spec] * 3,
        shapes[0],
        probes * elements * dofs,
        arguments[2],
        first_pre,
        second_pre,
        lax.all_to_all(products, ("gx", "gy", "gz"), split_axis=0, concat_axis=0),
    )
    return result.reshape(rhs.shape)


def solution(mesh):
    return jax.shard_map(
        functools.partial(per_device, mesh),
        mesh=mesh,
        in_specs=(
            P("gx", "gy", "gz", None, None, None),
            P("gx", "gy", "gz", None),
            P("gx", "gy", "gz"),
            P("gx", "gy", "gz", None),
            P("gx", "gy", "gz", None, None),
            P(),
            P(),
        ),
        out_specs=P("gx", "gy", "gz", None, None, None),
        check_vma=False,
    )
```

```python
import functools

import jax
import jax.numpy as jnp
from jax import lax
from jax.experimental import pallas as pl
from jax.experimental.pallas import tpu as pltpu
from jax.sharding import Mesh
from jax.sharding import PartitionSpec as P

coupling = 0.5
vmem_grant = 48 * 1024 * 1024
short_group = 4
lane_count = 128
fetch_pieces = 4
f32 = jnp.float32
bf16 = jnp.bfloat16
vmem_spec = pl.BlockSpec(memory_space=pltpu.VMEM)
smem_spec = pl.BlockSpec(memory_space=pltpu.SMEM)
hbm_spec = pl.BlockSpec(memory_space=pltpu.HBM)


def two_parts(value):
    high = value.astype(bf16)
    return high, (value - high.astype(f32)).astype(bf16)


def dot(left, right):
    return jnp.dot(left, right, preferred_element_type=f32)


def dot_transposed(left, right):
    return lax.dot_general(left, right, (((1,), (1,)), ((), ())), preferred_element_type=f32)


def times_matrix(rows, matrix):
    return times_parts(rows, *two_parts(matrix))


def times_parts(rows, mat_high, mat_low):
    row_high, row_low = two_parts(rows)
    return dot(
        jnp.concatenate([row_high, row_low, row_high], axis=1),
        jnp.concatenate([mat_high, mat_high, mat_low], axis=0),
    )


def split_index(index, dofs):
    if dofs & (dofs - 1) == 0:
        return lax.shift_right_arithmetic(index, dofs.bit_length() - 1), index & (dofs - 1)
    element = jnp.floor_divide(index, dofs)
    return element, index - element * dofs


def slot_of(target, links_ref, index_ref):
    slot = jnp.int32(-1)
    for position in range(links_ref.shape[-1]):
        slot = jnp.where(links_ref[0, 0, 0, position] == target, jnp.int32(position), slot)
    row = index_ref[0, 0, 0, pl.ds(jnp.maximum(slot, 0), 1), :]
    return jnp.where(slot >= 0, row, -1)


def hot_elements(flat_row, elements, dofs):
    element, _ = split_index(flat_row, dofs)
    return lax.broadcasted_iota(jnp.int32, (elements, flat_row.shape[1]), 0) == element


def hot_dofs(flat_row, dofs):
    _, dof = split_index(flat_row, dofs)
    shape = (dofs, flat_row.shape[1])
    line = lax.broadcasted_iota(jnp.int32, shape, 0).astype(jnp.int16)
    hit = line == jnp.broadcast_to(dof.astype(jnp.int16), shape)
    return jnp.where(hit, jnp.ones(shape, bf16), jnp.zeros(shape, bf16))


def as_column(row):
    elements = row.shape[1]
    line = lax.broadcasted_iota(jnp.int32, (elements, elements), 0)
    column = lax.broadcasted_iota(jnp.int32, (elements, elements), 1)
    spread = jnp.where(line == column, jnp.broadcast_to(row, (elements, elements)), 0.0)
    return jnp.sum(spread, axis=1, keepdims=True)


def wide(column, probes, dofs):
    return jnp.broadcast_to(jnp.concatenate([column] * probes, axis=0), (probes * column.shape[0], dofs))


def take_faces(fields, over_elements, over_dofs):
    elements = over_elements.shape[0]
    picked = dot(
        jnp.concatenate(two_parts(fields), axis=1), jnp.concatenate([over_dofs, over_dofs], axis=0)
    )
    return [
        jnp.sum(jnp.where(over_elements, picked[low : low + elements], 0.0), axis=0, keepdims=True)
        for low in range(0, fields.shape[0], elements)
    ]


def spread_faces(values, over_elements):
    highs = [value.astype(bf16).astype(f32) for value in values]
    lows = [value - high for value, high in zip(values, highs)]
    return jnp.concatenate(
        [jnp.where(over_elements, part, 0.0).astype(bf16) for part in highs + lows], axis=0
    )


def add_faces(spreads, over_dofs):
    parts = dot_transposed(jnp.concatenate(spreads, axis=1), over_dofs)
    rows = parts.shape[0] // 2
    return parts[:rows] + parts[rows:]


def as_row(lines, lanes):
    count = -(-len(lines) // 8) * 8
    spare = jnp.zeros((count - len(lines), lines[0].shape[1]), f32)
    sums = jnp.sum(jnp.concatenate(lines + [spare], axis=0), axis=1, keepdims=True)
    line = lax.broadcasted_iota(jnp.int32, (count, lanes), 0)
    lane = lax.broadcasted_iota(jnp.int32, (count, lanes), 1)
    return jnp.sum(jnp.where(line == lane, sums, 0.0), axis=0, keepdims=True)


def inner_products(first_img, second_img, source, probes, products_ref):
    elements = source.shape[0] // probes
    pairs = (
        (first_img, first_img),
        (first_img, second_img),
        (second_img, second_img),
        (first_img, source),
        (second_img, source),
    )
    lines = []
    for left, right in pairs:
        product = left * right
        for probe in range(probes):
            lines.append(
                jnp.sum(product[probe * elements : (probe + 1) * elements], axis=0, keepdims=True)
            )
    products_ref[...] = as_row(lines, products_ref.shape[-1])


class PieceCopy:
    def __init__(self, held, here, arrived):
        rows = here.shape[-2]
        count = fetch_pieces if rows % (8 * fetch_pieces) == 0 else 1
        size = rows // count
        self.copies = []
        for piece in range(count):
            place = (slice(None),) * (len(here.shape) - 2) + (pl.ds(piece * size, size),)
            whole = count == 1
            source, target = (held, here) if whole else (held.at[place], here.at[place])
            self.copies.append(pltpu.make_async_copy(source, target, arrived.at[piece]))
            self.copies[-1].start()

    def wait(self):
        for copy in self.copies:
            copy.wait()


def live_column(count_ref, elements):
    return lax.broadcasted_iota(jnp.int32, (elements, 1), 0) < count_ref[0, 0, 0]


def begin(refs, partner, count_ref, prepare):
    links_hbm, index_hbm, visc_hbm, rhs_hbm, *matrices_hbm = refs["operands"]
    links_ref, index_ref, visc_ref, rhs_ref, *matrix_refs, arrived = refs["scratch"]
    pairs = (
        (links_hbm, links_ref),
        (index_hbm, index_ref),
        (rhs_hbm, rhs_ref),
        (matrices_hbm[0], matrix_refs[0]),
        (visc_hbm, visc_ref),
        *zip(matrices_hbm[1:], matrix_refs[1:]),
    )
    copies = [
        PieceCopy(held, here, arrived.at[place]) for place, (held, here) in enumerate(pairs)
    ]
    copies[0].wait()
    copies[1].wait()
    slots_ref = refs["slots"]
    me = lax.axis_index("gz")
    for step in range(1, slots_ref.shape[0] + 1):
        slots_ref[step - 1] = slot_of(partner(me, step), links_ref, index_ref)
    prepare()
    copies[4].wait()
    probes, elements, dofs = rhs_ref.shape[3:]
    live = jnp.ones((elements, 1), f32)
    if count_ref is not None:
        live = live_column(count_ref, elements).astype(f32)
    visc = as_column(visc_ref[0, 0])
    up = wide(live * visc, probes, dofs)
    down = wide(live / visc, probes, dofs)
    refs["up"][...] = up
    refs["down"][...] = down
    copies[2].wait()
    source = rhs_ref[...].reshape(probes * elements, dofs)
    if count_ref is not None:
        source = source * wide(live, probes, dofs)
    refs["source"][...] = source
    copies[3].wait()
    smoother = two_parts(matrix_refs[0][...])
    first_pre = times_parts(source, *smoother) * down
    refs["first"][...] = first_pre
    for copy in copies[5:]:
        copy.wait()
    return first_pre, up, down, smoother


def message_places(steps, probes):
    values = steps * probes
    return values, values + probes, values + probes + steps


def message_length(steps, probes, width):
    return -(-(message_places(steps, probes)[2] * (width // lane_count) + 1) // 8) * 8


def write_row(message_ref, place, row):
    pieces = row.shape[1] // lane_count
    for piece in range(pieces):
        line = place * pieces + piece
        message_ref[line : line + 1, :] = row[:, piece * lane_count : (piece + 1) * lane_count]


def read_row(message_ref, place, width):
    pieces = width // lane_count
    lines = range(place * pieces, (place + 1) * pieces)
    return jnp.concatenate([message_ref[line : line + 1, :] for line in lines], axis=1)


def near_first_kernel(*refs):
    operands, refs = refs[:6], refs[6:]
    first_ref, source_ref, up_ref, down_ref, base_ref, slots_ref, hot_ref = refs[:7]
    part_refs, refs = refs[7:11], refs[11:]
    steps, _, width = slots_ref.shape
    leave_refs, scratch = refs[:steps], refs[steps:]
    visc_ref, rhs_ref, _, k_ref = scratch[2:6]
    probes, elements, dofs = rhs_ref.shape[3:]

    def prepare():
        for step in range(steps):
            hot_ref[:, step * width : (step + 1) * width] = hot_dofs(slots_ref[step], dofs)

    first_pre, up, down, smoother = begin(
        {
            "operands": operands,
            "scratch": scratch,
            "slots": slots_ref,
            "up": up_ref,
            "down": down_ref,
            "source": source_ref,
            "first": first_ref,
        },
        lambda me, step: me ^ step,
        None,
        prepare,
    )
    stiffness = two_parts(k_ref[...])
    base = times_parts(first_pre, *stiffness) * up
    base_ref[...] = base
    fields = jnp.concatenate([first_pre, times_parts(base, *smoother) * down], axis=0)
    for part_ref, part in zip(part_refs, smoother + stiffness):
        part_ref[...] = part
    second_at, index_at, visc_at = message_places(steps, probes)
    for step in range(1, steps + 1):
        flat_row = slots_ref[step - 1]
        over_elements = hot_elements(flat_row, elements, dofs)
        over_dofs = hot_ref[:, (step - 1) * width : step * width]
        taken = take_faces(fields, over_elements, over_dofs)
        for probe in range(probes):
            write_row(leave_refs[step - 1], second_at + probe, taken[probes + probe])
            for leave_ref in leave_refs:
                write_row(leave_ref, (step - 1) * probes + probe, taken[probe])
        for leave_ref in leave_refs:
            write_row(leave_ref, index_at + step - 1, flat_row.astype(f32))
    visc_line = visc_at * (width // lane_count)
    for leave_ref in leave_refs:
        leave_ref[visc_line : visc_line + 1, :elements] = visc_ref[0, 0]


def near_second_kernel(
    probes, count_ref, source_ref, up_ref, down_ref, base_ref, slots_ref, hot_ref,
    p_high_ref, p_low_ref, k_high_ref, k_low_ref, mine_ref, *refs
):
    came_refs = refs[:-2]
    second_ref, products_ref = refs[-2:]
    steps, _, width = slots_ref.shape
    members = steps + 1
    rows, dofs = source_ref.shape
    elements = rows // probes
    second_at, index_at, visc_at = message_places(steps, probes)

    def message(step):
        return mine_ref if step == 0 else came_refs[step - 1]

    def inbound_first(member, step):
        sent = message(member ^ step)
        return [
            read_row(sent, (step - 1) * probes + probe, width) for probe in range(probes)
        ]

    own_elements = [hot_elements(slots_ref[step], elements, dofs) for step in range(steps)]

    def placed_here(values):
        return add_faces(
            [spread_faces(values[step], own_elements[step]) for step in range(steps)], hot_ref[...]
        )

    up, down = up_ref[...], down_ref[...]
    live = wide(live_column(count_ref, elements).astype(f32), probes, dofs) > 0.0
    placed = placed_here([inbound_first(0, step) for step in range(1, members)])
    image = jnp.where(live, base_ref[...] - coupling * placed, 0.0)
    images, back = [image], []
    for member in range(1, members):
        rows_of = [
            read_row(message(member), index_at + step, width).astype(jnp.int32)
            for step in range(steps)
        ]
        over_elements = [hot_elements(flat_row, elements, dofs) for flat_row in rows_of]
        over_dofs = [hot_dofs(flat_row, dofs) for flat_row in rows_of]
        spreads = [
            spread_faces(inbound_first(member, step + 1), over_elements[step])
            for step in range(steps)
        ]
        images.append(-coupling * add_faces(spreads, jnp.concatenate(over_dofs, axis=1)))
        back.append((over_elements[member - 1], over_dofs[member - 1]))
    smooth = times_parts(jnp.concatenate(images, axis=0), p_high_ref[...], p_low_ref[...])
    second_pre = smooth[:rows] * down
    second_ref[...] = second_pre
    values = []
    visc_line = visc_at * (width // lane_count)
    for member in range(1, members):
        sent = message(member)
        visc = as_column(sent[visc_line : visc_line + 1, :elements])
        scale = wide(1.0 / visc, probes, dofs)
        change = smooth[member * rows : (member + 1) * rows] * scale
        taken = take_faces(change, *back[member - 1])
        values.append(
            [taken[probe] + read_row(sent, second_at + probe, width) for probe in range(probes)]
        )
    placed = placed_here(values)
    second_img = times_parts(second_pre, k_high_ref[...], k_low_ref[...]) * up - coupling * placed
    second_img = jnp.where(live, second_img, 0.0)
    source = jnp.where(live, source_ref[...], 0.0)
    inner_products(image, second_img, source, probes, products_ref)


def leave_faces(field, probes, slots_ref, leave_ref):
    elements, dofs = field.shape[0] // probes, field.shape[1]
    members = slots_ref.shape[0] + 1
    me = lax.axis_index("gz")
    for shift in range(1, members):
        flat_row = slots_ref[shift - 1]
        taken = take_faces(field, hot_elements(flat_row, elements, dofs), hot_dofs(flat_row, dofs))
        target = lax.rem(me + shift, members)
        for probe in range(probes):
            leave_ref[target, pl.ds(probe, 1), :] = taken[probe]
    leave_ref[me] = jnp.zeros(leave_ref.shape[1:], f32)


def placed_faces(shape, probes, slots_ref, came_ref):
    rows, dofs = shape
    elements = rows // probes
    members = slots_ref.shape[0] + 1
    me = lax.axis_index("gz")
    total = jnp.zeros(shape, f32)
    for shift in range(1, members):
        flat_row = slots_ref[shift - 1]
        came = came_ref[lax.rem(me + shift, members)]
        values = [came[probe : probe + 1, :] for probe in range(probes)]
        spread = spread_faces(values, hot_elements(flat_row, elements, dofs))
        total += add_faces([spread], hot_dofs(flat_row, dofs))
    return total


def far_first_kernel(*refs):
    count_ref, *operands = refs[:6]
    refs = refs[6:]
    first_ref, source_ref, up_ref, down_ref, slots_ref, leave_ref = refs[:6]
    members = slots_ref.shape[0] + 1
    first_pre, *_ = begin(
        {
            "operands": operands,
            "scratch": refs[6:],
            "slots": slots_ref,
            "up": up_ref,
            "down": down_ref,
            "source": source_ref,
            "first": first_ref,
        },
        lambda me, step: lax.rem(me + step, members),
        count_ref,
        lambda: None,
    )
    leave_faces(first_pre, leave_ref.shape[1], slots_ref, leave_ref)


def far_second_kernel(
    slots_ref, up_ref, down_ref, first_ref, k_ref, p_ref, came_ref,
    image_ref, second_ref, leave_ref,
):
    probes = came_ref.shape[1]
    up = up_ref[...]
    placed = placed_faces(first_ref.shape, probes, slots_ref, came_ref)
    image = times_matrix(first_ref[...], k_ref[...]) * up - jnp.where(up > 0.0, coupling * placed, 0.0)
    image_ref[...] = image
    second_pre = times_matrix(image, p_ref[...]) * down_ref[...]
    second_ref[...] = second_pre
    leave_faces(second_pre, probes, slots_ref, leave_ref)


def far_third_kernel(
    slots_ref, up_ref, source_ref, image_ref, second_ref, k_ref, came_ref, products_ref
):
    probes = came_ref.shape[1]
    up = up_ref[...]
    placed = placed_faces(source_ref.shape, probes, slots_ref, came_ref)
    second_img = times_matrix(second_ref[...], k_ref[...]) * up - jnp.where(up > 0.0, coupling * placed, 0.0)
    inner_products(image_ref[...], second_img, source_ref[...], probes, products_ref)


def last_kernel(probes, count_ref, first_ref, second_ref, parts_ref, out_ref):
    rows, _ = first_ref.shape
    elements = rows // probes
    total = jnp.sum(parts_ref[...], axis=0)
    live = live_column(count_ref, elements)
    for probe in range(probes):
        self_one, cross_mid, self_two, load_one, load_two = (
            total[:, place * probes + probe : place * probes + probe + 1] for place in range(5)
        )
        determinant = self_one * self_two - cross_mid * cross_mid
        weight_one = (self_two * load_one - cross_mid * load_two) / determinant
        weight_two = (self_one * load_two - cross_mid * load_one) / determinant
        block = pl.ds(probe * elements, elements)
        value = weight_one * first_ref[block, :] + weight_two * second_ref[block, :]
        out_ref[block, :] = jnp.where(live, value, 0.0)


def call(kernel, in_specs, out_shapes, flops, *args, scratch=()):
    return pl.pallas_call(
        kernel,
        out_shape=out_shapes,
        in_specs=in_specs,
        out_specs=jax.tree.map(lambda _: vmem_spec, out_shapes),
        scratch_shapes=scratch,
        compiler_params=pltpu.CompilerParams(vmem_limit_bytes=vmem_grant),
        cost_estimate=pl.CostEstimate(flops=flops, bytes_accessed=1 << 20, transcendentals=0),
    )(*args)


def begin_call(kernel, out_shapes, flops, scalars, *fetched):
    links, *others = fetched
    scratch = [pltpu.SMEM(links.shape, links.dtype)]
    scratch += [pltpu.VMEM(value.shape, value.dtype) for value in others]
    return call(
        kernel,
        [smem_spec] * len(scalars) + [hbm_spec] * len(fetched),
        out_shapes,
        flops,
        *scalars,
        *(pltpu.with_memory_space_constraint(value, pltpu.HBM) for value in fetched),
        scratch=scratch + [pltpu.SemaphoreType.DMA((len(fetched), fetch_pieces))],
    )


def near_steps(members, shapes, arguments):
    rhs, viscosity, counts, neighbours, face_index, k_matrix, p_matrix = arguments
    field, slots_shape, products_shape = shapes
    rows, dofs = field.shape
    steps, _, width = slots_shape.shape
    probes = rhs.shape[3]
    flops = 8 * rows * dofs * steps * width
    hot = jax.ShapeDtypeStruct((dofs, steps * width), bf16)
    message = jax.ShapeDtypeStruct((message_length(steps, probes, width), lane_count), f32)
    part = jax.ShapeDtypeStruct(p_matrix.shape, bf16)
    first_pre, source, up, down, base, slots, hot_own, *rest = begin_call(
        near_first_kernel,
        [field] * 5 + [slots_shape, hot] + [part] * 4 + [message] * steps,
        2 * flops,
        (),
        neighbours,
        face_index,
        viscosity,
        rhs,
        p_matrix,
        k_matrix,
    )
    parts, leaving = rest[:4], rest[4:]
    came = [
        lax.ppermute(
            leaving[step - 1], "gz", [(source, source ^ step) for source in range(members)]
        )
        for step in range(1, members)
    ]
    second_pre, products = call(
        functools.partial(near_second_kernel, probes),
        [smem_spec] + [vmem_spec] * (11 + steps),
        [field, products_shape],
        6 * flops,
        counts,
        source,
        up,
        down,
        base,
        slots,
        hot_own,
        *parts,
        leaving[0],
        *came,
    )
    return first_pre, second_pre, products


def far_steps(members, shapes, arguments):
    rhs, viscosity, counts, neighbours, face_index, k_matrix, p_matrix = arguments
    field, slots_shape, products_shape = shapes
    rows, dofs = field.shape
    shifts, _, width = slots_shape.shape
    flops = 8 * rows * dofs * shifts * width
    faces = jax.ShapeDtypeStruct((members, rhs.shape[3], width), f32)

    def exchange(value):
        return lax.all_to_all(value, "gz", split_axis=0, concat_axis=0)

    first_pre, source, up, down, slots, leaving = begin_call(
        far_first_kernel,
        [field] * 4 + [slots_shape, faces],
        flops,
        (counts,),
        neighbours,
        face_index,
        viscosity,
        rhs,
        p_matrix,
    )
    first_img, second_pre, leaving = call(
        far_second_kernel,
        [vmem_spec] * 7,
        [field, field, faces],
        2 * flops,
        slots,
        up,
        down,
        first_pre,
        k_matrix,
        p_matrix,
        exchange(leaving),
    )
    products = call(
        far_third_kernel,
        [vmem_spec] * 7,
        products_shape,
        flops,
        slots,
        up,
        source,
        first_img,
        second_pre,
        k_matrix,
        exchange(leaving),
    )
    return first_pre, second_pre, products


def all_rows(row, mesh):
    if mesh.shape["pair"] == 2:
        row = row + lax.ppermute(row, "pair", [(0, 1), (1, 0)])
    count = mesh.size // mesh.shape["pair"]
    copies = jnp.broadcast_to(row[None], (count,) + row.shape)
    return lax.all_to_all(copies, ("gx", "gy", "gz"), split_axis=0, concat_axis=0)


def per_device(mesh, *arguments):
    rhs, face_index = arguments[0], arguments[4]
    probes, elements, dofs = rhs.shape[3:]
    members = mesh.shape["gz"]
    lanes = -(-5 * probes // 128) * 128
    shapes = (
        jax.ShapeDtypeStruct((probes * elements, dofs), f32),
        jax.ShapeDtypeStruct((members - 1, 1, face_index.shape[-1]), jnp.int32),
        jax.ShapeDtypeStruct((1, lanes), f32),
    )
    near = 1 < members <= short_group and elements <= face_index.shape[-1]
    near = near and elements * dofs < 1 << 24
    steps = near_steps if near else far_steps
    first_pre, second_pre, products = steps(members, shapes, arguments)
    result = call(
        functools.partial(last_kernel, probes),
        [smem_spec] + [vmem_spec] * 3,
        shapes[0],
        probes * elements * dofs,
        arguments[2],
        first_pre,
        second_pre,
        all_rows(products, mesh),
    )
    return result.reshape(rhs.shape)


def solution(mesh):
    outer, inner, length = (mesh.shape[axis] for axis in ("gx", "gy", "gz"))
    pair = 2 if outer % 2 == 0 else 1
    devices = mesh.devices.reshape(outer // pair, pair, inner, length)
    split = Mesh(devices, ("gx", "pair", "gy", "gz"))
    rows = ("gx", "pair")
    return jax.shard_map(
        functools.partial(per_device, split),
        mesh=split,
        in_specs=(
            P(rows, "gy", "gz", None, None, None),
            P(rows, "gy", "gz", None),
            P(rows, "gy", "gz"),
            P(rows, "gy", "gz", None),
            P(rows, "gy", "gz", None, None),
            P(),
            P(),
        ),
        out_specs=P(rows, "gy", "gz", None, None, None),
        check_vma=False,
    )
```

```python
import functools

import jax
import jax.numpy as jnp
from jax import lax
from jax.experimental import pallas as pl
from jax.experimental.pallas import tpu as pltpu
from jax.sharding import PartitionSpec as P

coupling = 0.5
vmem_grant = 48 * 1024 * 1024
short_group = 4
lane_count = 128
f32 = jnp.float32
bf16 = jnp.bfloat16
vmem_spec = pl.BlockSpec(memory_space=pltpu.VMEM)
smem_spec = pl.BlockSpec(memory_space=pltpu.SMEM)
hbm_spec = pl.BlockSpec(memory_space=pltpu.HBM)


def two_parts(value):
    high = value.astype(bf16)
    return high, (value - high.astype(f32)).astype(bf16)


def dot(left, right):
    return jnp.dot(left, right, preferred_element_type=f32)


def dot_transposed(left, right):
    return lax.dot_general(left, right, (((1,), (1,)), ((), ())), preferred_element_type=f32)


def times_matrix(rows, matrix):
    return times_parts(rows, *two_parts(matrix))


def times_parts(rows, mat_high, mat_low):
    row_high, row_low = two_parts(rows)
    return dot(
        jnp.concatenate([row_high, row_low, row_high], axis=1),
        jnp.concatenate([mat_high, mat_high, mat_low], axis=0),
    )


def times_parts_once(rows, mat_high, mat_low):
    row_high = rows.astype(bf16)
    return dot(
        jnp.concatenate([row_high, row_high], axis=1),
        jnp.concatenate([mat_high, mat_low], axis=0),
    )


def split_index(index, dofs):
    if dofs & (dofs - 1) == 0:
        return lax.shift_right_arithmetic(index, dofs.bit_length() - 1), index & (dofs - 1)
    element = jnp.floor_divide(index, dofs)
    return element, index - element * dofs


def slot_of(target, links_ref, index_ref):
    slot = jnp.int32(-1)
    for position in range(links_ref.shape[-1]):
        slot = jnp.where(links_ref[0, 0, 0, position] == target, jnp.int32(position), slot)
    row = index_ref[0, 0, 0, pl.ds(jnp.maximum(slot, 0), 1), :]
    return jnp.where(slot >= 0, row, -1)


def hot_elements(flat_row, elements, dofs):
    element, _ = split_index(flat_row, dofs)
    return lax.broadcasted_iota(jnp.int32, (elements, flat_row.shape[1]), 0) == element


def hot_dofs(flat_row, dofs):
    _, dof = split_index(flat_row, dofs)
    shape = (dofs, flat_row.shape[1])
    line = lax.broadcasted_iota(jnp.int32, shape, 0).astype(jnp.int16)
    hit = line == jnp.broadcast_to(dof.astype(jnp.int16), shape)
    return jnp.where(hit, jnp.ones(shape, bf16), jnp.zeros(shape, bf16))


def as_column(row):
    elements = row.shape[1]
    line = lax.broadcasted_iota(jnp.int32, (elements, elements), 0)
    column = lax.broadcasted_iota(jnp.int32, (elements, elements), 1)
    spread = jnp.where(line == column, jnp.broadcast_to(row, (elements, elements)), 0.0)
    return jnp.sum(spread, axis=1, keepdims=True)


def wide(column, probes, dofs):
    return jnp.broadcast_to(jnp.concatenate([column] * probes, axis=0), (probes * column.shape[0], dofs))


def take_faces(parts, over_elements, over_dofs):
    elements = over_elements.shape[0]
    picked = dot(
        jnp.concatenate(parts, axis=1), jnp.concatenate([over_dofs] * len(parts), axis=0)
    )
    return [
        jnp.sum(jnp.where(over_elements, picked[low : low + elements], 0.0), axis=0, keepdims=True)
        for low in range(0, picked.shape[0], elements)
    ]


def spread_faces(values, over_elements):
    return jnp.concatenate(
        [jnp.where(over_elements, value, 0.0).astype(bf16) for value in values], axis=0
    )


def high_low(values):
    highs = [value.astype(bf16).astype(f32) for value in values]
    return highs + [value - high for value, high in zip(values, highs)]


def add_faces(spreads, over_dofs):
    return dot_transposed(jnp.concatenate(spreads, axis=1), over_dofs)


def folded(parts):
    rows = parts.shape[0] // 2
    return parts[:rows] + parts[rows:]


def as_row(lines, lanes):
    count = -(-len(lines) // 8) * 8
    spare = jnp.zeros((count - len(lines), lines[0].shape[1]), f32)
    sums = jnp.sum(jnp.concatenate(lines + [spare], axis=0), axis=1, keepdims=True)
    line = lax.broadcasted_iota(jnp.int32, (count, lanes), 0)
    lane = lax.broadcasted_iota(jnp.int32, (count, lanes), 1)
    return jnp.sum(jnp.where(line == lane, sums, 0.0), axis=0, keepdims=True)


def inner_products(first_img, second_img, source, probes, products_ref):
    elements = source.shape[0] // probes
    pairs = (
        (first_img, first_img),
        (first_img, second_img),
        (second_img, second_img),
        (first_img, source),
        (second_img, source),
    )
    lines = []
    for left, right in pairs:
        product = left * right
        for probe in range(probes):
            lines.append(
                jnp.sum(product[probe * elements : (probe + 1) * elements], axis=0, keepdims=True)
            )
    products_ref[...] = jnp.broadcast_to(as_row(lines, products_ref.shape[-1]), products_ref.shape)


def live_column(count_ref, elements):
    return lax.broadcasted_iota(jnp.int32, (elements, 1), 0) < count_ref[0, 0, 0]


def begin(refs, partner, count_ref, prepare):
    links_hbm, index_hbm, visc_hbm, rhs_hbm, *matrices_hbm = refs["operands"]
    links_ref, index_ref, visc_ref, rhs_ref, *matrix_refs, arrived = refs["scratch"]
    pairs = (
        (links_hbm, links_ref),
        (index_hbm, index_ref),
        (rhs_hbm, rhs_ref),
        (matrices_hbm[0], matrix_refs[0]),
        (visc_hbm, visc_ref),
        *zip(matrices_hbm[1:], matrix_refs[1:]),
    )
    copies = [
        pltpu.make_async_copy(held, here, arrived.at[place])
        for place, (held, here) in enumerate(pairs)
    ]
    for copy in copies:
        copy.start()
    copies[0].wait()
    copies[1].wait()
    slots_ref = refs["slots"]
    me = lax.axis_index("gz")
    for step in range(1, slots_ref.shape[0] + 1):
        slots_ref[step - 1] = slot_of(partner(me, step), links_ref, index_ref)
    prepare()
    copies[4].wait()
    probes, elements, dofs = rhs_ref.shape[3:]
    live = jnp.ones((elements, 1), f32)
    if count_ref is not None:
        live = live_column(count_ref, elements).astype(f32)
    visc = as_column(visc_ref[0, 0])
    up = wide(live * visc, probes, dofs)
    down = wide(live / visc, probes, dofs)
    refs["up"][...] = up
    refs["down"][...] = down
    copies[2].wait()
    source = rhs_ref[...].reshape(probes * elements, dofs)
    if count_ref is not None:
        source = source * wide(live, probes, dofs)
    refs["source"][...] = source
    copies[3].wait()
    smoother = two_parts(matrix_refs[0][...])
    first_pre = times_parts(source, *smoother) * down
    refs["first"][...] = first_pre
    for copy in copies[5:]:
        copy.wait()
    return first_pre, up, down, smoother


def message_places(steps, probes):
    values = steps * probes
    return values, values + probes, values + probes + steps


def message_length(steps, probes, width):
    return -(-(message_places(steps, probes)[2] * (width // lane_count) + 1) // 8) * 8


def write_row(message_ref, place, row):
    pieces = row.shape[1] // lane_count
    for piece in range(pieces):
        line = place * pieces + piece
        message_ref[line : line + 1, :] = row[:, piece * lane_count : (piece + 1) * lane_count]


def read_row(message_ref, place, width):
    pieces = width // lane_count
    lines = range(place * pieces, (place + 1) * pieces)
    return jnp.concatenate([message_ref[line : line + 1, :] for line in lines], axis=1)


def near_first_kernel(*refs):
    operands, refs = refs[:6], refs[6:]
    first_ref, source_ref, up_ref, down_ref, base_ref, slots_ref, hot_ref = refs[:7]
    part_refs, refs = refs[7:11], refs[11:]
    steps, _, width = slots_ref.shape
    leave_refs, scratch = refs[:steps], refs[steps:]
    visc_ref, rhs_ref, _, k_ref = scratch[2:6]
    probes, elements, dofs = rhs_ref.shape[3:]

    def prepare():
        for step in range(steps):
            hot_ref[:, step * width : (step + 1) * width] = hot_dofs(slots_ref[step], dofs)

    first_pre, up, down, smoother = begin(
        {
            "operands": operands,
            "scratch": scratch,
            "slots": slots_ref,
            "up": up_ref,
            "down": down_ref,
            "source": source_ref,
            "first": first_ref,
        },
        lambda me, step: me ^ step,
        None,
        prepare,
    )
    stiffness = two_parts(k_ref[...])
    base = times_parts(first_pre, *stiffness) * up
    base_ref[...] = base
    first_parts = two_parts(first_pre)
    second_parts = [(times_parts_once(base, *smoother) * down).astype(bf16)]
    for part_ref, part in zip(part_refs, smoother + stiffness):
        part_ref[...] = part
    second_at, index_at, visc_at = message_places(steps, probes)
    for step in range(1, steps + 1):
        flat_row = slots_ref[step - 1]
        over_elements = hot_elements(flat_row, elements, dofs)
        over_dofs = hot_ref[:, (step - 1) * width : step * width]
        first_rows = take_faces(first_parts, over_elements, over_dofs)
        second_rows = take_faces(second_parts, over_elements, over_dofs)
        for probe in range(probes):
            write_row(leave_refs[step - 1], second_at + probe, second_rows[probe])
            for leave_ref in leave_refs:
                write_row(leave_ref, (step - 1) * probes + probe, first_rows[probe])
        for leave_ref in leave_refs:
            write_row(leave_ref, index_at + step - 1, flat_row.astype(f32))
    visc_line = visc_at * (width // lane_count)
    for leave_ref in leave_refs:
        leave_ref[visc_line : visc_line + 1, :elements] = visc_ref[0, 0]


def near_second_kernel(
    probes, count_ref, source_ref, up_ref, down_ref, base_ref, slots_ref, hot_ref,
    p_high_ref, p_low_ref, k_high_ref, k_low_ref, mine_ref, *refs
):
    came_refs = refs[:-2]
    second_ref, products_ref = refs[-2:]
    steps, _, width = slots_ref.shape
    members = steps + 1
    rows, dofs = source_ref.shape
    elements = rows // probes
    second_at, index_at, visc_at = message_places(steps, probes)

    def message(step):
        return mine_ref if step == 0 else came_refs[step - 1]

    def inbound_first(member, step):
        sent = message(member ^ step)
        return [
            read_row(sent, (step - 1) * probes + probe, width) for probe in range(probes)
        ]

    own_elements = [hot_elements(slots_ref[step], elements, dofs) for step in range(steps)]

    def placed_here(values):
        spreads = [spread_faces(values[step], own_elements[step]) for step in range(steps)]
        return add_faces(spreads, hot_ref[...])

    up, down = up_ref[...], down_ref[...]
    live = wide(live_column(count_ref, elements).astype(f32), probes, dofs) > 0.0
    placed = folded(placed_here([high_low(inbound_first(0, step)) for step in range(1, members)]))
    image = jnp.where(live, base_ref[...] - coupling * placed, 0.0)
    changes, back = [], []
    for member in range(1, members):
        rows_of = [
            read_row(message(member), index_at + step, width).astype(jnp.int32)
            for step in range(steps)
        ]
        over_elements = [hot_elements(flat_row, elements, dofs) for flat_row in rows_of]
        over_dofs = [hot_dofs(flat_row, dofs) for flat_row in rows_of]
        spreads = [
            spread_faces(inbound_first(member, step + 1), over_elements[step])
            for step in range(steps)
        ]
        changes.append(-coupling * add_faces(spreads, jnp.concatenate(over_dofs, axis=1)))
        back.append((over_elements[member - 1], over_dofs[member - 1]))
    second_pre = times_parts(image, p_high_ref[...], p_low_ref[...]) * down
    changes = times_parts_once(jnp.concatenate(changes, axis=0), p_high_ref[...], p_low_ref[...])
    second_ref[...] = second_pre
    values = []
    visc_line = visc_at * (width // lane_count)
    for member in range(1, members):
        sent = message(member)
        visc = as_column(sent[visc_line : visc_line + 1, :elements])
        scale = wide(1.0 / visc, probes, dofs)
        change = changes[(member - 1) * rows : member * rows] * scale
        taken = take_faces([change.astype(bf16)], *back[member - 1])
        values.append(
            [taken[probe] + read_row(sent, second_at + probe, width) for probe in range(probes)]
        )
    placed = placed_here(values)
    second_img = times_parts_once(second_pre, k_high_ref[...], k_low_ref[...])
    second_img = second_img * up - coupling * placed
    second_img = jnp.where(live, second_img, 0.0)
    source = jnp.where(live, source_ref[...], 0.0)
    inner_products(image, second_img, source, probes, products_ref)


def leave_faces(field, probes, slots_ref, leave_ref):
    elements, dofs = field.shape[0] // probes, field.shape[1]
    members = slots_ref.shape[0] + 1
    me = lax.axis_index("gz")
    for shift in range(1, members):
        flat_row = slots_ref[shift - 1]
        over_elements = hot_elements(flat_row, elements, dofs)
        taken = take_faces(two_parts(field), over_elements, hot_dofs(flat_row, dofs))
        target = lax.rem(me + shift, members)
        for probe in range(probes):
            leave_ref[target, pl.ds(probe, 1), :] = taken[probe]
    leave_ref[me] = jnp.zeros(leave_ref.shape[1:], f32)


def placed_faces(shape, probes, slots_ref, came_ref):
    rows, dofs = shape
    elements = rows // probes
    members = slots_ref.shape[0] + 1
    me = lax.axis_index("gz")
    total = jnp.zeros(shape, f32)
    for shift in range(1, members):
        flat_row = slots_ref[shift - 1]
        came = came_ref[lax.rem(me + shift, members)]
        values = [came[probe : probe + 1, :] for probe in range(probes)]
        spread = spread_faces(high_low(values), hot_elements(flat_row, elements, dofs))
        total += folded(add_faces([spread], hot_dofs(flat_row, dofs)))
    return total


def far_first_kernel(*refs):
    count_ref, *operands = refs[:6]
    refs = refs[6:]
    first_ref, source_ref, up_ref, down_ref, slots_ref, leave_ref = refs[:6]
    members = slots_ref.shape[0] + 1
    first_pre, *_ = begin(
        {
            "operands": operands,
            "scratch": refs[6:],
            "slots": slots_ref,
            "up": up_ref,
            "down": down_ref,
            "source": source_ref,
            "first": first_ref,
        },
        lambda me, step: lax.rem(me + step, members),
        count_ref,
        lambda: None,
    )
    leave_faces(first_pre, leave_ref.shape[1], slots_ref, leave_ref)


def far_second_kernel(
    slots_ref, up_ref, down_ref, first_ref, k_ref, p_ref, came_ref,
    image_ref, second_ref, leave_ref,
):
    probes = came_ref.shape[1]
    up = up_ref[...]
    placed = placed_faces(first_ref.shape, probes, slots_ref, came_ref)
    image = times_matrix(first_ref[...], k_ref[...]) * up - jnp.where(up > 0.0, coupling * placed, 0.0)
    image_ref[...] = image
    second_pre = times_matrix(image, p_ref[...]) * down_ref[...]
    second_ref[...] = second_pre
    leave_faces(second_pre, probes, slots_ref, leave_ref)


def far_third_kernel(
    slots_ref, up_ref, source_ref, image_ref, second_ref, k_ref, came_ref, products_ref
):
    probes = came_ref.shape[1]
    up = up_ref[...]
    placed = placed_faces(source_ref.shape, probes, slots_ref, came_ref)
    second_img = times_matrix(second_ref[...], k_ref[...]) * up - jnp.where(up > 0.0, coupling * placed, 0.0)
    inner_products(image_ref[...], second_img, source_ref[...], probes, products_ref)


def last_kernel(probes, count_ref, first_ref, second_ref, parts_ref, out_ref):
    rows, _ = first_ref.shape
    elements = rows // probes
    total = jnp.sum(parts_ref[...], axis=0)
    live = live_column(count_ref, elements)
    for probe in range(probes):
        self_one, cross_mid, self_two, load_one, load_two = (
            total[:, place * probes + probe : place * probes + probe + 1] for place in range(5)
        )
        determinant = self_one * self_two - cross_mid * cross_mid
        weight_one = (self_two * load_one - cross_mid * load_two) / determinant
        weight_two = (self_one * load_two - cross_mid * load_one) / determinant
        block = pl.ds(probe * elements, elements)
        value = weight_one * first_ref[block, :] + weight_two * second_ref[block, :]
        out_ref[block, :] = jnp.where(live, value, 0.0)


def call(kernel, in_specs, out_shapes, flops, *args, scratch=()):
    return pl.pallas_call(
        kernel,
        out_shape=out_shapes,
        in_specs=in_specs,
        out_specs=jax.tree.map(lambda _: vmem_spec, out_shapes),
        scratch_shapes=scratch,
        compiler_params=pltpu.CompilerParams(vmem_limit_bytes=vmem_grant),
        cost_estimate=pl.CostEstimate(flops=flops, bytes_accessed=1 << 20, transcendentals=0),
    )(*args)


def begin_call(kernel, out_shapes, flops, scalars, *fetched):
    links, *others = fetched
    scratch = [pltpu.SMEM(links.shape, links.dtype)]
    scratch += [pltpu.VMEM(value.shape, value.dtype) for value in others]
    return call(
        kernel,
        [smem_spec] * len(scalars) + [hbm_spec] * len(fetched),
        out_shapes,
        flops,
        *scalars,
        *(pltpu.with_memory_space_constraint(value, pltpu.HBM) for value in fetched),
        scratch=scratch + [pltpu.SemaphoreType.DMA((len(fetched),))],
    )


def near_steps(members, shapes, arguments):
    rhs, viscosity, counts, neighbours, face_index, k_matrix, p_matrix = arguments
    field, slots_shape, products_shape = shapes
    rows, dofs = field.shape
    steps, _, width = slots_shape.shape
    probes = rhs.shape[3]
    flops = 8 * rows * dofs * steps * width
    hot = jax.ShapeDtypeStruct((dofs, steps * width), bf16)
    message = jax.ShapeDtypeStruct((message_length(steps, probes, width), lane_count), f32)
    part = jax.ShapeDtypeStruct(p_matrix.shape, bf16)
    first_pre, source, up, down, base, slots, hot_own, *rest = begin_call(
        near_first_kernel,
        [field] * 5 + [slots_shape, hot] + [part] * 4 + [message] * steps,
        2 * flops,
        (),
        neighbours,
        face_index,
        viscosity,
        rhs,
        p_matrix,
        k_matrix,
    )
    parts, leaving = rest[:4], rest[4:]
    came = [
        lax.ppermute(
            leaving[step - 1], "gz", [(source, source ^ step) for source in range(members)]
        )
        for step in range(1, members)
    ]
    second_pre, products = call(
        functools.partial(near_second_kernel, probes),
        [smem_spec] + [vmem_spec] * (11 + steps),
        [field, products_shape],
        6 * flops,
        counts,
        source,
        up,
        down,
        base,
        slots,
        hot_own,
        *parts,
        leaving[0],
        *came,
    )
    return first_pre, second_pre, products


def far_steps(members, shapes, arguments):
    rhs, viscosity, counts, neighbours, face_index, k_matrix, p_matrix = arguments
    field, slots_shape, products_shape = shapes
    rows, dofs = field.shape
    shifts, _, width = slots_shape.shape
    flops = 8 * rows * dofs * shifts * width
    faces = jax.ShapeDtypeStruct((members, rhs.shape[3], width), f32)

    def exchange(value):
        return lax.all_to_all(value, "gz", split_axis=0, concat_axis=0)

    first_pre, source, up, down, slots, leaving = begin_call(
        far_first_kernel,
        [field] * 4 + [slots_shape, faces],
        flops,
        (counts,),
        neighbours,
        face_index,
        viscosity,
        rhs,
        p_matrix,
    )
    first_img, second_pre, leaving = call(
        far_second_kernel,
        [vmem_spec] * 7,
        [field, field, faces],
        2 * flops,
        slots,
        up,
        down,
        first_pre,
        k_matrix,
        p_matrix,
        exchange(leaving),
    )
    products = call(
        far_third_kernel,
        [vmem_spec] * 7,
        products_shape,
        flops,
        slots,
        up,
        source,
        first_img,
        second_pre,
        k_matrix,
        exchange(leaving),
    )
    return first_pre, second_pre, products


def per_device(mesh, *arguments):
    rhs, face_index = arguments[0], arguments[4]
    probes, elements, dofs = rhs.shape[3:]
    members = mesh.shape["gz"]
    lanes = -(-5 * probes // 128) * 128
    shapes = (
        jax.ShapeDtypeStruct((probes * elements, dofs), f32),
        jax.ShapeDtypeStruct((members - 1, 1, face_index.shape[-1]), jnp.int32),
        jax.ShapeDtypeStruct((mesh.size, 1, lanes), f32),
    )
    near = 1 < members <= short_group and elements <= face_index.shape[-1]
    near = near and elements * dofs < 1 << 24
    steps = near_steps if near else far_steps
    first_pre, second_pre, products = steps(members, shapes, arguments)
    result = call(
        functools.partial(last_kernel, probes),
        [smem_spec] + [vmem_spec] * 3,
        shapes[0],
        probes * elements * dofs,
        arguments[2],
        first_pre,
        second_pre,
        lax.all_to_all(products, ("gx", "gy", "gz"), split_axis=0, concat_axis=0),
    )
    return result.reshape(rhs.shape)


def solution(mesh):
    return jax.shard_map(
        functools.partial(per_device, mesh),
        mesh=mesh,
        in_specs=(
            P("gx", "gy", "gz", None, None, None),
            P("gx", "gy", "gz", None),
            P("gx", "gy", "gz"),
            P("gx", "gy", "gz", None),
            P("gx", "gy", "gz", None, None),
            P(),
            P(),
        ),
        out_specs=P("gx", "gy", "gz", None, None, None),
        check_vma=False,
    )
```

```python
import functools

import jax
import jax.numpy as jnp
from jax import lax
from jax.experimental import pallas as pl
from jax.experimental.pallas import tpu as pltpu
from jax.sharding import PartitionSpec as P

coupling = 0.5
vmem_grant = 48 * 1024 * 1024
short_group = 4
lane_count = 128
f32 = jnp.float32
bf16 = jnp.bfloat16
vmem_spec = pl.BlockSpec(memory_space=pltpu.VMEM)
smem_spec = pl.BlockSpec(memory_space=pltpu.SMEM)
hbm_spec = pl.BlockSpec(memory_space=pltpu.HBM)


def two_parts(value):
    high = value.astype(bf16)
    return high, (value - high.astype(f32)).astype(bf16)


def dot(left, right):
    return jnp.dot(left, right, preferred_element_type=f32)


def times_matrix(rows, matrix):
    return times_parts(rows, *two_parts(matrix))


def times_parts(rows, mat_high, mat_low):
    row_high, row_low = two_parts(rows)
    return dot(
        jnp.concatenate([row_high, row_low, row_high], axis=1),
        jnp.concatenate([mat_high, mat_high, mat_low], axis=0),
    )


def times_parts_once(rows, mat_high, mat_low):
    row_high = rows.astype(bf16)
    return dot(
        jnp.concatenate([row_high, row_high], axis=1),
        jnp.concatenate([mat_high, mat_low], axis=0),
    )


def split_index(index, dofs):
    if dofs & (dofs - 1) == 0:
        return lax.shift_right_arithmetic(index, dofs.bit_length() - 1), index & (dofs - 1)
    element = jnp.floor_divide(index, dofs)
    return element, index - element * dofs


def slot_of(target, links_ref, index_ref):
    slot = jnp.int32(-1)
    for position in range(links_ref.shape[-1]):
        slot = jnp.where(links_ref[0, 0, 0, position] == target, jnp.int32(position), slot)
    row = index_ref[0, 0, 0, pl.ds(jnp.maximum(slot, 0), 1), :]
    return jnp.where(slot >= 0, row, -1)


def hot_elements(flat_row, elements, dofs):
    element, _ = split_index(flat_row, dofs)
    return lax.broadcasted_iota(jnp.int32, (elements, flat_row.shape[1]), 0) == element


def hot_dofs(flat_row, dofs):
    _, dof = split_index(flat_row, dofs)
    shape = (dofs, flat_row.shape[1])
    line = lax.broadcasted_iota(jnp.int32, shape, 0).astype(jnp.int16)
    hit = line == jnp.broadcast_to(dof.astype(jnp.int16), shape)
    return jnp.where(hit, jnp.ones(shape, bf16), jnp.zeros(shape, bf16))


def hot_rows(flat_rows, dofs):
    shape = (flat_rows[0].shape[1], dofs)
    spare = [jnp.zeros((8 - len(flat_rows) % 8, shape[0]), jnp.int32)]
    _, dof = split_index(jnp.concatenate(flat_rows + spare, axis=0), dofs)
    columns = jnp.transpose(dof.astype(f32)).astype(jnp.int32)
    lane = lax.broadcasted_iota(jnp.int32, shape, 1).astype(jnp.int16)
    hits = []
    for slot in range(len(flat_rows)):
        column = jnp.broadcast_to(columns[:, slot : slot + 1], shape).astype(jnp.int16)
        hits.append(jnp.where(lane == column, jnp.ones(shape, bf16), jnp.zeros(shape, bf16)))
    return jnp.concatenate(hits, axis=0)


def as_column(row):
    elements = row.shape[1]
    line = lax.broadcasted_iota(jnp.int32, (elements, elements), 0)
    column = lax.broadcasted_iota(jnp.int32, (elements, elements), 1)
    spread = jnp.where(line == column, jnp.broadcast_to(row, (elements, elements)), 0.0)
    return jnp.sum(spread, axis=1, keepdims=True)


def wide(column, probes, dofs):
    return jnp.broadcast_to(jnp.concatenate([column] * probes, axis=0), (probes * column.shape[0], dofs))


def take_faces(parts, over_elements, over_dofs):
    elements = over_elements.shape[0]
    picked = dot(
        jnp.concatenate(parts, axis=1), jnp.concatenate([over_dofs] * len(parts), axis=0)
    )
    return [
        jnp.sum(jnp.where(over_elements, picked[low : low + elements], 0.0), axis=0, keepdims=True)
        for low in range(0, picked.shape[0], elements)
    ]


def spread_faces(values, over_elements):
    return jnp.concatenate(
        [jnp.where(over_elements, value, 0.0).astype(bf16) for value in values], axis=0
    )


def high_low(values):
    highs = [value.astype(bf16).astype(f32) for value in values]
    return highs + [value - high for value, high in zip(values, highs)]


def add_faces(spreads, over_dofs):
    return dot(jnp.concatenate(spreads, axis=1), over_dofs)


def folded(parts):
    rows = parts.shape[0] // 2
    return parts[:rows] + parts[rows:]


def as_row(lines, lanes):
    count = -(-len(lines) // 8) * 8
    spare = jnp.zeros((count - len(lines), lines[0].shape[1]), f32)
    sums = jnp.sum(jnp.concatenate(lines + [spare], axis=0), axis=1, keepdims=True)
    line = lax.broadcasted_iota(jnp.int32, (count, lanes), 0)
    lane = lax.broadcasted_iota(jnp.int32, (count, lanes), 1)
    return jnp.sum(jnp.where(line == lane, sums, 0.0), axis=0, keepdims=True)


def inner_products(first_img, second_img, source, probes, products_ref):
    elements = source.shape[0] // probes
    pairs = (
        (first_img, first_img),
        (first_img, second_img),
        (second_img, second_img),
        (first_img, source),
        (second_img, source),
    )
    lines = []
    for left, right in pairs:
        product = left * right
        for probe in range(probes):
            lines.append(
                jnp.sum(product[probe * elements : (probe + 1) * elements], axis=0, keepdims=True)
            )
    products_ref[...] = jnp.broadcast_to(as_row(lines, products_ref.shape[-1]), products_ref.shape)


def live_column(count_ref, elements):
    return lax.broadcasted_iota(jnp.int32, (elements, 1), 0) < count_ref[0, 0, 0]


def begin(refs, partner, count_ref):
    links_hbm, index_hbm, visc_hbm, rhs_hbm, *matrices_hbm = refs["operands"]
    links_ref, index_ref, visc_ref, rhs_ref, *matrix_refs, arrived = refs["scratch"]
    pairs = (
        (links_hbm, links_ref),
        (index_hbm, index_ref),
        (rhs_hbm, rhs_ref),
        (matrices_hbm[0], matrix_refs[0]),
        (visc_hbm, visc_ref),
        *zip(matrices_hbm[1:], matrix_refs[1:]),
    )
    copies = [
        pltpu.make_async_copy(held, here, arrived.at[place])
        for place, (held, here) in enumerate(pairs)
    ]
    for copy in copies:
        copy.start()
    copies[0].wait()
    copies[1].wait()
    slots_ref = refs["slots"]
    me = lax.axis_index("gz")
    for step in range(1, slots_ref.shape[0] + 1):
        slots_ref[step - 1] = slot_of(partner(me, step), links_ref, index_ref)
    copies[4].wait()
    probes, elements, dofs = rhs_ref.shape[3:]
    live = jnp.ones((elements, 1), f32)
    if count_ref is not None:
        live = live_column(count_ref, elements).astype(f32)
    visc = as_column(visc_ref[0, 0])
    up = wide(live * visc, probes, dofs)
    down = wide(live / visc, probes, dofs)
    refs["up"][...] = up
    refs["down"][...] = down
    copies[2].wait()
    source = rhs_ref[...].reshape(probes * elements, dofs)
    if count_ref is not None:
        source = source * wide(live, probes, dofs)
    refs["source"][...] = source
    copies[3].wait()
    smoother = two_parts(matrix_refs[0][...])
    first_pre = times_parts(source, *smoother) * down
    refs["first"][...] = first_pre
    for copy in copies[5:]:
        copy.wait()
    return first_pre, up, down, smoother


def message_places(steps, probes):
    values = steps * probes
    return values, values + probes, values + probes + steps


def message_length(steps, probes, width):
    return -(-(message_places(steps, probes)[2] * (width // lane_count) + 1) // 8) * 8


def write_row(message_ref, place, row):
    pieces = row.shape[1] // lane_count
    for piece in range(pieces):
        line = place * pieces + piece
        message_ref[line : line + 1, :] = row[:, piece * lane_count : (piece + 1) * lane_count]


def read_row(message_ref, place, width):
    pieces = width // lane_count
    lines = range(place * pieces, (place + 1) * pieces)
    return jnp.concatenate([message_ref[line : line + 1, :] for line in lines], axis=1)


def near_first_kernel(*refs):
    operands, refs = refs[:6], refs[6:]
    first_ref, source_ref, up_ref, down_ref, base_ref, slots_ref = refs[:6]
    part_refs, refs = refs[6:10], refs[10:]
    steps, _, width = slots_ref.shape
    leave_refs, scratch = refs[:steps], refs[steps:]
    visc_ref, rhs_ref, _, k_ref = scratch[2:6]
    probes, elements, dofs = rhs_ref.shape[3:]
    first_pre, up, down, smoother = begin(
        {
            "operands": operands,
            "scratch": scratch,
            "slots": slots_ref,
            "up": up_ref,
            "down": down_ref,
            "source": source_ref,
            "first": first_ref,
        },
        lambda me, step: me ^ step,
        None,
    )
    stiffness = two_parts(k_ref[...])
    base = times_parts(first_pre, *stiffness) * up
    base_ref[...] = base
    first_parts = two_parts(first_pre)
    second_parts = [(times_parts_once(base, *smoother) * down).astype(bf16)]
    for part_ref, part in zip(part_refs, smoother + stiffness):
        part_ref[...] = part
    second_at, index_at, visc_at = message_places(steps, probes)
    for step in range(1, steps + 1):
        flat_row = slots_ref[step - 1]
        over_elements = hot_elements(flat_row, elements, dofs)
        over_dofs = hot_dofs(flat_row, dofs)
        first_rows = take_faces(first_parts, over_elements, over_dofs)
        second_rows = take_faces(second_parts, over_elements, over_dofs)
        for probe in range(probes):
            write_row(leave_refs[step - 1], second_at + probe, second_rows[probe])
            for leave_ref in leave_refs:
                write_row(leave_ref, (step - 1) * probes + probe, first_rows[probe])
        for leave_ref in leave_refs:
            write_row(leave_ref, index_at + step - 1, flat_row.astype(f32))
    visc_line = visc_at * (width // lane_count)
    for leave_ref in leave_refs:
        leave_ref[visc_line : visc_line + 1, :elements] = visc_ref[0, 0]


def near_second_kernel(
    probes, count_ref, source_ref, up_ref, down_ref, base_ref, slots_ref,
    p_high_ref, p_low_ref, k_high_ref, k_low_ref, mine_ref, *refs
):
    came_refs = refs[:-2]
    second_ref, products_ref = refs[-2:]
    steps, _, width = slots_ref.shape
    members = steps + 1
    rows, dofs = source_ref.shape
    elements = rows // probes
    second_at, index_at, visc_at = message_places(steps, probes)

    def message(step):
        return mine_ref if step == 0 else came_refs[step - 1]

    def inbound_first(member, step):
        sent = message(member ^ step)
        return [
            read_row(sent, (step - 1) * probes + probe, width) for probe in range(probes)
        ]

    own_rows = [slots_ref[step] for step in range(steps)]
    own_elements = [hot_elements(flat_row, elements, dofs) for flat_row in own_rows]
    own_dofs = hot_rows(own_rows, dofs)

    def placed_here(values):
        spreads = [spread_faces(values[step], own_elements[step]) for step in range(steps)]
        return add_faces(spreads, own_dofs)

    up, down = up_ref[...], down_ref[...]
    live = wide(live_column(count_ref, elements).astype(f32), probes, dofs) > 0.0
    placed = folded(placed_here([high_low(inbound_first(0, step)) for step in range(1, members)]))
    image = jnp.where(live, base_ref[...] - coupling * placed, 0.0)
    changes, back = [], []
    for member in range(1, members):
        rows_of = [
            read_row(message(member), index_at + step, width).astype(jnp.int32)
            for step in range(steps)
        ]
        over_elements = [hot_elements(flat_row, elements, dofs) for flat_row in rows_of]
        spreads = [
            spread_faces(inbound_first(member, step + 1), over_elements[step])
            for step in range(steps)
        ]
        changes.append(-coupling * add_faces(spreads, hot_rows(rows_of, dofs)))
        back.append((over_elements[member - 1], hot_dofs(rows_of[member - 1], dofs)))
    second_pre = times_parts(image, p_high_ref[...], p_low_ref[...]) * down
    changes = times_parts_once(jnp.concatenate(changes, axis=0), p_high_ref[...], p_low_ref[...])
    second_ref[...] = second_pre
    values = []
    visc_line = visc_at * (width // lane_count)
    for member in range(1, members):
        sent = message(member)
        visc = as_column(sent[visc_line : visc_line + 1, :elements])
        scale = wide(1.0 / visc, probes, dofs)
        change = changes[(member - 1) * rows : member * rows] * scale
        taken = take_faces([change.astype(bf16)], *back[member - 1])
        values.append(
            [taken[probe] + read_row(sent, second_at + probe, width) for probe in range(probes)]
        )
    placed = placed_here(values)
    second_img = times_parts_once(second_pre, k_high_ref[...], k_low_ref[...])
    second_img = second_img * up - coupling * placed
    second_img = jnp.where(live, second_img, 0.0)
    source = jnp.where(live, source_ref[...], 0.0)
    inner_products(image, second_img, source, probes, products_ref)


def leave_faces(field, probes, slots_ref, leave_ref):
    elements, dofs = field.shape[0] // probes, field.shape[1]
    members = slots_ref.shape[0] + 1
    me = lax.axis_index("gz")
    for shift in range(1, members):
        flat_row = slots_ref[shift - 1]
        over_elements = hot_elements(flat_row, elements, dofs)
        taken = take_faces(two_parts(field), over_elements, hot_dofs(flat_row, dofs))
        target = lax.rem(me + shift, members)
        for probe in range(probes):
            leave_ref[target, pl.ds(probe, 1), :] = taken[probe]
    leave_ref[me] = jnp.zeros(leave_ref.shape[1:], f32)


def placed_faces(shape, probes, slots_ref, came_ref):
    rows, dofs = shape
    elements = rows // probes
    members = slots_ref.shape[0] + 1
    me = lax.axis_index("gz")
    total = jnp.zeros(shape, f32)
    for shift in range(1, members):
        flat_row = slots_ref[shift - 1]
        came = came_ref[lax.rem(me + shift, members)]
        values = [came[probe : probe + 1, :] for probe in range(probes)]
        spread = spread_faces(high_low(values), hot_elements(flat_row, elements, dofs))
        total += folded(add_faces([spread], hot_rows([flat_row], dofs)))
    return total


def far_first_kernel(*refs):
    count_ref, *operands = refs[:6]
    refs = refs[6:]
    first_ref, source_ref, up_ref, down_ref, slots_ref, leave_ref = refs[:6]
    members = slots_ref.shape[0] + 1
    first_pre, *_ = begin(
        {
            "operands": operands,
            "scratch": refs[6:],
            "slots": slots_ref,
            "up": up_ref,
            "down": down_ref,
            "source": source_ref,
            "first": first_ref,
        },
        lambda me, step: lax.rem(me + step, members),
        count_ref,
    )
    leave_faces(first_pre, leave_ref.shape[1], slots_ref, leave_ref)


def far_second_kernel(
    slots_ref, up_ref, down_ref, first_ref, k_ref, p_ref, came_ref,
    image_ref, second_ref, leave_ref,
):
    probes = came_ref.shape[1]
    up = up_ref[...]
    placed = placed_faces(first_ref.shape, probes, slots_ref, came_ref)
    image = times_matrix(first_ref[...], k_ref[...]) * up - jnp.where(up > 0.0, coupling * placed, 0.0)
    image_ref[...] = image
    second_pre = times_matrix(image, p_ref[...]) * down_ref[...]
    second_ref[...] = second_pre
    leave_faces(second_pre, probes, slots_ref, leave_ref)


def far_third_kernel(
    slots_ref, up_ref, source_ref, image_ref, second_ref, k_ref, came_ref, products_ref
):
    probes = came_ref.shape[1]
    up = up_ref[...]
    placed = placed_faces(source_ref.shape, probes, slots_ref, came_ref)
    second_img = times_matrix(second_ref[...], k_ref[...]) * up - jnp.where(up > 0.0, coupling * placed, 0.0)
    inner_products(image_ref[...], second_img, source_ref[...], probes, products_ref)


def last_kernel(probes, count_ref, first_ref, second_ref, parts_ref, out_ref):
    rows, _ = first_ref.shape
    elements = rows // probes
    total = jnp.sum(parts_ref[...], axis=0)
    live = live_column(count_ref, elements)
    for probe in range(probes):
        self_one, cross_mid, self_two, load_one, load_two = (
            total[:, place * probes + probe : place * probes + probe + 1] for place in range(5)
        )
        determinant = self_one * self_two - cross_mid * cross_mid
        weight_one = (self_two * load_one - cross_mid * load_two) / determinant
        weight_two = (self_one * load_two - cross_mid * load_one) / determinant
        block = pl.ds(probe * elements, elements)
        value = weight_one * first_ref[block, :] + weight_two * second_ref[block, :]
        out_ref[block, :] = jnp.where(live, value, 0.0)


def call(kernel, in_specs, out_shapes, flops, *args, scratch=()):
    return pl.pallas_call(
        kernel,
        out_shape=out_shapes,
        in_specs=in_specs,
        out_specs=jax.tree.map(lambda _: vmem_spec, out_shapes),
        scratch_shapes=scratch,
        compiler_params=pltpu.CompilerParams(vmem_limit_bytes=vmem_grant),
        cost_estimate=pl.CostEstimate(flops=flops, bytes_accessed=1 << 20, transcendentals=0),
    )(*args)


def begin_call(kernel, out_shapes, flops, scalars, *fetched):
    links, *others = fetched
    scratch = [pltpu.SMEM(links.shape, links.dtype)]
    scratch += [pltpu.VMEM(value.shape, value.dtype) for value in others]
    return call(
        kernel,
        [smem_spec] * len(scalars) + [hbm_spec] * len(fetched),
        out_shapes,
        flops,
        *scalars,
        *(pltpu.with_memory_space_constraint(value, pltpu.HBM) for value in fetched),
        scratch=scratch + [pltpu.SemaphoreType.DMA((len(fetched),))],
    )


def near_steps(members, shapes, arguments):
    rhs, viscosity, counts, neighbours, face_index, k_matrix, p_matrix = arguments
    field, slots_shape, products_shape = shapes
    rows, dofs = field.shape
    steps, _, width = slots_shape.shape
    probes = rhs.shape[3]
    flops = 8 * rows * dofs * steps * width
    message = jax.ShapeDtypeStruct((message_length(steps, probes, width), lane_count), f32)
    part = jax.ShapeDtypeStruct(p_matrix.shape, bf16)
    first_pre, source, up, down, base, slots, *rest = begin_call(
        near_first_kernel,
        [field] * 5 + [slots_shape] + [part] * 4 + [message] * steps,
        2 * flops,
        (),
        neighbours,
        face_index,
        viscosity,
        rhs,
        p_matrix,
        k_matrix,
    )
    parts, leaving = rest[:4], rest[4:]
    came = [
        lax.ppermute(
            leaving[step - 1], "gz", [(source, source ^ step) for source in range(members)]
        )
        for step in range(1, members)
    ]
    second_pre, products = call(
        functools.partial(near_second_kernel, probes),
        [smem_spec] + [vmem_spec] * (10 + steps),
        [field, products_shape],
        6 * flops,
        counts,
        source,
        up,
        down,
        base,
        slots,
        *parts,
        leaving[0],
        *came,
    )
    return first_pre, second_pre, products


def far_steps(members, shapes, arguments):
    rhs, viscosity, counts, neighbours, face_index, k_matrix, p_matrix = arguments
    field, slots_shape, products_shape = shapes
    rows, dofs = field.shape
    shifts, _, width = slots_shape.shape
    flops = 8 * rows * dofs * shifts * width
    faces = jax.ShapeDtypeStruct((members, rhs.shape[3], width), f32)

    def exchange(value):
        return lax.all_to_all(value, "gz", split_axis=0, concat_axis=0)

    first_pre, source, up, down, slots, leaving = begin_call(
        far_first_kernel,
        [field] * 4 + [slots_shape, faces],
        flops,
        (counts,),
        neighbours,
        face_index,
        viscosity,
        rhs,
        p_matrix,
    )
    first_img, second_pre, leaving = call(
        far_second_kernel,
        [vmem_spec] * 7,
        [field, field, faces],
        2 * flops,
        slots,
        up,
        down,
        first_pre,
        k_matrix,
        p_matrix,
        exchange(leaving),
    )
    products = call(
        far_third_kernel,
        [vmem_spec] * 7,
        products_shape,
        flops,
        slots,
        up,
        source,
        first_img,
        second_pre,
        k_matrix,
        exchange(leaving),
    )
    return first_pre, second_pre, products


def per_device(mesh, *arguments):
    rhs, face_index = arguments[0], arguments[4]
    probes, elements, dofs = rhs.shape[3:]
    members = mesh.shape["gz"]
    lanes = -(-5 * probes // 128) * 128
    shapes = (
        jax.ShapeDtypeStruct((probes * elements, dofs), f32),
        jax.ShapeDtypeStruct((members - 1, 1, face_index.shape[-1]), jnp.int32),
        jax.ShapeDtypeStruct((mesh.size, 1, lanes), f32),
    )
    near = 1 < members <= short_group and elements <= face_index.shape[-1]
    near = near and elements * dofs < 1 << 24
    steps = near_steps if near else far_steps
    first_pre, second_pre, products = steps(members, shapes, arguments)
    result = call(
        functools.partial(last_kernel, probes),
        [smem_spec] + [vmem_spec] * 3,
        shapes[0],
        probes * elements * dofs,
        arguments[2],
        first_pre,
        second_pre,
        lax.all_to_all(products, ("gx", "gy", "gz"), split_axis=0, concat_axis=0),
    )
    return result.reshape(rhs.shape)


def solution(mesh):
    return jax.shard_map(
        functools.partial(per_device, mesh),
        mesh=mesh,
        in_specs=(
            P("gx", "gy", "gz", None, None, None),
            P("gx", "gy", "gz", None),
            P("gx", "gy", "gz"),
            P("gx", "gy", "gz", None),
            P("gx", "gy", "gz", None, None),
            P(),
            P(),
        ),
        out_specs=P("gx", "gy", "gz", None, None, None),
        check_vma=False,
    )
```

```python
import functools

import jax
import jax.numpy as jnp
from jax import lax
from jax.experimental import pallas as pl
from jax.experimental.pallas import tpu as pltpu
from jax.sharding import PartitionSpec as P

coupling = 0.5
vmem_grant = 48 * 1024 * 1024
short_group = 4
lane_count = 128
f32 = jnp.float32
bf16 = jnp.bfloat16
vmem_spec = pl.BlockSpec(memory_space=pltpu.VMEM)
smem_spec = pl.BlockSpec(memory_space=pltpu.SMEM)
hbm_spec = pl.BlockSpec(memory_space=pltpu.HBM)


def two_parts(value):
    high = value.astype(bf16)
    return high, (value - high.astype(f32)).astype(bf16)


def dot(left, right):
    return jnp.dot(left, right, preferred_element_type=f32)


def dot_transposed(left, right):
    return lax.dot_general(left, right, (((1,), (1,)), ((), ())), preferred_element_type=f32)


def times_matrix(rows, matrix):
    return times_parts(rows, *two_parts(matrix))


def times_parts(rows, mat_high, mat_low):
    count = rows.shape[0]
    row_high, row_low = two_parts(rows)
    both = dot(jnp.concatenate([row_high, row_low], axis=0), mat_high)
    return both[:count] + (both[count:] + dot(row_high, mat_low))


def times_parts_once(rows, mat_high, mat_low):
    row_high = rows.astype(bf16)
    return dot(
        jnp.concatenate([row_high, row_high], axis=1),
        jnp.concatenate([mat_high, mat_low], axis=0),
    )


def split_index(index, dofs):
    if dofs & (dofs - 1) == 0:
        return lax.shift_right_arithmetic(index, dofs.bit_length() - 1), index & (dofs - 1)
    element = jnp.floor_divide(index, dofs)
    return element, index - element * dofs


def slot_of(target, links_ref, index_ref):
    slot = jnp.int32(-1)
    for position in range(links_ref.shape[-1]):
        slot = jnp.where(links_ref[0, 0, 0, position] == target, jnp.int32(position), slot)
    row = index_ref[0, 0, 0, pl.ds(jnp.maximum(slot, 0), 1), :]
    return jnp.where(slot >= 0, row, -1)


def hot_elements(flat_row, elements, dofs):
    element, _ = split_index(flat_row, dofs)
    return lax.broadcasted_iota(jnp.int32, (elements, flat_row.shape[1]), 0) == element


def hot_dofs(flat_row, dofs):
    _, dof = split_index(flat_row, dofs)
    shape = (dofs, flat_row.shape[1])
    line = lax.broadcasted_iota(jnp.int32, shape, 0).astype(jnp.int16)
    hit = line == jnp.broadcast_to(dof.astype(jnp.int16), shape)
    return jnp.where(hit, jnp.ones(shape, bf16), jnp.zeros(shape, bf16))


def as_column(row):
    elements = row.shape[1]
    line = lax.broadcasted_iota(jnp.int32, (elements, elements), 0)
    column = lax.broadcasted_iota(jnp.int32, (elements, elements), 1)
    spread = jnp.where(line == column, jnp.broadcast_to(row, (elements, elements)), 0.0)
    return jnp.sum(spread, axis=1, keepdims=True)


def wide(column, probes, dofs):
    return jnp.broadcast_to(jnp.concatenate([column] * probes, axis=0), (probes * column.shape[0], dofs))


def take_faces(picked, over_elements):
    elements = over_elements.shape[0]
    return [
        jnp.sum(jnp.where(over_elements, picked[low : low + elements], 0.0), axis=0, keepdims=True)
        for low in range(0, picked.shape[0], elements)
    ]


def spread_faces(values, over_elements):
    return jnp.concatenate(
        [jnp.where(over_elements, value, 0.0).astype(bf16) for value in values], axis=0
    )


def high_low(values):
    highs = [value.astype(bf16).astype(f32) for value in values]
    return highs + [value - high for value, high in zip(values, highs)]


def add_faces(spreads, over_dofs):
    return dot_transposed(jnp.concatenate(spreads, axis=1), over_dofs)


def add_faces_once(spreads, over_dofs):
    return jnp.transpose(dot_transposed(over_dofs, jnp.concatenate(spreads, axis=1)))


def folded(parts):
    rows = parts.shape[0] // 2
    return parts[:rows] + parts[rows:]


def as_row(lines, lanes):
    count = -(-len(lines) // 8) * 8
    spare = jnp.zeros((count - len(lines), lines[0].shape[1]), f32)
    sums = jnp.sum(jnp.concatenate(lines + [spare], axis=0), axis=1, keepdims=True)
    line = lax.broadcasted_iota(jnp.int32, (count, lanes), 0)
    lane = lax.broadcasted_iota(jnp.int32, (count, lanes), 1)
    return jnp.sum(jnp.where(line == lane, sums, 0.0), axis=0, keepdims=True)


def inner_products(first_img, second_img, source, probes, products_ref):
    elements = source.shape[0] // probes
    pairs = (
        (first_img, first_img),
        (first_img, second_img),
        (second_img, second_img),
        (first_img, source),
        (second_img, source),
    )
    lines = []
    for left, right in pairs:
        product = left * right
        for probe in range(probes):
            lines.append(
                jnp.sum(product[probe * elements : (probe + 1) * elements], axis=0, keepdims=True)
            )
    products_ref[...] = jnp.broadcast_to(as_row(lines, products_ref.shape[-1]), products_ref.shape)


def live_column(count_ref, elements):
    return lax.broadcasted_iota(jnp.int32, (elements, 1), 0) < count_ref[0, 0, 0]


def begin(refs, partner, count_ref, prepare):
    links_hbm, index_hbm, visc_hbm, rhs_hbm, *matrices_hbm = refs["operands"]
    links_ref, index_ref, visc_ref, rhs_ref, *matrix_refs, arrived = refs["scratch"]
    pairs = (
        (links_hbm, links_ref),
        (index_hbm, index_ref),
        (rhs_hbm, rhs_ref),
        (matrices_hbm[0], matrix_refs[0]),
        (visc_hbm, visc_ref),
        *zip(matrices_hbm[1:], matrix_refs[1:]),
    )
    copies = [
        pltpu.make_async_copy(held, here, arrived.at[place])
        for place, (held, here) in enumerate(pairs)
    ]
    for copy in copies:
        copy.start()
    copies[0].wait()
    copies[1].wait()
    slots_ref = refs["slots"]
    me = lax.axis_index("gz")
    for step in range(1, slots_ref.shape[0] + 1):
        slots_ref[step - 1] = slot_of(partner(me, step), links_ref, index_ref)
    prepare()
    copies[4].wait()
    probes, elements, dofs = rhs_ref.shape[3:]
    live = jnp.ones((elements, 1), f32)
    if count_ref is not None:
        live = live_column(count_ref, elements).astype(f32)
    visc = as_column(visc_ref[0, 0])
    up = wide(live * visc, probes, dofs)
    down = wide(live / visc, probes, dofs)
    refs["up"][...] = up
    refs["down"][...] = down
    copies[2].wait()
    source = rhs_ref[...].reshape(probes * elements, dofs)
    if count_ref is not None:
        source = source * wide(live, probes, dofs)
    refs["source"][...] = source
    copies[3].wait()
    smoother = two_parts(matrix_refs[0][...])
    first_pre = times_parts(source, *smoother) * down
    refs["first"][...] = first_pre
    for copy in copies[5:]:
        copy.wait()
    return first_pre, up, down, smoother


def message_places(steps, probes):
    values = steps * probes
    return values, values + probes, values + probes + steps


def message_length(steps, probes, width):
    return -(-(message_places(steps, probes)[2] * (width // lane_count) + 1) // 8) * 8


def write_row(message_ref, place, row):
    pieces = row.shape[1] // lane_count
    for piece in range(pieces):
        line = place * pieces + piece
        message_ref[line : line + 1, :] = row[:, piece * lane_count : (piece + 1) * lane_count]


def read_row(message_ref, place, width):
    pieces = width // lane_count
    lines = range(place * pieces, (place + 1) * pieces)
    return jnp.concatenate([message_ref[line : line + 1, :] for line in lines], axis=1)


def near_first_kernel(*refs):
    operands, refs = refs[:6], refs[6:]
    first_ref, source_ref, up_ref, down_ref, base_ref, slots_ref, hot_ref = refs[:7]
    part_refs, refs = refs[7:11], refs[11:]
    steps, _, width = slots_ref.shape
    leave_refs, scratch = refs[:steps], refs[steps:]
    visc_ref, rhs_ref, _, k_ref = scratch[2:6]
    probes, elements, dofs = rhs_ref.shape[3:]

    def prepare():
        for step in range(steps):
            hot_ref[:, step * width : (step + 1) * width] = hot_dofs(slots_ref[step], dofs)

    first_pre, up, down, smoother = begin(
        {
            "operands": operands,
            "scratch": scratch,
            "slots": slots_ref,
            "up": up_ref,
            "down": down_ref,
            "source": source_ref,
            "first": first_ref,
        },
        lambda me, step: me ^ step,
        None,
        prepare,
    )
    stiffness = two_parts(k_ref[...])
    base = times_parts(first_pre, *stiffness) * up
    base_ref[...] = base
    second_part = (times_parts_once(base, *smoother) * down).astype(bf16)
    stacked = jnp.concatenate([*two_parts(first_pre), second_part], axis=0)
    rows = probes * elements
    for part_ref, part in zip(part_refs, smoother + stiffness):
        part_ref[...] = part
    second_at, index_at, visc_at = message_places(steps, probes)
    for step in range(1, steps + 1):
        flat_row = slots_ref[step - 1]
        over_elements = hot_elements(flat_row, elements, dofs)
        over_dofs = hot_ref[:, (step - 1) * width : step * width]
        picked = dot(stacked, over_dofs)
        first_rows = take_faces(folded(picked[: 2 * rows]), over_elements)
        second_rows = take_faces(picked[2 * rows :], over_elements)
        for probe in range(probes):
            write_row(leave_refs[step - 1], second_at + probe, second_rows[probe])
            for leave_ref in leave_refs:
                write_row(leave_ref, (step - 1) * probes + probe, first_rows[probe])
        for leave_ref in leave_refs:
            write_row(leave_ref, index_at + step - 1, flat_row.astype(f32))
    visc_line = visc_at * (width // lane_count)
    for leave_ref in leave_refs:
        leave_ref[visc_line : visc_line + 1, :elements] = visc_ref[0, 0]


def near_second_kernel(
    probes, count_ref, source_ref, up_ref, down_ref, base_ref, slots_ref, hot_ref,
    p_high_ref, p_low_ref, k_high_ref, k_low_ref, mine_ref, *refs
):
    came_refs = refs[:-2]
    second_ref, products_ref = refs[-2:]
    steps, _, width = slots_ref.shape
    members = steps + 1
    rows, dofs = source_ref.shape
    elements = rows // probes
    second_at, index_at, visc_at = message_places(steps, probes)

    def message(step):
        return mine_ref if step == 0 else came_refs[step - 1]

    def inbound_first(member, step):
        sent = message(member ^ step)
        return [
            read_row(sent, (step - 1) * probes + probe, width) for probe in range(probes)
        ]

    own_elements = [hot_elements(slots_ref[step], elements, dofs) for step in range(steps)]

    def placed_here(values):
        spreads = [spread_faces(values[step], own_elements[step]) for step in range(steps)]
        add = add_faces if len(values[0]) > probes else add_faces_once
        return add(spreads, hot_ref[...])

    up, down = up_ref[...], down_ref[...]
    live = wide(live_column(count_ref, elements).astype(f32), probes, dofs) > 0.0
    placed = folded(placed_here([high_low(inbound_first(0, step)) for step in range(1, members)]))
    image = jnp.where(live, base_ref[...] - coupling * placed, 0.0)
    changes, back = [], []
    for member in range(1, members):
        rows_of = [
            read_row(message(member), index_at + step, width).astype(jnp.int32)
            for step in range(steps)
        ]
        over_elements = [hot_elements(flat_row, elements, dofs) for flat_row in rows_of]
        over_dofs = [hot_dofs(flat_row, dofs) for flat_row in rows_of]
        spreads = [
            spread_faces(inbound_first(member, step + 1), over_elements[step])
            for step in range(steps)
        ]
        changes.append(-coupling * add_faces_once(spreads, jnp.concatenate(over_dofs, axis=1)))
        back.append((over_elements[member - 1], over_dofs[member - 1]))
    second_pre = times_parts(image, p_high_ref[...], p_low_ref[...]) * down
    changes = times_parts_once(jnp.concatenate(changes, axis=0), p_high_ref[...], p_low_ref[...])
    second_ref[...] = second_pre
    values = []
    visc_line = visc_at * (width // lane_count)
    for member in range(1, members):
        sent = message(member)
        visc = as_column(sent[visc_line : visc_line + 1, :elements])
        scale = wide(1.0 / visc, probes, dofs)
        change = changes[(member - 1) * rows : member * rows] * scale
        over_elements, over_dofs = back[member - 1]
        taken = take_faces(dot(change.astype(bf16), over_dofs), over_elements)
        values.append(
            [taken[probe] + read_row(sent, second_at + probe, width) for probe in range(probes)]
        )
    placed = placed_here(values)
    second_img = times_parts_once(second_pre, k_high_ref[...], k_low_ref[...])
    second_img = second_img * up - coupling * placed
    second_img = jnp.where(live, second_img, 0.0)
    source = jnp.where(live, source_ref[...], 0.0)
    inner_products(image, second_img, source, probes, products_ref)


def leave_faces(field, probes, slots_ref, leave_ref):
    elements, dofs = field.shape[0] // probes, field.shape[1]
    members = slots_ref.shape[0] + 1
    me = lax.axis_index("gz")
    for shift in range(1, members):
        flat_row = slots_ref[shift - 1]
        over_elements = hot_elements(flat_row, elements, dofs)
        parts = jnp.concatenate(two_parts(field), axis=0)
        taken = take_faces(folded(dot(parts, hot_dofs(flat_row, dofs))), over_elements)
        target = lax.rem(me + shift, members)
        for probe in range(probes):
            leave_ref[target, pl.ds(probe, 1), :] = taken[probe]
    leave_ref[me] = jnp.zeros(leave_ref.shape[1:], f32)


def placed_faces(shape, probes, slots_ref, came_ref):
    rows, dofs = shape
    elements = rows // probes
    members = slots_ref.shape[0] + 1
    me = lax.axis_index("gz")
    total = jnp.zeros(shape, f32)
    for shift in range(1, members):
        flat_row = slots_ref[shift - 1]
        came = came_ref[lax.rem(me + shift, members)]
        values = [came[probe : probe + 1, :] for probe in range(probes)]
        spread = spread_faces(high_low(values), hot_elements(flat_row, elements, dofs))
        total += folded(add_faces([spread], hot_dofs(flat_row, dofs)))
    return total


def far_first_kernel(*refs):
    count_ref, *operands = refs[:6]
    refs = refs[6:]
    first_ref, source_ref, up_ref, down_ref, slots_ref, leave_ref = refs[:6]
    members = slots_ref.shape[0] + 1
    first_pre, *_ = begin(
        {
            "operands": operands,
            "scratch": refs[6:],
            "slots": slots_ref,
            "up": up_ref,
            "down": down_ref,
            "source": source_ref,
            "first": first_ref,
        },
        lambda me, step: lax.rem(me + step, members),
        count_ref,
        lambda: None,
    )
    leave_faces(first_pre, leave_ref.shape[1], slots_ref, leave_ref)


def far_second_kernel(
    slots_ref, up_ref, down_ref, first_ref, k_ref, p_ref, came_ref,
    image_ref, second_ref, leave_ref,
):
    probes = came_ref.shape[1]
    up = up_ref[...]
    placed = placed_faces(first_ref.shape, probes, slots_ref, came_ref)
    image = times_matrix(first_ref[...], k_ref[...]) * up - jnp.where(up > 0.0, coupling * placed, 0.0)
    image_ref[...] = image
    second_pre = times_matrix(image, p_ref[...]) * down_ref[...]
    second_ref[...] = second_pre
    leave_faces(second_pre, probes, slots_ref, leave_ref)


def far_third_kernel(
    slots_ref, up_ref, source_ref, image_ref, second_ref, k_ref, came_ref, products_ref
):
    probes = came_ref.shape[1]
    up = up_ref[...]
    placed = placed_faces(source_ref.shape, probes, slots_ref, came_ref)
    second_img = times_matrix(second_ref[...], k_ref[...]) * up - jnp.where(up > 0.0, coupling * placed, 0.0)
    inner_products(image_ref[...], second_img, source_ref[...], probes, products_ref)


def last_kernel(probes, count_ref, first_ref, second_ref, parts_ref, out_ref):
    rows, _ = first_ref.shape
    elements = rows // probes
    total = jnp.sum(parts_ref[...], axis=0)
    live = live_column(count_ref, elements)
    for probe in range(probes):
        self_one, cross_mid, self_two, load_one, load_two = (
            total[:, place * probes + probe : place * probes + probe + 1] for place in range(5)
        )
        determinant = self_one * self_two - cross_mid * cross_mid
        weight_one = (self_two * load_one - cross_mid * load_two) / determinant
        weight_two = (self_one * load_two - cross_mid * load_one) / determinant
        block = pl.ds(probe * elements, elements)
        value = weight_one * first_ref[block, :] + weight_two * second_ref[block, :]
        out_ref[block, :] = jnp.where(live, value, 0.0)


def call(kernel, in_specs, out_shapes, flops, *args, scratch=()):
    return pl.pallas_call(
        kernel,
        out_shape=out_shapes,
        in_specs=in_specs,
        out_specs=jax.tree.map(lambda _: vmem_spec, out_shapes),
        scratch_shapes=scratch,
        compiler_params=pltpu.CompilerParams(vmem_limit_bytes=vmem_grant),
        cost_estimate=pl.CostEstimate(flops=flops, bytes_accessed=1 << 20, transcendentals=0),
    )(*args)


def begin_call(kernel, out_shapes, flops, scalars, *fetched):
    links, *others = fetched
    scratch = [pltpu.SMEM(links.shape, links.dtype)]
    scratch += [pltpu.VMEM(value.shape, value.dtype) for value in others]
    return call(
        kernel,
        [smem_spec] * len(scalars) + [hbm_spec] * len(fetched),
        out_shapes,
        flops,
        *scalars,
        *(pltpu.with_memory_space_constraint(value, pltpu.HBM) for value in fetched),
        scratch=scratch + [pltpu.SemaphoreType.DMA((len(fetched),))],
    )


def near_steps(members, shapes, arguments):
    rhs, viscosity, counts, neighbours, face_index, k_matrix, p_matrix = arguments
    field, slots_shape, products_shape = shapes
    rows, dofs = field.shape
    steps, _, width = slots_shape.shape
    probes = rhs.shape[3]
    flops = 8 * rows * dofs * steps * width
    hot = jax.ShapeDtypeStruct((dofs, steps * width), bf16)
    message = jax.ShapeDtypeStruct((message_length(steps, probes, width), lane_count), f32)
    part = jax.ShapeDtypeStruct(p_matrix.shape, bf16)
    first_pre, source, up, down, base, slots, hot_own, *rest = begin_call(
        near_first_kernel,
        [field] * 5 + [slots_shape, hot] + [part] * 4 + [message] * steps,
        2 * flops,
        (),
        neighbours,
        face_index,
        viscosity,
        rhs,
        p_matrix,
        k_matrix,
    )
    parts, leaving = rest[:4], rest[4:]
    came = [
        lax.ppermute(
            leaving[step - 1], "gz", [(source, source ^ step) for source in range(members)]
        )
        for step in range(1, members)
    ]
    second_pre, products = call(
        functools.partial(near_second_kernel, probes),
        [smem_spec] + [vmem_spec] * (11 + steps),
        [field, products_shape],
        6 * flops,
        counts,
        source,
        up,
        down,
        base,
        slots,
        hot_own,
        *parts,
        leaving[0],
        *came,
    )
    return first_pre, second_pre, products


def far_steps(members, shapes, arguments):
    rhs, viscosity, counts, neighbours, face_index, k_matrix, p_matrix = arguments
    field, slots_shape, products_shape = shapes
    rows, dofs = field.shape
    shifts, _, width = slots_shape.shape
    flops = 8 * rows * dofs * shifts * width
    faces = jax.ShapeDtypeStruct((members, rhs.shape[3], width), f32)

    def exchange(value):
        return lax.all_to_all(value, "gz", split_axis=0, concat_axis=0)

    first_pre, source, up, down, slots, leaving = begin_call(
        far_first_kernel,
        [field] * 4 + [slots_shape, faces],
        flops,
        (counts,),
        neighbours,
        face_index,
        viscosity,
        rhs,
        p_matrix,
    )
    first_img, second_pre, leaving = call(
        far_second_kernel,
        [vmem_spec] * 7,
        [field, field, faces],
        2 * flops,
        slots,
        up,
        down,
        first_pre,
        k_matrix,
        p_matrix,
        exchange(leaving),
    )
    products = call(
        far_third_kernel,
        [vmem_spec] * 7,
        products_shape,
        flops,
        slots,
        up,
        source,
        first_img,
        second_pre,
        k_matrix,
        exchange(leaving),
    )
    return first_pre, second_pre, products


def per_device(mesh, *arguments):
    rhs, face_index = arguments[0], arguments[4]
    probes, elements, dofs = rhs.shape[3:]
    members = mesh.shape["gz"]
    lanes = -(-5 * probes // 128) * 128
    shapes = (
        jax.ShapeDtypeStruct((probes * elements, dofs), f32),
        jax.ShapeDtypeStruct((members - 1, 1, face_index.shape[-1]), jnp.int32),
        jax.ShapeDtypeStruct((mesh.size, 1, lanes), f32),
    )
    near = 1 < members <= short_group and elements <= face_index.shape[-1]
    near = near and elements * dofs < 1 << 24
    steps = near_steps if near else far_steps
    first_pre, second_pre, products = steps(members, shapes, arguments)
    result = call(
        functools.partial(last_kernel, probes),
        [smem_spec] + [vmem_spec] * 3,
        shapes[0],
        probes * elements * dofs,
        arguments[2],
        first_pre,
        second_pre,
        lax.all_to_all(products, ("gx", "gy", "gz"), split_axis=0, concat_axis=0),
    )
    return result.reshape(rhs.shape)


def solution(mesh):
    return jax.shard_map(
        functools.partial(per_device, mesh),
        mesh=mesh,
        in_specs=(
            P("gx", "gy", "gz", None, None, None),
            P("gx", "gy", "gz", None),
            P("gx", "gy", "gz"),
            P("gx", "gy", "gz", None),
            P("gx", "gy", "gz", None, None),
            P(),
            P(),
        ),
        out_specs=P("gx", "gy", "gz", None, None, None),
        check_vma=False,
    )
```

```python
import functools

import jax
import jax.numpy as jnp
from jax import lax
from jax.experimental import pallas as pl
from jax.experimental.pallas import tpu as pltpu
from jax.sharding import PartitionSpec as P

coupling = 0.5
vmem_grant = 48 * 1024 * 1024
short_group = 4
lane_count = 128
f32 = jnp.float32
bf16 = jnp.bfloat16
vmem_spec = pl.BlockSpec(memory_space=pltpu.VMEM)
smem_spec = pl.BlockSpec(memory_space=pltpu.SMEM)
hbm_spec = pl.BlockSpec(memory_space=pltpu.HBM)


def two_parts(value):
    high = value.astype(bf16)
    return high, (value - high.astype(f32)).astype(bf16)


def dot(left, right):
    return jnp.dot(left, right, preferred_element_type=f32)


def dot_transposed(left, right):
    return lax.dot_general(left, right, (((1,), (1,)), ((), ())), preferred_element_type=f32)


def times_matrix(rows, matrix):
    return times_parts(rows, *two_parts(matrix))


def times_parts(rows, mat_high, mat_low):
    count = rows.shape[0]
    row_high, row_low = two_parts(rows)
    both = dot(jnp.concatenate([row_high, row_low], axis=0), mat_high)
    return both[:count] + (both[count:] + dot(row_high, mat_low))


def times_parts_once(rows, mat_high, mat_low):
    row_high = rows.astype(bf16)
    return dot(
        jnp.concatenate([row_high, row_high], axis=1),
        jnp.concatenate([mat_high, mat_low], axis=0),
    )


def split_index(index, dofs):
    if dofs & (dofs - 1) == 0:
        return lax.shift_right_arithmetic(index, dofs.bit_length() - 1), index & (dofs - 1)
    element = jnp.floor_divide(index, dofs)
    return element, index - element * dofs


def slot_of(target, links_ref, index_ref):
    slot = jnp.int32(-1)
    for position in range(links_ref.shape[-1]):
        slot = jnp.where(links_ref[0, 0, 0, position] == target, jnp.int32(position), slot)
    row = index_ref[0, 0, 0, pl.ds(jnp.maximum(slot, 0), 1), :]
    return jnp.where(slot >= 0, row, -1)


def hot_elements(flat_row, elements, dofs):
    element, _ = split_index(flat_row, dofs)
    return lax.broadcasted_iota(jnp.int32, (elements, flat_row.shape[1]), 0) == element


def hot_dofs(flat_row, dofs):
    _, dof = split_index(flat_row, dofs)
    shape = (dofs, flat_row.shape[1])
    line = lax.broadcasted_iota(jnp.int32, shape, 0).astype(jnp.int16)
    hit = line == jnp.broadcast_to(dof.astype(jnp.int16), shape)
    return jnp.where(hit, jnp.ones(shape, bf16), jnp.zeros(shape, bf16))


def as_column(row):
    elements = row.shape[1]
    line = lax.broadcasted_iota(jnp.int32, (elements, elements), 0)
    column = lax.broadcasted_iota(jnp.int32, (elements, elements), 1)
    spread = jnp.where(line == column, jnp.broadcast_to(row, (elements, elements)), 0.0)
    return jnp.sum(spread, axis=1, keepdims=True)


def wide(column, probes, dofs):
    return jnp.broadcast_to(jnp.concatenate([column] * probes, axis=0), (probes * column.shape[0], dofs))


def take_faces(picked, over_elements):
    elements = over_elements.shape[0]
    return [
        jnp.sum(jnp.where(over_elements, picked[low : low + elements], 0.0), axis=0, keepdims=True)
        for low in range(0, picked.shape[0], elements)
    ]


def spread_faces(values, over_elements):
    return jnp.concatenate(
        [jnp.where(over_elements, value, 0.0).astype(bf16) for value in values], axis=0
    )


def high_low(values):
    highs = [value.astype(bf16).astype(f32) for value in values]
    return highs + [value - high for value, high in zip(values, highs)]


def add_faces(spreads, over_dofs):
    return dot_transposed(jnp.concatenate(spreads, axis=1), over_dofs)


def add_faces_once(spreads, over_dofs):
    return jnp.transpose(dot_transposed(over_dofs, jnp.concatenate(spreads, axis=1)))


def folded(parts):
    rows = parts.shape[0] // 2
    return parts[:rows] + parts[rows:]


def as_row(lines, lanes):
    count = -(-len(lines) // 8) * 8
    spare = jnp.zeros((count - len(lines), lines[0].shape[1]), f32)
    sums = jnp.sum(jnp.concatenate(lines + [spare], axis=0), axis=1, keepdims=True)
    line = lax.broadcasted_iota(jnp.int32, (count, lanes), 0)
    lane = lax.broadcasted_iota(jnp.int32, (count, lanes), 1)
    return jnp.sum(jnp.where(line == lane, sums, 0.0), axis=0, keepdims=True)


def inner_products(first_img, second_img, source, probes, products_ref):
    elements = source.shape[0] // probes
    pairs = (
        (first_img, first_img),
        (first_img, second_img),
        (second_img, second_img),
        (first_img, source),
        (second_img, source),
    )
    lines = []
    for left, right in pairs:
        product = left * right
        for probe in range(probes):
            lines.append(
                jnp.sum(product[probe * elements : (probe + 1) * elements], axis=0, keepdims=True)
            )
    products_ref[...] = jnp.broadcast_to(as_row(lines, products_ref.shape[-1]), products_ref.shape)


def live_column(count_ref, elements):
    return lax.broadcasted_iota(jnp.int32, (elements, 1), 0) < count_ref[0, 0, 0]


def begin(refs, partner, count_ref, prepare):
    links_hbm, index_hbm, visc_hbm, rhs_hbm, *matrices_hbm = refs["operands"]
    links_ref, index_ref, visc_ref, rhs_ref, *matrix_refs, arrived = refs["scratch"]
    pairs = (
        (links_hbm, links_ref),
        (index_hbm, index_ref),
        (rhs_hbm, rhs_ref),
        (matrices_hbm[0], matrix_refs[0]),
        (visc_hbm, visc_ref),
        *zip(matrices_hbm[1:], matrix_refs[1:]),
    )
    copies = [
        pltpu.make_async_copy(held, here, arrived.at[place])
        for place, (held, here) in enumerate(pairs)
    ]
    for copy in copies:
        copy.start()
    copies[0].wait()
    copies[1].wait()
    slots_ref = refs["slots"]
    me = lax.axis_index("gz")
    for step in range(1, slots_ref.shape[0] + 1):
        slots_ref[step - 1] = slot_of(partner(me, step), links_ref, index_ref)
    prepare()
    copies[4].wait()
    probes, elements, dofs = rhs_ref.shape[3:]
    live = jnp.ones((elements, 1), f32)
    if count_ref is not None:
        live = live_column(count_ref, elements).astype(f32)
    visc = as_column(visc_ref[0, 0])
    up = wide(live * visc, probes, dofs)
    down = wide(live / visc, probes, dofs)
    refs["up"][...] = up
    refs["down"][...] = down
    copies[2].wait()
    source = rhs_ref[...].reshape(probes * elements, dofs)
    if count_ref is not None:
        source = source * wide(live, probes, dofs)
    refs["source"][...] = source
    copies[3].wait()
    smoother = two_parts(matrix_refs[0][...])
    first_pre = times_parts(source, *smoother) * down
    refs["first"][...] = first_pre
    for copy in copies[5:]:
        copy.wait()
    return first_pre, up, down, smoother


def message_places(steps, probes):
    values = steps * probes
    return values, values + probes, values + probes + steps


def message_length(steps, probes, width):
    return -(-(message_places(steps, probes)[2] * (width // lane_count) + 1) // 8) * 8


def write_row(message_ref, place, row):
    pieces = row.shape[1] // lane_count
    for piece in range(pieces):
        line = place * pieces + piece
        message_ref[line : line + 1, :] = row[:, piece * lane_count : (piece + 1) * lane_count]


def read_row(message_ref, place, width):
    pieces = width // lane_count
    lines = range(place * pieces, (place + 1) * pieces)
    return jnp.concatenate([message_ref[line : line + 1, :] for line in lines], axis=1)


def near_first_kernel(*refs):
    operands, refs = refs[:6], refs[6:]
    first_ref, source_ref, up_ref, down_ref, base_ref, slots_ref, hot_ref = refs[:7]
    part_refs, refs = refs[7:11], refs[11:]
    steps, _, width = slots_ref.shape
    leave_refs, scratch = refs[:steps], refs[steps:]
    visc_ref, rhs_ref, _, k_ref = scratch[2:6]
    probes, elements, dofs = rhs_ref.shape[3:]

    def prepare():
        for step in range(steps):
            hot_ref[:, step * width : (step + 1) * width] = hot_dofs(slots_ref[step], dofs)

    first_pre, up, down, smoother = begin(
        {
            "operands": operands,
            "scratch": scratch,
            "slots": slots_ref,
            "up": up_ref,
            "down": down_ref,
            "source": source_ref,
            "first": first_ref,
        },
        lambda me, step: me ^ step,
        None,
        prepare,
    )
    stiffness = two_parts(k_ref[...])
    base = times_parts(first_pre, *stiffness) * up
    base_ref[...] = base
    second_part = (times_parts_once(base, *smoother) * down).astype(bf16)
    stacked = jnp.concatenate([*two_parts(first_pre), second_part], axis=0)
    rows = probes * elements
    for part_ref, part in zip(part_refs, smoother + stiffness):
        part_ref[...] = part
    second_at, index_at, visc_at = message_places(steps, probes)
    for step in range(1, steps + 1):
        flat_row = slots_ref[step - 1]
        over_elements = hot_elements(flat_row, elements, dofs)
        over_dofs = hot_ref[:, (step - 1) * width : step * width]
        picked = dot(stacked, over_dofs)
        first_rows = take_faces(folded(picked[: 2 * rows]), over_elements)
        second_rows = take_faces(picked[2 * rows :], over_elements)
        for probe in range(probes):
            write_row(leave_refs[step - 1], second_at + probe, second_rows[probe])
            for leave_ref in leave_refs:
                write_row(leave_ref, (step - 1) * probes + probe, first_rows[probe])
        for leave_ref in leave_refs:
            write_row(leave_ref, index_at + step - 1, flat_row.astype(f32))
    visc_line = visc_at * (width // lane_count)
    for leave_ref in leave_refs:
        leave_ref[visc_line : visc_line + 1, :elements] = visc_ref[0, 0]


def near_second_kernel(
    probes, count_ref, source_ref, up_ref, down_ref, base_ref, slots_ref, hot_ref,
    p_high_ref, p_low_ref, k_high_ref, k_low_ref, mine_ref, *refs
):
    came_refs = refs[:-2]
    second_ref, products_ref = refs[-2:]
    steps, _, width = slots_ref.shape
    members = steps + 1
    rows, dofs = source_ref.shape
    elements = rows // probes
    second_at, index_at, visc_at = message_places(steps, probes)

    def message(step):
        return mine_ref if step == 0 else came_refs[step - 1]

    def inbound_first(member, step):
        sent = message(member ^ step)
        return [
            read_row(sent, (step - 1) * probes + probe, width) for probe in range(probes)
        ]

    own_elements = [hot_elements(slots_ref[step], elements, dofs) for step in range(steps)]

    def placed_here(values):
        spreads = [spread_faces(values[step], own_elements[step]) for step in range(steps)]
        add = add_faces if len(values[0]) > probes else add_faces_once
        return add(spreads, hot_ref[...])

    up, down = up_ref[...], down_ref[...]
    live = wide(live_column(count_ref, elements).astype(f32), probes, dofs) > 0.0
    placed = folded(placed_here([high_low(inbound_first(0, step)) for step in range(1, members)]))
    image = jnp.where(live, base_ref[...] - coupling * placed, 0.0)
    second_pre = times_parts(image, p_high_ref[...], p_low_ref[...]) * down
    second_ref[...] = second_pre
    smoother = jnp.concatenate([p_high_ref[...], p_low_ref[...]], axis=0)
    visc_line = visc_at * (width // lane_count)
    values = []
    for member in range(1, members):
        sent = message(member)
        rows_of = [
            read_row(sent, index_at + step, width).astype(jnp.int32) for step in range(steps)
        ]
        over_elements = [hot_elements(flat_row, elements, dofs) for flat_row in rows_of]
        over_dofs = [hot_dofs(flat_row, dofs) for flat_row in rows_of]
        spreads = [
            spread_faces(inbound_first(member, step + 1), over_elements[step])
            for step in range(steps)
        ]
        scale = wide(-coupling / as_column(sent[visc_line : visc_line + 1, :elements]), probes, dofs)
        change = add_faces_once(spreads, jnp.concatenate(over_dofs, axis=1)) * scale
        change = change.astype(bf16)
        smoother_faces = dot(smoother, over_dofs[member - 1]).astype(bf16)
        picked = dot(jnp.concatenate([change, change], axis=1), smoother_faces)
        taken = take_faces(picked, over_elements[member - 1])
        values.append(
            [taken[probe] + read_row(sent, second_at + probe, width) for probe in range(probes)]
        )
    placed = placed_here(values)
    second_img = times_parts_once(second_pre, k_high_ref[...], k_low_ref[...])
    second_img = second_img * up - coupling * placed
    second_img = jnp.where(live, second_img, 0.0)
    source = jnp.where(live, source_ref[...], 0.0)
    inner_products(image, second_img, source, probes, products_ref)


def leave_faces(field, probes, slots_ref, leave_ref):
    elements, dofs = field.shape[0] // probes, field.shape[1]
    members = slots_ref.shape[0] + 1
    me = lax.axis_index("gz")
    for shift in range(1, members):
        flat_row = slots_ref[shift - 1]
        over_elements = hot_elements(flat_row, elements, dofs)
        parts = jnp.concatenate(two_parts(field), axis=0)
        taken = take_faces(folded(dot(parts, hot_dofs(flat_row, dofs))), over_elements)
        target = lax.rem(me + shift, members)
        for probe in range(probes):
            leave_ref[target, pl.ds(probe, 1), :] = taken[probe]
    leave_ref[me] = jnp.zeros(leave_ref.shape[1:], f32)


def placed_faces(shape, probes, slots_ref, came_ref):
    rows, dofs = shape
    elements = rows // probes
    members = slots_ref.shape[0] + 1
    me = lax.axis_index("gz")
    total = jnp.zeros(shape, f32)
    for shift in range(1, members):
        flat_row = slots_ref[shift - 1]
        came = came_ref[lax.rem(me + shift, members)]
        values = [came[probe : probe + 1, :] for probe in range(probes)]
        spread = spread_faces(high_low(values), hot_elements(flat_row, elements, dofs))
        total += folded(add_faces([spread], hot_dofs(flat_row, dofs)))
    return total


def far_first_kernel(*refs):
    count_ref, *operands = refs[:6]
    refs = refs[6:]
    first_ref, source_ref, up_ref, down_ref, slots_ref, leave_ref = refs[:6]
    members = slots_ref.shape[0] + 1
    first_pre, *_ = begin(
        {
            "operands": operands,
            "scratch": refs[6:],
            "slots": slots_ref,
            "up": up_ref,
            "down": down_ref,
            "source": source_ref,
            "first": first_ref,
        },
        lambda me, step: lax.rem(me + step, members),
        count_ref,
        lambda: None,
    )
    leave_faces(first_pre, leave_ref.shape[1], slots_ref, leave_ref)


def far_second_kernel(
    slots_ref, up_ref, down_ref, first_ref, k_ref, p_ref, came_ref,
    image_ref, second_ref, leave_ref,
):
    probes = came_ref.shape[1]
    up = up_ref[...]
    placed = placed_faces(first_ref.shape, probes, slots_ref, came_ref)
    image = times_matrix(first_ref[...], k_ref[...]) * up - jnp.where(up > 0.0, coupling * placed, 0.0)
    image_ref[...] = image
    second_pre = times_matrix(image, p_ref[...]) * down_ref[...]
    second_ref[...] = second_pre
    leave_faces(second_pre, probes, slots_ref, leave_ref)


def far_third_kernel(
    slots_ref, up_ref, source_ref, image_ref, second_ref, k_ref, came_ref, products_ref
):
    probes = came_ref.shape[1]
    up = up_ref[...]
    placed = placed_faces(source_ref.shape, probes, slots_ref, came_ref)
    second_img = times_matrix(second_ref[...], k_ref[...]) * up - jnp.where(up > 0.0, coupling * placed, 0.0)
    inner_products(image_ref[...], second_img, source_ref[...], probes, products_ref)


def last_kernel(probes, count_ref, first_ref, second_ref, parts_ref, out_ref):
    rows, _ = first_ref.shape
    elements = rows // probes
    total = jnp.sum(parts_ref[...], axis=0)
    live = live_column(count_ref, elements)
    for probe in range(probes):
        self_one, cross_mid, self_two, load_one, load_two = (
            total[:, place * probes + probe : place * probes + probe + 1] for place in range(5)
        )
        determinant = self_one * self_two - cross_mid * cross_mid
        weight_one = (self_two * load_one - cross_mid * load_two) / determinant
        weight_two = (self_one * load_two - cross_mid * load_one) / determinant
        block = pl.ds(probe * elements, elements)
        value = weight_one * first_ref[block, :] + weight_two * second_ref[block, :]
        out_ref[block, :] = jnp.where(live, value, 0.0)


def call(kernel, in_specs, out_shapes, flops, *args, scratch=()):
    return pl.pallas_call(
        kernel,
        out_shape=out_shapes,
        in_specs=in_specs,
        out_specs=jax.tree.map(lambda _: vmem_spec, out_shapes),
        scratch_shapes=scratch,
        compiler_params=pltpu.CompilerParams(vmem_limit_bytes=vmem_grant),
        cost_estimate=pl.CostEstimate(flops=flops, bytes_accessed=1 << 20, transcendentals=0),
    )(*args)


def begin_call(kernel, out_shapes, flops, scalars, *fetched):
    links, *others = fetched
    scratch = [pltpu.SMEM(links.shape, links.dtype)]
    scratch += [pltpu.VMEM(value.shape, value.dtype) for value in others]
    return call(
        kernel,
        [smem_spec] * len(scalars) + [hbm_spec] * len(fetched),
        out_shapes,
        flops,
        *scalars,
        *(pltpu.with_memory_space_constraint(value, pltpu.HBM) for value in fetched),
        scratch=scratch + [pltpu.SemaphoreType.DMA((len(fetched),))],
    )


def near_steps(members, shapes, arguments):
    rhs, viscosity, counts, neighbours, face_index, k_matrix, p_matrix = arguments
    field, slots_shape, products_shape = shapes
    rows, dofs = field.shape
    steps, _, width = slots_shape.shape
    probes = rhs.shape[3]
    flops = 8 * rows * dofs * steps * width
    hot = jax.ShapeDtypeStruct((dofs, steps * width), bf16)
    message = jax.ShapeDtypeStruct((message_length(steps, probes, width), lane_count), f32)
    part = jax.ShapeDtypeStruct(p_matrix.shape, bf16)
    first_pre, source, up, down, base, slots, hot_own, *rest = begin_call(
        near_first_kernel,
        [field] * 5 + [slots_shape, hot] + [part] * 4 + [message] * steps,
        2 * flops,
        (),
        neighbours,
        face_index,
        viscosity,
        rhs,
        p_matrix,
        k_matrix,
    )
    parts, leaving = rest[:4], rest[4:]
    came = [
        lax.ppermute(
            leaving[step - 1], "gz", [(source, source ^ step) for source in range(members)]
        )
        for step in range(1, members)
    ]
    second_pre, products = call(
        functools.partial(near_second_kernel, probes),
        [smem_spec] + [vmem_spec] * (11 + steps),
        [field, products_shape],
        6 * flops,
        counts,
        source,
        up,
        down,
        base,
        slots,
        hot_own,
        *parts,
        leaving[0],
        *came,
    )
    return first_pre, second_pre, products


def far_steps(members, shapes, arguments):
    rhs, viscosity, counts, neighbours, face_index, k_matrix, p_matrix = arguments
    field, slots_shape, products_shape = shapes
    rows, dofs = field.shape
    shifts, _, width = slots_shape.shape
    flops = 8 * rows * dofs * shifts * width
    faces = jax.ShapeDtypeStruct((members, rhs.shape[3], width), f32)

    def exchange(value):
        return lax.all_to_all(value, "gz", split_axis=0, concat_axis=0)

    first_pre, source, up, down, slots, leaving = begin_call(
        far_first_kernel,
        [field] * 4 + [slots_shape, faces],
        flops,
        (counts,),
        neighbours,
        face_index,
        viscosity,
        rhs,
        p_matrix,
    )
    first_img, second_pre, leaving = call(
        far_second_kernel,
        [vmem_spec] * 7,
        [field, field, faces],
        2 * flops,
        slots,
        up,
        down,
        first_pre,
        k_matrix,
        p_matrix,
        exchange(leaving),
    )
    products = call(
        far_third_kernel,
        [vmem_spec] * 7,
        products_shape,
        flops,
        slots,
        up,
        source,
        first_img,
        second_pre,
        k_matrix,
        exchange(leaving),
    )
    return first_pre, second_pre, products


def per_device(mesh, *arguments):
    rhs, face_index = arguments[0], arguments[4]
    probes, elements, dofs = rhs.shape[3:]
    members = mesh.shape["gz"]
    lanes = -(-5 * probes // 128) * 128
    shapes = (
        jax.ShapeDtypeStruct((probes * elements, dofs), f32),
        jax.ShapeDtypeStruct((members - 1, 1, face_index.shape[-1]), jnp.int32),
        jax.ShapeDtypeStruct((mesh.size, 1, lanes), f32),
    )
    near = 1 < members <= short_group and elements <= face_index.shape[-1]
    near = near and elements * dofs < 1 << 24
    steps = near_steps if near else far_steps
    first_pre, second_pre, products = steps(members, shapes, arguments)
    result = call(
        functools.partial(last_kernel, probes),
        [smem_spec] + [vmem_spec] * 3,
        shapes[0],
        probes * elements * dofs,
        arguments[2],
        first_pre,
        second_pre,
        lax.all_to_all(products, ("gx", "gy", "gz"), split_axis=0, concat_axis=0),
    )
    return result.reshape(rhs.shape)


def solution(mesh):
    return jax.shard_map(
        functools.partial(per_device, mesh),
        mesh=mesh,
        in_specs=(
            P("gx", "gy", "gz", None, None, None),
            P("gx", "gy", "gz", None),
            P("gx", "gy", "gz"),
            P("gx", "gy", "gz", None),
            P("gx", "gy", "gz", None, None),
            P(),
            P(),
        ),
        out_specs=P("gx", "gy", "gz", None, None, None),
        check_vma=False,
    )
```

```python
import functools

import jax
import jax.numpy as jnp
from jax import lax
from jax.experimental import pallas as pl
from jax.experimental.pallas import tpu as pltpu
from jax.sharding import PartitionSpec as P

coupling = 0.5
vmem_grant = 48 * 1024 * 1024
short_group = 4
lane_count = 128
f32 = jnp.float32
bf16 = jnp.bfloat16
vmem_spec = pl.BlockSpec(memory_space=pltpu.VMEM)
smem_spec = pl.BlockSpec(memory_space=pltpu.SMEM)
hbm_spec = pl.BlockSpec(memory_space=pltpu.HBM)


def two_parts(value):
    high = value.astype(bf16)
    return high, (value - high.astype(f32)).astype(bf16)


def dot(left, right):
    return jnp.dot(left, right, preferred_element_type=f32)


def dot_transposed(left, right):
    return lax.dot_general(left, right, (((1,), (1,)), ((), ())), preferred_element_type=f32)


def times_matrix(rows, matrix):
    return times_parts(rows, *two_parts(matrix))


def times_parts(rows, mat_high, mat_low):
    count = rows.shape[0]
    row_high, row_low = two_parts(rows)
    both = dot(jnp.concatenate([row_high, row_low], axis=0), mat_high)
    return both[:count] + (both[count:] + dot(row_high, mat_low))


def times_parts_once(rows, mat_high, mat_low):
    row_high = rows.astype(bf16)
    return dot(
        jnp.concatenate([row_high, row_high], axis=1),
        jnp.concatenate([mat_high, mat_low], axis=0),
    )


def split_index(index, dofs):
    if dofs & (dofs - 1) == 0:
        return lax.shift_right_arithmetic(index, dofs.bit_length() - 1), index & (dofs - 1)
    element = jnp.floor_divide(index, dofs)
    return element, index - element * dofs


def slot_of(target, links_ref, index_ref):
    slot = jnp.int32(-1)
    for position in range(links_ref.shape[-1]):
        slot = jnp.where(links_ref[0, 0, 0, position] == target, jnp.int32(position), slot)
    row = index_ref[0, 0, 0, pl.ds(jnp.maximum(slot, 0), 1), :]
    return jnp.where(slot >= 0, row, -1)


def hot_elements(flat_row, elements, dofs):
    element, _ = split_index(flat_row, dofs)
    return lax.broadcasted_iota(jnp.int32, (elements, flat_row.shape[1]), 0) == element


def hot_dofs(flat_row, dofs):
    _, dof = split_index(flat_row, dofs)
    shape = (dofs, flat_row.shape[1])
    line = lax.broadcasted_iota(jnp.int32, shape, 0).astype(jnp.int16)
    hit = line == jnp.broadcast_to(dof.astype(jnp.int16), shape)
    return jnp.where(hit, jnp.ones(shape, bf16), jnp.zeros(shape, bf16))


def as_column(row):
    elements = row.shape[1]
    line = lax.broadcasted_iota(jnp.int32, (elements, elements), 0)
    column = lax.broadcasted_iota(jnp.int32, (elements, elements), 1)
    spread = jnp.where(line == column, jnp.broadcast_to(row, (elements, elements)), 0.0)
    return jnp.sum(spread, axis=1, keepdims=True)


def wide(column, probes, dofs):
    return jnp.broadcast_to(jnp.concatenate([column] * probes, axis=0), (probes * column.shape[0], dofs))


def take_faces(picked, over_elements):
    elements = over_elements.shape[0]
    return [
        jnp.sum(jnp.where(over_elements, picked[low : low + elements], 0.0), axis=0, keepdims=True)
        for low in range(0, picked.shape[0], elements)
    ]


def spread_faces(values, over_elements):
    return jnp.concatenate(
        [jnp.where(over_elements, value, 0.0).astype(bf16) for value in values], axis=0
    )


def high_low(values):
    highs = [value.astype(bf16).astype(f32) for value in values]
    return highs + [value - high for value, high in zip(values, highs)]


def add_faces(spreads, over_dofs):
    return dot_transposed(jnp.concatenate(spreads, axis=1), over_dofs)


def add_faces_once(spreads, over_dofs):
    return jnp.transpose(dot_transposed(over_dofs, jnp.concatenate(spreads, axis=1)))


def folded(parts):
    rows = parts.shape[0] // 2
    return parts[:rows] + parts[rows:]


def as_row(lines, lanes):
    count = -(-len(lines) // 8) * 8
    spare = jnp.zeros((count - len(lines), lines[0].shape[1]), f32)
    sums = jnp.sum(jnp.concatenate(lines + [spare], axis=0), axis=1, keepdims=True)
    line = lax.broadcasted_iota(jnp.int32, (count, lanes), 0)
    lane = lax.broadcasted_iota(jnp.int32, (count, lanes), 1)
    return jnp.sum(jnp.where(line == lane, sums, 0.0), axis=0, keepdims=True)


def inner_products(first_img, second_img, source, probes, products_ref):
    elements = source.shape[0] // probes
    pairs = (
        (first_img, first_img),
        (first_img, second_img),
        (second_img, second_img),
        (first_img, source),
        (second_img, source),
    )
    lines = []
    for left, right in pairs:
        product = left * right
        for probe in range(probes):
            lines.append(
                jnp.sum(product[probe * elements : (probe + 1) * elements], axis=0, keepdims=True)
            )
    products_ref[...] = jnp.broadcast_to(as_row(lines, products_ref.shape[-1]), products_ref.shape)


def live_column(count_ref, elements):
    return lax.broadcasted_iota(jnp.int32, (elements, 1), 0) < count_ref[0, 0, 0]


def begin(refs, partner, count_ref, prepare):
    links_hbm, index_hbm, visc_hbm, rhs_hbm, *matrices_hbm = refs["operands"]
    links_ref, index_ref, visc_ref, rhs_ref, *matrix_refs, arrived = refs["scratch"]
    pairs = (
        (links_hbm, links_ref),
        (index_hbm, index_ref),
        (rhs_hbm, rhs_ref),
        (matrices_hbm[0], matrix_refs[0]),
        (visc_hbm, visc_ref),
        *zip(matrices_hbm[1:], matrix_refs[1:]),
    )
    copies = [
        pltpu.make_async_copy(held, here, arrived.at[place])
        for place, (held, here) in enumerate(pairs)
    ]
    for copy in copies:
        copy.start()
    copies[0].wait()
    copies[1].wait()
    slots_ref = refs["slots"]
    me = lax.axis_index("gz")
    for step in range(1, slots_ref.shape[0] + 1):
        slots_ref[step - 1] = slot_of(partner(me, step), links_ref, index_ref)
    prepare()
    copies[4].wait()
    probes, elements, dofs = rhs_ref.shape[3:]
    live = jnp.ones((elements, 1), f32)
    if count_ref is not None:
        live = live_column(count_ref, elements).astype(f32)
    visc = as_column(visc_ref[0, 0])
    up = wide(live * visc, probes, dofs)
    down = wide(live / visc, probes, dofs)
    refs["up"][...] = up
    refs["down"][...] = down
    copies[2].wait()
    source = rhs_ref[...].reshape(probes * elements, dofs)
    if count_ref is not None:
        source = source * wide(live, probes, dofs)
    refs["source"][...] = source
    copies[3].wait()
    smoother = two_parts(matrix_refs[0][...])
    first_pre = times_parts(source, *smoother) * down
    refs["first"][...] = first_pre

    def wait_rest():
        for copy in copies[5:]:
            copy.wait()

    return first_pre, up, down, smoother, wait_rest


def message_places(steps, probes):
    values = steps * probes
    return values, values + probes, values + probes + steps


def message_length(steps, probes, width):
    return -(-(message_places(steps, probes)[2] * (width // lane_count) + 1) // 8) * 8


def write_row(message_ref, place, row):
    pieces = row.shape[1] // lane_count
    for piece in range(pieces):
        line = place * pieces + piece
        message_ref[line : line + 1, :] = row[:, piece * lane_count : (piece + 1) * lane_count]


def read_row(message_ref, place, width):
    pieces = width // lane_count
    lines = range(place * pieces, (place + 1) * pieces)
    return jnp.concatenate([message_ref[line : line + 1, :] for line in lines], axis=1)


def near_first_kernel(*refs):
    operands, refs = refs[:6], refs[6:]
    first_ref, source_ref, up_ref, down_ref, base_ref, slots_ref, hot_ref = refs[:7]
    part_refs, refs = refs[7:11], refs[11:]
    steps, _, width = slots_ref.shape
    leave_refs, scratch = refs[:steps], refs[steps:]
    visc_ref, rhs_ref, _, k_ref = scratch[2:6]
    probes, elements, dofs = rhs_ref.shape[3:]

    def prepare():
        for step in range(steps):
            hot_ref[:, step * width : (step + 1) * width] = hot_dofs(slots_ref[step], dofs)

    first_pre, up, down, smoother, wait_rest = begin(
        {
            "operands": operands,
            "scratch": scratch,
            "slots": slots_ref,
            "up": up_ref,
            "down": down_ref,
            "source": source_ref,
            "first": first_ref,
        },
        lambda me, step: me ^ step,
        None,
        prepare,
    )
    wait_rest()
    second_at, index_at, visc_at = message_places(steps, probes)
    slots = [slots_ref[step] for step in range(steps)]
    over_elements = [hot_elements(flat_row, elements, dofs) for flat_row in slots]
    over_dofs = [hot_ref[:, step * width : (step + 1) * width] for step in range(steps)]
    stacked = jnp.concatenate(two_parts(first_pre), axis=0)
    for step in range(steps):
        first_rows = take_faces(folded(dot(stacked, over_dofs[step])), over_elements[step])
        for leave_ref in leave_refs:
            for probe in range(probes):
                write_row(leave_ref, step * probes + probe, first_rows[probe])
            write_row(leave_ref, index_at + step, slots[step].astype(f32))
    stiffness = two_parts(k_ref[...])
    base = times_parts(first_pre, *stiffness) * up
    base_ref[...] = base
    second_part = (times_parts_once(base, *smoother) * down).astype(bf16)
    for step in range(steps):
        second_rows = take_faces(dot(second_part, over_dofs[step]), over_elements[step])
        for probe in range(probes):
            write_row(leave_refs[step], second_at + probe, second_rows[probe])
    for part_ref, part in zip(part_refs, smoother + stiffness):
        part_ref[...] = part
    visc_line = visc_at * (width // lane_count)
    for leave_ref in leave_refs:
        leave_ref[visc_line : visc_line + 1, :elements] = visc_ref[0, 0]


def near_second_kernel(
    probes, count_ref, source_ref, up_ref, down_ref, base_ref, slots_ref, hot_ref,
    p_high_ref, p_low_ref, k_high_ref, k_low_ref, mine_ref, *refs
):
    came_refs = refs[:-2]
    second_ref, products_ref = refs[-2:]
    steps, _, width = slots_ref.shape
    members = steps + 1
    rows, dofs = source_ref.shape
    elements = rows // probes
    second_at, index_at, visc_at = message_places(steps, probes)

    def message(step):
        return mine_ref if step == 0 else came_refs[step - 1]

    def inbound_first(member, step):
        sent = message(member ^ step)
        return [
            read_row(sent, (step - 1) * probes + probe, width) for probe in range(probes)
        ]

    own_elements = [hot_elements(slots_ref[step], elements, dofs) for step in range(steps)]

    def placed_here(values):
        spreads = [spread_faces(values[step], own_elements[step]) for step in range(steps)]
        add = add_faces if len(values[0]) > probes else add_faces_once
        return add(spreads, hot_ref[...])

    up, down = up_ref[...], down_ref[...]
    live = wide(live_column(count_ref, elements).astype(f32), probes, dofs) > 0.0
    placed = folded(placed_here([high_low(inbound_first(0, step)) for step in range(1, members)]))
    image = jnp.where(live, base_ref[...] - coupling * placed, 0.0)
    changes, back = [], []
    for member in range(1, members):
        rows_of = [
            read_row(message(member), index_at + step, width).astype(jnp.int32)
            for step in range(steps)
        ]
        over_elements = [hot_elements(flat_row, elements, dofs) for flat_row in rows_of]
        over_dofs = [hot_dofs(flat_row, dofs) for flat_row in rows_of]
        spreads = [
            spread_faces(inbound_first(member, step + 1), over_elements[step])
            for step in range(steps)
        ]
        changes.append(-coupling * add_faces_once(spreads, jnp.concatenate(over_dofs, axis=1)))
        back.append((over_elements[member - 1], over_dofs[member - 1]))
    second_pre = times_parts(image, p_high_ref[...], p_low_ref[...]) * down
    changes = times_parts_once(jnp.concatenate(changes, axis=0), p_high_ref[...], p_low_ref[...])
    second_ref[...] = second_pre
    values = []
    visc_line = visc_at * (width // lane_count)
    for member in range(1, members):
        sent = message(member)
        visc = as_column(sent[visc_line : visc_line + 1, :elements])
        scale = wide(1.0 / visc, probes, dofs)
        change = changes[(member - 1) * rows : member * rows] * scale
        over_elements, over_dofs = back[member - 1]
        taken = take_faces(dot(change.astype(bf16), over_dofs), over_elements)
        values.append(
            [taken[probe] + read_row(sent, second_at + probe, width) for probe in range(probes)]
        )
    placed = placed_here(values)
    second_img = times_parts_once(second_pre, k_high_ref[...], k_low_ref[...])
    second_img = second_img * up - coupling * placed
    second_img = jnp.where(live, second_img, 0.0)
    source = jnp.where(live, source_ref[...], 0.0)
    inner_products(image, second_img, source, probes, products_ref)


def leave_faces(field, probes, slots_ref, leave_ref):
    elements, dofs = field.shape[0] // probes, field.shape[1]
    members = slots_ref.shape[0] + 1
    me = lax.axis_index("gz")
    for shift in range(1, members):
        flat_row = slots_ref[shift - 1]
        over_elements = hot_elements(flat_row, elements, dofs)
        parts = jnp.concatenate(two_parts(field), axis=0)
        taken = take_faces(folded(dot(parts, hot_dofs(flat_row, dofs))), over_elements)
        target = lax.rem(me + shift, members)
        for probe in range(probes):
            leave_ref[target, pl.ds(probe, 1), :] = taken[probe]
    leave_ref[me] = jnp.zeros(leave_ref.shape[1:], f32)


def placed_faces(shape, probes, slots_ref, came_ref):
    rows, dofs = shape
    elements = rows // probes
    members = slots_ref.shape[0] + 1
    me = lax.axis_index("gz")
    total = jnp.zeros(shape, f32)
    for shift in range(1, members):
        flat_row = slots_ref[shift - 1]
        came = came_ref[lax.rem(me + shift, members)]
        values = [came[probe : probe + 1, :] for probe in range(probes)]
        spread = spread_faces(high_low(values), hot_elements(flat_row, elements, dofs))
        total += folded(add_faces([spread], hot_dofs(flat_row, dofs)))
    return total


def far_first_kernel(*refs):
    count_ref, *operands = refs[:6]
    refs = refs[6:]
    first_ref, source_ref, up_ref, down_ref, slots_ref, leave_ref = refs[:6]
    members = slots_ref.shape[0] + 1
    first_pre, *_ = begin(
        {
            "operands": operands,
            "scratch": refs[6:],
            "slots": slots_ref,
            "up": up_ref,
            "down": down_ref,
            "source": source_ref,
            "first": first_ref,
        },
        lambda me, step: lax.rem(me + step, members),
        count_ref,
        lambda: None,
    )
    leave_faces(first_pre, leave_ref.shape[1], slots_ref, leave_ref)


def far_second_kernel(
    slots_ref, up_ref, down_ref, first_ref, k_ref, p_ref, came_ref,
    image_ref, second_ref, leave_ref,
):
    probes = came_ref.shape[1]
    up = up_ref[...]
    placed = placed_faces(first_ref.shape, probes, slots_ref, came_ref)
    image = times_matrix(first_ref[...], k_ref[...]) * up - jnp.where(up > 0.0, coupling * placed, 0.0)
    image_ref[...] = image
    second_pre = times_matrix(image, p_ref[...]) * down_ref[...]
    second_ref[...] = second_pre
    leave_faces(second_pre, probes, slots_ref, leave_ref)


def far_third_kernel(
    slots_ref, up_ref, source_ref, image_ref, second_ref, k_ref, came_ref, products_ref
):
    probes = came_ref.shape[1]
    up = up_ref[...]
    placed = placed_faces(source_ref.shape, probes, slots_ref, came_ref)
    second_img = times_matrix(second_ref[...], k_ref[...]) * up - jnp.where(up > 0.0, coupling * placed, 0.0)
    inner_products(image_ref[...], second_img, source_ref[...], probes, products_ref)


def last_kernel(
    probes, count_ref, first_ref, second_ref, parts_ref, out_hbm, out_ref, left
):
    rows, _ = first_ref.shape
    elements = rows // probes
    total = jnp.sum(parts_ref[...], axis=0)
    live = live_column(count_ref, elements)
    weights = []
    for probe in range(probes):
        self_one, cross_mid, self_two, load_one, load_two = (
            total[:, place * probes + probe : place * probes + probe + 1] for place in range(5)
        )
        determinant = self_one * self_two - cross_mid * cross_mid
        weight_one = (self_two * load_one - cross_mid * load_two) / determinant
        weight_two = (self_one * load_two - cross_mid * load_one) / determinant
        weights.append((weight_one, weight_two))
    copies = []
    for probe, (weight_one, weight_two) in enumerate(weights):
        block = pl.ds(probe * elements, elements)
        value = weight_one * first_ref[block, :] + weight_two * second_ref[block, :]
        out_ref[block, :] = jnp.where(live, value, 0.0)
        copies.append(pltpu.make_async_copy(out_ref.at[block], out_hbm.at[block], left.at[probe]))
        copies[-1].start()
    for copy in copies:
        copy.wait()


def call(kernel, in_specs, out_shapes, flops, *args, scratch=(), out_spec=vmem_spec):
    return pl.pallas_call(
        kernel,
        out_shape=out_shapes,
        in_specs=in_specs,
        out_specs=jax.tree.map(lambda _: out_spec, out_shapes),
        scratch_shapes=scratch,
        compiler_params=pltpu.CompilerParams(vmem_limit_bytes=vmem_grant),
        cost_estimate=pl.CostEstimate(flops=flops, bytes_accessed=1 << 20, transcendentals=0),
    )(*args)


def begin_call(kernel, out_shapes, flops, scalars, *fetched):
    links, *others = fetched
    scratch = [pltpu.SMEM(links.shape, links.dtype)]
    scratch += [pltpu.VMEM(value.shape, value.dtype) for value in others]
    return call(
        kernel,
        [smem_spec] * len(scalars) + [hbm_spec] * len(fetched),
        out_shapes,
        flops,
        *scalars,
        *(pltpu.with_memory_space_constraint(value, pltpu.HBM) for value in fetched),
        scratch=scratch + [pltpu.SemaphoreType.DMA((len(fetched),))],
    )


def near_steps(members, shapes, arguments):
    rhs, viscosity, counts, neighbours, face_index, k_matrix, p_matrix = arguments
    field, slots_shape, products_shape = shapes
    rows, dofs = field.shape
    steps, _, width = slots_shape.shape
    probes = rhs.shape[3]
    flops = 8 * rows * dofs * steps * width
    hot = jax.ShapeDtypeStruct((dofs, steps * width), bf16)
    message = jax.ShapeDtypeStruct((message_length(steps, probes, width), lane_count), f32)
    part = jax.ShapeDtypeStruct(p_matrix.shape, bf16)
    first_pre, source, up, down, base, slots, hot_own, *rest = begin_call(
        near_first_kernel,
        [field] * 5 + [slots_shape, hot] + [part] * 4 + [message] * steps,
        2 * flops,
        (),
        neighbours,
        face_index,
        viscosity,
        rhs,
        p_matrix,
        k_matrix,
    )
    parts, leaving = rest[:4], rest[4:]
    came = [
        lax.ppermute(
            leaving[step - 1], "gz", [(source, source ^ step) for source in range(members)]
        )
        for step in range(1, members)
    ]
    second_pre, products = call(
        functools.partial(near_second_kernel, probes),
        [smem_spec] + [vmem_spec] * (11 + steps),
        [field, products_shape],
        6 * flops,
        counts,
        source,
        up,
        down,
        base,
        slots,
        hot_own,
        *parts,
        leaving[0],
        *came,
    )
    return first_pre, second_pre, products


def far_steps(members, shapes, arguments):
    rhs, viscosity, counts, neighbours, face_index, k_matrix, p_matrix = arguments
    field, slots_shape, products_shape = shapes
    rows, dofs = field.shape
    shifts, _, width = slots_shape.shape
    flops = 8 * rows * dofs * shifts * width
    faces = jax.ShapeDtypeStruct((members, rhs.shape[3], width), f32)

    def exchange(value):
        return lax.all_to_all(value, "gz", split_axis=0, concat_axis=0)

    first_pre, source, up, down, slots, leaving = begin_call(
        far_first_kernel,
        [field] * 4 + [slots_shape, faces],
        flops,
        (counts,),
        neighbours,
        face_index,
        viscosity,
        rhs,
        p_matrix,
    )
    first_img, second_pre, leaving = call(
        far_second_kernel,
        [vmem_spec] * 7,
        [field, field, faces],
        2 * flops,
        slots,
        up,
        down,
        first_pre,
        k_matrix,
        p_matrix,
        exchange(leaving),
    )
    products = call(
        far_third_kernel,
        [vmem_spec] * 7,
        products_shape,
        flops,
        slots,
        up,
        source,
        first_img,
        second_pre,
        k_matrix,
        exchange(leaving),
    )
    return first_pre, second_pre, products


def per_device(mesh, *arguments):
    rhs, face_index = arguments[0], arguments[4]
    probes, elements, dofs = rhs.shape[3:]
    members = mesh.shape["gz"]
    lanes = -(-5 * probes // 128) * 128
    shapes = (
        jax.ShapeDtypeStruct((probes * elements, dofs), f32),
        jax.ShapeDtypeStruct((members - 1, 1, face_index.shape[-1]), jnp.int32),
        jax.ShapeDtypeStruct((mesh.size, 1, lanes), f32),
    )
    near = 1 < members <= short_group and elements <= face_index.shape[-1]
    near = near and elements * dofs < 1 << 24
    steps = near_steps if near else far_steps
    first_pre, second_pre, products = steps(members, shapes, arguments)
    result = call(
        functools.partial(last_kernel, probes),
        [smem_spec] + [vmem_spec] * 3,
        shapes[0],
        probes * elements * dofs,
        arguments[2],
        first_pre,
        second_pre,
        lax.all_to_all(products, ("gx", "gy", "gz"), split_axis=0, concat_axis=0),
        scratch=[pltpu.VMEM(shapes[0].shape, f32), pltpu.SemaphoreType.DMA((probes,))],
        out_spec=hbm_spec,
    )
    return result.reshape(rhs.shape)


def solution(mesh):
    return jax.shard_map(
        functools.partial(per_device, mesh),
        mesh=mesh,
        in_specs=(
            P("gx", "gy", "gz", None, None, None),
            P("gx", "gy", "gz", None),
            P("gx", "gy", "gz"),
            P("gx", "gy", "gz", None),
            P("gx", "gy", "gz", None, None),
            P(),
            P(),
        ),
        out_specs=P("gx", "gy", "gz", None, None, None),
        check_vma=False,
    )
```

```python
import functools

import jax
import jax.numpy as jnp
from jax import lax
from jax.experimental import pallas as pl
from jax.experimental.pallas import tpu as pltpu
from jax.sharding import PartitionSpec as P

coupling = 0.5
vmem_grant = 48 * 1024 * 1024
short_group = 4
lane_count = 128
f32 = jnp.float32
bf16 = jnp.bfloat16
vmem_spec = pl.BlockSpec(memory_space=pltpu.VMEM)
smem_spec = pl.BlockSpec(memory_space=pltpu.SMEM)
hbm_spec = pl.BlockSpec(memory_space=pltpu.HBM)


def two_parts(value):
    high = value.astype(bf16)
    return high, (value - high.astype(f32)).astype(bf16)


def dot(left, right):
    return jnp.dot(left, right, preferred_element_type=f32)


def dot_transposed(left, right):
    return lax.dot_general(left, right, (((1,), (1,)), ((), ())), preferred_element_type=f32)


def times_matrix(rows, matrix):
    return times_parts(rows, *two_parts(matrix))


def times_parts(rows, mat_high, mat_low):
    count = rows.shape[0]
    row_high, row_low = two_parts(rows)
    both = dot(jnp.concatenate([row_high, row_low], axis=0), mat_high)
    return both[:count] + (both[count:] + dot(row_high, mat_low))


def times_parts_once(rows, mat_high, mat_low):
    row_high = rows.astype(bf16)
    return dot(
        jnp.concatenate([row_high, row_high], axis=1),
        jnp.concatenate([mat_high, mat_low], axis=0),
    )


def split_index(index, dofs):
    if dofs & (dofs - 1) == 0:
        return lax.shift_right_arithmetic(index, dofs.bit_length() - 1), index & (dofs - 1)
    element = jnp.floor_divide(index, dofs)
    return element, index - element * dofs


def slot_of(target, links_ref, index_ref):
    slot = jnp.int32(-1)
    for position in range(links_ref.shape[-1]):
        slot = jnp.where(links_ref[0, 0, 0, position] == target, jnp.int32(position), slot)
    row = index_ref[0, 0, 0, pl.ds(jnp.maximum(slot, 0), 1), :]
    return jnp.where(slot >= 0, row, -1)


def hot_elements(flat_row, elements, dofs):
    element, _ = split_index(flat_row, dofs)
    return lax.broadcasted_iota(jnp.int32, (elements, flat_row.shape[1]), 0) == element


def hot_dofs(flat_row, dofs):
    _, dof = split_index(flat_row, dofs)
    shape = (dofs, flat_row.shape[1])
    line = lax.broadcasted_iota(jnp.int32, shape, 0).astype(jnp.int16)
    hit = line == jnp.broadcast_to(dof.astype(jnp.int16), shape)
    return jnp.where(hit, jnp.ones(shape, bf16), jnp.zeros(shape, bf16))


def as_column(row):
    elements = row.shape[1]
    line = lax.broadcasted_iota(jnp.int32, (elements, elements), 0)
    column = lax.broadcasted_iota(jnp.int32, (elements, elements), 1)
    spread = jnp.where(line == column, jnp.broadcast_to(row, (elements, elements)), 0.0)
    return jnp.sum(spread, axis=1, keepdims=True)


def wide(column, probes, dofs):
    return jnp.broadcast_to(jnp.concatenate([column] * probes, axis=0), (probes * column.shape[0], dofs))


def take_faces(picked, over_elements):
    elements = over_elements.shape[0]
    return [
        jnp.sum(jnp.where(over_elements, picked[low : low + elements], 0.0), axis=0, keepdims=True)
        for low in range(0, picked.shape[0], elements)
    ]


def spread_faces(values, over_elements):
    return jnp.concatenate(
        [jnp.where(over_elements, value, 0.0).astype(bf16) for value in values], axis=0
    )


def high_low(values):
    highs = [value.astype(bf16).astype(f32) for value in values]
    return highs + [value - high for value, high in zip(values, highs)]


def add_faces(spreads, over_dofs):
    return dot_transposed(jnp.concatenate(spreads, axis=1), over_dofs)


def add_faces_once(spreads, over_dofs):
    return jnp.transpose(dot_transposed(over_dofs, jnp.concatenate(spreads, axis=1)))


def folded(parts):
    rows = parts.shape[0] // 2
    return parts[:rows] + parts[rows:]


def as_row(lines, lanes):
    count = -(-len(lines) // 8) * 8
    spare = jnp.zeros((count - len(lines), lines[0].shape[1]), f32)
    sums = jnp.sum(jnp.concatenate(lines + [spare], axis=0), axis=1, keepdims=True)
    line = lax.broadcasted_iota(jnp.int32, (count, lanes), 0)
    lane = lax.broadcasted_iota(jnp.int32, (count, lanes), 1)
    return jnp.sum(jnp.where(line == lane, sums, 0.0), axis=0, keepdims=True)


def inner_products(first_img, second_img, source, probes, products_ref):
    elements = source.shape[0] // probes
    pairs = (
        (first_img, first_img),
        (first_img, second_img),
        (second_img, second_img),
        (first_img, source),
        (second_img, source),
    )
    lines = []
    for left, right in pairs:
        product = left * right
        for probe in range(probes):
            lines.append(
                jnp.sum(product[probe * elements : (probe + 1) * elements], axis=0, keepdims=True)
            )
    products_ref[...] = jnp.broadcast_to(as_row(lines, products_ref.shape[-1]), products_ref.shape)


def live_column(count_ref, elements):
    return lax.broadcasted_iota(jnp.int32, (elements, 1), 0) < count_ref[0, 0, 0]


def begin(refs, partner, count_ref):
    links_hbm, index_hbm, visc_hbm, rhs_hbm, *matrices_hbm = refs["operands"]
    links_ref, index_ref, visc_ref, rhs_ref, *matrix_refs, arrived = refs["scratch"]
    pairs = (
        (links_hbm, links_ref),
        (index_hbm, index_ref),
        (rhs_hbm, rhs_ref),
        (matrices_hbm[0], matrix_refs[0]),
        (visc_hbm, visc_ref),
        *zip(matrices_hbm[1:], matrix_refs[1:]),
    )
    copies = [
        pltpu.make_async_copy(held, here, arrived.at[place])
        for place, (held, here) in enumerate(pairs)
    ]
    for copy in copies:
        copy.start()
    for copy in copies:
        copy.wait()
    probes, elements, dofs = rhs_ref.shape[3:]
    live = jnp.ones((elements, 1), f32)
    if count_ref is not None:
        live = live_column(count_ref, elements).astype(f32)
    visc = as_column(visc_ref[0, 0])
    up = wide(live * visc, probes, dofs)
    down = wide(live / visc, probes, dofs)
    source = rhs_ref[...].reshape(probes * elements, dofs)
    if count_ref is not None:
        source = source * wide(live, probes, dofs)
    smoother = two_parts(matrix_refs[0][...])
    first_pre = times_parts(source, *smoother) * down
    refs["up"][...] = up
    refs["down"][...] = down
    refs["source"][...] = source
    refs["first"][...] = first_pre
    slots_ref = refs["slots"]
    me = lax.axis_index("gz")
    slots = []
    for step in range(1, slots_ref.shape[0] + 1):
        slots.append(slot_of(partner(me, step), links_ref, index_ref))
        slots_ref[step - 1] = slots[-1]
    return first_pre, up, down, smoother, slots


def message_places(steps, probes):
    values = steps * probes
    return values, values + probes, values + probes + steps


def message_length(steps, probes, width):
    return -(-(message_places(steps, probes)[2] * (width // lane_count) + 1) // 8) * 8


def write_row(message_ref, place, row):
    pieces = row.shape[1] // lane_count
    for piece in range(pieces):
        line = place * pieces + piece
        message_ref[line : line + 1, :] = row[:, piece * lane_count : (piece + 1) * lane_count]


def read_row(message_ref, place, width):
    pieces = width // lane_count
    lines = range(place * pieces, (place + 1) * pieces)
    return jnp.concatenate([message_ref[line : line + 1, :] for line in lines], axis=1)


def near_first_kernel(*refs):
    operands, refs = refs[:6], refs[6:]
    first_ref, source_ref, up_ref, down_ref, base_ref, slots_ref, hot_ref = refs[:7]
    part_refs, refs = refs[7:11], refs[11:]
    steps, _, width = slots_ref.shape
    leave_refs, scratch = refs[:steps], refs[steps:]
    visc_ref, rhs_ref, _, k_ref = scratch[2:6]
    probes, elements, dofs = rhs_ref.shape[3:]
    first_pre, up, down, smoother, slots = begin(
        {
            "operands": operands,
            "scratch": scratch,
            "slots": slots_ref,
            "up": up_ref,
            "down": down_ref,
            "source": source_ref,
            "first": first_ref,
        },
        lambda me, step: me ^ step,
        None,
    )
    stiffness = two_parts(k_ref[...])
    base = times_parts(first_pre, *stiffness) * up
    base_ref[...] = base
    second_part = (times_parts_once(base, *smoother) * down).astype(bf16)
    stacked = jnp.concatenate([*two_parts(first_pre), second_part], axis=0)
    rows = probes * elements
    for part_ref, part in zip(part_refs, smoother + stiffness):
        part_ref[...] = part
    second_at, index_at, visc_at = message_places(steps, probes)
    for step in range(1, steps + 1):
        flat_row = slots[step - 1]
        over_elements = hot_elements(flat_row, elements, dofs)
        over_dofs = hot_dofs(flat_row, dofs)
        hot_ref[:, (step - 1) * width : step * width] = over_dofs
        picked = dot(stacked, over_dofs)
        first_rows = take_faces(folded(picked[: 2 * rows]), over_elements)
        second_rows = take_faces(picked[2 * rows :], over_elements)
        for probe in range(probes):
            write_row(leave_refs[step - 1], second_at + probe, second_rows[probe])
            for leave_ref in leave_refs:
                write_row(leave_ref, (step - 1) * probes + probe, first_rows[probe])
        for leave_ref in leave_refs:
            write_row(leave_ref, index_at + step - 1, flat_row.astype(f32))
    visc_line = visc_at * (width // lane_count)
    for leave_ref in leave_refs:
        leave_ref[visc_line : visc_line + 1, :elements] = visc_ref[0, 0]


def near_second_kernel(
    probes, count_ref, source_ref, up_ref, down_ref, base_ref, slots_ref, hot_ref,
    p_high_ref, p_low_ref, k_high_ref, k_low_ref, mine_ref, *refs
):
    came_refs = refs[:-2]
    second_ref, products_ref = refs[-2:]
    steps, _, width = slots_ref.shape
    members = steps + 1
    rows, dofs = source_ref.shape
    elements = rows // probes
    second_at, index_at, visc_at = message_places(steps, probes)

    def message(step):
        return mine_ref if step == 0 else came_refs[step - 1]

    def inbound_first(member, step):
        sent = message(member ^ step)
        return [
            read_row(sent, (step - 1) * probes + probe, width) for probe in range(probes)
        ]

    own_elements = [hot_elements(slots_ref[step], elements, dofs) for step in range(steps)]

    def placed_here(values):
        spreads = [spread_faces(values[step], own_elements[step]) for step in range(steps)]
        add = add_faces if len(values[0]) > probes else add_faces_once
        return add(spreads, hot_ref[...])

    up, down = up_ref[...], down_ref[...]
    live = wide(live_column(count_ref, elements).astype(f32), probes, dofs) > 0.0
    placed = folded(placed_here([high_low(inbound_first(0, step)) for step in range(1, members)]))
    image = jnp.where(live, base_ref[...] - coupling * placed, 0.0)
    changes, back = [], []
    for member in range(1, members):
        rows_of = [
            read_row(message(member), index_at + step, width).astype(jnp.int32)
            for step in range(steps)
        ]
        over_elements = [hot_elements(flat_row, elements, dofs) for flat_row in rows_of]
        over_dofs = [hot_dofs(flat_row, dofs) for flat_row in rows_of]
        spreads = [
            spread_faces(inbound_first(member, step + 1), over_elements[step])
            for step in range(steps)
        ]
        changes.append(-coupling * add_faces_once(spreads, jnp.concatenate(over_dofs, axis=1)))
        back.append((over_elements[member - 1], over_dofs[member - 1]))
    second_pre = times_parts(image, p_high_ref[...], p_low_ref[...]) * down
    changes = times_parts_once(jnp.concatenate(changes, axis=0), p_high_ref[...], p_low_ref[...])
    second_ref[...] = second_pre
    values = []
    visc_line = visc_at * (width // lane_count)
    for member in range(1, members):
        sent = message(member)
        visc = as_column(sent[visc_line : visc_line + 1, :elements])
        scale = wide(1.0 / visc, probes, dofs)
        change = changes[(member - 1) * rows : member * rows] * scale
        over_elements, over_dofs = back[member - 1]
        taken = take_faces(dot(change.astype(bf16), over_dofs), over_elements)
        values.append(
            [taken[probe] + read_row(sent, second_at + probe, width) for probe in range(probes)]
        )
    placed = placed_here(values)
    second_img = times_parts_once(second_pre, k_high_ref[...], k_low_ref[...])
    second_img = second_img * up - coupling * placed
    second_img = jnp.where(live, second_img, 0.0)
    source = jnp.where(live, source_ref[...], 0.0)
    inner_products(image, second_img, source, probes, products_ref)


def leave_faces(field, probes, slots_ref, leave_ref):
    elements, dofs = field.shape[0] // probes, field.shape[1]
    members = slots_ref.shape[0] + 1
    me = lax.axis_index("gz")
    for shift in range(1, members):
        flat_row = slots_ref[shift - 1]
        over_elements = hot_elements(flat_row, elements, dofs)
        parts = jnp.concatenate(two_parts(field), axis=0)
        taken = take_faces(folded(dot(parts, hot_dofs(flat_row, dofs))), over_elements)
        target = lax.rem(me + shift, members)
        for probe in range(probes):
            leave_ref[target, pl.ds(probe, 1), :] = taken[probe]
    leave_ref[me] = jnp.zeros(leave_ref.shape[1:], f32)


def placed_faces(shape, probes, slots_ref, came_ref):
    rows, dofs = shape
    elements = rows // probes
    members = slots_ref.shape[0] + 1
    me = lax.axis_index("gz")
    total = jnp.zeros(shape, f32)
    for shift in range(1, members):
        flat_row = slots_ref[shift - 1]
        came = came_ref[lax.rem(me + shift, members)]
        values = [came[probe : probe + 1, :] for probe in range(probes)]
        spread = spread_faces(high_low(values), hot_elements(flat_row, elements, dofs))
        total += folded(add_faces([spread], hot_dofs(flat_row, dofs)))
    return total


def far_first_kernel(*refs):
    count_ref, *operands = refs[:6]
    refs = refs[6:]
    first_ref, source_ref, up_ref, down_ref, slots_ref, leave_ref = refs[:6]
    members = slots_ref.shape[0] + 1
    first_pre, *_ = begin(
        {
            "operands": operands,
            "scratch": refs[6:],
            "slots": slots_ref,
            "up": up_ref,
            "down": down_ref,
            "source": source_ref,
            "first": first_ref,
        },
        lambda me, step: lax.rem(me + step, members),
        count_ref,
    )
    leave_faces(first_pre, leave_ref.shape[1], slots_ref, leave_ref)


def far_second_kernel(
    slots_ref, up_ref, down_ref, first_ref, k_ref, p_ref, came_ref,
    image_ref, second_ref, leave_ref,
):
    probes = came_ref.shape[1]
    up = up_ref[...]
    placed = placed_faces(first_ref.shape, probes, slots_ref, came_ref)
    image = times_matrix(first_ref[...], k_ref[...]) * up - jnp.where(up > 0.0, coupling * placed, 0.0)
    image_ref[...] = image
    second_pre = times_matrix(image, p_ref[...]) * down_ref[...]
    second_ref[...] = second_pre
    leave_faces(second_pre, probes, slots_ref, leave_ref)


def far_third_kernel(
    slots_ref, up_ref, source_ref, image_ref, second_ref, k_ref, came_ref, products_ref
):
    probes = came_ref.shape[1]
    up = up_ref[...]
    placed = placed_faces(source_ref.shape, probes, slots_ref, came_ref)
    second_img = times_matrix(second_ref[...], k_ref[...]) * up - jnp.where(up > 0.0, coupling * placed, 0.0)
    inner_products(image_ref[...], second_img, source_ref[...], probes, products_ref)


def last_kernel(probes, count_ref, first_ref, second_ref, parts_ref, out_ref):
    rows, _ = first_ref.shape
    elements = rows // probes
    total = jnp.sum(parts_ref[...], axis=0)
    live = live_column(count_ref, elements)
    for probe in range(probes):
        self_one, cross_mid, self_two, load_one, load_two = (
            total[:, place * probes + probe : place * probes + probe + 1] for place in range(5)
        )
        determinant = self_one * self_two - cross_mid * cross_mid
        weight_one = (self_two * load_one - cross_mid * load_two) / determinant
        weight_two = (self_one * load_two - cross_mid * load_one) / determinant
        block = pl.ds(probe * elements, elements)
        value = weight_one * first_ref[block, :] + weight_two * second_ref[block, :]
        out_ref[block, :] = jnp.where(live, value, 0.0)


def call(kernel, in_specs, out_shapes, flops, *args, scratch=()):
    return pl.pallas_call(
        kernel,
        out_shape=out_shapes,
        in_specs=in_specs,
        out_specs=jax.tree.map(lambda _: vmem_spec, out_shapes),
        scratch_shapes=scratch,
        compiler_params=pltpu.CompilerParams(vmem_limit_bytes=vmem_grant),
        cost_estimate=pl.CostEstimate(flops=flops, bytes_accessed=1 << 20, transcendentals=0),
    )(*args)


def begin_call(kernel, out_shapes, flops, scalars, *fetched):
    links, *others = fetched
    scratch = [pltpu.SMEM(links.shape, links.dtype)]
    scratch += [pltpu.VMEM(value.shape, value.dtype) for value in others]
    return call(
        kernel,
        [smem_spec] * len(scalars) + [hbm_spec] * len(fetched),
        out_shapes,
        flops,
        *scalars,
        *(pltpu.with_memory_space_constraint(value, pltpu.HBM) for value in fetched),
        scratch=scratch + [pltpu.SemaphoreType.DMA((len(fetched),))],
    )


def near_steps(members, shapes, arguments):
    rhs, viscosity, counts, neighbours, face_index, k_matrix, p_matrix = arguments
    field, slots_shape, products_shape = shapes
    rows, dofs = field.shape
    steps, _, width = slots_shape.shape
    probes = rhs.shape[3]
    flops = 8 * rows * dofs * steps * width
    hot = jax.ShapeDtypeStruct((dofs, steps * width), bf16)
    message = jax.ShapeDtypeStruct((message_length(steps, probes, width), lane_count), f32)
    part = jax.ShapeDtypeStruct(p_matrix.shape, bf16)
    first_pre, source, up, down, base, slots, hot_own, *rest = begin_call(
        near_first_kernel,
        [field] * 5 + [slots_shape, hot] + [part] * 4 + [message] * steps,
        2 * flops,
        (),
        neighbours,
        face_index,
        viscosity,
        rhs,
        p_matrix,
        k_matrix,
    )
    parts, leaving = rest[:4], rest[4:]
    came = [
        lax.ppermute(
            leaving[step - 1], "gz", [(source, source ^ step) for source in range(members)]
        )
        for step in range(1, members)
    ]
    second_pre, products = call(
        functools.partial(near_second_kernel, probes),
        [smem_spec] + [vmem_spec] * (11 + steps),
        [field, products_shape],
        6 * flops,
        counts,
        source,
        up,
        down,
        base,
        slots,
        hot_own,
        *parts,
        leaving[0],
        *came,
    )
    return first_pre, second_pre, products


def far_steps(members, shapes, arguments):
    rhs, viscosity, counts, neighbours, face_index, k_matrix, p_matrix = arguments
    field, slots_shape, products_shape = shapes
    rows, dofs = field.shape
    shifts, _, width = slots_shape.shape
    flops = 8 * rows * dofs * shifts * width
    faces = jax.ShapeDtypeStruct((members, rhs.shape[3], width), f32)

    def exchange(value):
        return lax.all_to_all(value, "gz", split_axis=0, concat_axis=0)

    first_pre, source, up, down, slots, leaving = begin_call(
        far_first_kernel,
        [field] * 4 + [slots_shape, faces],
        flops,
        (counts,),
        neighbours,
        face_index,
        viscosity,
        rhs,
        p_matrix,
    )
    first_img, second_pre, leaving = call(
        far_second_kernel,
        [vmem_spec] * 7,
        [field, field, faces],
        2 * flops,
        slots,
        up,
        down,
        first_pre,
        k_matrix,
        p_matrix,
        exchange(leaving),
    )
    products = call(
        far_third_kernel,
        [vmem_spec] * 7,
        products_shape,
        flops,
        slots,
        up,
        source,
        first_img,
        second_pre,
        k_matrix,
        exchange(leaving),
    )
    return first_pre, second_pre, products


def per_device(mesh, *arguments):
    rhs, face_index = arguments[0], arguments[4]
    probes, elements, dofs = rhs.shape[3:]
    members = mesh.shape["gz"]
    lanes = -(-5 * probes // 128) * 128
    shapes = (
        jax.ShapeDtypeStruct((probes * elements, dofs), f32),
        jax.ShapeDtypeStruct((members - 1, 1, face_index.shape[-1]), jnp.int32),
        jax.ShapeDtypeStruct((mesh.size, 1, lanes), f32),
    )
    near = 1 < members <= short_group and elements <= face_index.shape[-1]
    near = near and elements * dofs < 1 << 24
    steps = near_steps if near else far_steps
    first_pre, second_pre, products = steps(members, shapes, arguments)
    result = call(
        functools.partial(last_kernel, probes),
        [smem_spec] + [vmem_spec] * 3,
        shapes[0],
        probes * elements * dofs,
        arguments[2],
        first_pre,
        second_pre,
        lax.all_to_all(products, ("gx", "gy", "gz"), split_axis=0, concat_axis=0),
    )
    return result.reshape(rhs.shape)


def solution(mesh):
    return jax.shard_map(
        functools.partial(per_device, mesh),
        mesh=mesh,
        in_specs=(
            P("gx", "gy", "gz", None, None, None),
            P("gx", "gy", "gz", None),
            P("gx", "gy", "gz"),
            P("gx", "gy", "gz", None),
            P("gx", "gy", "gz", None, None),
            P(),
            P(),
        ),
        out_specs=P("gx", "gy", "gz", None, None, None),
        check_vma=False,
    )
```

```python
import functools

import jax
import jax.numpy as jnp
from jax import lax
from jax.experimental import pallas as pl
from jax.experimental.pallas import tpu as pltpu
from jax.sharding import PartitionSpec as P

coupling = 0.5
vmem_grant = 48 * 1024 * 1024
short_group = 4
lane_count = 128
f32 = jnp.float32
bf16 = jnp.bfloat16
vmem_spec = pl.BlockSpec(memory_space=pltpu.VMEM)
smem_spec = pl.BlockSpec(memory_space=pltpu.SMEM)
hbm_spec = pl.BlockSpec(memory_space=pltpu.HBM)


def two_parts(value):
    high = value.astype(bf16)
    return high, (value - high.astype(f32)).astype(bf16)


def dot(left, right):
    return jnp.dot(left, right, preferred_element_type=f32)


def dot_transposed(left, right):
    return lax.dot_general(left, right, (((1,), (1,)), ((), ())), preferred_element_type=f32)


def times_matrix(rows, matrix):
    return times_parts(rows, *two_parts(matrix))


def times_parts(rows, mat_high, mat_low):
    count = rows.shape[0]
    row_high, row_low = two_parts(rows)
    both = dot(jnp.concatenate([row_high, row_low], axis=0), mat_high)
    return both[:count] + (both[count:] + dot(row_high, mat_low))


def times_parts_once(rows, mat_high, mat_low):
    row_high = rows.astype(bf16)
    return dot(
        jnp.concatenate([row_high, row_high], axis=1),
        jnp.concatenate([mat_high, mat_low], axis=0),
    )


def split_index(index, dofs):
    if dofs & (dofs - 1) == 0:
        return lax.shift_right_arithmetic(index, dofs.bit_length() - 1), index & (dofs - 1)
    element = jnp.floor_divide(index, dofs)
    return element, index - element * dofs


def slot_of(target, links_ref, index_ref):
    slot = jnp.int32(-1)
    for position in range(links_ref.shape[-1]):
        slot = jnp.where(links_ref[0, 0, 0, position] == target, jnp.int32(position), slot)
    row = index_ref[0, 0, 0, pl.ds(jnp.maximum(slot, 0), 1), :]
    return jnp.where(slot >= 0, row, -1)


def hot_elements(flat_row, elements, dofs):
    element, _ = split_index(flat_row, dofs)
    return lax.broadcasted_iota(jnp.int32, (elements, flat_row.shape[1]), 0) == element


def hot_dofs(flat_row, dofs):
    _, dof = split_index(flat_row, dofs)
    shape = (dofs, flat_row.shape[1])
    line = lax.broadcasted_iota(jnp.int32, shape, 0).astype(jnp.int16)
    hit = line == jnp.broadcast_to(dof.astype(jnp.int16), shape)
    return jnp.where(hit, jnp.ones(shape, bf16), jnp.zeros(shape, bf16))


def as_column(row):
    elements = row.shape[1]
    line = lax.broadcasted_iota(jnp.int32, (elements, elements), 0)
    column = lax.broadcasted_iota(jnp.int32, (elements, elements), 1)
    spread = jnp.where(line == column, jnp.broadcast_to(row, (elements, elements)), 0.0)
    return jnp.sum(spread, axis=1, keepdims=True)


def wide(column, probes, dofs):
    return jnp.broadcast_to(jnp.concatenate([column] * probes, axis=0), (probes * column.shape[0], dofs))


def take_faces(picked, over_elements):
    elements = over_elements.shape[0]
    return [
        jnp.sum(jnp.where(over_elements, picked[low : low + elements], 0.0), axis=0, keepdims=True)
        for low in range(0, picked.shape[0], elements)
    ]


def spread_faces(values, over_elements):
    return jnp.concatenate(
        [jnp.where(over_elements, value, 0.0).astype(bf16) for value in values], axis=0
    )


def high_low(values):
    highs = [value.astype(bf16).astype(f32) for value in values]
    return highs + [value - high for value, high in zip(values, highs)]


def add_faces(spreads, over_dofs):
    return dot_transposed(jnp.concatenate(spreads, axis=1), over_dofs)


def add_faces_once(spreads, over_dofs):
    return jnp.transpose(dot_transposed(over_dofs, jnp.concatenate(spreads, axis=1)))


def folded(parts):
    rows = parts.shape[0] // 2
    return parts[:rows] + parts[rows:]


def as_row(lines, lanes):
    count = -(-len(lines) // 8) * 8
    spare = jnp.zeros((count - len(lines), lines[0].shape[1]), f32)
    sums = jnp.sum(jnp.concatenate(lines + [spare], axis=0), axis=1, keepdims=True)
    line = lax.broadcasted_iota(jnp.int32, (count, lanes), 0)
    lane = lax.broadcasted_iota(jnp.int32, (count, lanes), 1)
    return jnp.sum(jnp.where(line == lane, sums, 0.0), axis=0, keepdims=True)


def inner_products(first_img, second_img, source, probes, products_ref):
    elements = source.shape[0] // probes
    pairs = (
        (first_img, first_img),
        (first_img, second_img),
        (second_img, second_img),
        (first_img, source),
        (second_img, source),
    )
    lines = []
    for left, right in pairs:
        product = left * right
        for probe in range(probes):
            lines.append(
                jnp.sum(product[probe * elements : (probe + 1) * elements], axis=0, keepdims=True)
            )
    products_ref[...] = jnp.broadcast_to(as_row(lines, products_ref.shape[-1]), products_ref.shape)


def live_column(count_ref, elements):
    return lax.broadcasted_iota(jnp.int32, (elements, 1), 0) < count_ref[0, 0, 0]


def begin(refs, partner, count_ref, prepare):
    links_hbm, index_hbm, visc_hbm, rhs_hbm, *matrices_hbm = refs["operands"]
    links_ref, index_ref, visc_ref, rhs_ref, *matrix_refs, arrived = refs["scratch"]
    pairs = (
        (links_hbm, links_ref),
        (index_hbm, index_ref),
        (rhs_hbm, rhs_ref),
        (matrices_hbm[0], matrix_refs[0]),
        (visc_hbm, visc_ref),
        *zip(matrices_hbm[1:], matrix_refs[1:]),
    )
    copies = [
        pltpu.make_async_copy(held, here, arrived.at[place])
        for place, (held, here) in enumerate(pairs)
    ]
    for copy in copies:
        copy.start()
    copies[0].wait()
    copies[1].wait()
    slots_ref = refs["slots"]
    me = lax.axis_index("gz")
    for step in range(1, slots_ref.shape[0] + 1):
        slots_ref[step - 1] = slot_of(partner(me, step), links_ref, index_ref)
    prepare()
    copies[4].wait()
    probes, elements, dofs = rhs_ref.shape[3:]
    live = jnp.ones((elements, 1), f32)
    if count_ref is not None:
        live = live_column(count_ref, elements).astype(f32)
    visc = as_column(visc_ref[0, 0])
    up = wide(live * visc, probes, dofs)
    down = wide(live / visc, probes, dofs)
    refs["up"][...] = up
    refs["down"][...] = down
    copies[2].wait()
    source = rhs_ref[...].reshape(probes * elements, dofs)
    if count_ref is not None:
        source = source * wide(live, probes, dofs)
    refs["source"][...] = source
    copies[3].wait()
    smoother = two_parts(matrix_refs[0][...])
    first_pre = times_parts(source, *smoother) * down
    refs["first"][...] = first_pre
    for copy in copies[5:]:
        copy.wait()
    return first_pre, up, down, smoother


def message_places(steps, probes):
    values = steps * probes
    return values, values + probes, values + probes + steps


def message_length(steps, probes, width):
    return message_places(steps, probes)[2] * (width // lane_count) + 1


def write_row(message_ref, place, row):
    pieces = row.shape[1] // lane_count
    for piece in range(pieces):
        lanes = slice(piece * lane_count, (piece + 1) * lane_count)
        message_ref[place * pieces + piece] = row[:, lanes]


def read_row(message_ref, place, width):
    pieces = width // lane_count
    lines = range(place * pieces, (place + 1) * pieces)
    return jnp.concatenate([message_ref[line] for line in lines], axis=1)


def near_first_kernel(*refs):
    operands, refs = refs[:6], refs[6:]
    first_ref, source_ref, up_ref, down_ref, base_ref, slots_ref, hot_ref = refs[:7]
    part_refs, refs = refs[7:11], refs[11:]
    steps, _, width = slots_ref.shape
    leave_refs, scratch = refs[:steps], refs[steps:]
    visc_ref, rhs_ref, _, k_ref = scratch[2:6]
    probes, elements, dofs = rhs_ref.shape[3:]

    def prepare():
        for step in range(steps):
            hot_ref[:, step * width : (step + 1) * width] = hot_dofs(slots_ref[step], dofs)

    first_pre, up, down, smoother = begin(
        {
            "operands": operands,
            "scratch": scratch,
            "slots": slots_ref,
            "up": up_ref,
            "down": down_ref,
            "source": source_ref,
            "first": first_ref,
        },
        lambda me, step: me ^ step,
        None,
        prepare,
    )
    stiffness = two_parts(k_ref[...])
    base = times_parts(first_pre, *stiffness) * up
    base_ref[...] = base
    second_part = (times_parts_once(base, *smoother) * down).astype(bf16)
    stacked = jnp.concatenate([*two_parts(first_pre), second_part], axis=0)
    rows = probes * elements
    for part_ref, part in zip(part_refs, smoother + stiffness):
        part_ref[...] = part
    second_at, index_at, visc_at = message_places(steps, probes)
    for step in range(1, steps + 1):
        flat_row = slots_ref[step - 1]
        over_elements = hot_elements(flat_row, elements, dofs)
        over_dofs = hot_ref[:, (step - 1) * width : step * width]
        picked = dot(stacked, over_dofs)
        first_rows = take_faces(folded(picked[: 2 * rows]), over_elements)
        second_rows = take_faces(picked[2 * rows :], over_elements)
        for probe in range(probes):
            write_row(leave_refs[step - 1], second_at + probe, second_rows[probe])
            for leave_ref in leave_refs:
                write_row(leave_ref, (step - 1) * probes + probe, first_rows[probe])
        for leave_ref in leave_refs:
            write_row(leave_ref, index_at + step - 1, flat_row.astype(f32))
    visc_line = visc_at * (width // lane_count)
    for leave_ref in leave_refs:
        leave_ref[visc_line, :, :elements] = visc_ref[0, 0]


def near_second_kernel(
    probes, count_ref, source_ref, up_ref, down_ref, base_ref, slots_ref, hot_ref,
    p_high_ref, p_low_ref, k_high_ref, k_low_ref, mine_ref, *refs
):
    came_refs = refs[:-2]
    second_ref, products_ref = refs[-2:]
    steps, _, width = slots_ref.shape
    members = steps + 1
    rows, dofs = source_ref.shape
    elements = rows // probes
    second_at, index_at, visc_at = message_places(steps, probes)

    def message(step):
        return mine_ref if step == 0 else came_refs[step - 1]

    def inbound_first(member, step):
        sent = message(member ^ step)
        return [
            read_row(sent, (step - 1) * probes + probe, width) for probe in range(probes)
        ]

    own_elements = [hot_elements(slots_ref[step], elements, dofs) for step in range(steps)]

    def placed_here(values):
        spreads = [spread_faces(values[step], own_elements[step]) for step in range(steps)]
        add = add_faces if len(values[0]) > probes else add_faces_once
        return add(spreads, hot_ref[...])

    up, down = up_ref[...], down_ref[...]
    live = wide(live_column(count_ref, elements).astype(f32), probes, dofs) > 0.0
    placed = folded(placed_here([high_low(inbound_first(0, step)) for step in range(1, members)]))
    image = jnp.where(live, base_ref[...] - coupling * placed, 0.0)
    changes, back = [], []
    for member in range(1, members):
        rows_of = [
            read_row(message(member), index_at + step, width).astype(jnp.int32)
            for step in range(steps)
        ]
        over_elements = [hot_elements(flat_row, elements, dofs) for flat_row in rows_of]
        over_dofs = [hot_dofs(flat_row, dofs) for flat_row in rows_of]
        spreads = [
            spread_faces(inbound_first(member, step + 1), over_elements[step])
            for step in range(steps)
        ]
        changes.append(-coupling * add_faces_once(spreads, jnp.concatenate(over_dofs, axis=1)))
        back.append((over_elements[member - 1], over_dofs[member - 1]))
    second_pre = times_parts(image, p_high_ref[...], p_low_ref[...]) * down
    changes = times_parts_once(jnp.concatenate(changes, axis=0), p_high_ref[...], p_low_ref[...])
    second_ref[...] = second_pre
    values = []
    visc_line = visc_at * (width // lane_count)
    for member in range(1, members):
        sent = message(member)
        visc = as_column(sent[visc_line, :, :elements])
        scale = wide(1.0 / visc, probes, dofs)
        change = changes[(member - 1) * rows : member * rows] * scale
        over_elements, over_dofs = back[member - 1]
        taken = take_faces(dot(change.astype(bf16), over_dofs), over_elements)
        values.append(
            [taken[probe] + read_row(sent, second_at + probe, width) for probe in range(probes)]
        )
    placed = placed_here(values)
    second_img = times_parts_once(second_pre, k_high_ref[...], k_low_ref[...])
    second_img = second_img * up - coupling * placed
    second_img = jnp.where(live, second_img, 0.0)
    source = jnp.where(live, source_ref[...], 0.0)
    inner_products(image, second_img, source, probes, products_ref)


def leave_faces(field, probes, slots_ref, leave_ref):
    elements, dofs = field.shape[0] // probes, field.shape[1]
    members = slots_ref.shape[0] + 1
    me = lax.axis_index("gz")
    for shift in range(1, members):
        flat_row = slots_ref[shift - 1]
        over_elements = hot_elements(flat_row, elements, dofs)
        parts = jnp.concatenate(two_parts(field), axis=0)
        taken = take_faces(folded(dot(parts, hot_dofs(flat_row, dofs))), over_elements)
        target = lax.rem(me + shift, members)
        for probe in range(probes):
            leave_ref[target, pl.ds(probe, 1), :] = taken[probe]
    leave_ref[me] = jnp.zeros(leave_ref.shape[1:], f32)


def placed_faces(shape, probes, slots_ref, came_ref):
    rows, dofs = shape
    elements = rows // probes
    members = slots_ref.shape[0] + 1
    me = lax.axis_index("gz")
    total = jnp.zeros(shape, f32)
    for shift in range(1, members):
        flat_row = slots_ref[shift - 1]
        came = came_ref[lax.rem(me + shift, members)]
        values = [came[probe : probe + 1, :] for probe in range(probes)]
        spread = spread_faces(high_low(values), hot_elements(flat_row, elements, dofs))
        total += folded(add_faces([spread], hot_dofs(flat_row, dofs)))
    return total


def far_first_kernel(*refs):
    count_ref, *operands = refs[:6]
    refs = refs[6:]
    first_ref, source_ref, up_ref, down_ref, slots_ref, leave_ref = refs[:6]
    members = slots_ref.shape[0] + 1
    first_pre, *_ = begin(
        {
            "operands": operands,
            "scratch": refs[6:],
            "slots": slots_ref,
            "up": up_ref,
            "down": down_ref,
            "source": source_ref,
            "first": first_ref,
        },
        lambda me, step: lax.rem(me + step, members),
        count_ref,
        lambda: None,
    )
    leave_faces(first_pre, leave_ref.shape[1], slots_ref, leave_ref)


def far_second_kernel(
    slots_ref, up_ref, down_ref, first_ref, k_ref, p_ref, came_ref,
    image_ref, second_ref, leave_ref,
):
    probes = came_ref.shape[1]
    up = up_ref[...]
    placed = placed_faces(first_ref.shape, probes, slots_ref, came_ref)
    image = times_matrix(first_ref[...], k_ref[...]) * up - jnp.where(up > 0.0, coupling * placed, 0.0)
    image_ref[...] = image
    second_pre = times_matrix(image, p_ref[...]) * down_ref[...]
    second_ref[...] = second_pre
    leave_faces(second_pre, probes, slots_ref, leave_ref)


def far_third_kernel(
    slots_ref, up_ref, source_ref, image_ref, second_ref, k_ref, came_ref, products_ref
):
    probes = came_ref.shape[1]
    up = up_ref[...]
    placed = placed_faces(source_ref.shape, probes, slots_ref, came_ref)
    second_img = times_matrix(second_ref[...], k_ref[...]) * up - jnp.where(up > 0.0, coupling * placed, 0.0)
    inner_products(image_ref[...], second_img, source_ref[...], probes, products_ref)


def last_kernel(probes, count_ref, first_ref, second_ref, parts_ref, out_ref):
    rows, _ = first_ref.shape
    elements = rows // probes
    total = jnp.sum(parts_ref[...], axis=0)
    live = live_column(count_ref, elements)
    for probe in range(probes):
        self_one, cross_mid, self_two, load_one, load_two = (
            total[:, place * probes + probe : place * probes + probe + 1] for place in range(5)
        )
        determinant = self_one * self_two - cross_mid * cross_mid
        weight_one = (self_two * load_one - cross_mid * load_two) / determinant
        weight_two = (self_one * load_two - cross_mid * load_one) / determinant
        block = pl.ds(probe * elements, elements)
        value = weight_one * first_ref[block, :] + weight_two * second_ref[block, :]
        out_ref[block, :] = jnp.where(live, value, 0.0)


def call(kernel, in_specs, out_shapes, flops, *args, scratch=()):
    return pl.pallas_call(
        kernel,
        out_shape=out_shapes,
        in_specs=in_specs,
        out_specs=jax.tree.map(lambda _: vmem_spec, out_shapes),
        scratch_shapes=scratch,
        compiler_params=pltpu.CompilerParams(vmem_limit_bytes=vmem_grant),
        cost_estimate=pl.CostEstimate(flops=flops, bytes_accessed=1 << 20, transcendentals=0),
    )(*args)


def begin_call(kernel, out_shapes, flops, scalars, *fetched):
    links, *others = fetched
    scratch = [pltpu.SMEM(links.shape, links.dtype)]
    scratch += [pltpu.VMEM(value.shape, value.dtype) for value in others]
    return call(
        kernel,
        [smem_spec] * len(scalars) + [hbm_spec] * len(fetched),
        out_shapes,
        flops,
        *scalars,
        *(pltpu.with_memory_space_constraint(value, pltpu.HBM) for value in fetched),
        scratch=scratch + [pltpu.SemaphoreType.DMA((len(fetched),))],
    )


def near_steps(members, shapes, arguments):
    rhs, viscosity, counts, neighbours, face_index, k_matrix, p_matrix = arguments
    field, slots_shape, products_shape = shapes
    rows, dofs = field.shape
    steps, _, width = slots_shape.shape
    probes = rhs.shape[3]
    flops = 8 * rows * dofs * steps * width
    hot = jax.ShapeDtypeStruct((dofs, steps * width), bf16)
    message = jax.ShapeDtypeStruct((message_length(steps, probes, width), 1, lane_count), f32)
    part = jax.ShapeDtypeStruct(p_matrix.shape, bf16)
    first_pre, source, up, down, base, slots, hot_own, *rest = begin_call(
        near_first_kernel,
        [field] * 5 + [slots_shape, hot] + [part] * 4 + [message] * steps,
        2 * flops,
        (),
        neighbours,
        face_index,
        viscosity,
        rhs,
        p_matrix,
        k_matrix,
    )
    parts, leaving = rest[:4], rest[4:]
    came = [
        lax.ppermute(
            leaving[step - 1], "gz", [(source, source ^ step) for source in range(members)]
        )
        for step in range(1, members)
    ]
    second_pre, products = call(
        functools.partial(near_second_kernel, probes),
        [smem_spec] + [vmem_spec] * (11 + steps),
        [field, products_shape],
        6 * flops,
        counts,
        source,
        up,
        down,
        base,
        slots,
        hot_own,
        *parts,
        leaving[0],
        *came,
    )
    return first_pre, second_pre, products


def far_steps(members, shapes, arguments):
    rhs, viscosity, counts, neighbours, face_index, k_matrix, p_matrix = arguments
    field, slots_shape, products_shape = shapes
    rows, dofs = field.shape
    shifts, _, width = slots_shape.shape
    flops = 8 * rows * dofs * shifts * width
    faces = jax.ShapeDtypeStruct((members, rhs.shape[3], width), f32)

    def exchange(value):
        return lax.all_to_all(value, "gz", split_axis=0, concat_axis=0)

    first_pre, source, up, down, slots, leaving = begin_call(
        far_first_kernel,
        [field] * 4 + [slots_shape, faces],
        flops,
        (counts,),
        neighbours,
        face_index,
        viscosity,
        rhs,
        p_matrix,
    )
    first_img, second_pre, leaving = call(
        far_second_kernel,
        [vmem_spec] * 7,
        [field, field, faces],
        2 * flops,
        slots,
        up,
        down,
        first_pre,
        k_matrix,
        p_matrix,
        exchange(leaving),
    )
    products = call(
        far_third_kernel,
        [vmem_spec] * 7,
        products_shape,
        flops,
        slots,
        up,
        source,
        first_img,
        second_pre,
        k_matrix,
        exchange(leaving),
    )
    return first_pre, second_pre, products


def per_device(mesh, *arguments):
    rhs, face_index = arguments[0], arguments[4]
    probes, elements, dofs = rhs.shape[3:]
    members = mesh.shape["gz"]
    lanes = -(-5 * probes // 128) * 128
    shapes = (
        jax.ShapeDtypeStruct((probes * elements, dofs), f32),
        jax.ShapeDtypeStruct((members - 1, 1, face_index.shape[-1]), jnp.int32),
        jax.ShapeDtypeStruct((mesh.size, 1, lanes), f32),
    )
    near = 1 < members <= short_group and elements <= face_index.shape[-1]
    near = near and elements * dofs < 1 << 24
    steps = near_steps if near else far_steps
    first_pre, second_pre, products = steps(members, shapes, arguments)
    result = call(
        functools.partial(last_kernel, probes),
        [smem_spec] + [vmem_spec] * 3,
        shapes[0],
        probes * elements * dofs,
        arguments[2],
        first_pre,
        second_pre,
        lax.all_to_all(products, ("gx", "gy", "gz"), split_axis=0, concat_axis=0),
    )
    return result.reshape(rhs.shape)


def solution(mesh):
    return jax.shard_map(
        functools.partial(per_device, mesh),
        mesh=mesh,
        in_specs=(
            P("gx", "gy", "gz", None, None, None),
            P("gx", "gy", "gz", None),
            P("gx", "gy", "gz"),
            P("gx", "gy", "gz", None),
            P("gx", "gy", "gz", None, None),
            P(),
            P(),
        ),
        out_specs=P("gx", "gy", "gz", None, None, None),
        check_vma=False,
    )
```

```python
import functools

import jax
import jax.numpy as jnp
from jax import lax
from jax.experimental import pallas as pl
from jax.experimental.pallas import tpu as pltpu
from jax.sharding import PartitionSpec as P

coupling = 0.5
vmem_grant = 48 * 1024 * 1024
short_group = 4
lane_count = 128
f32 = jnp.float32
bf16 = jnp.bfloat16
vmem_spec = pl.BlockSpec(memory_space=pltpu.VMEM)
smem_spec = pl.BlockSpec(memory_space=pltpu.SMEM)
hbm_spec = pl.BlockSpec(memory_space=pltpu.HBM)


def two_parts(value):
    high = value.astype(bf16)
    return high, (value - high.astype(f32)).astype(bf16)


def dot(left, right):
    return jnp.dot(left, right, preferred_element_type=f32)


def dot_transposed(left, right):
    return lax.dot_general(left, right, (((1,), (1,)), ((), ())), preferred_element_type=f32)


def times_matrix(rows, matrix):
    return times_parts(rows, *two_parts(matrix))


def times_parts(rows, mat_high, mat_low):
    count = rows.shape[0]
    row_high, row_low = two_parts(rows)
    both = dot(jnp.concatenate([row_high, row_low], axis=0), mat_high)
    return both[:count] + (both[count:] + dot(row_high, mat_low))


def times_parts_once(rows, mat_high, mat_low):
    row_high = rows.astype(bf16)
    return dot(
        jnp.concatenate([row_high, row_high], axis=1),
        jnp.concatenate([mat_high, mat_low], axis=0),
    )


def split_index(index, dofs):
    if dofs & (dofs - 1) == 0:
        return lax.shift_right_arithmetic(index, dofs.bit_length() - 1), index & (dofs - 1)
    element = jnp.floor_divide(index, dofs)
    return element, index - element * dofs


def slot_of(target, links_ref, index_ref):
    slot = jnp.int32(-1)
    for position in range(links_ref.shape[-1]):
        slot = jnp.where(links_ref[0, 0, 0, position] == target, jnp.int32(position), slot)
    row = index_ref[0, 0, 0, pl.ds(jnp.maximum(slot, 0), 1), :]
    return jnp.where(slot >= 0, row, -1)


def hot_elements(flat_row, elements, dofs):
    element, _ = split_index(flat_row, dofs)
    return lax.broadcasted_iota(jnp.int32, (elements, flat_row.shape[1]), 0) == element


def hot_dofs(flat_row, dofs):
    _, dof = split_index(flat_row, dofs)
    shape = (dofs, flat_row.shape[1])
    line = lax.broadcasted_iota(jnp.int32, shape, 0).astype(jnp.int16)
    hit = line == jnp.broadcast_to(dof.astype(jnp.int16), shape)
    return jnp.where(hit, jnp.ones(shape, bf16), jnp.zeros(shape, bf16))


def as_column(row):
    elements = row.shape[1]
    line = lax.broadcasted_iota(jnp.int32, (elements, elements), 0)
    column = lax.broadcasted_iota(jnp.int32, (elements, elements), 1)
    spread = jnp.where(line == column, jnp.broadcast_to(row, (elements, elements)), 0.0)
    return jnp.sum(spread, axis=1, keepdims=True)


def wide(column, probes, dofs):
    return jnp.broadcast_to(jnp.concatenate([column] * probes, axis=0), (probes * column.shape[0], dofs))


def take_faces(picked, over_elements):
    elements = over_elements.shape[0]
    return [
        jnp.sum(jnp.where(over_elements, picked[low : low + elements], 0.0), axis=0, keepdims=True)
        for low in range(0, picked.shape[0], elements)
    ]


def spread_faces(values, over_elements):
    return jnp.concatenate(
        [jnp.where(over_elements, value, 0.0).astype(bf16) for value in values], axis=0
    )


def high_low(values):
    highs = [value.astype(bf16).astype(f32) for value in values]
    return highs + [value - high for value, high in zip(values, highs)]


def add_faces(spreads, over_dofs):
    return dot_transposed(jnp.concatenate(spreads, axis=1), over_dofs)


def add_faces_once(spreads, over_dofs):
    return jnp.transpose(dot_transposed(over_dofs, jnp.concatenate(spreads, axis=1)))


def folded(parts):
    rows = parts.shape[0] // 2
    return parts[:rows] + parts[rows:]


def as_row(lines, lanes):
    count = -(-len(lines) // 8) * 8
    spare = jnp.zeros((count - len(lines), lines[0].shape[1]), f32)
    sums = jnp.sum(jnp.concatenate(lines + [spare], axis=0), axis=1, keepdims=True)
    line = lax.broadcasted_iota(jnp.int32, (count, lanes), 0)
    lane = lax.broadcasted_iota(jnp.int32, (count, lanes), 1)
    return jnp.sum(jnp.where(line == lane, sums, 0.0), axis=0, keepdims=True)


def inner_products(first_img, second_img, source, probes, products_ref):
    elements = source.shape[0] // probes
    pairs = (
        (first_img, first_img),
        (first_img, second_img),
        (second_img, second_img),
        (first_img, source),
        (second_img, source),
    )
    lines = []
    for left, right in pairs:
        product = left * right
        for probe in range(probes):
            lines.append(
                jnp.sum(product[probe * elements : (probe + 1) * elements], axis=0, keepdims=True)
            )
    products_ref[...] = jnp.broadcast_to(as_row(lines, products_ref.shape[-1]), products_ref.shape)


def live_column(count_ref, elements):
    return lax.broadcasted_iota(jnp.int32, (elements, 1), 0) < count_ref[0, 0, 0]


def begin(refs, partner, count_ref, prepare):
    links_hbm, index_hbm, visc_hbm, rhs_hbm, *matrices_hbm = refs["operands"]
    links_ref, index_ref, visc_ref, rhs_ref, *matrix_refs, arrived = refs["scratch"]
    pairs = (
        (links_hbm, links_ref),
        (index_hbm, index_ref),
        (rhs_hbm, rhs_ref),
        (matrices_hbm[0], matrix_refs[0]),
        (visc_hbm, visc_ref),
        *zip(matrices_hbm[1:], matrix_refs[1:]),
    )
    copies = [
        pltpu.make_async_copy(held, here, arrived.at[place])
        for place, (held, here) in enumerate(pairs)
    ]
    for copy in copies:
        copy.start()
    copies[0].wait()
    copies[1].wait()
    slots_ref = refs["slots"]
    me = lax.axis_index("gz")
    for step in range(1, slots_ref.shape[0] + 1):
        slots_ref[step - 1] = slot_of(partner(me, step), links_ref, index_ref)
    prepare()
    copies[4].wait()
    probes, elements, dofs = rhs_ref.shape[3:]
    live = jnp.ones((elements, 1), f32)
    if count_ref is not None:
        live = live_column(count_ref, elements).astype(f32)
    visc = as_column(visc_ref[0, 0])
    up = wide(live * visc, probes, dofs)
    down = wide(live / visc, probes, dofs)
    refs["up"][...] = up
    refs["down"][...] = down
    copies[2].wait()
    source = rhs_ref[...].reshape(probes * elements, dofs)
    if count_ref is not None:
        source = source * wide(live, probes, dofs)
    refs["source"][...] = source
    copies[3].wait()
    smoother = two_parts(matrix_refs[0][...])
    first_pre = times_parts(source, *smoother) * down
    refs["first"][...] = first_pre
    for copy in copies[5:]:
        copy.wait()
    return first_pre, up, down, smoother


def message_places(steps, probes):
    values = steps * probes
    return values, values + probes, values + probes + steps


def message_length(steps, probes, width):
    return message_places(steps, probes)[2] * (width // lane_count) + 1


def write_row(message_ref, place, row):
    pieces = row.shape[1] // lane_count
    for piece in range(pieces):
        lanes = slice(piece * lane_count, (piece + 1) * lane_count)
        message_ref[place * pieces + piece] = row[:, lanes]


def read_row(message_ref, place, width):
    pieces = width // lane_count
    lines = range(place * pieces, (place + 1) * pieces)
    return jnp.concatenate([message_ref[line] for line in lines], axis=1)


def near_first_kernel(*refs):
    operands, refs = refs[:6], refs[6:]
    first_ref, source_ref, up_ref, down_ref, base_ref, slots_ref, hot_ref = refs[:7]
    part_refs, refs = refs[7:11], refs[11:]
    steps, _, width = slots_ref.shape
    leave_refs, scratch = refs[:steps], refs[steps:]
    visc_ref, rhs_ref, _, k_ref = scratch[2:6]
    probes, elements, dofs = rhs_ref.shape[3:]

    def prepare():
        for step in range(steps):
            hot_ref[:, step * width : (step + 1) * width] = hot_dofs(slots_ref[step], dofs)

    first_pre, up, down, smoother = begin(
        {
            "operands": operands,
            "scratch": scratch,
            "slots": slots_ref,
            "up": up_ref,
            "down": down_ref,
            "source": source_ref,
            "first": first_ref,
        },
        lambda me, step: me ^ step,
        None,
        prepare,
    )
    stiffness = two_parts(k_ref[...])
    base = times_parts(first_pre, *stiffness) * up
    base_ref[...] = base
    second_part = (times_parts_once(base, *smoother) * down).astype(bf16)
    stacked = jnp.concatenate([*two_parts(first_pre), second_part], axis=0)
    rows = probes * elements
    for part_ref, part in zip(part_refs, smoother + stiffness):
        part_ref[...] = part
    second_at, index_at, visc_at = message_places(steps, probes)
    for step in range(1, steps + 1):
        flat_row = slots_ref[step - 1]
        over_elements = hot_elements(flat_row, elements, dofs)
        over_dofs = hot_ref[:, (step - 1) * width : step * width]
        picked = dot(stacked, over_dofs)
        first_rows = take_faces(folded(picked[: 2 * rows]), over_elements)
        second_rows = take_faces(picked[2 * rows :], over_elements)
        for probe in range(probes):
            write_row(leave_refs[step - 1], second_at + probe, second_rows[probe])
            for leave_ref in leave_refs:
                write_row(leave_ref, (step - 1) * probes + probe, first_rows[probe])
        for leave_ref in leave_refs:
            write_row(leave_ref, index_at + step - 1, flat_row.astype(f32))
    visc_line = visc_at * (width // lane_count)
    for leave_ref in leave_refs:
        leave_ref[visc_line, :, :elements] = visc_ref[0, 0]


def near_second_kernel(
    probes, count_ref, source_ref, up_ref, down_ref, base_ref, slots_ref, hot_ref,
    p_high_ref, p_low_ref, k_high_ref, k_low_ref, mine_ref, *refs
):
    came_refs = refs[:-2]
    second_ref, products_ref = refs[-2:]
    steps, _, width = slots_ref.shape
    members = steps + 1
    rows, dofs = source_ref.shape
    elements = rows // probes
    second_at, index_at, visc_at = message_places(steps, probes)

    def message(step):
        return mine_ref if step == 0 else came_refs[step - 1]

    def inbound_first(member, step):
        sent = message(member ^ step)
        return [
            read_row(sent, (step - 1) * probes + probe, width) for probe in range(probes)
        ]

    own_elements = [hot_elements(slots_ref[step], elements, dofs) for step in range(steps)]

    def placed_here(values):
        spreads = [spread_faces(values[step], own_elements[step]) for step in range(steps)]
        add = add_faces if len(values[0]) > probes else add_faces_once
        return add(spreads, hot_ref[...])

    up, down = up_ref[...], down_ref[...]
    live = wide(live_column(count_ref, elements).astype(f32), probes, dofs) > 0.0
    placed = folded(placed_here([high_low(inbound_first(0, step)) for step in range(1, members)]))
    image = jnp.where(live, base_ref[...] - coupling * placed, 0.0)
    changes, back = [], []
    for member in range(1, members):
        rows_of = [
            read_row(message(member), index_at + step, width).astype(jnp.int32)
            for step in range(steps)
        ]
        over_elements = [hot_elements(flat_row, elements, dofs) for flat_row in rows_of]
        over_dofs = [hot_dofs(flat_row, dofs) for flat_row in rows_of]
        spreads = [
            spread_faces(inbound_first(member, step + 1), over_elements[step])
            for step in range(steps)
        ]
        changes.append(-coupling * add_faces_once(spreads, jnp.concatenate(over_dofs, axis=1)))
        back.append((over_elements[member - 1], over_dofs[member - 1]))
    second_pre = times_parts(image, p_high_ref[...], p_low_ref[...]) * down
    changes = times_parts_once(jnp.concatenate(changes, axis=0), p_high_ref[...], p_low_ref[...])
    second_ref[...] = second_pre
    values = []
    visc_line = visc_at * (width // lane_count)
    for member in range(1, members):
        sent = message(member)
        visc = as_column(sent[visc_line, :, :elements])
        scale = wide(1.0 / visc, probes, dofs)
        change = changes[(member - 1) * rows : member * rows] * scale
        over_elements, over_dofs = back[member - 1]
        taken = take_faces(dot(change.astype(bf16), over_dofs), over_elements)
        values.append(
            [taken[probe] + read_row(sent, second_at + probe, width) for probe in range(probes)]
        )
    placed = placed_here(values)
    second_img = times_parts_once(second_pre, k_high_ref[...], k_low_ref[...])
    second_img = second_img * up - coupling * placed
    second_img = jnp.where(live, second_img, 0.0)
    source = jnp.where(live, source_ref[...], 0.0)
    inner_products(image, second_img, source, probes, products_ref)


def leave_faces(field, probes, slots_ref, leave_ref):
    elements, dofs = field.shape[0] // probes, field.shape[1]
    members = slots_ref.shape[0] + 1
    me = lax.axis_index("gz")
    for shift in range(1, members):
        flat_row = slots_ref[shift - 1]
        over_elements = hot_elements(flat_row, elements, dofs)
        parts = jnp.concatenate(two_parts(field), axis=0)
        taken = take_faces(folded(dot(parts, hot_dofs(flat_row, dofs))), over_elements)
        target = lax.rem(me + shift, members)
        for probe in range(probes):
            leave_ref[target, pl.ds(probe, 1), :] = taken[probe]
    leave_ref[me] = jnp.zeros(leave_ref.shape[1:], f32)


def placed_faces(shape, probes, slots_ref, came_ref):
    rows, dofs = shape
    elements = rows // probes
    members = slots_ref.shape[0] + 1
    me = lax.axis_index("gz")
    total = jnp.zeros(shape, f32)
    for shift in range(1, members):
        flat_row = slots_ref[shift - 1]
        came = came_ref[lax.rem(me + shift, members)]
        values = [came[probe : probe + 1, :] for probe in range(probes)]
        spread = spread_faces(high_low(values), hot_elements(flat_row, elements, dofs))
        total += folded(add_faces([spread], hot_dofs(flat_row, dofs)))
    return total


def far_first_kernel(*refs):
    count_ref, *operands = refs[:6]
    refs = refs[6:]
    first_ref, source_ref, up_ref, down_ref, slots_ref, leave_ref = refs[:6]
    members = slots_ref.shape[0] + 1
    first_pre, *_ = begin(
        {
            "operands": operands,
            "scratch": refs[6:],
            "slots": slots_ref,
            "up": up_ref,
            "down": down_ref,
            "source": source_ref,
            "first": first_ref,
        },
        lambda me, step: lax.rem(me + step, members),
        count_ref,
        lambda: None,
    )
    leave_faces(first_pre, leave_ref.shape[1], slots_ref, leave_ref)


def far_second_kernel(
    slots_ref, up_ref, down_ref, first_ref, k_ref, p_ref, came_ref,
    image_ref, second_ref, leave_ref,
):
    probes = came_ref.shape[1]
    up = up_ref[...]
    placed = placed_faces(first_ref.shape, probes, slots_ref, came_ref)
    image = times_matrix(first_ref[...], k_ref[...]) * up - jnp.where(up > 0.0, coupling * placed, 0.0)
    image_ref[...] = image
    second_pre = times_matrix(image, p_ref[...]) * down_ref[...]
    second_ref[...] = second_pre
    leave_faces(second_pre, probes, slots_ref, leave_ref)


def far_third_kernel(
    slots_ref, up_ref, source_ref, image_ref, second_ref, k_ref, came_ref, products_ref
):
    probes = came_ref.shape[1]
    up = up_ref[...]
    placed = placed_faces(source_ref.shape, probes, slots_ref, came_ref)
    second_img = times_matrix(second_ref[...], k_ref[...]) * up - jnp.where(up > 0.0, coupling * placed, 0.0)
    inner_products(image_ref[...], second_img, source_ref[...], probes, products_ref)


def last_kernel(probes, count_ref, first_ref, second_ref, parts_ref, out_ref):
    rows, _ = first_ref.shape
    elements = rows // probes
    total = jnp.sum(parts_ref[...], axis=0)
    live = live_column(count_ref, elements)
    for probe in range(probes):
        self_one, cross_mid, self_two, load_one, load_two = (
            total[:, place * probes + probe : place * probes + probe + 1] for place in range(5)
        )
        determinant = self_one * self_two - cross_mid * cross_mid
        weight_one = (self_two * load_one - cross_mid * load_two) / determinant
        weight_two = (self_one * load_two - cross_mid * load_one) / determinant
        block = pl.ds(probe * elements, elements)
        value = weight_one * first_ref[block, :] + weight_two * second_ref[block, :]
        out_ref[block, :] = jnp.where(live, value, 0.0)


def call(kernel, in_specs, out_shapes, flops, *args, scratch=()):
    return pl.pallas_call(
        kernel,
        out_shape=out_shapes,
        in_specs=in_specs,
        out_specs=jax.tree.map(lambda _: vmem_spec, out_shapes),
        scratch_shapes=scratch,
        compiler_params=pltpu.CompilerParams(vmem_limit_bytes=vmem_grant),
        cost_estimate=pl.CostEstimate(flops=flops, bytes_accessed=1 << 20, transcendentals=0),
    )(*args)


def begin_call(kernel, out_shapes, flops, scalars, *fetched):
    links, *others = fetched
    scratch = [pltpu.SMEM(links.shape, links.dtype)]
    scratch += [pltpu.VMEM(value.shape, value.dtype) for value in others]
    return call(
        kernel,
        [smem_spec] * len(scalars) + [hbm_spec] * len(fetched),
        out_shapes,
        flops,
        *scalars,
        *(pltpu.with_memory_space_constraint(value, pltpu.HBM) for value in fetched),
        scratch=scratch + [pltpu.SemaphoreType.DMA((len(fetched),))],
    )


def near_steps(members, shapes, arguments):
    rhs, viscosity, counts, neighbours, face_index, k_matrix, p_matrix = arguments
    field, slots_shape, products_shape = shapes
    rows, dofs = field.shape
    steps, _, width = slots_shape.shape
    probes = rhs.shape[3]
    flops = 8 * rows * dofs * steps * width
    hot = jax.ShapeDtypeStruct((dofs, steps * width), bf16)
    message = jax.ShapeDtypeStruct((message_length(steps, probes, width), 1, lane_count), f32)
    part = jax.ShapeDtypeStruct(p_matrix.shape, bf16)
    first_pre, source, up, down, base, slots, hot_own, *rest = begin_call(
        near_first_kernel,
        [field] * 5 + [slots_shape, hot] + [part] * 4 + [message] * steps,
        2 * flops,
        (),
        neighbours,
        face_index,
        viscosity,
        rhs,
        p_matrix,
        k_matrix,
    )
    parts, leaving = rest[:4], rest[4:]
    order = [1] + list(range(members - 1, 1, -1))
    came = [
        lax.ppermute(
            leaving[step - 1], "gz", [(source, source ^ step) for source in range(members)]
        )
        for step in order
    ]
    second_pre, products = call(
        functools.partial(near_second_kernel, probes),
        [smem_spec] + [vmem_spec] * (11 + steps),
        [field, products_shape],
        6 * flops,
        counts,
        source,
        up,
        down,
        base,
        slots,
        hot_own,
        *parts,
        leaving[order[-1] - 1],
        *(came[order.index(step)] for step in range(1, members)),
    )
    return first_pre, second_pre, products


def far_steps(members, shapes, arguments):
    rhs, viscosity, counts, neighbours, face_index, k_matrix, p_matrix = arguments
    field, slots_shape, products_shape = shapes
    rows, dofs = field.shape
    shifts, _, width = slots_shape.shape
    flops = 8 * rows * dofs * shifts * width
    faces = jax.ShapeDtypeStruct((members, rhs.shape[3], width), f32)

    def exchange(value):
        return lax.all_to_all(value, "gz", split_axis=0, concat_axis=0)

    first_pre, source, up, down, slots, leaving = begin_call(
        far_first_kernel,
        [field] * 4 + [slots_shape, faces],
        flops,
        (counts,),
        neighbours,
        face_index,
        viscosity,
        rhs,
        p_matrix,
    )
    first_img, second_pre, leaving = call(
        far_second_kernel,
        [vmem_spec] * 7,
        [field, field, faces],
        2 * flops,
        slots,
        up,
        down,
        first_pre,
        k_matrix,
        p_matrix,
        exchange(leaving),
    )
    products = call(
        far_third_kernel,
        [vmem_spec] * 7,
        products_shape,
        flops,
        slots,
        up,
        source,
        first_img,
        second_pre,
        k_matrix,
        exchange(leaving),
    )
    return first_pre, second_pre, products


def per_device(mesh, *arguments):
    rhs, face_index = arguments[0], arguments[4]
    probes, elements, dofs = rhs.shape[3:]
    members = mesh.shape["gz"]
    lanes = -(-5 * probes // 128) * 128
    shapes = (
        jax.ShapeDtypeStruct((probes * elements, dofs), f32),
        jax.ShapeDtypeStruct((members - 1, 1, face_index.shape[-1]), jnp.int32),
        jax.ShapeDtypeStruct((mesh.size, 1, lanes), f32),
    )
    near = 1 < members <= short_group and elements <= face_index.shape[-1]
    near = near and elements * dofs < 1 << 24
    steps = near_steps if near else far_steps
    first_pre, second_pre, products = steps(members, shapes, arguments)
    result = call(
        functools.partial(last_kernel, probes),
        [smem_spec] + [vmem_spec] * 3,
        shapes[0],
        probes * elements * dofs,
        arguments[2],
        first_pre,
        second_pre,
        lax.all_to_all(products, ("gx", "gy", "gz"), split_axis=0, concat_axis=0),
    )
    return result.reshape(rhs.shape)


def solution(mesh):
    return jax.shard_map(
        functools.partial(per_device, mesh),
        mesh=mesh,
        in_specs=(
            P("gx", "gy", "gz", None, None, None),
            P("gx", "gy", "gz", None),
            P("gx", "gy", "gz"),
            P("gx", "gy", "gz", None),
            P("gx", "gy", "gz", None, None),
            P(),
            P(),
        ),
        out_specs=P("gx", "gy", "gz", None, None, None),
        check_vma=False,
    )
```

```python
import functools

import jax
import jax.numpy as jnp
from jax import lax
from jax.experimental import pallas as pl
from jax.experimental.pallas import tpu as pltpu
from jax.sharding import PartitionSpec as P

coupling = 0.5
vmem_grant = 48 * 1024 * 1024
short_group = 4
lane_count = 128
f32 = jnp.float32
bf16 = jnp.bfloat16
vmem_spec = pl.BlockSpec(memory_space=pltpu.VMEM)
smem_spec = pl.BlockSpec(memory_space=pltpu.SMEM)
hbm_spec = pl.BlockSpec(memory_space=pltpu.HBM)


def two_parts(value):
    high = value.astype(bf16)
    return high, (value - high.astype(f32)).astype(bf16)


def dot(left, right):
    return jnp.dot(left, right, preferred_element_type=f32)


def dot_transposed(left, right):
    return lax.dot_general(left, right, (((1,), (1,)), ((), ())), preferred_element_type=f32)


def times_matrix(rows, matrix):
    return times_parts(rows, *two_parts(matrix))


def times_parts(rows, mat_high, mat_low):
    count = rows.shape[0]
    row_high, row_low = two_parts(rows)
    both = dot(jnp.concatenate([row_high, row_low], axis=0), mat_high)
    return both[:count] + (both[count:] + dot(row_high, mat_low))


def times_parts_once(rows, mat_high, mat_low):
    row_high = rows.astype(bf16)
    return dot(
        jnp.concatenate([row_high, row_high], axis=1),
        jnp.concatenate([mat_high, mat_low], axis=0),
    )


def split_index(index, dofs):
    if dofs & (dofs - 1) == 0:
        return lax.shift_right_arithmetic(index, dofs.bit_length() - 1), index & (dofs - 1)
    element = jnp.floor_divide(index, dofs)
    return element, index - element * dofs


def slot_of(target, links_ref, index_ref):
    slot = jnp.int32(-1)
    for position in range(links_ref.shape[-1]):
        slot = jnp.where(links_ref[0, 0, 0, position] == target, jnp.int32(position), slot)
    row = index_ref[0, 0, 0, pl.ds(jnp.maximum(slot, 0), 1), :]
    return jnp.where(slot >= 0, row, -1)


def hot_elements(flat_row, elements, dofs):
    element, _ = split_index(flat_row, dofs)
    return lax.broadcasted_iota(jnp.int32, (elements, flat_row.shape[1]), 0) == element


def hot_dofs(flat_row, dofs):
    _, dof = split_index(flat_row, dofs)
    shape = (dofs, flat_row.shape[1])
    line = lax.broadcasted_iota(jnp.int32, shape, 0).astype(jnp.int16)
    hit = line == jnp.broadcast_to(dof.astype(jnp.int16), shape)
    return jnp.where(hit, jnp.ones(shape, bf16), jnp.zeros(shape, bf16))


def as_column(row):
    elements = row.shape[1]
    line = lax.broadcasted_iota(jnp.int32, (elements, elements), 0)
    column = lax.broadcasted_iota(jnp.int32, (elements, elements), 1)
    spread = jnp.where(line == column, jnp.broadcast_to(row, (elements, elements)), 0.0)
    return jnp.sum(spread, axis=1, keepdims=True)


def wide(column, probes, dofs):
    return jnp.broadcast_to(jnp.concatenate([column] * probes, axis=0), (probes * column.shape[0], dofs))


def take_faces(picked, over_elements):
    elements = over_elements.shape[0]
    return [
        jnp.sum(jnp.where(over_elements, picked[low : low + elements], 0.0), axis=0, keepdims=True)
        for low in range(0, picked.shape[0], elements)
    ]


def spread_faces(values, over_elements):
    return jnp.concatenate(
        [jnp.where(over_elements, value, 0.0).astype(bf16) for value in values], axis=0
    )


def high_low(values):
    highs = [value.astype(bf16).astype(f32) for value in values]
    return highs + [value - high for value, high in zip(values, highs)]


def add_faces(spreads, over_dofs):
    return dot_transposed(jnp.concatenate(spreads, axis=1), over_dofs)


def add_faces_once(spreads, over_dofs):
    return jnp.transpose(dot_transposed(over_dofs, jnp.concatenate(spreads, axis=1)))


def folded(parts):
    rows = parts.shape[0] // 2
    return parts[:rows] + parts[rows:]


def as_row(lines, lanes):
    count = -(-len(lines) // 8) * 8
    spare = jnp.zeros((count - len(lines), lines[0].shape[1]), f32)
    sums = jnp.sum(jnp.concatenate(lines + [spare], axis=0), axis=1, keepdims=True)
    line = lax.broadcasted_iota(jnp.int32, (count, lanes), 0)
    lane = lax.broadcasted_iota(jnp.int32, (count, lanes), 1)
    return jnp.sum(jnp.where(line == lane, sums, 0.0), axis=0, keepdims=True)


def inner_products(first_img, second_img, source, probes, products_ref):
    elements = source.shape[0] // probes
    pairs = (
        (first_img, first_img),
        (first_img, second_img),
        (second_img, second_img),
        (first_img, source),
        (second_img, source),
    )
    lines = []
    for left, right in pairs:
        product = left * right
        for probe in range(probes):
            lines.append(
                jnp.sum(product[probe * elements : (probe + 1) * elements], axis=0, keepdims=True)
            )
    products_ref[...] = jnp.broadcast_to(as_row(lines, products_ref.shape[-1]), products_ref.shape)


def live_column(count_ref, elements):
    return lax.broadcasted_iota(jnp.int32, (elements, 1), 0) < count_ref[0, 0, 0]


def begin(refs, partner, count_ref, prepare):
    links_hbm, index_hbm, visc_hbm, rhs_hbm, *matrices_hbm = refs["operands"]
    links_ref, index_ref, visc_ref, rhs_ref, *matrix_refs, arrived = refs["scratch"]
    pairs = (
        (links_hbm, links_ref),
        (index_hbm, index_ref),
        (rhs_hbm, rhs_ref),
        (matrices_hbm[0], matrix_refs[0]),
        (visc_hbm, visc_ref),
        *zip(matrices_hbm[1:], matrix_refs[1:]),
    )
    copies = [
        pltpu.make_async_copy(held, here, arrived.at[place])
        for place, (held, here) in enumerate(pairs)
    ]
    for copy in copies:
        copy.start()
    copies[0].wait()
    copies[1].wait()
    slots_ref = refs["slots"]
    me = lax.axis_index("gz")
    for step in range(1, slots_ref.shape[0] + 1):
        slots_ref[step - 1] = slot_of(partner(me, step), links_ref, index_ref)
    prepare()
    copies[4].wait()
    probes, elements, dofs = rhs_ref.shape[3:]
    live = jnp.ones((elements, 1), f32)
    if count_ref is not None:
        live = live_column(count_ref, elements).astype(f32)
    visc = as_column(visc_ref[0, 0])
    up = wide(live * visc, probes, dofs)
    down = wide(live / visc, probes, dofs)
    refs["up"][...] = up
    refs["down"][...] = down
    copies[2].wait()
    source = rhs_ref[...].reshape(probes * elements, dofs)
    if count_ref is not None:
        source = source * wide(live, probes, dofs)
    refs["source"][...] = source
    copies[3].wait()
    smoother = two_parts(matrix_refs[0][...])
    first_pre = times_parts(source, *smoother) * down
    refs["first"][...] = first_pre
    for copy in copies[5:]:
        copy.wait()
    return first_pre, up, down, smoother


def message_places(steps, probes):
    values = steps * probes
    return values, values + probes, values + probes + steps


def message_length(steps, probes, width):
    return message_places(steps, probes)[2] * (width // lane_count) + 1


def write_row(message_ref, place, row):
    pieces = row.shape[1] // lane_count
    for piece in range(pieces):
        lanes = slice(piece * lane_count, (piece + 1) * lane_count)
        message_ref[place * pieces + piece] = row[:, lanes]


def read_row(message_ref, place, width):
    pieces = width // lane_count
    lines = range(place * pieces, (place + 1) * pieces)
    return jnp.concatenate([message_ref[line] for line in lines], axis=1)


def near_first_kernel(*refs):
    operands, refs = refs[:6], refs[6:]
    first_ref, source_ref, up_ref, down_ref, base_ref, slots_ref, hot_ref = refs[:7]
    part_refs, refs = refs[7:11], refs[11:]
    steps, _, width = slots_ref.shape
    leave_refs, scratch = refs[:steps], refs[steps:]
    visc_ref, rhs_ref, _, k_ref = scratch[2:6]
    probes, elements, dofs = rhs_ref.shape[3:]

    def prepare():
        for step in range(steps):
            hot_ref[:, step * width : (step + 1) * width] = hot_dofs(slots_ref[step], dofs)

    first_pre, up, down, smoother = begin(
        {
            "operands": operands,
            "scratch": scratch,
            "slots": slots_ref,
            "up": up_ref,
            "down": down_ref,
            "source": source_ref,
            "first": first_ref,
        },
        lambda me, step: me ^ step,
        None,
        prepare,
    )
    stiffness = two_parts(k_ref[...])
    base = times_parts(first_pre, *stiffness) * up
    base_ref[...] = base
    second_part = (times_parts_once(base, *smoother) * down).astype(bf16)
    stacked = jnp.concatenate([*two_parts(first_pre), second_part], axis=0)
    rows = probes * elements
    for part_ref, part in zip(part_refs, smoother + stiffness):
        part_ref[...] = part
    second_at, index_at, visc_at = message_places(steps, probes)
    for step in range(1, steps + 1):
        flat_row = slots_ref[step - 1]
        over_elements = hot_elements(flat_row, elements, dofs)
        over_dofs = hot_ref[:, (step - 1) * width : step * width]
        picked = dot(stacked, over_dofs)
        first_rows = take_faces(folded(picked[: 2 * rows]), over_elements)
        second_rows = take_faces(picked[2 * rows :], over_elements)
        for probe in range(probes):
            write_row(leave_refs[step - 1], second_at + probe, second_rows[probe])
            for leave_ref in leave_refs:
                write_row(leave_ref, (step - 1) * probes + probe, first_rows[probe])
        for leave_ref in leave_refs:
            write_row(leave_ref, index_at + step - 1, flat_row.astype(f32))
    visc_line = visc_at * (width // lane_count)
    for leave_ref in leave_refs:
        leave_ref[visc_line, :, :elements] = visc_ref[0, 0]


def near_second_kernel(
    probes, count_ref, source_ref, up_ref, down_ref, base_ref, slots_ref, hot_ref,
    p_high_ref, p_low_ref, k_high_ref, k_low_ref, mine_ref, *refs
):
    came_refs = refs[:-2]
    second_ref, products_ref = refs[-2:]
    steps, _, width = slots_ref.shape
    members = steps + 1
    rows, dofs = source_ref.shape
    elements = rows // probes
    second_at, index_at, visc_at = message_places(steps, probes)

    def message(step):
        return mine_ref if step == 0 else came_refs[step - 1]

    def inbound_first(member, step):
        sent = message(member ^ step)
        return [
            read_row(sent, (step - 1) * probes + probe, width) for probe in range(probes)
        ]

    own_elements = [hot_elements(slots_ref[step], elements, dofs) for step in range(steps)]

    def placed_here(values):
        spreads = [spread_faces(values[step], own_elements[step]) for step in range(steps)]
        add = add_faces if len(values[0]) > probes else add_faces_once
        return add(spreads, hot_ref[...])

    up, down = up_ref[...], down_ref[...]
    live = wide(live_column(count_ref, elements).astype(f32), probes, dofs) > 0.0
    placed = folded(placed_here([high_low(inbound_first(0, step)) for step in range(1, members)]))
    image = jnp.where(live, base_ref[...] - coupling * placed, 0.0)
    changes, back = [], []
    for member in range(1, members):
        rows_of = [
            read_row(message(member), index_at + step, width).astype(jnp.int32)
            for step in range(steps)
        ]
        over_elements = [hot_elements(flat_row, elements, dofs) for flat_row in rows_of]
        over_dofs = [hot_dofs(flat_row, dofs) for flat_row in rows_of]
        spreads = [
            spread_faces(inbound_first(member, step + 1), over_elements[step])
            for step in range(steps)
        ]
        changes.append(-coupling * add_faces_once(spreads, jnp.concatenate(over_dofs, axis=1)))
        back.append((over_elements[member - 1], over_dofs[member - 1]))
    second_pre = times_parts(image, p_high_ref[...], p_low_ref[...]) * down
    changes = times_parts_once(jnp.concatenate(changes, axis=0), p_high_ref[...], p_low_ref[...])
    second_ref[...] = second_pre
    values = []
    visc_line = visc_at * (width // lane_count)
    for member in range(1, members):
        sent = message(member)
        visc = as_column(sent[visc_line, :, :elements])
        scale = wide(1.0 / visc, probes, dofs)
        change = changes[(member - 1) * rows : member * rows] * scale
        over_elements, over_dofs = back[member - 1]
        taken = take_faces(dot(change.astype(bf16), over_dofs), over_elements)
        values.append(
            [taken[probe] + read_row(sent, second_at + probe, width) for probe in range(probes)]
        )
    placed = placed_here(values)
    second_img = times_parts_once(second_pre, k_high_ref[...], k_low_ref[...])
    second_img = second_img * up - coupling * placed
    second_img = jnp.where(live, second_img, 0.0)
    source = jnp.where(live, source_ref[...], 0.0)
    inner_products(image, second_img, source, probes, products_ref)


def leave_faces(field, probes, slots_ref, leave_ref):
    elements, dofs = field.shape[0] // probes, field.shape[1]
    members = slots_ref.shape[0] + 1
    me = lax.axis_index("gz")
    for shift in range(1, members):
        flat_row = slots_ref[shift - 1]
        over_elements = hot_elements(flat_row, elements, dofs)
        parts = jnp.concatenate(two_parts(field), axis=0)
        taken = take_faces(folded(dot(parts, hot_dofs(flat_row, dofs))), over_elements)
        target = lax.rem(me + shift, members)
        for probe in range(probes):
            leave_ref[target, pl.ds(probe, 1), :] = taken[probe]
    leave_ref[me] = jnp.zeros(leave_ref.shape[1:], f32)


def placed_faces(shape, probes, slots_ref, came_ref):
    rows, dofs = shape
    elements = rows // probes
    members = slots_ref.shape[0] + 1
    me = lax.axis_index("gz")
    total = jnp.zeros(shape, f32)
    for shift in range(1, members):
        flat_row = slots_ref[shift - 1]
        came = came_ref[lax.rem(me + shift, members)]
        values = [came[probe : probe + 1, :] for probe in range(probes)]
        spread = spread_faces(high_low(values), hot_elements(flat_row, elements, dofs))
        total += folded(add_faces([spread], hot_dofs(flat_row, dofs)))
    return total


def far_first_kernel(*refs):
    count_ref, *operands = refs[:6]
    refs = refs[6:]
    first_ref, source_ref, up_ref, down_ref, slots_ref, leave_ref = refs[:6]
    members = slots_ref.shape[0] + 1
    first_pre, *_ = begin(
        {
            "operands": operands,
            "scratch": refs[6:],
            "slots": slots_ref,
            "up": up_ref,
            "down": down_ref,
            "source": source_ref,
            "first": first_ref,
        },
        lambda me, step: lax.rem(me + step, members),
        count_ref,
        lambda: None,
    )
    leave_faces(first_pre, leave_ref.shape[1], slots_ref, leave_ref)


def far_second_kernel(
    slots_ref, up_ref, down_ref, first_ref, k_ref, p_ref, came_ref,
    image_ref, second_ref, leave_ref,
):
    probes = came_ref.shape[1]
    up = up_ref[...]
    placed = placed_faces(first_ref.shape, probes, slots_ref, came_ref)
    image = times_matrix(first_ref[...], k_ref[...]) * up - jnp.where(up > 0.0, coupling * placed, 0.0)
    image_ref[...] = image
    second_pre = times_matrix(image, p_ref[...]) * down_ref[...]
    second_ref[...] = second_pre
    leave_faces(second_pre, probes, slots_ref, leave_ref)


def far_third_kernel(
    slots_ref, up_ref, source_ref, image_ref, second_ref, k_ref, came_ref, products_ref
):
    probes = came_ref.shape[1]
    up = up_ref[...]
    placed = placed_faces(source_ref.shape, probes, slots_ref, came_ref)
    second_img = times_matrix(second_ref[...], k_ref[...]) * up - jnp.where(up > 0.0, coupling * placed, 0.0)
    inner_products(image_ref[...], second_img, source_ref[...], probes, products_ref)


def last_kernel(probes, count_ref, first_ref, second_ref, parts_ref, out_ref):
    rows, _ = first_ref.shape
    elements = rows // probes
    total = jnp.sum(parts_ref[...], axis=0)
    live = live_column(count_ref, elements)
    for probe in range(probes):
        self_one, cross_mid, self_two, load_one, load_two = (
            total[:, place * probes + probe : place * probes + probe + 1] for place in range(5)
        )
        determinant = self_one * self_two - cross_mid * cross_mid
        weight_one = (self_two * load_one - cross_mid * load_two) / determinant
        weight_two = (self_one * load_two - cross_mid * load_one) / determinant
        block = pl.ds(probe * elements, elements)
        value = weight_one * first_ref[block, :] + weight_two * second_ref[block, :]
        out_ref[block, :] = jnp.where(live, value, 0.0)


def call(kernel, in_specs, out_shapes, flops, *args, scratch=()):
    return pl.pallas_call(
        kernel,
        out_shape=out_shapes,
        in_specs=in_specs,
        out_specs=jax.tree.map(lambda _: vmem_spec, out_shapes),
        scratch_shapes=scratch,
        compiler_params=pltpu.CompilerParams(vmem_limit_bytes=vmem_grant),
        cost_estimate=pl.CostEstimate(flops=flops, bytes_accessed=1 << 20, transcendentals=0),
    )(*args)


def begin_call(kernel, out_shapes, flops, scalars, *fetched):
    links, *others = fetched
    scratch = [pltpu.SMEM(links.shape, links.dtype)]
    scratch += [pltpu.VMEM(value.shape, value.dtype) for value in others]
    return call(
        kernel,
        [smem_spec] * len(scalars) + [hbm_spec] * len(fetched),
        out_shapes,
        flops,
        *scalars,
        *(pltpu.with_memory_space_constraint(value, pltpu.HBM) for value in fetched),
        scratch=scratch + [pltpu.SemaphoreType.DMA((len(fetched),))],
    )


def near_steps(members, shapes, arguments):
    rhs, viscosity, counts, neighbours, face_index, k_matrix, p_matrix = arguments
    field, slots_shape, products_shape = shapes
    rows, dofs = field.shape
    steps, _, width = slots_shape.shape
    probes = rhs.shape[3]
    flops = 8 * rows * dofs * steps * width
    hot = jax.ShapeDtypeStruct((dofs, steps * width), bf16)
    message = jax.ShapeDtypeStruct((message_length(steps, probes, width), 1, lane_count), f32)
    part = jax.ShapeDtypeStruct(p_matrix.shape, bf16)
    first_pre, source, up, down, base, slots, hot_own, *rest = begin_call(
        near_first_kernel,
        [field] * 5 + [slots_shape, hot] + [part] * 4 + [message] * steps,
        2 * flops,
        (),
        neighbours,
        face_index,
        viscosity,
        rhs,
        p_matrix,
        k_matrix,
    )
    parts, leaving = rest[:4], rest[4:]
    came = [
        lax.ppermute(
            leaving[step - 1], "gz", [(source, source ^ step) for source in range(members)]
        )
        for step in range(1, members)
    ]
    second_pre, products = call(
        functools.partial(near_second_kernel, probes),
        [smem_spec] + [vmem_spec] * (11 + steps),
        [field, products_shape],
        6 * flops,
        counts,
        source,
        up,
        down,
        base,
        slots,
        hot_own,
        *parts,
        leaving[0],
        *came,
    )
    return first_pre, second_pre, products


def far_steps(members, shapes, arguments):
    rhs, viscosity, counts, neighbours, face_index, k_matrix, p_matrix = arguments
    field, slots_shape, products_shape = shapes
    rows, dofs = field.shape
    shifts, _, width = slots_shape.shape
    flops = 8 * rows * dofs * shifts * width
    faces = jax.ShapeDtypeStruct((members, rhs.shape[3], width), f32)

    def exchange(value):
        return lax.all_to_all(value, "gz", split_axis=0, concat_axis=0)

    first_pre, source, up, down, slots, leaving = begin_call(
        far_first_kernel,
        [field] * 4 + [slots_shape, faces],
        flops,
        (counts,),
        neighbours,
        face_index,
        viscosity,
        rhs,
        p_matrix,
    )
    first_img, second_pre, leaving = call(
        far_second_kernel,
        [vmem_spec] * 7,
        [field, field, faces],
        2 * flops,
        slots,
        up,
        down,
        first_pre,
        k_matrix,
        p_matrix,
        exchange(leaving),
    )
    products = call(
        far_third_kernel,
        [vmem_spec] * 7,
        products_shape,
        flops,
        slots,
        up,
        source,
        first_img,
        second_pre,
        k_matrix,
        exchange(leaving),
    )
    return first_pre, second_pre, products


def per_device(mesh, *arguments):
    rhs, face_index = arguments[0], arguments[4]
    probes, elements, dofs = rhs.shape[3:]
    members = mesh.shape["gz"]
    lanes = -(-5 * probes // 128) * 128
    shapes = (
        jax.ShapeDtypeStruct((probes * elements, dofs), f32),
        jax.ShapeDtypeStruct((members - 1, 1, face_index.shape[-1]), jnp.int32),
        jax.ShapeDtypeStruct((mesh.size, 1, lanes), f32),
    )
    near = 1 < members <= short_group and elements <= face_index.shape[-1]
    near = near and elements * dofs < 1 << 24
    steps = near_steps if near else far_steps
    first_pre, second_pre, products = steps(members, shapes, arguments)
    result = call(
        functools.partial(last_kernel, probes),
        [smem_spec] + [vmem_spec] * 3,
        shapes[0],
        probes * elements * dofs,
        arguments[2],
        first_pre,
        second_pre,
        lax.all_to_all(
            products,
            ("gx", "gy", "gz"),
            split_axis=0,
            concat_axis=0,
            axis_index_groups=[list(range(mesh.size - 1, -1, -1))],
        ),
    )
    return result.reshape(rhs.shape)


def solution(mesh):
    return jax.shard_map(
        functools.partial(per_device, mesh),
        mesh=mesh,
        in_specs=(
            P("gx", "gy", "gz", None, None, None),
            P("gx", "gy", "gz", None),
            P("gx", "gy", "gz"),
            P("gx", "gy", "gz", None),
            P("gx", "gy", "gz", None, None),
            P(),
            P(),
        ),
        out_specs=P("gx", "gy", "gz", None, None, None),
        check_vma=False,
    )
```

```python
import functools

import jax
import jax.numpy as jnp
from jax import lax
from jax.experimental import pallas as pl
from jax.experimental.pallas import tpu as pltpu
from jax.sharding import PartitionSpec as P

coupling = 0.5
vmem_grant = 48 * 1024 * 1024
short_group = 4
lane_count = 128
f32 = jnp.float32
bf16 = jnp.bfloat16
vmem_spec = pl.BlockSpec(memory_space=pltpu.VMEM)
smem_spec = pl.BlockSpec(memory_space=pltpu.SMEM)
hbm_spec = pl.BlockSpec(memory_space=pltpu.HBM)


def two_parts(value):
    high = value.astype(bf16)
    return high, (value - high.astype(f32)).astype(bf16)


def dot(left, right):
    return jnp.dot(left, right, preferred_element_type=f32)


def dot_transposed(left, right):
    return lax.dot_general(left, right, (((1,), (1,)), ((), ())), preferred_element_type=f32)


def times_matrix(rows, matrix):
    return times_parts(rows, *two_parts(matrix))


def times_parts(rows, mat_high, mat_low):
    return parts_product(two_parts(rows), (mat_high, mat_low))


def parts_product(left, right):
    count = left[0].shape[0]
    both = dot(jnp.concatenate(left, axis=0), right[0])
    return both[:count] + (both[count:] + dot(left[0], right[1]))


def times_parts_once(rows, mat_high, mat_low):
    row_high = rows.astype(bf16)
    return dot(
        jnp.concatenate([row_high, row_high], axis=1),
        jnp.concatenate([mat_high, mat_low], axis=0),
    )


def split_index(index, dofs):
    if dofs & (dofs - 1) == 0:
        return lax.shift_right_arithmetic(index, dofs.bit_length() - 1), index & (dofs - 1)
    element = jnp.floor_divide(index, dofs)
    return element, index - element * dofs


def slot_of(target, links_ref, index_ref):
    slot = jnp.int32(-1)
    for position in range(links_ref.shape[-1]):
        slot = jnp.where(links_ref[0, 0, 0, position] == target, jnp.int32(position), slot)
    row = index_ref[0, 0, 0, pl.ds(jnp.maximum(slot, 0), 1), :]
    return jnp.where(slot >= 0, row, -1)


def hot_elements(flat_row, elements, dofs):
    element, _ = split_index(flat_row, dofs)
    return lax.broadcasted_iota(jnp.int32, (elements, flat_row.shape[1]), 0) == element


def hot_dofs(flat_row, dofs):
    _, dof = split_index(flat_row, dofs)
    shape = (dofs, flat_row.shape[1])
    line = lax.broadcasted_iota(jnp.int32, shape, 0).astype(jnp.int16)
    hit = line == jnp.broadcast_to(dof.astype(jnp.int16), shape)
    return jnp.where(hit, jnp.ones(shape, bf16), jnp.zeros(shape, bf16))


def as_column(row):
    elements = row.shape[1]
    line = lax.broadcasted_iota(jnp.int32, (elements, elements), 0)
    column = lax.broadcasted_iota(jnp.int32, (elements, elements), 1)
    spread = jnp.where(line == column, jnp.broadcast_to(row, (elements, elements)), 0.0)
    return jnp.sum(spread, axis=1, keepdims=True)


def wide(column, probes, dofs):
    return jnp.broadcast_to(jnp.concatenate([column] * probes, axis=0), (probes * column.shape[0], dofs))


def take_faces(picked, over_elements):
    elements = over_elements.shape[0]
    return [
        jnp.sum(jnp.where(over_elements, picked[low : low + elements], 0.0), axis=0, keepdims=True)
        for low in range(0, picked.shape[0], elements)
    ]


def spread_faces(values, over_elements):
    return jnp.concatenate(
        [jnp.where(over_elements, value, 0.0).astype(bf16) for value in values], axis=0
    )


def high_low(values):
    highs = [value.astype(bf16).astype(f32) for value in values]
    return highs + [value - high for value, high in zip(values, highs)]


def add_faces(spreads, over_dofs):
    return dot_transposed(jnp.concatenate(spreads, axis=1), over_dofs)


def add_faces_once(spreads, over_dofs):
    return jnp.transpose(dot_transposed(over_dofs, jnp.concatenate(spreads, axis=1)))


def folded(parts):
    rows = parts.shape[0] // 2
    return parts[:rows] + parts[rows:]


def as_row(lines, lanes):
    count = -(-len(lines) // 8) * 8
    spare = jnp.zeros((count - len(lines), lines[0].shape[1]), f32)
    sums = jnp.sum(jnp.concatenate(lines + [spare], axis=0), axis=1, keepdims=True)
    line = lax.broadcasted_iota(jnp.int32, (count, lanes), 0)
    lane = lax.broadcasted_iota(jnp.int32, (count, lanes), 1)
    return jnp.sum(jnp.where(line == lane, sums, 0.0), axis=0, keepdims=True)


def inner_products(first_img, second_img, source, probes, products_ref):
    elements = source.shape[0] // probes
    pairs = (
        (first_img, first_img),
        (first_img, second_img),
        (second_img, second_img),
        (first_img, source),
        (second_img, source),
    )
    lines = []
    for left, right in pairs:
        product = left * right
        for probe in range(probes):
            lines.append(
                jnp.sum(product[probe * elements : (probe + 1) * elements], axis=0, keepdims=True)
            )
    products_ref[...] = jnp.broadcast_to(as_row(lines, products_ref.shape[-1]), products_ref.shape)


def live_column(count_ref, elements):
    return lax.broadcasted_iota(jnp.int32, (elements, 1), 0) < count_ref[0, 0, 0]


def begin(refs, partner, count_ref, prepare):
    links_hbm, index_hbm, visc_hbm, rhs_hbm, *matrices_hbm = refs["operands"]
    links_ref, index_ref, visc_ref, rhs_ref, *matrix_refs, arrived = refs["scratch"]
    pairs = (
        (links_hbm, links_ref),
        (index_hbm, index_ref),
        (rhs_hbm, rhs_ref),
        (matrices_hbm[0], matrix_refs[0]),
        (visc_hbm, visc_ref),
        *zip(matrices_hbm[1:], matrix_refs[1:]),
    )
    copies = [
        pltpu.make_async_copy(held, here, arrived.at[place])
        for place, (held, here) in enumerate(pairs)
    ]
    for copy in copies:
        copy.start()
    copies[0].wait()
    copies[1].wait()
    slots_ref = refs["slots"]
    me = lax.axis_index("gz")
    for step in range(1, slots_ref.shape[0] + 1):
        slots_ref[step - 1] = slot_of(partner(me, step), links_ref, index_ref)
    prepare()
    copies[4].wait()
    probes, elements, dofs = rhs_ref.shape[3:]
    live = jnp.ones((elements, 1), f32)
    if count_ref is not None:
        live = live_column(count_ref, elements).astype(f32)
    visc = as_column(visc_ref[0, 0])
    up = wide(live * visc, probes, dofs)
    down = wide(live / visc, probes, dofs)
    refs["up"][...] = up
    refs["down"][...] = down
    copies[2].wait()
    source = rhs_ref[...].reshape(probes * elements, dofs)
    if count_ref is not None:
        source = source * wide(live, probes, dofs)
    refs["source"][...] = source
    copies[3].wait()
    smoother = two_parts(matrix_refs[0][...])
    first_pre = times_parts(source, *smoother) * down
    refs["first"][...] = first_pre
    for copy in copies[5:]:
        copy.wait()
    return first_pre, up, down, smoother


def message_places(steps, probes):
    values = steps * probes
    return values, values + probes, values + probes + steps


def message_length(steps, probes, width):
    return message_places(steps, probes)[2] * (width // lane_count) + 1


def write_row(message_ref, place, row):
    pieces = row.shape[1] // lane_count
    for piece in range(pieces):
        lanes = slice(piece * lane_count, (piece + 1) * lane_count)
        message_ref[place * pieces + piece] = row[:, lanes]


def read_row(message_ref, place, width):
    pieces = width // lane_count
    lines = range(place * pieces, (place + 1) * pieces)
    return jnp.concatenate([message_ref[line] for line in lines], axis=1)


def near_first_kernel(*refs):
    operands, refs = refs[:6], refs[6:]
    first_ref, source_ref, up_ref, down_ref, base_ref, slots_ref, hot_ref = refs[:7]
    part_refs, refs = refs[7:11], refs[11:]
    steps, _, width = slots_ref.shape
    leave_refs, scratch = refs[:steps], refs[steps:]
    visc_ref, rhs_ref, _, k_ref = scratch[2:6]
    probes, elements, dofs = rhs_ref.shape[3:]

    def prepare():
        for step in range(steps):
            hot_ref[:, step * width : (step + 1) * width] = hot_dofs(slots_ref[step], dofs)

    first_pre, up, down, smoother = begin(
        {
            "operands": operands,
            "scratch": scratch,
            "slots": slots_ref,
            "up": up_ref,
            "down": down_ref,
            "source": source_ref,
            "first": first_ref,
        },
        lambda me, step: me ^ step,
        None,
        prepare,
    )
    stiffness = two_parts(k_ref[...])
    base = times_parts(first_pre, *stiffness) * up
    base_ref[...] = base
    both = two_parts(parts_product(stiffness, smoother))
    second_part = (times_parts_once(first_pre, *both)).astype(bf16)
    stacked = jnp.concatenate([*two_parts(first_pre), second_part], axis=0)
    rows = probes * elements
    for part_ref, part in zip(part_refs, smoother + stiffness):
        part_ref[...] = part
    second_at, index_at, visc_at = message_places(steps, probes)
    for step in range(1, steps + 1):
        flat_row = slots_ref[step - 1]
        over_elements = hot_elements(flat_row, elements, dofs)
        over_dofs = hot_ref[:, (step - 1) * width : step * width]
        picked = dot(stacked, over_dofs)
        first_rows = take_faces(folded(picked[: 2 * rows]), over_elements)
        second_rows = take_faces(picked[2 * rows :], over_elements)
        for probe in range(probes):
            write_row(leave_refs[step - 1], second_at + probe, second_rows[probe])
            for leave_ref in leave_refs:
                write_row(leave_ref, (step - 1) * probes + probe, first_rows[probe])
        for leave_ref in leave_refs:
            write_row(leave_ref, index_at + step - 1, flat_row.astype(f32))
    visc_line = visc_at * (width // lane_count)
    for leave_ref in leave_refs:
        leave_ref[visc_line, :, :elements] = visc_ref[0, 0]


def near_second_kernel(
    probes, count_ref, source_ref, up_ref, down_ref, base_ref, slots_ref, hot_ref,
    p_high_ref, p_low_ref, k_high_ref, k_low_ref, mine_ref, *refs
):
    came_refs = refs[:-2]
    second_ref, products_ref = refs[-2:]
    steps, _, width = slots_ref.shape
    members = steps + 1
    rows, dofs = source_ref.shape
    elements = rows // probes
    second_at, index_at, visc_at = message_places(steps, probes)

    def message(step):
        return mine_ref if step == 0 else came_refs[step - 1]

    def inbound_first(member, step):
        sent = message(member ^ step)
        return [
            read_row(sent, (step - 1) * probes + probe, width) for probe in range(probes)
        ]

    own_elements = [hot_elements(slots_ref[step], elements, dofs) for step in range(steps)]

    def placed_here(values):
        spreads = [spread_faces(values[step], own_elements[step]) for step in range(steps)]
        add = add_faces if len(values[0]) > probes else add_faces_once
        return add(spreads, hot_ref[...])

    up, down = up_ref[...], down_ref[...]
    live = wide(live_column(count_ref, elements).astype(f32), probes, dofs) > 0.0
    placed = folded(placed_here([high_low(inbound_first(0, step)) for step in range(1, members)]))
    image = jnp.where(live, base_ref[...] - coupling * placed, 0.0)
    changes, back = [], []
    for member in range(1, members):
        rows_of = [
            read_row(message(member), index_at + step, width).astype(jnp.int32)
            for step in range(steps)
        ]
        over_elements = [hot_elements(flat_row, elements, dofs) for flat_row in rows_of]
        over_dofs = [hot_dofs(flat_row, dofs) for flat_row in rows_of]
        spreads = [
            spread_faces(inbound_first(member, step + 1), over_elements[step])
            for step in range(steps)
        ]
        changes.append(-coupling * add_faces_once(spreads, jnp.concatenate(over_dofs, axis=1)))
        back.append((over_elements[member - 1], over_dofs[member - 1]))
    second_pre = times_parts(image, p_high_ref[...], p_low_ref[...]) * down
    changes = times_parts_once(jnp.concatenate(changes, axis=0), p_high_ref[...], p_low_ref[...])
    second_ref[...] = second_pre
    values = []
    visc_line = visc_at * (width // lane_count)
    for member in range(1, members):
        sent = message(member)
        visc = as_column(sent[visc_line, :, :elements])
        scale = wide(1.0 / visc, probes, dofs)
        change = changes[(member - 1) * rows : member * rows] * scale
        over_elements, over_dofs = back[member - 1]
        taken = take_faces(dot(change.astype(bf16), over_dofs), over_elements)
        values.append(
            [taken[probe] + read_row(sent, second_at + probe, width) for probe in range(probes)]
        )
    placed = placed_here(values)
    second_img = times_parts_once(second_pre, k_high_ref[...], k_low_ref[...])
    second_img = second_img * up - coupling * placed
    second_img = jnp.where(live, second_img, 0.0)
    source = jnp.where(live, source_ref[...], 0.0)
    inner_products(image, second_img, source, probes, products_ref)


def leave_faces(field, probes, slots_ref, leave_ref):
    elements, dofs = field.shape[0] // probes, field.shape[1]
    members = slots_ref.shape[0] + 1
    me = lax.axis_index("gz")
    for shift in range(1, members):
        flat_row = slots_ref[shift - 1]
        over_elements = hot_elements(flat_row, elements, dofs)
        parts = jnp.concatenate(two_parts(field), axis=0)
        taken = take_faces(folded(dot(parts, hot_dofs(flat_row, dofs))), over_elements)
        target = lax.rem(me + shift, members)
        for probe in range(probes):
            leave_ref[target, pl.ds(probe, 1), :] = taken[probe]
    leave_ref[me] = jnp.zeros(leave_ref.shape[1:], f32)


def placed_faces(shape, probes, slots_ref, came_ref):
    rows, dofs = shape
    elements = rows // probes
    members = slots_ref.shape[0] + 1
    me = lax.axis_index("gz")
    total = jnp.zeros(shape, f32)
    for shift in range(1, members):
        flat_row = slots_ref[shift - 1]
        came = came_ref[lax.rem(me + shift, members)]
        values = [came[probe : probe + 1, :] for probe in range(probes)]
        spread = spread_faces(high_low(values), hot_elements(flat_row, elements, dofs))
        total += folded(add_faces([spread], hot_dofs(flat_row, dofs)))
    return total


def far_first_kernel(*refs):
    count_ref, *operands = refs[:6]
    refs = refs[6:]
    first_ref, source_ref, up_ref, down_ref, slots_ref, leave_ref = refs[:6]
    members = slots_ref.shape[0] + 1
    first_pre, *_ = begin(
        {
            "operands": operands,
            "scratch": refs[6:],
            "slots": slots_ref,
            "up": up_ref,
            "down": down_ref,
            "source": source_ref,
            "first": first_ref,
        },
        lambda me, step: lax.rem(me + step, members),
        count_ref,
        lambda: None,
    )
    leave_faces(first_pre, leave_ref.shape[1], slots_ref, leave_ref)


def far_second_kernel(
    slots_ref, up_ref, down_ref, first_ref, k_ref, p_ref, came_ref,
    image_ref, second_ref, leave_ref,
):
    probes = came_ref.shape[1]
    up = up_ref[...]
    placed = placed_faces(first_ref.shape, probes, slots_ref, came_ref)
    image = times_matrix(first_ref[...], k_ref[...]) * up - jnp.where(up > 0.0, coupling * placed, 0.0)
    image_ref[...] = image
    second_pre = times_matrix(image, p_ref[...]) * down_ref[...]
    second_ref[...] = second_pre
    leave_faces(second_pre, probes, slots_ref, leave_ref)


def far_third_kernel(
    slots_ref, up_ref, source_ref, image_ref, second_ref, k_ref, came_ref, products_ref
):
    probes = came_ref.shape[1]
    up = up_ref[...]
    placed = placed_faces(source_ref.shape, probes, slots_ref, came_ref)
    second_img = times_matrix(second_ref[...], k_ref[...]) * up - jnp.where(up > 0.0, coupling * placed, 0.0)
    inner_products(image_ref[...], second_img, source_ref[...], probes, products_ref)


def last_kernel(probes, count_ref, first_ref, second_ref, parts_ref, out_ref):
    rows, _ = first_ref.shape
    elements = rows // probes
    total = jnp.sum(parts_ref[...], axis=0)
    live = live_column(count_ref, elements)
    for probe in range(probes):
        self_one, cross_mid, self_two, load_one, load_two = (
            total[:, place * probes + probe : place * probes + probe + 1] for place in range(5)
        )
        determinant = self_one * self_two - cross_mid * cross_mid
        weight_one = (self_two * load_one - cross_mid * load_two) / determinant
        weight_two = (self_one * load_two - cross_mid * load_one) / determinant
        block = pl.ds(probe * elements, elements)
        value = weight_one * first_ref[block, :] + weight_two * second_ref[block, :]
        out_ref[block, :] = jnp.where(live, value, 0.0)


def call(kernel, in_specs, out_shapes, flops, *args, scratch=()):
    return pl.pallas_call(
        kernel,
        out_shape=out_shapes,
        in_specs=in_specs,
        out_specs=jax.tree.map(lambda _: vmem_spec, out_shapes),
        scratch_shapes=scratch,
        compiler_params=pltpu.CompilerParams(vmem_limit_bytes=vmem_grant),
        cost_estimate=pl.CostEstimate(flops=flops, bytes_accessed=1 << 20, transcendentals=0),
    )(*args)


def begin_call(kernel, out_shapes, flops, scalars, *fetched):
    links, *others = fetched
    scratch = [pltpu.SMEM(links.shape, links.dtype)]
    scratch += [pltpu.VMEM(value.shape, value.dtype) for value in others]
    return call(
        kernel,
        [smem_spec] * len(scalars) + [hbm_spec] * len(fetched),
        out_shapes,
        flops,
        *scalars,
        *(pltpu.with_memory_space_constraint(value, pltpu.HBM) for value in fetched),
        scratch=scratch + [pltpu.SemaphoreType.DMA((len(fetched),))],
    )


def near_steps(members, shapes, arguments):
    rhs, viscosity, counts, neighbours, face_index, k_matrix, p_matrix = arguments
    field, slots_shape, products_shape = shapes
    rows, dofs = field.shape
    steps, _, width = slots_shape.shape
    probes = rhs.shape[3]
    flops = 8 * rows * dofs * steps * width
    hot = jax.ShapeDtypeStruct((dofs, steps * width), bf16)
    message = jax.ShapeDtypeStruct((message_length(steps, probes, width), 1, lane_count), f32)
    part = jax.ShapeDtypeStruct(p_matrix.shape, bf16)
    first_pre, source, up, down, base, slots, hot_own, *rest = begin_call(
        near_first_kernel,
        [field] * 5 + [slots_shape, hot] + [part] * 4 + [message] * steps,
        2 * flops,
        (),
        neighbours,
        face_index,
        viscosity,
        rhs,
        p_matrix,
        k_matrix,
    )
    parts, leaving = rest[:4], rest[4:]
    came = [
        lax.ppermute(
            leaving[step - 1], "gz", [(source, source ^ step) for source in range(members)]
        )
        for step in range(1, members)
    ]
    second_pre, products = call(
        functools.partial(near_second_kernel, probes),
        [smem_spec] + [vmem_spec] * (11 + steps),
        [field, products_shape],
        6 * flops,
        counts,
        source,
        up,
        down,
        base,
        slots,
        hot_own,
        *parts,
        leaving[0],
        *came,
    )
    return first_pre, second_pre, products


def far_steps(members, shapes, arguments):
    rhs, viscosity, counts, neighbours, face_index, k_matrix, p_matrix = arguments
    field, slots_shape, products_shape = shapes
    rows, dofs = field.shape
    shifts, _, width = slots_shape.shape
    flops = 8 * rows * dofs * shifts * width
    faces = jax.ShapeDtypeStruct((members, rhs.shape[3], width), f32)

    def exchange(value):
        return lax.all_to_all(value, "gz", split_axis=0, concat_axis=0)

    first_pre, source, up, down, slots, leaving = begin_call(
        far_first_kernel,
        [field] * 4 + [slots_shape, faces],
        flops,
        (counts,),
        neighbours,
        face_index,
        viscosity,
        rhs,
        p_matrix,
    )
    first_img, second_pre, leaving = call(
        far_second_kernel,
        [vmem_spec] * 7,
        [field, field, faces],
        2 * flops,
        slots,
        up,
        down,
        first_pre,
        k_matrix,
        p_matrix,
        exchange(leaving),
    )
    products = call(
        far_third_kernel,
        [vmem_spec] * 7,
        products_shape,
        flops,
        slots,
        up,
        source,
        first_img,
        second_pre,
        k_matrix,
        exchange(leaving),
    )
    return first_pre, second_pre, products


def per_device(mesh, *arguments):
    rhs, face_index = arguments[0], arguments[4]
    probes, elements, dofs = rhs.shape[3:]
    members = mesh.shape["gz"]
    lanes = -(-5 * probes // 128) * 128
    shapes = (
        jax.ShapeDtypeStruct((probes * elements, dofs), f32),
        jax.ShapeDtypeStruct((members - 1, 1, face_index.shape[-1]), jnp.int32),
        jax.ShapeDtypeStruct((mesh.size, 1, lanes), f32),
    )
    near = 1 < members <= short_group and elements <= face_index.shape[-1]
    near = near and elements * dofs < 1 << 24
    steps = near_steps if near else far_steps
    first_pre, second_pre, products = steps(members, shapes, arguments)
    result = call(
        functools.partial(last_kernel, probes),
        [smem_spec] + [vmem_spec] * 3,
        shapes[0],
        probes * elements * dofs,
        arguments[2],
        first_pre,
        second_pre,
        lax.all_to_all(products, ("gx", "gy", "gz"), split_axis=0, concat_axis=0),
    )
    return result.reshape(rhs.shape)


def solution(mesh):
    return jax.shard_map(
        functools.partial(per_device, mesh),
        mesh=mesh,
        in_specs=(
            P("gx", "gy", "gz", None, None, None),
            P("gx", "gy", "gz", None),
            P("gx", "gy", "gz"),
            P("gx", "gy", "gz", None),
            P("gx", "gy", "gz", None, None),
            P(),
            P(),
        ),
        out_specs=P("gx", "gy", "gz", None, None, None),
        check_vma=False,
    )
```

```python
import functools

import jax
import jax.numpy as jnp
from jax import lax
from jax.experimental import pallas as pl
from jax.experimental.pallas import tpu as pltpu
from jax.sharding import PartitionSpec as P

coupling = 0.5
vmem_grant = 48 * 1024 * 1024
short_group = 4
lane_count = 128
f32 = jnp.float32
bf16 = jnp.bfloat16
vmem_spec = pl.BlockSpec(memory_space=pltpu.VMEM)
smem_spec = pl.BlockSpec(memory_space=pltpu.SMEM)
hbm_spec = pl.BlockSpec(memory_space=pltpu.HBM)


def two_parts(value):
    high = value.astype(bf16)
    return high, (value - high.astype(f32)).astype(bf16)


def dot(left, right):
    return jnp.dot(left, right, preferred_element_type=f32)


def dot_transposed(left, right):
    return lax.dot_general(left, right, (((1,), (1,)), ((), ())), preferred_element_type=f32)


def times_matrix(rows, matrix):
    return times_parts(rows, *two_parts(matrix))


def times_parts(rows, mat_high, mat_low):
    row_high, row_low = two_parts(rows)
    return dot(
        jnp.concatenate([row_high, row_low, row_high], axis=1),
        jnp.concatenate([mat_high, mat_high, mat_low], axis=0),
    )


def times_parts_once(rows, mat_high, mat_low):
    row_high = rows.astype(bf16)
    return dot(
        jnp.concatenate([row_high, row_high], axis=1),
        jnp.concatenate([mat_high, mat_low], axis=0),
    )


def split_index(index, dofs):
    if dofs & (dofs - 1) == 0:
        return lax.shift_right_arithmetic(index, dofs.bit_length() - 1), index & (dofs - 1)
    element = jnp.floor_divide(index, dofs)
    return element, index - element * dofs


def slot_of(target, links_ref, index_ref):
    slot = jnp.int32(-1)
    for position in range(links_ref.shape[-1]):
        slot = jnp.where(links_ref[0, 0, 0, position] == target, jnp.int32(position), slot)
    row = index_ref[0, 0, 0, pl.ds(jnp.maximum(slot, 0), 1), :]
    return jnp.where(slot >= 0, row, -1)


def hot_elements(flat_row, elements, dofs):
    element, _ = split_index(flat_row, dofs)
    return lax.broadcasted_iota(jnp.int32, (elements, flat_row.shape[1]), 0) == element


def hot_dofs(flat_row, dofs):
    _, dof = split_index(flat_row, dofs)
    shape = (dofs, flat_row.shape[1])
    line = lax.broadcasted_iota(jnp.int32, shape, 0).astype(jnp.int16)
    hit = line == jnp.broadcast_to(dof.astype(jnp.int16), shape)
    return jnp.where(hit, jnp.ones(shape, bf16), jnp.zeros(shape, bf16))


def as_column(row):
    elements = row.shape[1]
    line = lax.broadcasted_iota(jnp.int32, (elements, elements), 0)
    column = lax.broadcasted_iota(jnp.int32, (elements, elements), 1)
    spread = jnp.where(line == column, jnp.broadcast_to(row, (elements, elements)), 0.0)
    return jnp.sum(spread, axis=1, keepdims=True)


def wide(column, probes, dofs):
    return jnp.broadcast_to(jnp.concatenate([column] * probes, axis=0), (probes * column.shape[0], dofs))


def take_faces(picked, over_elements):
    elements = over_elements.shape[0]
    return [
        jnp.sum(jnp.where(over_elements, picked[low : low + elements], 0.0), axis=0, keepdims=True)
        for low in range(0, picked.shape[0], elements)
    ]


def spread_faces(values, over_elements):
    return jnp.concatenate(
        [jnp.where(over_elements, value, 0.0).astype(bf16) for value in values], axis=0
    )


def high_low(values):
    highs = [value.astype(bf16).astype(f32) for value in values]
    return highs + [value - high for value, high in zip(values, highs)]


def add_faces(spreads, over_dofs):
    return dot_transposed(jnp.concatenate(spreads, axis=1), over_dofs)


def add_faces_once(spreads, over_dofs):
    return jnp.transpose(dot_transposed(over_dofs, jnp.concatenate(spreads, axis=1)))


def folded(parts):
    rows = parts.shape[0] // 2
    return parts[:rows] + parts[rows:]


def as_row(lines, lanes):
    count = -(-len(lines) // 8) * 8
    spare = jnp.zeros((count - len(lines), lines[0].shape[1]), f32)
    sums = jnp.sum(jnp.concatenate(lines + [spare], axis=0), axis=1, keepdims=True)
    line = lax.broadcasted_iota(jnp.int32, (count, lanes), 0)
    lane = lax.broadcasted_iota(jnp.int32, (count, lanes), 1)
    return jnp.sum(jnp.where(line == lane, sums, 0.0), axis=0, keepdims=True)


def inner_products(first_img, second_img, source, probes, products_ref):
    elements = source.shape[0] // probes
    pairs = (
        (first_img, first_img),
        (first_img, second_img),
        (second_img, second_img),
        (first_img, source),
        (second_img, source),
    )
    lines = []
    for left, right in pairs:
        product = left * right
        for probe in range(probes):
            lines.append(
                jnp.sum(product[probe * elements : (probe + 1) * elements], axis=0, keepdims=True)
            )
    products_ref[...] = jnp.broadcast_to(as_row(lines, products_ref.shape[-1]), products_ref.shape)


def live_column(count_ref, elements):
    return lax.broadcasted_iota(jnp.int32, (elements, 1), 0) < count_ref[0, 0, 0]


def begin(refs, partner, count_ref, prepare):
    links_hbm, index_hbm, visc_hbm, rhs_hbm, *matrices_hbm = refs["operands"]
    links_ref, index_ref, visc_ref, rhs_ref, *matrix_refs, arrived = refs["scratch"]
    pairs = (
        (links_hbm, links_ref),
        (index_hbm, index_ref),
        (rhs_hbm, rhs_ref),
        (matrices_hbm[0], matrix_refs[0]),
        (visc_hbm, visc_ref),
        *zip(matrices_hbm[1:], matrix_refs[1:]),
    )
    copies = [
        pltpu.make_async_copy(held, here, arrived.at[place])
        for place, (held, here) in enumerate(pairs)
    ]
    for copy in copies:
        copy.start()
    copies[0].wait()
    copies[1].wait()
    slots_ref = refs["slots"]
    me = lax.axis_index("gz")
    for step in range(1, slots_ref.shape[0] + 1):
        slots_ref[step - 1] = slot_of(partner(me, step), links_ref, index_ref)
    prepare()
    copies[4].wait()
    probes, elements, dofs = rhs_ref.shape[3:]
    live = jnp.ones((elements, 1), f32)
    if count_ref is not None:
        live = live_column(count_ref, elements).astype(f32)
    visc = as_column(visc_ref[0, 0])
    up = wide(live * visc, probes, dofs)
    down = wide(live / visc, probes, dofs)
    refs["up"][...] = up
    refs["down"][...] = down
    copies[2].wait()
    source = rhs_ref[...].reshape(probes * elements, dofs)
    if count_ref is not None:
        source = source * wide(live, probes, dofs)
    refs["source"][...] = source
    copies[3].wait()
    smoother = two_parts(matrix_refs[0][...])
    first_pre = times_parts(source, *smoother) * down
    refs["first"][...] = first_pre
    for copy in copies[5:]:
        copy.wait()
    return first_pre, up, down, smoother


def message_places(steps, probes):
    values = steps * probes
    return values, values + probes, values + probes + steps


def message_length(steps, probes, width):
    return message_places(steps, probes)[2] * (width // lane_count) + 1


def write_row(message_ref, place, row):
    pieces = row.shape[1] // lane_count
    for piece in range(pieces):
        lanes = slice(piece * lane_count, (piece + 1) * lane_count)
        message_ref[place * pieces + piece] = row[:, lanes]


def read_row(message_ref, place, width):
    pieces = width // lane_count
    lines = range(place * pieces, (place + 1) * pieces)
    return jnp.concatenate([message_ref[line] for line in lines], axis=1)


def near_first_kernel(*refs):
    operands, refs = refs[:6], refs[6:]
    first_ref, source_ref, up_ref, down_ref, base_ref, slots_ref, hot_ref = refs[:7]
    part_refs, refs = refs[7:11], refs[11:]
    steps, _, width = slots_ref.shape
    leave_refs, scratch = refs[:steps], refs[steps:]
    visc_ref, rhs_ref, _, k_ref = scratch[2:6]
    probes, elements, dofs = rhs_ref.shape[3:]

    def prepare():
        for step in range(steps):
            hot_ref[:, step * width : (step + 1) * width] = hot_dofs(slots_ref[step], dofs)

    first_pre, up, down, smoother = begin(
        {
            "operands": operands,
            "scratch": scratch,
            "slots": slots_ref,
            "up": up_ref,
            "down": down_ref,
            "source": source_ref,
            "first": first_ref,
        },
        lambda me, step: me ^ step,
        None,
        prepare,
    )
    stiffness = two_parts(k_ref[...])
    product = times_parts(first_pre, *stiffness)
    base_ref[...] = product * up
    second_part = times_parts_once(product, *smoother).astype(bf16)
    stacked = jnp.concatenate([*two_parts(first_pre), second_part], axis=0)
    rows = probes * elements
    for part_ref, part in zip(part_refs, smoother + stiffness):
        part_ref[...] = part
    second_at, index_at, visc_at = message_places(steps, probes)
    for step in range(1, steps + 1):
        flat_row = slots_ref[step - 1]
        over_elements = hot_elements(flat_row, elements, dofs)
        over_dofs = hot_ref[:, (step - 1) * width : step * width]
        picked = dot(stacked, over_dofs)
        first_rows = take_faces(folded(picked[: 2 * rows]), over_elements)
        second_rows = take_faces(picked[2 * rows :], over_elements)
        for probe in range(probes):
            write_row(leave_refs[step - 1], second_at + probe, second_rows[probe])
            for leave_ref in leave_refs:
                write_row(leave_ref, (step - 1) * probes + probe, first_rows[probe])
        for leave_ref in leave_refs:
            write_row(leave_ref, index_at + step - 1, flat_row.astype(f32))
    visc_line = visc_at * (width // lane_count)
    for leave_ref in leave_refs:
        leave_ref[visc_line, :, :elements] = visc_ref[0, 0]


def near_second_kernel(
    probes, count_ref, source_ref, up_ref, down_ref, base_ref, slots_ref, hot_ref,
    p_high_ref, p_low_ref, k_high_ref, k_low_ref, mine_ref, *refs
):
    came_refs = refs[:-2]
    second_ref, products_ref = refs[-2:]
    steps, _, width = slots_ref.shape
    members = steps + 1
    rows, dofs = source_ref.shape
    elements = rows // probes
    second_at, index_at, visc_at = message_places(steps, probes)

    def message(step):
        return mine_ref if step == 0 else came_refs[step - 1]

    def inbound_first(member, step):
        sent = message(member ^ step)
        return [
            read_row(sent, (step - 1) * probes + probe, width) for probe in range(probes)
        ]

    own_elements = [hot_elements(slots_ref[step], elements, dofs) for step in range(steps)]

    def placed_here(values):
        spreads = [spread_faces(values[step], own_elements[step]) for step in range(steps)]
        add = add_faces if len(values[0]) > probes else add_faces_once
        return add(spreads, hot_ref[...])

    up, down = up_ref[...], down_ref[...]
    live = wide(live_column(count_ref, elements).astype(f32), probes, dofs) > 0.0
    placed = folded(placed_here([high_low(inbound_first(0, step)) for step in range(1, members)]))
    image = jnp.where(live, base_ref[...] - coupling * placed, 0.0)
    changes, back = [], []
    for member in range(1, members):
        rows_of = [
            read_row(message(member), index_at + step, width).astype(jnp.int32)
            for step in range(steps)
        ]
        over_elements = [hot_elements(flat_row, elements, dofs) for flat_row in rows_of]
        over_dofs = [hot_dofs(flat_row, dofs) for flat_row in rows_of]
        spreads = [
            spread_faces(inbound_first(member, step + 1), over_elements[step])
            for step in range(steps)
        ]
        changes.append(-coupling * add_faces_once(spreads, jnp.concatenate(over_dofs, axis=1)))
        back.append((over_elements[member - 1], over_dofs[member - 1]))
    second_pre = times_parts(image, p_high_ref[...], p_low_ref[...]) * down
    changes = times_parts_once(jnp.concatenate(changes, axis=0), p_high_ref[...], p_low_ref[...])
    second_ref[...] = second_pre
    values = []
    visc_line = visc_at * (width // lane_count)
    for member in range(1, members):
        sent = message(member)
        visc = as_column(sent[visc_line, :, :elements])
        scale = wide(1.0 / visc, probes, dofs)
        change = changes[(member - 1) * rows : member * rows] * scale
        over_elements, over_dofs = back[member - 1]
        taken = take_faces(dot(change.astype(bf16), over_dofs), over_elements)
        values.append(
            [taken[probe] + read_row(sent, second_at + probe, width) for probe in range(probes)]
        )
    placed = placed_here(values)
    second_img = times_parts_once(second_pre, k_high_ref[...], k_low_ref[...])
    second_img = second_img * up - coupling * placed
    second_img = jnp.where(live, second_img, 0.0)
    source = jnp.where(live, source_ref[...], 0.0)
    inner_products(image, second_img, source, probes, products_ref)


def leave_faces(field, probes, slots_ref, leave_ref):
    elements, dofs = field.shape[0] // probes, field.shape[1]
    members = slots_ref.shape[0] + 1
    me = lax.axis_index("gz")
    for shift in range(1, members):
        flat_row = slots_ref[shift - 1]
        over_elements = hot_elements(flat_row, elements, dofs)
        parts = jnp.concatenate(two_parts(field), axis=0)
        taken = take_faces(folded(dot(parts, hot_dofs(flat_row, dofs))), over_elements)
        target = lax.rem(me + shift, members)
        for probe in range(probes):
            leave_ref[target, pl.ds(probe, 1), :] = taken[probe]
    leave_ref[me] = jnp.zeros(leave_ref.shape[1:], f32)


def placed_faces(shape, probes, slots_ref, came_ref):
    rows, dofs = shape
    elements = rows // probes
    members = slots_ref.shape[0] + 1
    me = lax.axis_index("gz")
    total = jnp.zeros(shape, f32)
    for shift in range(1, members):
        flat_row = slots_ref[shift - 1]
        came = came_ref[lax.rem(me + shift, members)]
        values = [came[probe : probe + 1, :] for probe in range(probes)]
        spread = spread_faces(high_low(values), hot_elements(flat_row, elements, dofs))
        total += folded(add_faces([spread], hot_dofs(flat_row, dofs)))
    return total


def far_first_kernel(*refs):
    count_ref, *operands = refs[:6]
    refs = refs[6:]
    first_ref, source_ref, up_ref, down_ref, slots_ref, leave_ref = refs[:6]
    members = slots_ref.shape[0] + 1
    first_pre, *_ = begin(
        {
            "operands": operands,
            "scratch": refs[6:],
            "slots": slots_ref,
            "up": up_ref,
            "down": down_ref,
            "source": source_ref,
            "first": first_ref,
        },
        lambda me, step: lax.rem(me + step, members),
        count_ref,
        lambda: None,
    )
    leave_faces(first_pre, leave_ref.shape[1], slots_ref, leave_ref)


def far_second_kernel(
    slots_ref, up_ref, down_ref, first_ref, k_ref, p_ref, came_ref,
    image_ref, second_ref, leave_ref,
):
    probes = came_ref.shape[1]
    up = up_ref[...]
    placed = placed_faces(first_ref.shape, probes, slots_ref, came_ref)
    image = times_matrix(first_ref[...], k_ref[...]) * up - jnp.where(up > 0.0, coupling * placed, 0.0)
    image_ref[...] = image
    second_pre = times_matrix(image, p_ref[...]) * down_ref[...]
    second_ref[...] = second_pre
    leave_faces(second_pre, probes, slots_ref, leave_ref)


def far_third_kernel(
    slots_ref, up_ref, source_ref, image_ref, second_ref, k_ref, came_ref, products_ref
):
    probes = came_ref.shape[1]
    up = up_ref[...]
    placed = placed_faces(source_ref.shape, probes, slots_ref, came_ref)
    second_img = times_matrix(second_ref[...], k_ref[...]) * up - jnp.where(up > 0.0, coupling * placed, 0.0)
    inner_products(image_ref[...], second_img, source_ref[...], probes, products_ref)


def last_kernel(probes, count_ref, first_ref, second_ref, parts_ref, out_ref):
    rows, _ = first_ref.shape
    elements = rows // probes
    total = jnp.sum(parts_ref[...], axis=0)
    live = live_column(count_ref, elements)
    for probe in range(probes):
        self_one, cross_mid, self_two, load_one, load_two = (
            total[:, place * probes + probe : place * probes + probe + 1] for place in range(5)
        )
        determinant = self_one * self_two - cross_mid * cross_mid
        weight_one = (self_two * load_one - cross_mid * load_two) / determinant
        weight_two = (self_one * load_two - cross_mid * load_one) / determinant
        block = pl.ds(probe * elements, elements)
        value = weight_one * first_ref[block, :] + weight_two * second_ref[block, :]
        out_ref[block, :] = jnp.where(live, value, 0.0)


def call(kernel, in_specs, out_shapes, flops, *args, scratch=()):
    return pl.pallas_call(
        kernel,
        out_shape=out_shapes,
        in_specs=in_specs,
        out_specs=jax.tree.map(lambda _: vmem_spec, out_shapes),
        scratch_shapes=scratch,
        compiler_params=pltpu.CompilerParams(vmem_limit_bytes=vmem_grant),
        cost_estimate=pl.CostEstimate(flops=flops, bytes_accessed=1 << 20, transcendentals=0),
    )(*args)


def begin_call(kernel, out_shapes, flops, scalars, *fetched):
    links, *others = fetched
    scratch = [pltpu.SMEM(links.shape, links.dtype)]
    scratch += [pltpu.VMEM(value.shape, value.dtype) for value in others]
    return call(
        kernel,
        [smem_spec] * len(scalars) + [hbm_spec] * len(fetched),
        out_shapes,
        flops,
        *scalars,
        *(pltpu.with_memory_space_constraint(value, pltpu.HBM) for value in fetched),
        scratch=scratch + [pltpu.SemaphoreType.DMA((len(fetched),))],
    )


def near_steps(members, shapes, arguments):
    rhs, viscosity, counts, neighbours, face_index, k_matrix, p_matrix = arguments
    field, slots_shape, products_shape = shapes
    rows, dofs = field.shape
    steps, _, width = slots_shape.shape
    probes = rhs.shape[3]
    flops = 8 * rows * dofs * steps * width
    hot = jax.ShapeDtypeStruct((dofs, steps * width), bf16)
    message = jax.ShapeDtypeStruct((message_length(steps, probes, width), 1, lane_count), f32)
    part = jax.ShapeDtypeStruct(p_matrix.shape, bf16)
    first_pre, source, up, down, base, slots, hot_own, *rest = begin_call(
        near_first_kernel,
        [field] * 5 + [slots_shape, hot] + [part] * 4 + [message] * steps,
        2 * flops,
        (),
        neighbours,
        face_index,
        viscosity,
        rhs,
        p_matrix,
        k_matrix,
    )
    parts, leaving = rest[:4], rest[4:]
    came = [
        lax.ppermute(
            leaving[step - 1], "gz", [(source, source ^ step) for source in range(members)]
        )
        for step in range(1, members)
    ]
    second_pre, products = call(
        functools.partial(near_second_kernel, probes),
        [smem_spec] + [vmem_spec] * (11 + steps),
        [field, products_shape],
        6 * flops,
        counts,
        source,
        up,
        down,
        base,
        slots,
        hot_own,
        *parts,
        leaving[0],
        *came,
    )
    return first_pre, second_pre, products


def far_steps(members, shapes, arguments):
    rhs, viscosity, counts, neighbours, face_index, k_matrix, p_matrix = arguments
    field, slots_shape, products_shape = shapes
    rows, dofs = field.shape
    shifts, _, width = slots_shape.shape
    flops = 8 * rows * dofs * shifts * width
    faces = jax.ShapeDtypeStruct((members, rhs.shape[3], width), f32)

    def exchange(value):
        return lax.all_to_all(value, "gz", split_axis=0, concat_axis=0)

    first_pre, source, up, down, slots, leaving = begin_call(
        far_first_kernel,
        [field] * 4 + [slots_shape, faces],
        flops,
        (counts,),
        neighbours,
        face_index,
        viscosity,
        rhs,
        p_matrix,
    )
    first_img, second_pre, leaving = call(
        far_second_kernel,
        [vmem_spec] * 7,
        [field, field, faces],
        2 * flops,
        slots,
        up,
        down,
        first_pre,
        k_matrix,
        p_matrix,
        exchange(leaving),
    )
    products = call(
        far_third_kernel,
        [vmem_spec] * 7,
        products_shape,
        flops,
        slots,
        up,
        source,
        first_img,
        second_pre,
        k_matrix,
        exchange(leaving),
    )
    return first_pre, second_pre, products


def per_device(mesh, *arguments):
    rhs, face_index = arguments[0], arguments[4]
    probes, elements, dofs = rhs.shape[3:]
    members = mesh.shape["gz"]
    lanes = -(-5 * probes // 128) * 128
    shapes = (
        jax.ShapeDtypeStruct((probes * elements, dofs), f32),
        jax.ShapeDtypeStruct((members - 1, 1, face_index.shape[-1]), jnp.int32),
        jax.ShapeDtypeStruct((mesh.size, 1, lanes), f32),
    )
    near = 1 < members <= short_group and elements <= face_index.shape[-1]
    near = near and elements * dofs < 1 << 24
    steps = near_steps if near else far_steps
    first_pre, second_pre, products = steps(members, shapes, arguments)
    result = call(
        functools.partial(last_kernel, probes),
        [smem_spec] + [vmem_spec] * 3,
        shapes[0],
        probes * elements * dofs,
        arguments[2],
        first_pre,
        second_pre,
        lax.all_to_all(products, ("gx", "gy", "gz"), split_axis=0, concat_axis=0),
    )
    return result.reshape(rhs.shape)


def solution(mesh):
    return jax.shard_map(
        functools.partial(per_device, mesh),
        mesh=mesh,
        in_specs=(
            P("gx", "gy", "gz", None, None, None),
            P("gx", "gy", "gz", None),
            P("gx", "gy", "gz"),
            P("gx", "gy", "gz", None),
            P("gx", "gy", "gz", None, None),
            P(),
            P(),
        ),
        out_specs=P("gx", "gy", "gz", None, None, None),
        check_vma=False,
    )
```

```python
import functools

import jax
import jax.numpy as jnp
from jax import lax
from jax.experimental import pallas as pl
from jax.experimental.pallas import tpu as pltpu
from jax.sharding import PartitionSpec as P

coupling = 0.5
vmem_grant = 48 * 1024 * 1024
short_group = 4
lane_count = 128
f32 = jnp.float32
bf16 = jnp.bfloat16
vmem_spec = pl.BlockSpec(memory_space=pltpu.VMEM)
smem_spec = pl.BlockSpec(memory_space=pltpu.SMEM)
hbm_spec = pl.BlockSpec(memory_space=pltpu.HBM)


def two_parts(value):
    high = value.astype(bf16)
    return high, (value - high.astype(f32)).astype(bf16)


def dot(left, right):
    return jnp.dot(left, right, preferred_element_type=f32)


def dot_transposed(left, right):
    return lax.dot_general(left, right, (((1,), (1,)), ((), ())), preferred_element_type=f32)


def times_matrix(rows, matrix):
    return times_parts(rows, *two_parts(matrix))


def times_parts(rows, mat_high, mat_low):
    count = rows.shape[0]
    row_high, row_low = two_parts(rows)
    both = dot(jnp.concatenate([row_high, row_low], axis=0), mat_high)
    return both[:count] + (both[count:] + dot(row_high, mat_low))


def times_parts_once(rows, mat_high, mat_low):
    row_high = rows.astype(bf16)
    return dot(
        jnp.concatenate([row_high, row_high], axis=1),
        jnp.concatenate([mat_high, mat_low], axis=0),
    )


def split_index(index, dofs):
    if dofs & (dofs - 1) == 0:
        return lax.shift_right_arithmetic(index, dofs.bit_length() - 1), index & (dofs - 1)
    element = jnp.floor_divide(index, dofs)
    return element, index - element * dofs


def slot_of(target, links_ref, index_ref):
    slot = jnp.int32(-1)
    for position in range(links_ref.shape[-1]):
        slot = jnp.where(links_ref[0, 0, 0, position] == target, jnp.int32(position), slot)
    row = index_ref[0, 0, 0, pl.ds(jnp.maximum(slot, 0), 1), :]
    return jnp.where(slot >= 0, row, -1)


def hot_elements(flat_row, elements, dofs):
    element, _ = split_index(flat_row, dofs)
    return lax.broadcasted_iota(jnp.int32, (elements, flat_row.shape[1]), 0) == element


def hot_dofs(flat_row, dofs):
    _, dof = split_index(flat_row, dofs)
    shape = (dofs, flat_row.shape[1])
    line = lax.broadcasted_iota(jnp.int32, shape, 0).astype(jnp.int16)
    hit = line == jnp.broadcast_to(dof.astype(jnp.int16), shape)
    return jnp.where(hit, jnp.ones(shape, bf16), jnp.zeros(shape, bf16))


def as_column(row):
    elements = row.shape[1]
    line = lax.broadcasted_iota(jnp.int32, (elements, elements), 0)
    column = lax.broadcasted_iota(jnp.int32, (elements, elements), 1)
    spread = jnp.where(line == column, jnp.broadcast_to(row, (elements, elements)), 0.0)
    return jnp.sum(spread, axis=1, keepdims=True)


def wide(column, probes, dofs):
    return jnp.broadcast_to(jnp.concatenate([column] * probes, axis=0), (probes * column.shape[0], dofs))


def take_faces(picked, over_elements):
    elements = over_elements.shape[0]
    return [
        jnp.sum(jnp.where(over_elements, picked[low : low + elements], 0.0), axis=0, keepdims=True)
        for low in range(0, picked.shape[0], elements)
    ]


def spread_faces(values, over_elements):
    return jnp.concatenate(
        [jnp.where(over_elements, value, 0.0).astype(bf16) for value in values], axis=0
    )


def high_low(values):
    highs = [value.astype(bf16).astype(f32) for value in values]
    return highs + [value - high for value, high in zip(values, highs)]


def add_faces(spreads, over_dofs):
    return dot_transposed(jnp.concatenate(spreads, axis=1), over_dofs)


def add_faces_once(spreads, over_dofs):
    return jnp.transpose(dot_transposed(over_dofs, jnp.concatenate(spreads, axis=1)))


def folded(parts):
    rows = parts.shape[0] // 2
    return parts[:rows] + parts[rows:]


def as_row(lines, lanes):
    count = -(-len(lines) // 8) * 8
    spare = jnp.zeros((count - len(lines), lines[0].shape[1]), f32)
    sums = jnp.sum(jnp.concatenate(lines + [spare], axis=0), axis=1, keepdims=True)
    line = lax.broadcasted_iota(jnp.int32, (count, lanes), 0)
    lane = lax.broadcasted_iota(jnp.int32, (count, lanes), 1)
    return jnp.sum(jnp.where(line == lane, sums, 0.0), axis=0, keepdims=True)


def inner_products(first_img, second_img, source, probes, products_ref):
    elements = source.shape[0] // probes
    pairs = (
        (first_img, first_img),
        (first_img, second_img),
        (second_img, second_img),
        (first_img, source),
        (second_img, source),
    )
    lines = []
    for left, right in pairs:
        product = left * right
        for probe in range(probes):
            lines.append(
                jnp.sum(product[probe * elements : (probe + 1) * elements], axis=0, keepdims=True)
            )
    products_ref[...] = jnp.broadcast_to(as_row(lines, products_ref.shape[-1]), products_ref.shape)


def live_column(count_ref, elements):
    return lax.broadcasted_iota(jnp.int32, (elements, 1), 0) < count_ref[0, 0, 0]


def begin(refs, partner, count_ref, prepare):
    links_hbm, index_hbm, visc_hbm, rhs_hbm, *matrices_hbm = refs["operands"]
    links_ref, index_ref, visc_ref, rhs_ref, *matrix_refs, arrived = refs["scratch"]
    pairs = (
        (links_hbm, links_ref),
        (index_hbm, index_ref),
        (rhs_hbm, rhs_ref),
        (matrices_hbm[0], matrix_refs[0]),
        (visc_hbm, visc_ref),
        *zip(matrices_hbm[1:], matrix_refs[1:]),
    )
    copies = [
        pltpu.make_async_copy(held, here, arrived.at[place])
        for place, (held, here) in enumerate(pairs)
    ]
    for copy in copies:
        copy.start()
    copies[0].wait()
    copies[1].wait()
    slots_ref = refs["slots"]
    me = lax.axis_index("gz")
    for step in range(1, slots_ref.shape[0] + 1):
        slots_ref[step - 1] = slot_of(partner(me, step), links_ref, index_ref)
    prepare()
    copies[4].wait()
    probes, elements, dofs = rhs_ref.shape[3:]
    live = jnp.ones((elements, 1), f32)
    if count_ref is not None:
        live = live_column(count_ref, elements).astype(f32)
    visc = as_column(visc_ref[0, 0])
    up = wide(live * visc, probes, dofs)
    down = wide(live / visc, probes, dofs)
    if "up" in refs:
        refs["up"][...] = up
        refs["down"][...] = down
    copies[2].wait()
    source = rhs_ref[...].reshape(probes * elements, dofs)
    if count_ref is not None:
        source = source * wide(live, probes, dofs)
    if "source" in refs:
        refs["source"][...] = source
    copies[3].wait()
    smoother = two_parts(matrix_refs[0][...])
    first_pre = times_parts(source, *smoother) * down
    refs["first"][...] = first_pre
    for copy in copies[5:]:
        copy.wait()
    return first_pre, up, down, smoother


def message_places(steps, probes):
    values = steps * probes
    return values, values + probes, values + probes + steps


def message_length(steps, probes, width):
    return message_places(steps, probes)[2] * (width // lane_count) + 1


def write_row(message_ref, place, row):
    pieces = row.shape[1] // lane_count
    for piece in range(pieces):
        lanes = slice(piece * lane_count, (piece + 1) * lane_count)
        message_ref[place * pieces + piece] = row[:, lanes]


def read_row(message_ref, place, width):
    pieces = width // lane_count
    lines = range(place * pieces, (place + 1) * pieces)
    return jnp.concatenate([message_ref[line] for line in lines], axis=1)


def near_first_kernel(*refs):
    operands, refs = refs[:6], refs[6:]
    first_ref, base_ref, slots_ref, hot_ref = refs[:4]
    part_refs, refs = refs[4:8], refs[8:]
    steps, _, width = slots_ref.shape
    leave_refs, scratch = refs[:steps], refs[steps:]
    visc_ref, rhs_ref, _, k_ref = scratch[2:6]
    probes, elements, dofs = rhs_ref.shape[3:]

    def prepare():
        for step in range(steps):
            hot_ref[:, step * width : (step + 1) * width] = hot_dofs(slots_ref[step], dofs)

    first_pre, up, down, smoother = begin(
        {
            "operands": operands,
            "scratch": scratch,
            "slots": slots_ref,
            "first": first_ref,
        },
        lambda me, step: me ^ step,
        None,
        prepare,
    )
    stiffness = two_parts(k_ref[...])
    base = times_parts(first_pre, *stiffness) * up
    base_ref[...] = base
    second_part = (times_parts_once(base, *smoother) * down).astype(bf16)
    stacked = jnp.concatenate([*two_parts(first_pre), second_part], axis=0)
    rows = probes * elements
    for part_ref, part in zip(part_refs, smoother + stiffness):
        part_ref[...] = part
    second_at, index_at, visc_at = message_places(steps, probes)
    for step in range(1, steps + 1):
        flat_row = slots_ref[step - 1]
        over_elements = hot_elements(flat_row, elements, dofs)
        over_dofs = hot_ref[:, (step - 1) * width : step * width]
        picked = dot(stacked, over_dofs)
        first_rows = take_faces(folded(picked[: 2 * rows]), over_elements)
        second_rows = take_faces(picked[2 * rows :], over_elements)
        for probe in range(probes):
            write_row(leave_refs[step - 1], second_at + probe, second_rows[probe])
            for leave_ref in leave_refs:
                write_row(leave_ref, (step - 1) * probes + probe, first_rows[probe])
        for leave_ref in leave_refs:
            write_row(leave_ref, index_at + step - 1, flat_row.astype(f32))
    visc_line = visc_at * (width // lane_count)
    for leave_ref in leave_refs:
        leave_ref[visc_line, :, :elements] = visc_ref[0, 0]


def near_second_kernel(
    probes, count_ref, source_ref, base_ref, slots_ref, hot_ref,
    p_high_ref, p_low_ref, k_high_ref, k_low_ref, mine_ref, *refs
):
    came_refs = refs[:-2]
    second_ref, products_ref = refs[-2:]
    steps, _, width = slots_ref.shape
    members = steps + 1
    rows, dofs = source_ref.shape
    elements = rows // probes
    second_at, index_at, visc_at = message_places(steps, probes)

    def message(step):
        return mine_ref if step == 0 else came_refs[step - 1]

    def inbound_first(member, step):
        sent = message(member ^ step)
        return [
            read_row(sent, (step - 1) * probes + probe, width) for probe in range(probes)
        ]

    own_elements = [hot_elements(slots_ref[step], elements, dofs) for step in range(steps)]

    def placed_here(values):
        spreads = [spread_faces(values[step], own_elements[step]) for step in range(steps)]
        add = add_faces if len(values[0]) > probes else add_faces_once
        return add(spreads, hot_ref[...])

    visc_line = visc_at * (width // lane_count)
    own_visc = as_column(mine_ref[visc_line, :, :elements])
    up, down = wide(own_visc, probes, dofs), wide(1.0 / own_visc, probes, dofs)
    live = wide(live_column(count_ref, elements).astype(f32), probes, dofs) > 0.0
    placed = folded(placed_here([high_low(inbound_first(0, step)) for step in range(1, members)]))
    image = jnp.where(live, base_ref[...] - coupling * placed, 0.0)
    changes, back = [], []
    for member in range(1, members):
        rows_of = [
            read_row(message(member), index_at + step, width).astype(jnp.int32)
            for step in range(steps)
        ]
        over_elements = [hot_elements(flat_row, elements, dofs) for flat_row in rows_of]
        over_dofs = [hot_dofs(flat_row, dofs) for flat_row in rows_of]
        spreads = [
            spread_faces(inbound_first(member, step + 1), over_elements[step])
            for step in range(steps)
        ]
        changes.append(-coupling * add_faces_once(spreads, jnp.concatenate(over_dofs, axis=1)))
        back.append((over_elements[member - 1], over_dofs[member - 1]))
    second_pre = times_parts(image, p_high_ref[...], p_low_ref[...]) * down
    changes = times_parts_once(jnp.concatenate(changes, axis=0), p_high_ref[...], p_low_ref[...])
    second_ref[...] = second_pre
    values = []
    visc_line = visc_at * (width // lane_count)
    for member in range(1, members):
        sent = message(member)
        visc = as_column(sent[visc_line, :, :elements])
        scale = wide(1.0 / visc, probes, dofs)
        change = changes[(member - 1) * rows : member * rows] * scale
        over_elements, over_dofs = back[member - 1]
        taken = take_faces(dot(change.astype(bf16), over_dofs), over_elements)
        values.append(
            [taken[probe] + read_row(sent, second_at + probe, width) for probe in range(probes)]
        )
    placed = placed_here(values)
    second_img = times_parts_once(second_pre, k_high_ref[...], k_low_ref[...])
    second_img = second_img * up - coupling * placed
    second_img = jnp.where(live, second_img, 0.0)
    source = jnp.where(live, source_ref[...], 0.0)
    inner_products(image, second_img, source, probes, products_ref)


def leave_faces(field, probes, slots_ref, leave_ref):
    elements, dofs = field.shape[0] // probes, field.shape[1]
    members = slots_ref.shape[0] + 1
    me = lax.axis_index("gz")
    for shift in range(1, members):
        flat_row = slots_ref[shift - 1]
        over_elements = hot_elements(flat_row, elements, dofs)
        parts = jnp.concatenate(two_parts(field), axis=0)
        taken = take_faces(folded(dot(parts, hot_dofs(flat_row, dofs))), over_elements)
        target = lax.rem(me + shift, members)
        for probe in range(probes):
            leave_ref[target, pl.ds(probe, 1), :] = taken[probe]
    leave_ref[me] = jnp.zeros(leave_ref.shape[1:], f32)


def placed_faces(shape, probes, slots_ref, came_ref):
    rows, dofs = shape
    elements = rows // probes
    members = slots_ref.shape[0] + 1
    me = lax.axis_index("gz")
    total = jnp.zeros(shape, f32)
    for shift in range(1, members):
        flat_row = slots_ref[shift - 1]
        came = came_ref[lax.rem(me + shift, members)]
        values = [came[probe : probe + 1, :] for probe in range(probes)]
        spread = spread_faces(high_low(values), hot_elements(flat_row, elements, dofs))
        total += folded(add_faces([spread], hot_dofs(flat_row, dofs)))
    return total


def far_first_kernel(*refs):
    count_ref, *operands = refs[:6]
    refs = refs[6:]
    first_ref, source_ref, up_ref, down_ref, slots_ref, leave_ref = refs[:6]
    members = slots_ref.shape[0] + 1
    first_pre, *_ = begin(
        {
            "operands": operands,
            "scratch": refs[6:],
            "slots": slots_ref,
            "up": up_ref,
            "down": down_ref,
            "source": source_ref,
            "first": first_ref,
        },
        lambda me, step: lax.rem(me + step, members),
        count_ref,
        lambda: None,
    )
    leave_faces(first_pre, leave_ref.shape[1], slots_ref, leave_ref)


def far_second_kernel(
    slots_ref, up_ref, down_ref, first_ref, k_ref, p_ref, came_ref,
    image_ref, second_ref, leave_ref,
):
    probes = came_ref.shape[1]
    up = up_ref[...]
    placed = placed_faces(first_ref.shape, probes, slots_ref, came_ref)
    image = times_matrix(first_ref[...], k_ref[...]) * up - jnp.where(up > 0.0, coupling * placed, 0.0)
    image_ref[...] = image
    second_pre = times_matrix(image, p_ref[...]) * down_ref[...]
    second_ref[...] = second_pre
    leave_faces(second_pre, probes, slots_ref, leave_ref)


def far_third_kernel(
    slots_ref, up_ref, source_ref, image_ref, second_ref, k_ref, came_ref, products_ref
):
    probes = came_ref.shape[1]
    up = up_ref[...]
    placed = placed_faces(source_ref.shape, probes, slots_ref, came_ref)
    second_img = times_matrix(second_ref[...], k_ref[...]) * up - jnp.where(up > 0.0, coupling * placed, 0.0)
    inner_products(image_ref[...], second_img, source_ref[...], probes, products_ref)


def last_kernel(probes, count_ref, first_ref, second_ref, parts_ref, out_ref):
    rows, _ = first_ref.shape
    elements = rows // probes
    total = jnp.sum(parts_ref[...], axis=0)
    live = live_column(count_ref, elements)
    for probe in range(probes):
        self_one, cross_mid, self_two, load_one, load_two = (
            total[:, place * probes + probe : place * probes + probe + 1] for place in range(5)
        )
        determinant = self_one * self_two - cross_mid * cross_mid
        weight_one = (self_two * load_one - cross_mid * load_two) / determinant
        weight_two = (self_one * load_two - cross_mid * load_one) / determinant
        block = pl.ds(probe * elements, elements)
        value = weight_one * first_ref[block, :] + weight_two * second_ref[block, :]
        out_ref[block, :] = jnp.where(live, value, 0.0)


def call(kernel, in_specs, out_shapes, flops, *args, scratch=()):
    return pl.pallas_call(
        kernel,
        out_shape=out_shapes,
        in_specs=in_specs,
        out_specs=jax.tree.map(lambda _: vmem_spec, out_shapes),
        scratch_shapes=scratch,
        compiler_params=pltpu.CompilerParams(vmem_limit_bytes=vmem_grant),
        cost_estimate=pl.CostEstimate(flops=flops, bytes_accessed=1 << 20, transcendentals=0),
    )(*args)


def begin_call(kernel, out_shapes, flops, scalars, *fetched):
    links, *others = fetched
    scratch = [pltpu.SMEM(links.shape, links.dtype)]
    scratch += [pltpu.VMEM(value.shape, value.dtype) for value in others]
    return call(
        kernel,
        [smem_spec] * len(scalars) + [hbm_spec] * len(fetched),
        out_shapes,
        flops,
        *scalars,
        *(pltpu.with_memory_space_constraint(value, pltpu.HBM) for value in fetched),
        scratch=scratch + [pltpu.SemaphoreType.DMA((len(fetched),))],
    )


def near_steps(members, shapes, arguments):
    rhs, viscosity, counts, neighbours, face_index, k_matrix, p_matrix = arguments
    field, slots_shape, products_shape = shapes
    rows, dofs = field.shape
    steps, _, width = slots_shape.shape
    probes = rhs.shape[3]
    flops = 8 * rows * dofs * steps * width
    hot = jax.ShapeDtypeStruct((dofs, steps * width), bf16)
    message = jax.ShapeDtypeStruct((message_length(steps, probes, width), 1, lane_count), f32)
    part = jax.ShapeDtypeStruct(p_matrix.shape, bf16)
    first_pre, base, slots, hot_own, *rest = begin_call(
        near_first_kernel,
        [field] * 2 + [slots_shape, hot] + [part] * 4 + [message] * steps,
        2 * flops,
        (),
        neighbours,
        face_index,
        viscosity,
        rhs,
        p_matrix,
        k_matrix,
    )
    parts, leaving = rest[:4], rest[4:]
    came = [
        lax.ppermute(
            leaving[step - 1], "gz", [(source, source ^ step) for source in range(members)]
        )
        for step in range(1, members)
    ]
    second_pre, products = call(
        functools.partial(near_second_kernel, probes),
        [smem_spec] + [vmem_spec] * (9 + steps),
        [field, products_shape],
        6 * flops,
        counts,
        rhs.reshape(field.shape),
        base,
        slots,
        hot_own,
        *parts,
        leaving[0],
        *came,
    )
    return first_pre, second_pre, products


def far_steps(members, shapes, arguments):
    rhs, viscosity, counts, neighbours, face_index, k_matrix, p_matrix = arguments
    field, slots_shape, products_shape = shapes
    rows, dofs = field.shape
    shifts, _, width = slots_shape.shape
    flops = 8 * rows * dofs * shifts * width
    faces = jax.ShapeDtypeStruct((members, rhs.shape[3], width), f32)

    def exchange(value):
        return lax.all_to_all(value, "gz", split_axis=0, concat_axis=0)

    first_pre, source, up, down, slots, leaving = begin_call(
        far_first_kernel,
        [field] * 4 + [slots_shape, faces],
        flops,
        (counts,),
        neighbours,
        face_index,
        viscosity,
        rhs,
        p_matrix,
    )
    first_img, second_pre, leaving = call(
        far_second_kernel,
        [vmem_spec] * 7,
        [field, field, faces],
        2 * flops,
        slots,
        up,
        down,
        first_pre,
        k_matrix,
        p_matrix,
        exchange(leaving),
    )
    products = call(
        far_third_kernel,
        [vmem_spec] * 7,
        products_shape,
        flops,
        slots,
        up,
        source,
        first_img,
        second_pre,
        k_matrix,
        exchange(leaving),
    )
    return first_pre, second_pre, products


def per_device(mesh, *arguments):
    rhs, face_index = arguments[0], arguments[4]
    probes, elements, dofs = rhs.shape[3:]
    members = mesh.shape["gz"]
    lanes = -(-5 * probes // 128) * 128
    shapes = (
        jax.ShapeDtypeStruct((probes * elements, dofs), f32),
        jax.ShapeDtypeStruct((members - 1, 1, face_index.shape[-1]), jnp.int32),
        jax.ShapeDtypeStruct((mesh.size, 1, lanes), f32),
    )
    near = 1 < members <= short_group and elements <= face_index.shape[-1]
    near = near and elements * dofs < 1 << 24
    steps = near_steps if near else far_steps
    first_pre, second_pre, products = steps(members, shapes, arguments)
    result = call(
        functools.partial(last_kernel, probes),
        [smem_spec] + [vmem_spec] * 3,
        shapes[0],
        probes * elements * dofs,
        arguments[2],
        first_pre,
        second_pre,
        lax.all_to_all(products, ("gx", "gy", "gz"), split_axis=0, concat_axis=0),
    )
    return result.reshape(rhs.shape)


def solution(mesh):
    return jax.shard_map(
        functools.partial(per_device, mesh),
        mesh=mesh,
        in_specs=(
            P("gx", "gy", "gz", None, None, None),
            P("gx", "gy", "gz", None),
            P("gx", "gy", "gz"),
            P("gx", "gy", "gz", None),
            P("gx", "gy", "gz", None, None),
            P(),
            P(),
        ),
        out_specs=P("gx", "gy", "gz", None, None, None),
        check_vma=False,
    )
```

```python
import functools

import jax
import jax.numpy as jnp
from jax import lax
from jax.experimental import pallas as pl
from jax.experimental.pallas import tpu as pltpu
from jax.sharding import PartitionSpec as P

coupling = 0.5
vmem_grant = 48 * 1024 * 1024
short_group = 4
lane_count = 128
f32 = jnp.float32
bf16 = jnp.bfloat16
vmem_spec = pl.BlockSpec(memory_space=pltpu.VMEM)
smem_spec = pl.BlockSpec(memory_space=pltpu.SMEM)
hbm_spec = pl.BlockSpec(memory_space=pltpu.HBM)


def two_parts(value):
    high = value.astype(bf16)
    return high, (value - high.astype(f32)).astype(bf16)


def dot(left, right):
    return jnp.dot(left, right, preferred_element_type=f32)


def dot_transposed(left, right):
    return lax.dot_general(left, right, (((1,), (1,)), ((), ())), preferred_element_type=f32)


def times_matrix(rows, matrix):
    return times_parts(rows, *two_parts(matrix))


def times_parts(rows, mat_high, mat_low):
    count = rows.shape[0]
    row_high, row_low = two_parts(rows)
    both = dot(jnp.concatenate([row_high, row_low], axis=0), mat_high)
    return both[:count] + (both[count:] + dot(row_high, mat_low))


def times_parts_once(rows, mat_high, mat_low):
    row_high = rows.astype(bf16)
    return dot(
        jnp.concatenate([row_high, row_high], axis=1),
        jnp.concatenate([mat_high, mat_low], axis=0),
    )


def split_index(index, dofs):
    if dofs & (dofs - 1) == 0:
        return lax.shift_right_arithmetic(index, dofs.bit_length() - 1), index & (dofs - 1)
    element = jnp.floor_divide(index, dofs)
    return element, index - element * dofs


def slot_of(target, links_ref, index_ref):
    slot = jnp.int32(-1)
    for position in range(links_ref.shape[-1]):
        slot = jnp.where(links_ref[0, 0, 0, position] == target, jnp.int32(position), slot)
    row = index_ref[0, 0, 0, pl.ds(jnp.maximum(slot, 0), 1), :]
    return jnp.where(slot >= 0, row, -1)


def hot_elements(flat_row, elements, dofs):
    element, _ = split_index(flat_row, dofs)
    return lax.broadcasted_iota(jnp.int32, (elements, flat_row.shape[1]), 0) == element


def hot_dofs(flat_row, dofs):
    _, dof = split_index(flat_row, dofs)
    shape = (dofs, flat_row.shape[1])
    line = lax.broadcasted_iota(jnp.int32, shape, 0).astype(jnp.int16)
    hit = line == jnp.broadcast_to(dof.astype(jnp.int16), shape)
    return jnp.where(hit, jnp.ones(shape, bf16), jnp.zeros(shape, bf16))


def as_column(row):
    elements = row.shape[1]
    line = lax.broadcasted_iota(jnp.int32, (elements, elements), 0)
    column = lax.broadcasted_iota(jnp.int32, (elements, elements), 1)
    spread = jnp.where(line == column, jnp.broadcast_to(row, (elements, elements)), 0.0)
    return jnp.sum(spread, axis=1, keepdims=True)


def wide(column, probes, dofs):
    return jnp.broadcast_to(jnp.concatenate([column] * probes, axis=0), (probes * column.shape[0], dofs))


def take_faces(picked, over_elements):
    elements = over_elements.shape[0]
    return [
        jnp.sum(jnp.where(over_elements, picked[low : low + elements], 0.0), axis=0, keepdims=True)
        for low in range(0, picked.shape[0], elements)
    ]


def side_by_side(field, elements):
    half = elements // 2
    blocks = [
        jnp.concatenate([field[low : low + half], field[low + half : low + elements]], axis=1)
        for low in range(0, field.shape[0], elements)
    ]
    return jnp.concatenate(blocks, axis=0)


def spread_faces(values, over_elements):
    return jnp.concatenate(
        [jnp.where(over_elements, value, 0.0).astype(bf16) for value in values], axis=0
    )


def high_low(values):
    highs = [value.astype(bf16).astype(f32) for value in values]
    return highs + [value - high for value, high in zip(values, highs)]


def add_faces(spreads, over_dofs):
    return dot_transposed(jnp.concatenate(spreads, axis=1), over_dofs)


def add_faces_once(spreads, over_dofs):
    return jnp.transpose(dot_transposed(over_dofs, jnp.concatenate(spreads, axis=1)))


def folded(parts):
    rows = parts.shape[0] // 2
    return parts[:rows] + parts[rows:]


def as_row(lines, lanes):
    count = -(-len(lines) // 8) * 8
    spare = jnp.zeros((count - len(lines), lines[0].shape[1]), f32)
    sums = jnp.sum(jnp.concatenate(lines + [spare], axis=0), axis=1, keepdims=True)
    line = lax.broadcasted_iota(jnp.int32, (count, lanes), 0)
    lane = lax.broadcasted_iota(jnp.int32, (count, lanes), 1)
    return jnp.sum(jnp.where(line == lane, sums, 0.0), axis=0, keepdims=True)


def inner_products(first_img, second_img, source, probes, products_ref):
    elements = source.shape[0] // probes
    pairs = (
        (first_img, first_img),
        (first_img, second_img),
        (second_img, second_img),
        (first_img, source),
        (second_img, source),
    )
    lines = []
    for left, right in pairs:
        product = left * right
        for probe in range(probes):
            lines.append(
                jnp.sum(product[probe * elements : (probe + 1) * elements], axis=0, keepdims=True)
            )
    products_ref[...] = jnp.broadcast_to(as_row(lines, products_ref.shape[-1]), products_ref.shape)


def live_column(count_ref, elements):
    return lax.broadcasted_iota(jnp.int32, (elements, 1), 0) < count_ref[0, 0, 0]


def begin(refs, partner, count_ref, prepare):
    links_hbm, index_hbm, visc_hbm, rhs_hbm, *matrices_hbm = refs["operands"]
    links_ref, index_ref, visc_ref, rhs_ref, *matrix_refs, arrived = refs["scratch"]
    pairs = (
        (links_hbm, links_ref),
        (index_hbm, index_ref),
        (rhs_hbm, rhs_ref),
        (matrices_hbm[0], matrix_refs[0]),
        (visc_hbm, visc_ref),
        *zip(matrices_hbm[1:], matrix_refs[1:]),
    )
    copies = [
        pltpu.make_async_copy(held, here, arrived.at[place])
        for place, (held, here) in enumerate(pairs)
    ]
    for copy in copies:
        copy.start()
    copies[0].wait()
    copies[1].wait()
    slots_ref = refs["slots"]
    me = lax.axis_index("gz")
    for step in range(1, slots_ref.shape[0] + 1):
        slots_ref[step - 1] = slot_of(partner(me, step), links_ref, index_ref)
    prepare()
    copies[4].wait()
    probes, elements, dofs = rhs_ref.shape[3:]
    live = jnp.ones((elements, 1), f32)
    if count_ref is not None:
        live = live_column(count_ref, elements).astype(f32)
    visc = as_column(visc_ref[0, 0])
    up = wide(live * visc, probes, dofs)
    down = wide(live / visc, probes, dofs)
    refs["up"][...] = up
    refs["down"][...] = down
    copies[2].wait()
    source = rhs_ref[...].reshape(probes * elements, dofs)
    if count_ref is not None:
        source = source * wide(live, probes, dofs)
    refs["source"][...] = source
    copies[3].wait()
    smoother = two_parts(matrix_refs[0][...])
    first_pre = times_parts(source, *smoother) * down
    refs["first"][...] = first_pre
    for copy in copies[5:]:
        copy.wait()
    return first_pre, up, down, smoother


def message_places(steps, probes):
    values = steps * probes
    return values, values + probes, values + probes + steps


def message_length(steps, probes, width):
    return message_places(steps, probes)[2] * (width // lane_count) + 1


def write_row(message_ref, place, row):
    pieces = row.shape[1] // lane_count
    for piece in range(pieces):
        lanes = slice(piece * lane_count, (piece + 1) * lane_count)
        message_ref[place * pieces + piece] = row[:, lanes]


def read_row(message_ref, place, width):
    pieces = width // lane_count
    lines = range(place * pieces, (place + 1) * pieces)
    return jnp.concatenate([message_ref[line] for line in lines], axis=1)


def near_first_kernel(*refs):
    operands, refs = refs[:6], refs[6:]
    first_ref, source_ref, up_ref, down_ref, base_ref, slots_ref, hot_ref = refs[:7]
    part_refs, refs = refs[7:11], refs[11:]
    steps, _, width = slots_ref.shape
    leave_refs, scratch = refs[:steps], refs[steps:]
    visc_ref, rhs_ref, _, k_ref = scratch[2:6]
    probes, elements, dofs = rhs_ref.shape[3:]

    def prepare():
        for step in range(steps):
            hot_ref[:, step * width : (step + 1) * width] = hot_dofs(slots_ref[step], dofs)

    first_pre, up, down, smoother = begin(
        {
            "operands": operands,
            "scratch": scratch,
            "slots": slots_ref,
            "up": up_ref,
            "down": down_ref,
            "source": source_ref,
            "first": first_ref,
        },
        lambda me, step: me ^ step,
        None,
        prepare,
    )
    stiffness = two_parts(k_ref[...])
    base = times_parts(first_pre, *stiffness) * up
    base_ref[...] = base
    second_part = (times_parts_once(base, *smoother) * down).astype(bf16)
    half = elements // 2
    fields = [*two_parts(first_pre), second_part]
    stacked = jnp.concatenate([side_by_side(field, elements) for field in fields], axis=0)
    rows = probes * half
    for part_ref, part in zip(part_refs, smoother + stiffness):
        part_ref[...] = part
    second_at, index_at, visc_at = message_places(steps, probes)
    for step in range(1, steps + 1):
        flat_row = slots_ref[step - 1]
        element, _ = split_index(flat_row, dofs)
        lower = element >= half
        line = lax.broadcasted_iota(jnp.int32, (half, width), 0)
        over_elements = line == jnp.where(lower, element - half, element)
        over_dofs = hot_ref[:, (step - 1) * width : step * width]
        in_lower = over_dofs * lower.astype(f32).astype(bf16)
        picked = dot(stacked, jnp.concatenate([over_dofs - in_lower, in_lower], axis=0))
        first_rows = take_faces(folded(picked[: 2 * rows]), over_elements)
        second_rows = take_faces(picked[2 * rows :], over_elements)
        for probe in range(probes):
            write_row(leave_refs[step - 1], second_at + probe, second_rows[probe])
            for leave_ref in leave_refs:
                write_row(leave_ref, (step - 1) * probes + probe, first_rows[probe])
        for leave_ref in leave_refs:
            write_row(leave_ref, index_at + step - 1, flat_row.astype(f32))
    visc_line = visc_at * (width // lane_count)
    for leave_ref in leave_refs:
        leave_ref[visc_line, :, :elements] = visc_ref[0, 0]


def near_second_kernel(
    probes, count_ref, source_ref, up_ref, down_ref, base_ref, slots_ref, hot_ref,
    p_high_ref, p_low_ref, k_high_ref, k_low_ref, mine_ref, *refs
):
    came_refs = refs[:-2]
    second_ref, products_ref = refs[-2:]
    steps, _, width = slots_ref.shape
    members = steps + 1
    rows, dofs = source_ref.shape
    elements = rows // probes
    second_at, index_at, visc_at = message_places(steps, probes)

    def message(step):
        return mine_ref if step == 0 else came_refs[step - 1]

    def inbound_first(member, step):
        sent = message(member ^ step)
        return [
            read_row(sent, (step - 1) * probes + probe, width) for probe in range(probes)
        ]

    own_elements = [hot_elements(slots_ref[step], elements, dofs) for step in range(steps)]

    def placed_here(values):
        spreads = [spread_faces(values[step], own_elements[step]) for step in range(steps)]
        add = add_faces if len(values[0]) > probes else add_faces_once
        return add(spreads, hot_ref[...])

    up, down = up_ref[...], down_ref[...]
    live = wide(live_column(count_ref, elements).astype(f32), probes, dofs) > 0.0
    placed = folded(placed_here([high_low(inbound_first(0, step)) for step in range(1, members)]))
    image = jnp.where(live, base_ref[...] - coupling * placed, 0.0)
    changes, back = [], []
    for member in range(1, members):
        rows_of = [
            read_row(message(member), index_at + step, width).astype(jnp.int32)
            for step in range(steps)
        ]
        over_elements = [hot_elements(flat_row, elements, dofs) for flat_row in rows_of]
        over_dofs = [hot_dofs(flat_row, dofs) for flat_row in rows_of]
        spreads = [
            spread_faces(inbound_first(member, step + 1), over_elements[step])
            for step in range(steps)
        ]
        changes.append(-coupling * add_faces_once(spreads, jnp.concatenate(over_dofs, axis=1)))
        back.append((over_elements[member - 1], over_dofs[member - 1]))
    second_pre = times_parts(image, p_high_ref[...], p_low_ref[...]) * down
    changes = times_parts_once(jnp.concatenate(changes, axis=0), p_high_ref[...], p_low_ref[...])
    second_ref[...] = second_pre
    values = []
    visc_line = visc_at * (width // lane_count)
    for member in range(1, members):
        sent = message(member)
        visc = as_column(sent[visc_line, :, :elements])
        scale = wide(1.0 / visc, probes, dofs)
        change = changes[(member - 1) * rows : member * rows] * scale
        over_elements, over_dofs = back[member - 1]
        taken = take_faces(dot(change.astype(bf16), over_dofs), over_elements)
        values.append(
            [taken[probe] + read_row(sent, second_at + probe, width) for probe in range(probes)]
        )
    placed = placed_here(values)
    second_img = times_parts_once(second_pre, k_high_ref[...], k_low_ref[...])
    second_img = second_img * up - coupling * placed
    second_img = jnp.where(live, second_img, 0.0)
    source = jnp.where(live, source_ref[...], 0.0)
    inner_products(image, second_img, source, probes, products_ref)


def leave_faces(field, probes, slots_ref, leave_ref):
    elements, dofs = field.shape[0] // probes, field.shape[1]
    members = slots_ref.shape[0] + 1
    me = lax.axis_index("gz")
    for shift in range(1, members):
        flat_row = slots_ref[shift - 1]
        over_elements = hot_elements(flat_row, elements, dofs)
        parts = jnp.concatenate(two_parts(field), axis=0)
        taken = take_faces(folded(dot(parts, hot_dofs(flat_row, dofs))), over_elements)
        target = lax.rem(me + shift, members)
        for probe in range(probes):
            leave_ref[target, pl.ds(probe, 1), :] = taken[probe]
    leave_ref[me] = jnp.zeros(leave_ref.shape[1:], f32)


def placed_faces(shape, probes, slots_ref, came_ref):
    rows, dofs = shape
    elements = rows // probes
    members = slots_ref.shape[0] + 1
    me = lax.axis_index("gz")
    total = jnp.zeros(shape, f32)
    for shift in range(1, members):
        flat_row = slots_ref[shift - 1]
        came = came_ref[lax.rem(me + shift, members)]
        values = [came[probe : probe + 1, :] for probe in range(probes)]
        spread = spread_faces(high_low(values), hot_elements(flat_row, elements, dofs))
        total += folded(add_faces([spread], hot_dofs(flat_row, dofs)))
    return total


def far_first_kernel(*refs):
    count_ref, *operands = refs[:6]
    refs = refs[6:]
    first_ref, source_ref, up_ref, down_ref, slots_ref, leave_ref = refs[:6]
    members = slots_ref.shape[0] + 1
    first_pre, *_ = begin(
        {
            "operands": operands,
            "scratch": refs[6:],
            "slots": slots_ref,
            "up": up_ref,
            "down": down_ref,
            "source": source_ref,
            "first": first_ref,
        },
        lambda me, step: lax.rem(me + step, members),
        count_ref,
        lambda: None,
    )
    leave_faces(first_pre, leave_ref.shape[1], slots_ref, leave_ref)


def far_second_kernel(
    slots_ref, up_ref, down_ref, first_ref, k_ref, p_ref, came_ref,
    image_ref, second_ref, leave_ref,
):
    probes = came_ref.shape[1]
    up = up_ref[...]
    placed = placed_faces(first_ref.shape, probes, slots_ref, came_ref)
    image = times_matrix(first_ref[...], k_ref[...]) * up - jnp.where(up > 0.0, coupling * placed, 0.0)
    image_ref[...] = image
    second_pre = times_matrix(image, p_ref[...]) * down_ref[...]
    second_ref[...] = second_pre
    leave_faces(second_pre, probes, slots_ref, leave_ref)


def far_third_kernel(
    slots_ref, up_ref, source_ref, image_ref, second_ref, k_ref, came_ref, products_ref
):
    probes = came_ref.shape[1]
    up = up_ref[...]
    placed = placed_faces(source_ref.shape, probes, slots_ref, came_ref)
    second_img = times_matrix(second_ref[...], k_ref[...]) * up - jnp.where(up > 0.0, coupling * placed, 0.0)
    inner_products(image_ref[...], second_img, source_ref[...], probes, products_ref)


def last_kernel(probes, count_ref, first_ref, second_ref, parts_ref, out_ref):
    rows, _ = first_ref.shape
    elements = rows // probes
    total = jnp.sum(parts_ref[...], axis=0)
    live = live_column(count_ref, elements)
    for probe in range(probes):
        self_one, cross_mid, self_two, load_one, load_two = (
            total[:, place * probes + probe : place * probes + probe + 1] for place in range(5)
        )
        determinant = self_one * self_two - cross_mid * cross_mid
        weight_one = (self_two * load_one - cross_mid * load_two) / determinant
        weight_two = (self_one * load_two - cross_mid * load_one) / determinant
        block = pl.ds(probe * elements, elements)
        value = weight_one * first_ref[block, :] + weight_two * second_ref[block, :]
        out_ref[block, :] = jnp.where(live, value, 0.0)


def call(kernel, in_specs, out_shapes, flops, *args, scratch=()):
    return pl.pallas_call(
        kernel,
        out_shape=out_shapes,
        in_specs=in_specs,
        out_specs=jax.tree.map(lambda _: vmem_spec, out_shapes),
        scratch_shapes=scratch,
        compiler_params=pltpu.CompilerParams(vmem_limit_bytes=vmem_grant),
        cost_estimate=pl.CostEstimate(flops=flops, bytes_accessed=1 << 20, transcendentals=0),
    )(*args)


def begin_call(kernel, out_shapes, flops, scalars, *fetched):
    links, *others = fetched
    scratch = [pltpu.SMEM(links.shape, links.dtype)]
    scratch += [pltpu.VMEM(value.shape, value.dtype) for value in others]
    return call(
        kernel,
        [smem_spec] * len(scalars) + [hbm_spec] * len(fetched),
        out_shapes,
        flops,
        *scalars,
        *(pltpu.with_memory_space_constraint(value, pltpu.HBM) for value in fetched),
        scratch=scratch + [pltpu.SemaphoreType.DMA((len(fetched),))],
    )


def near_steps(members, shapes, arguments):
    rhs, viscosity, counts, neighbours, face_index, k_matrix, p_matrix = arguments
    field, slots_shape, products_shape = shapes
    rows, dofs = field.shape
    steps, _, width = slots_shape.shape
    probes = rhs.shape[3]
    flops = 8 * rows * dofs * steps * width
    hot = jax.ShapeDtypeStruct((dofs, steps * width), bf16)
    message = jax.ShapeDtypeStruct((message_length(steps, probes, width), 1, lane_count), f32)
    part = jax.ShapeDtypeStruct(p_matrix.shape, bf16)
    first_pre, source, up, down, base, slots, hot_own, *rest = begin_call(
        near_first_kernel,
        [field] * 5 + [slots_shape, hot] + [part] * 4 + [message] * steps,
        2 * flops,
        (),
        neighbours,
        face_index,
        viscosity,
        rhs,
        p_matrix,
        k_matrix,
    )
    parts, leaving = rest[:4], rest[4:]
    came = [
        lax.ppermute(
            leaving[step - 1], "gz", [(source, source ^ step) for source in range(members)]
        )
        for step in range(1, members)
    ]
    second_pre, products = call(
        functools.partial(near_second_kernel, probes),
        [smem_spec] + [vmem_spec] * (11 + steps),
        [field, products_shape],
        6 * flops,
        counts,
        source,
        up,
        down,
        base,
        slots,
        hot_own,
        *parts,
        leaving[0],
        *came,
    )
    return first_pre, second_pre, products


def far_steps(members, shapes, arguments):
    rhs, viscosity, counts, neighbours, face_index, k_matrix, p_matrix = arguments
    field, slots_shape, products_shape = shapes
    rows, dofs = field.shape
    shifts, _, width = slots_shape.shape
    flops = 8 * rows * dofs * shifts * width
    faces = jax.ShapeDtypeStruct((members, rhs.shape[3], width), f32)

    def exchange(value):
        return lax.all_to_all(value, "gz", split_axis=0, concat_axis=0)

    first_pre, source, up, down, slots, leaving = begin_call(
        far_first_kernel,
        [field] * 4 + [slots_shape, faces],
        flops,
        (counts,),
        neighbours,
        face_index,
        viscosity,
        rhs,
        p_matrix,
    )
    first_img, second_pre, leaving = call(
        far_second_kernel,
        [vmem_spec] * 7,
        [field, field, faces],
        2 * flops,
        slots,
        up,
        down,
        first_pre,
        k_matrix,
        p_matrix,
        exchange(leaving),
    )
    products = call(
        far_third_kernel,
        [vmem_spec] * 7,
        products_shape,
        flops,
        slots,
        up,
        source,
        first_img,
        second_pre,
        k_matrix,
        exchange(leaving),
    )
    return first_pre, second_pre, products


def per_device(mesh, *arguments):
    rhs, face_index = arguments[0], arguments[4]
    probes, elements, dofs = rhs.shape[3:]
    members = mesh.shape["gz"]
    lanes = -(-5 * probes // 128) * 128
    shapes = (
        jax.ShapeDtypeStruct((probes * elements, dofs), f32),
        jax.ShapeDtypeStruct((members - 1, 1, face_index.shape[-1]), jnp.int32),
        jax.ShapeDtypeStruct((mesh.size, 1, lanes), f32),
    )
    near = 1 < members <= short_group and elements <= face_index.shape[-1]
    near = near and elements * dofs < 1 << 24
    near = near and members & (members - 1) == 0 and elements % 32 == 0
    near = near and face_index.shape[-1] % lane_count == 0 and elements <= lane_count
    steps = near_steps if near else far_steps
    first_pre, second_pre, products = steps(members, shapes, arguments)
    result = call(
        functools.partial(last_kernel, probes),
        [smem_spec] + [vmem_spec] * 3,
        shapes[0],
        probes * elements * dofs,
        arguments[2],
        first_pre,
        second_pre,
        lax.all_to_all(products, ("gx", "gy", "gz"), split_axis=0, concat_axis=0),
    )
    return result.reshape(rhs.shape)


def solution(mesh):
    return jax.shard_map(
        functools.partial(per_device, mesh),
        mesh=mesh,
        in_specs=(
            P("gx", "gy", "gz", None, None, None),
            P("gx", "gy", "gz", None),
            P("gx", "gy", "gz"),
            P("gx", "gy", "gz", None),
            P("gx", "gy", "gz", None, None),
            P(),
            P(),
        ),
        out_specs=P("gx", "gy", "gz", None, None, None),
        check_vma=False,
    )
```

```python
import functools

import jax
import jax.numpy as jnp
from jax import lax
from jax.experimental import pallas as pl
from jax.experimental.pallas import tpu as pltpu
from jax.sharding import PartitionSpec as P

coupling = 0.5
vmem_grant = 48 * 1024 * 1024
short_group = 4
lane_count = 128
f32 = jnp.float32
bf16 = jnp.bfloat16
vmem_spec = pl.BlockSpec(memory_space=pltpu.VMEM)
smem_spec = pl.BlockSpec(memory_space=pltpu.SMEM)
hbm_spec = pl.BlockSpec(memory_space=pltpu.HBM)


def two_parts(value):
    high = value.astype(bf16)
    return high, (value - high.astype(f32)).astype(bf16)


def dot(left, right):
    return jnp.dot(left, right, preferred_element_type=f32)


def dot_transposed(left, right):
    return lax.dot_general(left, right, (((1,), (1,)), ((), ())), preferred_element_type=f32)


def times_matrix(rows, matrix):
    return times_parts(rows, *two_parts(matrix))


def times_parts(rows, mat_high, mat_low):
    count = rows.shape[0]
    row_high, row_low = two_parts(rows)
    both = dot(jnp.concatenate([row_high, row_low], axis=0), mat_high)
    return both[:count] + (both[count:] + dot(row_high, mat_low))


def times_parts_once(rows, mat_high, mat_low):
    row_high = rows.astype(bf16)
    return dot(
        jnp.concatenate([row_high, row_high], axis=1),
        jnp.concatenate([mat_high, mat_low], axis=0),
    )


def split_index(index, dofs):
    if dofs & (dofs - 1) == 0:
        return lax.shift_right_arithmetic(index, dofs.bit_length() - 1), index & (dofs - 1)
    element = jnp.floor_divide(index, dofs)
    return element, index - element * dofs


def slot_of(target, links_ref, index_ref):
    slot = jnp.int32(-1)
    for position in range(links_ref.shape[-1]):
        slot = jnp.where(links_ref[0, 0, 0, position] == target, jnp.int32(position), slot)
    row = index_ref[0, 0, 0, pl.ds(jnp.maximum(slot, 0), 1), :]
    return jnp.where(slot >= 0, row, -1)


def hot_elements(flat_row, elements, dofs):
    element, _ = split_index(flat_row, dofs)
    return lax.broadcasted_iota(jnp.int32, (elements, flat_row.shape[1]), 0) == element


def hot_dofs(flat_row, dofs):
    _, dof = split_index(flat_row, dofs)
    shape = (dofs, flat_row.shape[1])
    line = lax.broadcasted_iota(jnp.int32, shape, 0).astype(jnp.int16)
    hit = line == jnp.broadcast_to(dof.astype(jnp.int16), shape)
    return jnp.where(hit, jnp.ones(shape, bf16), jnp.zeros(shape, bf16))


def as_column(row):
    elements = row.shape[1]
    line = lax.broadcasted_iota(jnp.int32, (elements, elements), 0)
    column = lax.broadcasted_iota(jnp.int32, (elements, elements), 1)
    spread = jnp.where(line == column, jnp.broadcast_to(row, (elements, elements)), 0.0)
    return jnp.sum(spread, axis=1, keepdims=True)


def wide(column, probes, dofs):
    return jnp.broadcast_to(jnp.concatenate([column] * probes, axis=0), (probes * column.shape[0], dofs))


def take_faces(picked, over_elements):
    elements = over_elements.shape[0]
    return [
        jnp.sum(jnp.where(over_elements, picked[low : low + elements], 0.0), axis=0, keepdims=True)
        for low in range(0, picked.shape[0], elements)
    ]


def spread_faces(values, over_elements):
    return jnp.concatenate(
        [jnp.where(over_elements, value, 0.0).astype(bf16) for value in values], axis=0
    )


def high_low(values):
    highs = [value.astype(bf16).astype(f32) for value in values]
    return highs + [value - high for value, high in zip(values, highs)]


def add_faces(spreads, over_dofs):
    return dot_transposed(jnp.concatenate(spreads, axis=1), over_dofs)


def add_faces_once(spreads, over_dofs):
    return add_faces(spreads, over_dofs)


def folded(parts):
    rows = parts.shape[0] // 2
    return parts[:rows] + parts[rows:]


def as_row(lines, lanes):
    count = -(-len(lines) // 8) * 8
    spare = jnp.zeros((count - len(lines), lines[0].shape[1]), f32)
    sums = jnp.sum(jnp.concatenate(lines + [spare], axis=0), axis=1, keepdims=True)
    line = lax.broadcasted_iota(jnp.int32, (count, lanes), 0)
    lane = lax.broadcasted_iota(jnp.int32, (count, lanes), 1)
    return jnp.sum(jnp.where(line == lane, sums, 0.0), axis=0, keepdims=True)


def inner_products(first_img, second_img, source, probes, products_ref):
    elements = source.shape[0] // probes
    pairs = (
        (first_img, first_img),
        (first_img, second_img),
        (second_img, second_img),
        (first_img, source),
        (second_img, source),
    )
    lines = []
    for left, right in pairs:
        product = left * right
        for probe in range(probes):
            lines.append(
                jnp.sum(product[probe * elements : (probe + 1) * elements], axis=0, keepdims=True)
            )
    products_ref[...] = jnp.broadcast_to(as_row(lines, products_ref.shape[-1]), products_ref.shape)


def live_column(count_ref, elements):
    return lax.broadcasted_iota(jnp.int32, (elements, 1), 0) < count_ref[0, 0, 0]


def begin(refs, partner, count_ref, prepare):
    links_hbm, index_hbm, visc_hbm, rhs_hbm, *matrices_hbm = refs["operands"]
    links_ref, index_ref, visc_ref, rhs_ref, *matrix_refs, arrived = refs["scratch"]
    pairs = (
        (links_hbm, links_ref),
        (index_hbm, index_ref),
        (rhs_hbm, rhs_ref),
        (matrices_hbm[0], matrix_refs[0]),
        (visc_hbm, visc_ref),
        *zip(matrices_hbm[1:], matrix_refs[1:]),
    )
    copies = [
        pltpu.make_async_copy(held, here, arrived.at[place])
        for place, (held, here) in enumerate(pairs)
    ]
    for copy in copies:
        copy.start()
    copies[0].wait()
    copies[1].wait()
    slots_ref = refs["slots"]
    me = lax.axis_index("gz")
    for step in range(1, slots_ref.shape[0] + 1):
        slots_ref[step - 1] = slot_of(partner(me, step), links_ref, index_ref)
    prepare()
    copies[4].wait()
    probes, elements, dofs = rhs_ref.shape[3:]
    live = jnp.ones((elements, 1), f32)
    if count_ref is not None:
        live = live_column(count_ref, elements).astype(f32)
    visc = as_column(visc_ref[0, 0])
    up = wide(live * visc, probes, dofs)
    down = wide(live / visc, probes, dofs)
    refs["up"][...] = up
    refs["down"][...] = down
    copies[2].wait()
    source = rhs_ref[...].reshape(probes * elements, dofs)
    if count_ref is not None:
        source = source * wide(live, probes, dofs)
    refs["source"][...] = source
    copies[3].wait()
    smoother = two_parts(matrix_refs[0][...])
    first_pre = times_parts(source, *smoother) * down
    refs["first"][...] = first_pre
    for copy in copies[5:]:
        copy.wait()
    return first_pre, up, down, smoother


def message_places(steps, probes):
    values = steps * probes
    return values, values + probes, values + probes + steps


def message_length(steps, probes, width):
    return message_places(steps, probes)[2] * (width // lane_count) + 1


def write_row(message_ref, place, row):
    pieces = row.shape[1] // lane_count
    for piece in range(pieces):
        lanes = slice(piece * lane_count, (piece + 1) * lane_count)
        message_ref[place * pieces + piece] = row[:, lanes]


def read_row(message_ref, place, width):
    pieces = width // lane_count
    lines = range(place * pieces, (place + 1) * pieces)
    return jnp.concatenate([message_ref[line] for line in lines], axis=1)


def near_first_kernel(*refs):
    operands, refs = refs[:6], refs[6:]
    first_ref, source_ref, up_ref, down_ref, base_ref, slots_ref, hot_ref = refs[:7]
    part_refs, refs = refs[7:11], refs[11:]
    steps, _, width = slots_ref.shape
    leave_refs, scratch = refs[:steps], refs[steps:]
    visc_ref, rhs_ref, _, k_ref = scratch[2:6]
    probes, elements, dofs = rhs_ref.shape[3:]

    def prepare():
        for step in range(steps):
            hot_ref[:, step * width : (step + 1) * width] = hot_dofs(slots_ref[step], dofs)

    first_pre, up, down, smoother = begin(
        {
            "operands": operands,
            "scratch": scratch,
            "slots": slots_ref,
            "up": up_ref,
            "down": down_ref,
            "source": source_ref,
            "first": first_ref,
        },
        lambda me, step: me ^ step,
        None,
        prepare,
    )
    stiffness = two_parts(k_ref[...])
    base = times_parts(first_pre, *stiffness) * up
    base_ref[...] = base
    second_part = (times_parts_once(base, *smoother) * down).astype(bf16)
    stacked = jnp.concatenate([*two_parts(first_pre), second_part], axis=0)
    rows = probes * elements
    for part_ref, part in zip(part_refs, smoother + stiffness):
        part_ref[...] = part
    second_at, index_at, visc_at = message_places(steps, probes)
    for step in range(1, steps + 1):
        flat_row = slots_ref[step - 1]
        over_elements = hot_elements(flat_row, elements, dofs)
        over_dofs = hot_ref[:, (step - 1) * width : step * width]
        picked = dot(stacked, over_dofs)
        first_rows = take_faces(folded(picked[: 2 * rows]), over_elements)
        second_rows = take_faces(picked[2 * rows :], over_elements)
        for probe in range(probes):
            write_row(leave_refs[step - 1], second_at + probe, second_rows[probe])
            for leave_ref in leave_refs:
                write_row(leave_ref, (step - 1) * probes + probe, first_rows[probe])
        for leave_ref in leave_refs:
            write_row(leave_ref, index_at + step - 1, flat_row.astype(f32))
    visc_line = visc_at * (width // lane_count)
    for leave_ref in leave_refs:
        leave_ref[visc_line, :, :elements] = visc_ref[0, 0]


def near_second_kernel(
    probes, count_ref, source_ref, up_ref, down_ref, base_ref, slots_ref, hot_ref,
    p_high_ref, p_low_ref, k_high_ref, k_low_ref, mine_ref, *refs
):
    came_refs = refs[:-2]
    second_ref, products_ref = refs[-2:]
    steps, _, width = slots_ref.shape
    members = steps + 1
    rows, dofs = source_ref.shape
    elements = rows // probes
    second_at, index_at, visc_at = message_places(steps, probes)

    def message(step):
        return mine_ref if step == 0 else came_refs[step - 1]

    def inbound_first(member, step):
        sent = message(member ^ step)
        return [
            read_row(sent, (step - 1) * probes + probe, width) for probe in range(probes)
        ]

    own_elements = [hot_elements(slots_ref[step], elements, dofs) for step in range(steps)]

    def placed_here(values):
        spreads = [spread_faces(values[step], own_elements[step]) for step in range(steps)]
        add = add_faces if len(values[0]) > probes else add_faces_once
        return add(spreads, hot_ref[...])

    up, down = up_ref[...], down_ref[...]
    live = wide(live_column(count_ref, elements).astype(f32), probes, dofs) > 0.0
    placed = folded(placed_here([high_low(inbound_first(0, step)) for step in range(1, members)]))
    image = jnp.where(live, base_ref[...] - coupling * placed, 0.0)
    changes, back = [], []
    for member in range(1, members):
        rows_of = [
            read_row(message(member), index_at + step, width).astype(jnp.int32)
            for step in range(steps)
        ]
        over_elements = [hot_elements(flat_row, elements, dofs) for flat_row in rows_of]
        over_dofs = [hot_dofs(flat_row, dofs) for flat_row in rows_of]
        spreads = [
            spread_faces(inbound_first(member, step + 1), over_elements[step])
            for step in range(steps)
        ]
        changes.append(-coupling * add_faces_once(spreads, jnp.concatenate(over_dofs, axis=1)))
        back.append((over_elements[member - 1], over_dofs[member - 1]))
    second_pre = times_parts(image, p_high_ref[...], p_low_ref[...]) * down
    changes = times_parts_once(jnp.concatenate(changes, axis=0), p_high_ref[...], p_low_ref[...])
    second_ref[...] = second_pre
    values = []
    visc_line = visc_at * (width // lane_count)
    for member in range(1, members):
        sent = message(member)
        visc = as_column(sent[visc_line, :, :elements])
        scale = wide(1.0 / visc, probes, dofs)
        change = changes[(member - 1) * rows : member * rows] * scale
        over_elements, over_dofs = back[member - 1]
        taken = take_faces(dot(change.astype(bf16), over_dofs), over_elements)
        values.append(
            [taken[probe] + read_row(sent, second_at + probe, width) for probe in range(probes)]
        )
    placed = placed_here(values)
    second_img = times_parts_once(second_pre, k_high_ref[...], k_low_ref[...])
    second_img = second_img * up - coupling * placed
    second_img = jnp.where(live, second_img, 0.0)
    source = jnp.where(live, source_ref[...], 0.0)
    inner_products(image, second_img, source, probes, products_ref)


def leave_faces(field, probes, slots_ref, leave_ref):
    elements, dofs = field.shape[0] // probes, field.shape[1]
    members = slots_ref.shape[0] + 1
    me = lax.axis_index("gz")
    for shift in range(1, members):
        flat_row = slots_ref[shift - 1]
        over_elements = hot_elements(flat_row, elements, dofs)
        parts = jnp.concatenate(two_parts(field), axis=0)
        taken = take_faces(folded(dot(parts, hot_dofs(flat_row, dofs))), over_elements)
        target = lax.rem(me + shift, members)
        for probe in range(probes):
            leave_ref[target, pl.ds(probe, 1), :] = taken[probe]
    leave_ref[me] = jnp.zeros(leave_ref.shape[1:], f32)


def placed_faces(shape, probes, slots_ref, came_ref):
    rows, dofs = shape
    elements = rows // probes
    members = slots_ref.shape[0] + 1
    me = lax.axis_index("gz")
    total = jnp.zeros(shape, f32)
    for shift in range(1, members):
        flat_row = slots_ref[shift - 1]
        came = came_ref[lax.rem(me + shift, members)]
        values = [came[probe : probe + 1, :] for probe in range(probes)]
        spread = spread_faces(high_low(values), hot_elements(flat_row, elements, dofs))
        total += folded(add_faces([spread], hot_dofs(flat_row, dofs)))
    return total


def far_first_kernel(*refs):
    count_ref, *operands = refs[:6]
    refs = refs[6:]
    first_ref, source_ref, up_ref, down_ref, slots_ref, leave_ref = refs[:6]
    members = slots_ref.shape[0] + 1
    first_pre, *_ = begin(
        {
            "operands": operands,
            "scratch": refs[6:],
            "slots": slots_ref,
            "up": up_ref,
            "down": down_ref,
            "source": source_ref,
            "first": first_ref,
        },
        lambda me, step: lax.rem(me + step, members),
        count_ref,
        lambda: None,
    )
    leave_faces(first_pre, leave_ref.shape[1], slots_ref, leave_ref)


def far_second_kernel(
    slots_ref, up_ref, down_ref, first_ref, k_ref, p_ref, came_ref,
    image_ref, second_ref, leave_ref,
):
    probes = came_ref.shape[1]
    up = up_ref[...]
    placed = placed_faces(first_ref.shape, probes, slots_ref, came_ref)
    image = times_matrix(first_ref[...], k_ref[...]) * up - jnp.where(up > 0.0, coupling * placed, 0.0)
    image_ref[...] = image
    second_pre = times_matrix(image, p_ref[...]) * down_ref[...]
    second_ref[...] = second_pre
    leave_faces(second_pre, probes, slots_ref, leave_ref)


def far_third_kernel(
    slots_ref, up_ref, source_ref, image_ref, second_ref, k_ref, came_ref, products_ref
):
    probes = came_ref.shape[1]
    up = up_ref[...]
    placed = placed_faces(source_ref.shape, probes, slots_ref, came_ref)
    second_img = times_matrix(second_ref[...], k_ref[...]) * up - jnp.where(up > 0.0, coupling * placed, 0.0)
    inner_products(image_ref[...], second_img, source_ref[...], probes, products_ref)


def last_kernel(probes, count_ref, first_ref, second_ref, parts_ref, out_ref):
    rows, _ = first_ref.shape
    elements = rows // probes
    total = jnp.sum(parts_ref[...], axis=0)
    live = live_column(count_ref, elements)
    for probe in range(probes):
        self_one, cross_mid, self_two, load_one, load_two = (
            total[:, place * probes + probe : place * probes + probe + 1] for place in range(5)
        )
        determinant = self_one * self_two - cross_mid * cross_mid
        weight_one = (self_two * load_one - cross_mid * load_two) / determinant
        weight_two = (self_one * load_two - cross_mid * load_one) / determinant
        block = pl.ds(probe * elements, elements)
        value = weight_one * first_ref[block, :] + weight_two * second_ref[block, :]
        out_ref[block, :] = jnp.where(live, value, 0.0)


def call(kernel, in_specs, out_shapes, flops, *args, scratch=()):
    return pl.pallas_call(
        kernel,
        out_shape=out_shapes,
        in_specs=in_specs,
        out_specs=jax.tree.map(lambda _: vmem_spec, out_shapes),
        scratch_shapes=scratch,
        compiler_params=pltpu.CompilerParams(vmem_limit_bytes=vmem_grant),
        cost_estimate=pl.CostEstimate(flops=flops, bytes_accessed=1 << 20, transcendentals=0),
    )(*args)


def begin_call(kernel, out_shapes, flops, scalars, *fetched):
    links, *others = fetched
    scratch = [pltpu.SMEM(links.shape, links.dtype)]
    scratch += [pltpu.VMEM(value.shape, value.dtype) for value in others]
    return call(
        kernel,
        [smem_spec] * len(scalars) + [hbm_spec] * len(fetched),
        out_shapes,
        flops,
        *scalars,
        *(pltpu.with_memory_space_constraint(value, pltpu.HBM) for value in fetched),
        scratch=scratch + [pltpu.SemaphoreType.DMA((len(fetched),))],
    )


def near_steps(members, shapes, arguments):
    rhs, viscosity, counts, neighbours, face_index, k_matrix, p_matrix = arguments
    field, slots_shape, products_shape = shapes
    rows, dofs = field.shape
    steps, _, width = slots_shape.shape
    probes = rhs.shape[3]
    flops = 8 * rows * dofs * steps * width
    hot = jax.ShapeDtypeStruct((dofs, steps * width), bf16)
    message = jax.ShapeDtypeStruct((message_length(steps, probes, width), 1, lane_count), f32)
    part = jax.ShapeDtypeStruct(p_matrix.shape, bf16)
    first_pre, source, up, down, base, slots, hot_own, *rest = begin_call(
        near_first_kernel,
        [field] * 5 + [slots_shape, hot] + [part] * 4 + [message] * steps,
        2 * flops,
        (),
        neighbours,
        face_index,
        viscosity,
        rhs,
        p_matrix,
        k_matrix,
    )
    parts, leaving = rest[:4], rest[4:]
    came = [
        lax.ppermute(
            leaving[step - 1], "gz", [(source, source ^ step) for source in range(members)]
        )
        for step in range(1, members)
    ]
    second_pre, products = call(
        functools.partial(near_second_kernel, probes),
        [smem_spec] + [vmem_spec] * (11 + steps),
        [field, products_shape],
        6 * flops,
        counts,
        source,
        up,
        down,
        base,
        slots,
        hot_own,
        *parts,
        leaving[0],
        *came,
    )
    return first_pre, second_pre, products


def far_steps(members, shapes, arguments):
    rhs, viscosity, counts, neighbours, face_index, k_matrix, p_matrix = arguments
    field, slots_shape, products_shape = shapes
    rows, dofs = field.shape
    shifts, _, width = slots_shape.shape
    flops = 8 * rows * dofs * shifts * width
    faces = jax.ShapeDtypeStruct((members, rhs.shape[3], width), f32)

    def exchange(value):
        return lax.all_to_all(value, "gz", split_axis=0, concat_axis=0)

    first_pre, source, up, down, slots, leaving = begin_call(
        far_first_kernel,
        [field] * 4 + [slots_shape, faces],
        flops,
        (counts,),
        neighbours,
        face_index,
        viscosity,
        rhs,
        p_matrix,
    )
    first_img, second_pre, leaving = call(
        far_second_kernel,
        [vmem_spec] * 7,
        [field, field, faces],
        2 * flops,
        slots,
        up,
        down,
        first_pre,
        k_matrix,
        p_matrix,
        exchange(leaving),
    )
    products = call(
        far_third_kernel,
        [vmem_spec] * 7,
        products_shape,
        flops,
        slots,
        up,
        source,
        first_img,
        second_pre,
        k_matrix,
        exchange(leaving),
    )
    return first_pre, second_pre, products


def per_device(mesh, *arguments):
    rhs, face_index = arguments[0], arguments[4]
    probes, elements, dofs = rhs.shape[3:]
    members = mesh.shape["gz"]
    lanes = -(-5 * probes // 128) * 128
    shapes = (
        jax.ShapeDtypeStruct((probes * elements, dofs), f32),
        jax.ShapeDtypeStruct((members - 1, 1, face_index.shape[-1]), jnp.int32),
        jax.ShapeDtypeStruct((mesh.size, 1, lanes), f32),
    )
    near = 1 < members <= short_group and elements <= face_index.shape[-1]
    near = near and elements * dofs < 1 << 24
    near = near and members & (members - 1) == 0 and elements <= lane_count
    near = near and face_index.shape[-1] % lane_count == 0
    steps = near_steps if near else far_steps
    first_pre, second_pre, products = steps(members, shapes, arguments)
    result = call(
        functools.partial(last_kernel, probes),
        [smem_spec] + [vmem_spec] * 3,
        shapes[0],
        probes * elements * dofs,
        arguments[2],
        first_pre,
        second_pre,
        lax.all_to_all(products, ("gx", "gy", "gz"), split_axis=0, concat_axis=0),
    )
    return result.reshape(rhs.shape)


def solution(mesh):
    return jax.shard_map(
        functools.partial(per_device, mesh),
        mesh=mesh,
        in_specs=(
            P("gx", "gy", "gz", None, None, None),
            P("gx", "gy", "gz", None),
            P("gx", "gy", "gz"),
            P("gx", "gy", "gz", None),
            P("gx", "gy", "gz", None, None),
            P(),
            P(),
        ),
        out_specs=P("gx", "gy", "gz", None, None, None),
        check_vma=False,
    )
```
